128 devices in a mesh: dp: 32 (over y_lo, z, x), tensor: 4 (over y_hi, core).
Axes of the slice: x: 4, y: 4 (y_hi: 2, y_lo: 2; y = y_hi * 2 + y_lo), z: 4, core: 2. Of those that a mesh axis runs over, the one named last changes fastest.
Arguments:
- tokens: bfloat16 [32768, 1024], P(('dp', 'tensor')), may hold values from -6 to 6
- cotangent: bfloat16 [32768, 1024], P(('dp', 'tensor')), may hold values from -6 to 6
- qk_w: float32 [2, 1024, 1024], P(None, 'dp', 'tensor')
- vg_w: float32 [2, 1024, 1728], P(None, 'dp', 'tensor'), may hold values from -0.1875 to 0.1875
- mlp_w: float32 [2, 1024, 1728], P(None, 'dp', 'tensor'), may hold values from -0.1875 to 0.1875
- out_w: float32 [2, 1728, 1024], P(None, 'tensor', 'dp'), may hold values from -0.15625 to 0.15625
- qk_mom: float32 [2, 1024, 1024], P(None, 'dp', 'tensor'), may hold values from -512 to 512
- vg_mom: float32 [2, 1024, 1728], P(None, 'dp', 'tensor'), may hold values from -512 to 512
- mlp_mom: float32 [2, 1024, 1728], P(None, 'dp', 'tensor'), may hold values from -512 to 512
- out_mom: float32 [2, 1728, 1024], P(None, 'tensor', 'dp'), may hold values from -512 to 512
- norm_params: float32 [5824], replicated
- norm_moment: float32 [5824], replicated, may hold values from -128 to 128
- norm_second: float32 [5824], replicated, may hold values from 1736.704 to 6881.28
- decay_gap: float32 [4], P('tensor'), may hold values from 0.0005 to 0.03
- seq_length: int32 [64], replicated, may hold values from 1 to 1023, as said below
- seq_group: int32 [64], replicated, may hold values from 0 to 31, as said below
Outputs:
- mixed_out: bfloat16 [32768, 1024], P(('dp', 'tensor'))
- input_grad: float32 [32768, 1024], P(('dp', 'tensor'))
- qk_mom_new: float32 [2, 1024, 1024], P(None, 'dp', 'tensor')
- vg_mom_new: float32 [2, 1024, 1728], P(None, 'dp', 'tensor')
- mlp_mom_new: float32 [2, 1024, 1728], P(None, 'dp', 'tensor')
- out_mom_new: float32 [2, 1728, 1024], P(None, 'tensor', 'dp')
- qk_new: float32 [2, 1024, 1024], P(None, 'dp', 'tensor')
- vg_new: float32 [2, 1024, 1728], P(None, 'dp', 'tensor')
- mlp_new: float32 [2, 1024, 1728], P(None, 'dp', 'tensor')
- out_new: float32 [2, 1728, 1024], P(None, 'tensor', 'dp')
- norm_moment_new: float32 [5824], replicated
- norm_second_new: float32 [5824], replicated
- norm_new: float32 [5824], replicated
The draws below stay inside these ranges and needn't reach their ends.
Inputs may be any that keep to these rules, and one draw needn't show every extreme that they name: `seq_group`: every data group holds exactly 2 sequences. `seq_length`: in every group the lowest-numbered sequence is longer than (3) * 256 tokens; a group's lengths add up to between (3) * 256 + 2 and 1024, and some group reaches 1024.
All inputs are finite; a program needn't handle non-finite values.
Results may differ from the reference program's by a relative error of at most 0.0098.
Values may be sent and summed in bfloat16 or wider, within the bound.
No kernel may reach another device: no remote copies, remote signals or barrier semaphores. Data moves between devices by JAX's collectives and lax.ppermute only.
A program may use at most 128 MiB of HBM per device.

```python
import math
import jax
import jax.numpy as jnp
from jax import lax

D = 1024
HEADS = 4
VH = 432
FF = 1728
TOK_DEV = 256
SEQ_GROUP = 2
NS_ITERS = 5
OPT_STEP = 10
VD = 1728
SMALL = 5824
TOKENS = 32768
N_DP = 32
N_TENSOR = 4


def sequence_plan(key):
    keys = jax.random.split(key, 5)
    group_tok = N_TENSOR * TOK_DEV
    base = (N_TENSOR - 1) * TOK_DEV
    spare = group_tok - base - SEQ_GROUP
    totals = base + SEQ_GROUP + jax.random.randint(keys[0], (N_DP,), 0, spare + 1)
    full_group = jax.random.randint(keys[1], (), 0, N_DP)
    is_full = jnp.arange(N_DP) == full_group
    totals = jnp.where(is_full, group_tok, totals)
    room = totals - base - SEQ_GROUP + 1
    long_len = base + 1 + jax.random.randint(keys[2], (N_DP,), 0, 1 << 20) % room
    long_len = jnp.where(is_full, group_tok - SEQ_GROUP + 1, long_len)
    free = totals - long_len - (SEQ_GROUP - 1)
    shares = jax.random.randint(keys[3], (N_DP, SEQ_GROUP - 1), 1, 5)
    portion = free[:, None] * shares // jnp.sum(shares, axis=1, keepdims=True)
    portion = portion.at[:, -1].add(free - jnp.sum(portion, axis=1))
    lengths = jnp.concatenate([long_len[:, None], 1 + portion], axis=1).astype(jnp.int32)
    order = jnp.sort(jax.random.permutation(keys[4], N_DP * SEQ_GROUP).reshape(N_DP, SEQ_GROUP), axis=1)
    group_of = jnp.broadcast_to(jnp.arange(N_DP, dtype=jnp.int32)[:, None], (N_DP, SEQ_GROUP))
    seq_len = jnp.zeros((N_DP * SEQ_GROUP,), jnp.int32).at[order.reshape(-1)].set(lengths.reshape(-1))
    seq_grp = jnp.zeros((N_DP * SEQ_GROUP,), jnp.int32).at[order.reshape(-1)].set(group_of.reshape(-1))
    return (seq_len, seq_grp)


def draw_seq_length(key, part):
    plan = sequence_plan(key)
    return plan[0]


def draw_seq_group(key, part):
    plan = sequence_plan(key)
    return plan[1]


def draw_qk_w(key, part):
    key = jax.random.fold_in(key, 11)
    shared_key, own_key = jax.random.split(key)
    shared = jax.random.normal(shared_key, (D, D), jnp.float32)
    own = jax.random.normal(own_key, (D, D), jnp.float32)
    return jnp.stack([shared, 0.6 * shared + 0.8 * own]) * D ** (-0.5)


def draw_norm_params(key, part):
    key = jax.random.fold_in(key, 12)
    keys = jax.random.split(key, 5)
    gain_one = jax.random.uniform(keys[0], (D,), jnp.float32, 0.5, 1.5)
    shift_one = 0.3 * jax.random.normal(keys[1], (D,), jnp.float32)
    group_gain = jax.random.uniform(keys[2], (HEADS * VH,), jnp.float32, 0.5, 1.5)
    gain_two = jax.random.uniform(keys[3], (D,), jnp.float32, 0.5, 1.5)
    shift_two = 0.3 * jax.random.normal(keys[4], (D,), jnp.float32)
    return jnp.concatenate([gain_one, shift_one, group_gain, gain_two, shift_two])


def level_of(key, extent, cuts, low, top_value):
    def one(dim, blocks):
        heights = jax.random.uniform(jax.random.fold_in(jax.random.fold_in(key, 6), dim), (blocks,), jnp.float32, low / len(cuts), top_value / len(cuts))
        return jnp.repeat(jnp.exp(heights), extent[dim] // blocks).reshape((-1,) + (1,) * (len(extent) - dim - 1))

    level = one(*cuts[0])
    for cut in cuts[1:]:
        level = level * one(*cut)
    return level


def gaussian(key, shape, deviation, bound, cuts=(), held_as=jnp.bfloat16):
    values = jax.random.normal(key, shape, jnp.float32) * deviation
    if len(cuts) > 0:
        values = level_of(key, shape, cuts, -0.22, 0.18) * values
    return jnp.clip(values, min=-bound, max=bound).astype(held_as)


def setup_inputs(seed: int = 0) -> dict:
    key_of = jax.random.split(jax.random.key(seed), 17)
    return {
        "tokens": gaussian(key_of[0], (TOKENS, D), 1.0, 6.0, ((0, 128),)),
        "cotangent": gaussian(key_of[1], (TOKENS, D), 1.0, 6.0, ((0, 128),)),
        "qk_w": draw_qk_w(jax.random.fold_in(key_of[16], 71), 0),
        "vg_w": gaussian(key_of[3], (2, D, VD), D ** -0.5, 0.1875, ((1, 32), (2, 4)), jnp.float32),
        "mlp_w": gaussian(key_of[4], (2, D, FF), D ** -0.5, 0.1875, ((1, 32), (2, 4)), jnp.float32),
        "out_w": gaussian(key_of[5], (2, VD, D), VD ** -0.5, 0.15625, ((1, 4), (2, 32)), jnp.float32),
        "qk_mom": gaussian(key_of[6], (2, D, D), (0.5 * TOKENS ** 0.5), 512.0, ((1, 32), (2, 4)), jnp.float32),
        "vg_mom": gaussian(key_of[7], (2, D, VD), (0.5 * TOKENS ** 0.5), 512.0, ((1, 32), (2, 4)), jnp.float32),
        "mlp_mom": gaussian(key_of[8], (2, D, FF), (0.5 * TOKENS ** 0.5), 512.0, ((1, 32), (2, 4)), jnp.float32),
        "out_mom": gaussian(key_of[9], (2, VD, D), (0.5 * TOKENS ** 0.5), 512.0, ((1, 4), (2, 32)), jnp.float32),
        "norm_params": draw_norm_params(jax.random.fold_in(key_of[16], 71), 0),
        "norm_moment": gaussian(key_of[11], (SMALL,), (0.11 * TOKENS ** 0.5), 128.0, (), jnp.float32),
        "norm_second": jnp.clip(jnp.exp(jax.random.uniform(key_of[12], (SMALL,), jnp.float32, math.log(1736.704), math.log(6881.28))), 1736.704, 6881.28),
        "decay_gap": jnp.clip(jnp.exp(math.log(0.03) - 4.0943445 * jax.random.uniform(key_of[13], (HEADS,), jnp.float32) ** level_of(key_of[13], (HEADS,), ((0, 4),), -0.2, 0.2)), 0.0005, 0.03),
        "seq_length": draw_seq_length(jax.random.fold_in(key_of[16], 71), 0),
        "seq_group": draw_seq_group(jax.random.fold_in(key_of[16], 71), 0),
    }


norm_eps = 1e-05
group_eps = 0.01
ns_first = 3.4445
ns_second = -4.775
ns_third = 2.0315
muon_rate = 0.15
muon_beta = 0.95
decay_rate = 0.01
adam_rate = 0.6
beta_first = 0.9
beta_second = 0.95
adam_eps = 1e-08
highest = lax.Precision.HIGHEST

@jax.custom_vjp
def low(v):
    return lax.optimization_barrier(v.astype(jnp.bfloat16)).astype(jnp.float32)

@jax.custom_vjp
def low_back(v):
    return v

def low_keep(v):
    return (low(v), None)

def low_pass(kept, grad):
    return (grad,)

def back_keep(v):
    return (v, None)

def back_low(kept, grad):
    return (low(grad),)
low.defvjp(low_keep, low_pass)
low_back.defvjp(back_keep, back_low)

def matmul(left, right):
    return jnp.dot(left, right, precision=highest)

def layer_norm(values, gain, shift):
    centre = values - lax.optimization_barrier(jnp.mean(values, axis=-1, keepdims=True))
    spread = lax.rsqrt(lax.optimization_barrier(jnp.mean(centre * centre, axis=-1, keepdims=True)) + norm_eps)
    return centre * spread * gain + shift

def rotation_tables(slots, key_dim):
    freqs = 1.0 / 10000.0 ** jnp.linspace(0.0, 1.0, key_dim // 2, dtype=jnp.float32)
    angles = jnp.arange(slots, dtype=jnp.float32)[:, None] * freqs[None, :]
    return (jnp.cos(angles)[:, None, :], jnp.sin(angles)[:, None, :])

def rotate(values, cos_table, sin_table):
    pairs = values.reshape(values.shape[:-1] + (values.shape[-1] // 2, 2))
    first = pairs[..., 0]
    second = pairs[..., 1]
    turned = jnp.stack([first * cos_table - second * sin_table, second * cos_table + first * sin_table], axis=-1)
    return turned.reshape(values.shape)

def sequence_labels(seq_length, seq_group, group, slots):
    mine = seq_group == group
    lengths = jnp.where(mine, seq_length, 0).astype(jnp.int32)
    ends = jnp.cumsum(lengths, dtype=jnp.int32)
    starts = ends - lengths
    place = jnp.arange(slots, dtype=jnp.int32)[:, None]
    inside = mine[None, :] & (place >= starts[None, :]) & (place < ends[None, :])
    number = jnp.arange(1, seq_length.shape[0] + 1, dtype=jnp.int32)
    return lax.optimization_barrier(jnp.sum(jnp.where(inside, number[None, :], 0), axis=1, dtype=jnp.int32))

def decay_mask(labels, gaps):
    slots = labels.shape[0]
    place = jnp.arange(slots, dtype=jnp.int32)
    apart = place[:, None] - place[None, :]
    linked = (labels[:, None] == labels[None, :]) & (labels[:, None] > 0) & (apart >= 0)
    steps = jnp.maximum(apart, 0).astype(jnp.float32)
    weight = jnp.exp(steps[None, :, :] * jnp.log1p(-gaps)[:, None, None])
    return jnp.where(linked[None], weight, 0.0)

def orthogonal(matrix):
    current = matrix / (jnp.sqrt(jnp.sum(matrix * matrix)) + 1e-07)
    for turn in range(NS_ITERS):
        gram = matmul(current, current.T)
        blend = ns_second * gram + ns_third * matmul(gram, gram)
        current = ns_first * current + matmul(blend, current)
    return current

def reference(tokens, cotangent, qk_w, vg_w, mlp_w, out_w, qk_mom, vg_mom, mlp_mom, out_mom, norm_params, norm_moment, norm_second, decay_gap, seq_length, seq_group):
    width = D
    value_width = HEADS * VH
    key_dim = width // HEADS
    key_scale = key_dim ** (-0.5)
    slots = N_TENSOR * TOK_DEV
    labels_all = jax.vmap(lambda group: sequence_labels(seq_length, seq_group, group, slots))(jnp.arange(N_DP, dtype=jnp.int32))
    cos_table, sin_table = rotation_tables(slots, key_dim)

    def forward(inputs, query_key, value_gate, feed_in, feed_out, params):
        gain_one = params[0:width]
        shift_one = params[width:2 * width]
        group_gain = params[2 * width:2 * width + value_width]
        gain_two = params[2 * width + value_width:3 * width + value_width]
        shift_two = params[3 * width + value_width:4 * width + value_width]
        w_query = low(query_key[0])
        w_key = low(query_key[1])
        w_value = low(value_gate[0])
        w_gate = low(value_gate[1])
        w_ffgate = low(feed_in[0])
        w_ffup = low(feed_in[1])
        w_retout = low(feed_out[0])
        w_down = low(feed_out[1])

        def group_step(carry, item):
            rows, labels = item
            mask = decay_mask(labels, decay_gap)
            normed_one = low(layer_norm(rows, gain_one, shift_one))
            query = low_back(matmul(normed_one, w_query)).reshape(slots, HEADS, key_dim)
            keys = low_back(matmul(normed_one, w_key) * key_scale).reshape(slots, HEADS, key_dim)
            values = low(low_back(matmul(normed_one, w_value))).reshape(slots, HEADS, VH)
            gate = low_back(matmul(normed_one, w_gate))
            query_rot = low(rotate(query, cos_table, sin_table))
            key_rot = low(rotate(keys, cos_table, sin_table))
            scores = low_back(jnp.einsum('nhk,mhk->hnm', query_rot, key_rot, precision=highest))
            weights = low(scores * mask)
            retained = low_back(jnp.einsum('hnm,mhv->nhv', weights, values, precision=highest))
            normed = retained * lax.rsqrt(lax.optimization_barrier(jnp.mean(retained * retained, axis=-1, keepdims=True)) + group_eps)
            grouped = normed.reshape(slots, value_width) * group_gain
            mixed = low(grouped * (gate * jax.nn.sigmoid(gate)))
            middle = rows + low_back(matmul(mixed, w_retout))
            normed_two = low(layer_norm(middle, gain_two, shift_two))
            pre_gate = low_back(matmul(normed_two, w_ffgate))
            pre_up = low_back(matmul(normed_two, w_ffup))
            hidden = low(jax.nn.gelu(pre_gate, approximate=False) * pre_up)
            return (carry, middle + low_back(matmul(hidden, w_down)))
        carry, blocks = lax.scan(jax.checkpoint(group_step), None, (inputs.reshape(N_DP, slots, width), labels_all))
        return blocks.reshape(N_DP * slots, width)
    inputs = tokens.astype(jnp.float32)
    result, pullback = jax.vjp(forward, inputs, qk_w, vg_w, mlp_w, out_w, norm_params)
    grad_input, grad_qk, grad_vg, grad_mlp, grad_out, grad_small = pullback(cotangent.astype(jnp.float32))
    mom_qk = muon_beta * qk_mom + grad_qk
    mom_vg = muon_beta * vg_mom + grad_vg
    mom_mlp = muon_beta * mlp_mom + grad_mlp
    mom_out = muon_beta * out_mom + grad_out
    shrink = 1.0 - muon_rate * decay_rate
    square_scale = 0.2 * math.sqrt(width)
    wide_scale = 0.2 * math.sqrt(max(width, value_width))
    new_qk = qk_w * shrink - muon_rate * (jnp.stack([orthogonal(mom_qk[0]), orthogonal(mom_qk[1])]) * square_scale)
    new_vg = vg_w * shrink - muon_rate * (jnp.stack([orthogonal(mom_vg[0]), orthogonal(mom_vg[1])]) * wide_scale)
    new_mlp = mlp_w * shrink - muon_rate * (jnp.stack([orthogonal(mom_mlp[0]), orthogonal(mom_mlp[1])]) * wide_scale)
    new_out = out_w * shrink - muon_rate * (jnp.stack([orthogonal(mom_out[0].T).T, orthogonal(mom_out[1].T).T]) * wide_scale)
    moment_new = beta_first * norm_moment + (1.0 - beta_first) * grad_small
    second_new = beta_second * norm_second + (1.0 - beta_second) * grad_small * grad_small
    params_new = norm_params - adam_rate * (moment_new / (1.0 - beta_first ** OPT_STEP)) / (jnp.sqrt(second_new / (1.0 - beta_second ** OPT_STEP)) + adam_eps)
    return (result.astype(jnp.bfloat16), grad_input, mom_qk, mom_vg, mom_mlp, mom_out, new_qk, new_vg, new_mlp, new_out, moment_new, second_new, params_new)
```

```python
import math

import jax
import jax.numpy as jnp
import numpy as np
from jax import lax
from jax.sharding import Mesh
from jax.sharding import PartitionSpec as P

HEADS = 4
NS_ITERS = 5
OPT_STEP = 10
KEY = 256
VAL = 432
LANES = 512
BLOCK = 32

norm_eps = 1e-05
group_eps = 0.01
ns_first = 3.4445
ns_second = -4.775
ns_third = 2.0315
muon_rate = 0.15
muon_beta = 0.95
decay_rate = 0.01
adam_rate = 0.6
beta_first = 0.9
beta_second = 0.95
adam_eps = 1e-08

AXES = ("y_lo", "z_hi", "z_lo", "x", "y_hi", "core")
SIZES = (2, 2, 2, 4, 2, 2)
DP = ("y_lo", "z_hi", "z_lo", "x")
TENSOR = ("y_hi", "core")
bf16 = jnp.bfloat16
f32 = jnp.float32


def swap(values, axis):
    return lax.ppermute(values, axis, [(0, 1), (1, 0)])


def dot(left, right, dims):
    return lax.dot_general(left, right, (dims, ((), ())), preferred_element_type=f32)


def nn(left, right):
    return dot(left, right, ((1,), (0,)))


def nt(left, right):
    return dot(left, right, ((1,), (1,)))


def tn(left, right):
    return dot(left, right, ((0,), (0,)))


def split(values):
    high = lax.reduce_precision(values, 8, 7)
    return high.astype(bf16), (values - high).astype(bf16)


def widen(values):
    return jnp.pad(values, ((0, 0),) * (values.ndim - 1) + ((0, LANES - values.shape[-1]),))


def tensor_gather(own):
    far = swap(own, "y_hi")
    near = jnp.concatenate([own, far], axis=0)
    return jnp.concatenate([near, swap(near, "core")], axis=0)


def tensor_sum(make):
    other = swap(make(1).astype(bf16), "core")
    mine = make(0) + other.astype(f32)
    half = mine.shape[0] // 2
    return mine[:half] + swap(mine[half:].astype(bf16), "y_hi").astype(f32)


def normalize(values):
    centre = values - jnp.mean(values, axis=-1, keepdims=True)
    spread = lax.rsqrt(jnp.mean(centre * centre, axis=-1, keepdims=True) + norm_eps)
    return centre * spread, spread


def norm_back(grad_out, gain, normed, spread):
    grad_normed = grad_out * gain
    return spread * (
        grad_normed
        - jnp.mean(grad_normed, axis=-1, keepdims=True)
        - normed * jnp.mean(grad_normed * normed, axis=-1, keepdims=True)
    )


def rotate(values, cos_table, sin_table):
    half = KEY // 2
    first, second = values[:, :half], values[:, half:]
    return jnp.concatenate(
        [first * cos_table - second * sin_table, second * cos_table + first * sin_table], axis=1
    )


def pairs_apart(values):
    shape = values.shape
    return jnp.swapaxes(values.reshape(shape[:-1] + (KEY // 2, 2)), -1, -2).reshape(shape)


def pairs_together(values):
    shape = values.shape
    return jnp.swapaxes(values.reshape(shape[:-1] + (2, KEY // 2)), -1, -2).reshape(shape)


def sequence_labels(seq_length, seq_group, group, place):
    mine = seq_group == group
    lengths = jnp.where(mine, seq_length, 0)
    ends = jnp.cumsum(lengths, dtype=jnp.int32)
    starts = ends - lengths
    inside = mine[None, :] & (place[:, None] >= starts[None, :]) & (place[:, None] < ends[None, :])
    number = jnp.arange(1, seq_length.shape[0] + 1, dtype=jnp.int32)
    return jnp.sum(jnp.where(inside, number[None, :], 0), axis=1, dtype=jnp.int32)


def shards(
    tokens,
    cotangent,
    qk_w,
    vg_w,
    mlp_w,
    out_w,
    qk_mom,
    vg_mom,
    mlp_mom,
    out_mom,
    norm_params,
    norm_moment,
    norm_second,
    decay_gap,
    seq_length,
    seq_group,
):
    rows, width = tokens.shape
    slots = 4 * rows
    groups = 32
    value_width = 4 * VAL
    key_scale = KEY ** (-0.5)
    dp_index = lax.axis_index(DP)
    tensor_index = lax.axis_index(TENSOR)
    chunk_index = lax.axis_index(("y_lo", "z_hi"))

    gain_one = norm_params[0:width]
    shift_one = norm_params[width : 2 * width]
    group_gain = jnp.pad(
        lax.dynamic_slice_in_dim(norm_params, 2 * width + tensor_index * VAL, VAL),
        (0, LANES - VAL),
    )
    gain_two = norm_params[2 * width + value_width : 3 * width + value_width]
    shift_two = norm_params[3 * width + value_width : 4 * width + value_width]

    out_rows = jnp.swapaxes(out_w, 1, 2)
    packed = jnp.concatenate(
        [
            pairs_apart(qk_w[0]),
            pairs_apart(qk_w[1]),
            widen(vg_w[0]),
            widen(vg_w[1]),
            widen(mlp_w[0]),
            widen(mlp_w[1]),
            widen(out_rows[0]),
            widen(out_rows[1]),
        ],
        axis=1,
    ).astype(bf16)
    packed_far = swap(packed, "y_lo")
    first_half = lax.axis_index("y_lo") == 0
    pair = jnp.stack(
        [jnp.where(first_half, packed, packed_far), jnp.where(first_half, packed_far, packed)]
    )
    gathered = lax.all_gather(pair, ("z_hi", "z_lo", "x"), axis=1, tiled=True).reshape(width, -1)
    w_q = gathered[:, 0:256]
    w_k = gathered[:, 256:512]
    w_v, w_g, w_1, w_2, w_o, w_3 = (
        gathered[:, LANES * i : LANES * (i + 1)] for i in range(1, 7)
    )

    whole_tokens = tensor_gather(tokens)
    whole_cot = tensor_gather(cotangent)
    order = jnp.stack([tensor_index, tensor_index ^ 2, tensor_index ^ 1, tensor_index ^ 3])
    place = (order[:, None] * rows + jnp.arange(rows, dtype=jnp.int32)[None, :]).reshape(slots)

    freqs = 1.0 / 10000.0 ** np.linspace(0.0, 1.0, KEY // 2)
    angles = np.arange(slots)[:, None] * freqs[None, :]
    tables = jnp.asarray(
        np.concatenate([np.cos(angles), np.sin(angles)], axis=1).astype(np.float32)
    ).reshape(4, rows, KEY)
    turned = tables[order].reshape(slots, KEY)
    cos_table, sin_table = turned[:, : KEY // 2], turned[:, KEY // 2 :]

    labels = sequence_labels(seq_length, seq_group, dp_index, place)
    linked = (
        (labels[:, None] == labels[None, :])
        & (labels[:, None] > 0)
        & (place[:, None] >= place[None, :])
    )
    log_decay = jnp.log1p(-decay_gap[0])
    away = (place - slots // 2).astype(f32) * log_decay
    decay_row = jnp.exp(away)[:, None]
    decay_column = jnp.exp(-away)[None, :]

    def masked(scores):
        return jnp.where(linked, scores * (decay_row * decay_column), 0.0)

    hat_one, inv_one = normalize(whole_tokens.astype(f32))
    whole_one = (hat_one * gain_one + shift_one).astype(bf16)
    query = nn(whole_one, w_q)
    keys = nn(whole_one, w_k) * key_scale
    values = nn(whole_one, w_v).astype(bf16)
    gate = nn(whole_one, w_g)
    query_rot = rotate(query, cos_table, sin_table).astype(bf16)
    key_rot = rotate(keys, cos_table, sin_table).astype(bf16)
    weights = masked(nt(query_rot, key_rot)).astype(bf16)
    retained = nn(weights, values)
    inv_group = lax.rsqrt(
        jnp.sum(retained * retained, axis=-1, keepdims=True) * (1.0 / VAL) + group_eps
    )
    hat_group = retained * inv_group
    grouped = hat_group * group_gain
    sig_gate = jax.nn.sigmoid(gate)
    swish = gate * sig_gate
    mixed = (grouped * swish).astype(bf16)
    half = slots // 2
    inputs = tokens.astype(f32)
    middle = inputs + tensor_sum(lambda part: nt(mixed[part * half : (part + 1) * half], w_o))
    hat_two, inv_two = normalize(middle)
    whole_two = tensor_gather((hat_two * gain_two + shift_two).astype(bf16))
    pre_gate = nn(whole_two, w_1)
    pre_up = nn(whole_two, w_2)
    cumulative = 0.5 * (1.0 + lax.erf(pre_gate * (1.0 / math.sqrt(2.0))))
    gelu_gate = pre_gate * cumulative
    hidden = (gelu_gate * pre_up).astype(bf16)
    result = (
        middle + tensor_sum(lambda part: nt(hidden[part * half : (part + 1) * half], w_3))
    ).astype(bf16)

    grad_hidden = nn(whole_cot, w_3)
    density = jnp.exp(-0.5 * pre_gate * pre_gate) * (1.0 / math.sqrt(2.0 * math.pi))
    grad_gate = (grad_hidden * pre_up * (cumulative + pre_gate * density)).astype(bf16)
    grad_up = (grad_hidden * gelu_gate).astype(bf16)
    grad_normed_two = tensor_sum(
        lambda part: nt(grad_gate[part * half : (part + 1) * half], w_1)
        + nt(grad_up[part * half : (part + 1) * half], w_2)
    )
    early = jnp.concatenate(
        [
            tn(whole_two, grad_gate).astype(bf16),
            tn(whole_two, grad_up).astype(bf16),
            tn(whole_cot, hidden).astype(bf16),
        ],
        axis=1,
    )
    early_in = lax.all_to_all(
        early.reshape(groups, BLOCK, -1), DP, split_axis=0, concat_axis=0, tiled=True
    )
    early_sum = jnp.sum(early_in.astype(f32), axis=0)

    grad_middle = cotangent.astype(f32) + norm_back(grad_normed_two, gain_two, hat_two, inv_two)
    grad_one = tensor_gather(grad_middle.astype(bf16))
    gain_two_grad = jnp.sum(grad_normed_two * hat_two, axis=0)
    shift_two_grad = jnp.sum(grad_normed_two, axis=0)

    grad_mixed = nn(grad_one, w_o)
    grad_grouped = grad_mixed * swish
    grad_gate_ret = (grad_mixed * grouped * (sig_gate + swish * (1.0 - sig_gate))).astype(bf16)
    group_gain_grad = jnp.sum(grad_grouped * hat_group, axis=0)
    grad_hat = grad_grouped * group_gain
    grad_retained = (
        inv_group
        * (
            grad_hat
            - hat_group * (jnp.sum(grad_hat * hat_group, axis=-1, keepdims=True) * (1.0 / VAL))
        )
    ).astype(bf16)
    grad_scores = masked(nt(grad_retained, values)).astype(bf16)
    grad_values = tn(weights, grad_retained).astype(bf16)
    grad_query = rotate(nn(grad_scores, key_rot), cos_table, -sin_table).astype(bf16)
    grad_key = rotate(tn(grad_scores, query_rot), cos_table, -sin_table).astype(bf16)
    grad_normed_one = tensor_sum(
        lambda part: nt(grad_query[part * half : (part + 1) * half], w_q)
        + nt(grad_key[part * half : (part + 1) * half], w_k) * key_scale
        + nt(grad_values[part * half : (part + 1) * half], w_v)
        + nt(grad_gate_ret[part * half : (part + 1) * half], w_g)
    )
    own_hat, own_inv = hat_one[:rows], inv_one[:rows]
    gain_one_grad = jnp.sum(grad_normed_one * own_hat, axis=0)
    shift_one_grad = jnp.sum(grad_normed_one, axis=0)
    input_grad = grad_middle + norm_back(grad_normed_one, gain_one, own_hat, own_inv)

    small = jnp.stack(
        [
            gain_one_grad,
            shift_one_grad,
            gain_two_grad,
            shift_two_grad,
            jnp.pad(group_gain_grad, (0, width - LANES)),
        ],
        axis=1,
    )
    small_high, small_low = split(small)
    riders = jnp.pad(
        jnp.concatenate([small_high, small_low], axis=1), ((0, 0), (VAL, LANES - VAL - 10))
    )
    late = jnp.concatenate(
        [
            tn(whole_one, grad_query).astype(bf16),
            (tn(whole_one, grad_key) * key_scale).astype(bf16),
            tn(whole_one, grad_values).astype(bf16) + riders,
            tn(whole_one, grad_gate_ret).astype(bf16),
            tn(grad_one, mixed).astype(bf16),
        ],
        axis=1,
    )
    late_in = lax.all_to_all(
        late.reshape(groups, BLOCK, -1), DP, split_axis=0, concat_axis=0, tiled=True
    )
    late_sum = jnp.sum(late_in.astype(f32), axis=0)
    small_sum = late_sum[:, LANES + VAL : LANES + VAL + 10]
    small_sum = small_sum[:, :5] + small_sum[:, 5:]

    grad_qk = pairs_together(jnp.stack([late_sum[:, 0:256], late_sum[:, 256:512]]))
    grad_vg = jnp.stack([late_sum[:, 512 : 512 + VAL], late_sum[:, 1024 : 1024 + VAL]])
    grad_mlp = jnp.stack([early_sum[:, 0:VAL], early_sum[:, 512 : 512 + VAL]])
    grad_out_t = jnp.stack([late_sum[:, 1536 : 1536 + VAL], early_sum[:, 1024 : 1024 + VAL]])
    mom_qk = muon_beta * qk_mom + grad_qk
    mom_vg = muon_beta * vg_mom + grad_vg
    mom_mlp = muon_beta * mlp_mom + grad_mlp
    mom_out = muon_beta * out_mom + jnp.swapaxes(grad_out_t, 1, 2)

    piece_high, piece_low = split(small_sum)
    extra = jnp.pad(
        jnp.concatenate([piece_high, piece_low], axis=1), ((0, 0), (VAL, LANES - VAL - 10))
    )
    stacked = (
        jnp.concatenate(
            [widen(mom_qk), widen(mom_vg), widen(mom_mlp), widen(jnp.swapaxes(mom_out, 1, 2))],
            axis=0,
        ).astype(bf16)
        + extra[None]
    )
    both = jnp.stack([stacked, swap(stacked, "y_hi")], axis=1)
    spread = jnp.broadcast_to(both[None], (4,) + both.shape).reshape((groups,) + both.shape[1:])
    arrived = lax.all_to_all(spread, DP, split_axis=0, concat_axis=0, tiled=True)
    near = jnp.swapaxes(arrived, 0, 1).reshape(2, width, LANES)
    far = swap(near, "core")
    pieces = jnp.concatenate([near, far], axis=0)
    clean = jnp.where(jnp.arange(LANES) < VAL, pieces, jnp.zeros((), bf16))

    gram = sum(nt(clean[i], clean[i]) for i in range(4))
    diagonal = jnp.eye(width, dtype=f32)
    norm = jnp.sqrt(jnp.sum(gram * diagonal)) + 1e-07
    current = gram * (1.0 / (norm * norm))
    own = lax.dynamic_slice_in_dim(clean[0], chunk_index * 128, 128, 1).astype(f32) * (1.0 / norm)
    for turn in range(NS_ITERS):
        mean = jnp.sum(current * diagonal) * (1.0 / width)
        shifted = (current - mean * diagonal).astype(bf16)
        square = mean * mean * diagonal + (2.0 * mean) * (current - mean * diagonal) + nn(
            shifted, shifted
        )
        blend = ns_second * current + ns_third * square
        level = jnp.sum(blend * diagonal) * (1.0 / width)
        rest = (blend - level * diagonal).astype(bf16)
        alpha = ns_first + level
        high, low = split(own)
        own = alpha * own + (nn(rest, high) + nn(rest, low))
        if turn < NS_ITERS - 1:
            high, low = split(current)
            product = nn(high, rest) + nn(low, rest)
            high, low = split(product)
            twice = nn(rest, high) + nn(rest, low)
            current = (alpha * alpha) * current + alpha * (product + product.T) + twice
            current = 0.5 * (current + current.T)
    returned = lax.all_to_all(
        own.astype(bf16).reshape(groups, BLOCK, 128), DP, split_axis=0, concat_axis=0, tiled=True
    ).astype(f32)
    returned = jnp.concatenate([returned[8 * i : 8 * i + 8] for i in range(4)], axis=2)

    shrink = 1.0 - muon_rate * decay_rate
    square_scale = 0.2 * math.sqrt(width)
    wide_scale = 0.2 * math.sqrt(max(width, value_width))
    new_qk = qk_w * shrink - (muon_rate * square_scale) * returned[0:2, :, :KEY]
    new_vg = vg_w * shrink - (muon_rate * wide_scale) * returned[2:4, :, :VAL]
    new_mlp = mlp_w * shrink - (muon_rate * wide_scale) * returned[4:6, :, :VAL]
    new_out = out_w * shrink - (muon_rate * wide_scale) * jnp.swapaxes(returned[6:8, :, :VAL], 1, 2)

    rode = pieces[:, :, VAL : VAL + 10].astype(f32)
    rode = rode[:, :, :5] + rode[:, :, 5:]
    vectors = jnp.sum(rode[:, :, :4], axis=0)
    group_parts = rode[:, :VAL, 4]
    which = jnp.arange(4, dtype=jnp.int32)[:, None] == order[None, :]
    group_whole = jnp.sum(
        jnp.where(which[:, :, None], group_parts[None], 0.0), axis=1
    ).reshape(value_width)
    small_total = jnp.concatenate(
        [vectors[:, 0], vectors[:, 1], group_whole, vectors[:, 2], vectors[:, 3]]
    )
    moment_new = beta_first * norm_moment + (1.0 - beta_first) * small_total
    second_new = beta_second * norm_second + (1.0 - beta_second) * small_total * small_total
    params_new = norm_params - adam_rate * (moment_new / (1.0 - beta_first**OPT_STEP)) / (
        jnp.sqrt(second_new / (1.0 - beta_second**OPT_STEP)) + adam_eps
    )
    return (
        result,
        input_grad,
        mom_qk,
        mom_vg,
        mom_mlp,
        mom_out,
        new_qk,
        new_vg,
        new_mlp,
        new_out,
        moment_new,
        second_new,
        params_new,
    )


def solution(mesh):
    fine = Mesh(np.asarray(mesh.devices).reshape(SIZES), AXES)
    by_rows = P(DP + TENSOR, None)
    by_columns = P(None, DP, TENSOR)
    by_out = P(None, TENSOR, DP)
    return jax.shard_map(
        shards,
        mesh=fine,
        in_specs=(
            by_rows,
            by_rows,
            by_columns,
            by_columns,
            by_columns,
            by_out,
            by_columns,
            by_columns,
            by_columns,
            by_out,
            P(),
            P(),
            P(),
            P(TENSOR),
            P(),
            P(),
        ),
        out_specs=(
            by_rows,
            by_rows,
            by_columns,
            by_columns,
            by_columns,
            by_out,
            by_columns,
            by_columns,
            by_columns,
            by_out,
            P(),
            P(),
            P(),
        ),
        check_vma=False,
    )
```

```python
import math

import jax
import jax.numpy as jnp
import numpy as np
from jax import lax
from jax.experimental import pallas as pl
from jax.experimental.pallas import tpu as pltpu
from jax.sharding import Mesh
from jax.sharding import PartitionSpec as P

HEADS = 4
NS_ITERS = 5
OPT_STEP = 10
KEY = 256
VAL = 432
LANES = 512
BLOCK = 32

norm_eps = 1e-05
group_eps = 0.01
ns_first = 3.4445
ns_second = -4.775
ns_third = 2.0315
muon_rate = 0.15
muon_beta = 0.95
decay_rate = 0.01
adam_rate = 0.6
beta_first = 0.9
beta_second = 0.95
adam_eps = 1e-08

AXES = ("y_lo", "z_hi", "z_lo", "x", "y_hi", "core")
SIZES = (2, 2, 2, 4, 2, 2)
DP = ("y_lo", "z_hi", "z_lo", "x")
TENSOR = ("y_hi", "core")
bf16 = jnp.bfloat16
f32 = jnp.float32


def swap(values, axis):
    return lax.ppermute(values, axis, [(0, 1), (1, 0)])


def dot(left, right, dims):
    return lax.dot_general(left, right, (dims, ((), ())), preferred_element_type=f32)


def nn(left, right):
    return dot(left, right, ((1,), (0,)))


def nt(left, right):
    return dot(left, right, ((1,), (1,)))


def tn(left, right):
    return dot(left, right, ((0,), (0,)))


def split(values):
    high = lax.reduce_precision(values, 8, 7)
    return high.astype(bf16), (values - high).astype(bf16)


def widen(values):
    return jnp.pad(values, ((0, 0),) * (values.ndim - 1) + ((0, LANES - values.shape[-1]),))


def tensor_gather(own):
    far = swap(own, "y_hi")
    near = jnp.concatenate([own, far], axis=0)
    return jnp.concatenate([near, swap(near, "core")], axis=0)


def tensor_sum(make):
    other = swap(make(1).astype(bf16), "core")
    mine = make(0) + other.astype(f32)
    half = mine.shape[0] // 2
    return mine[:half] + swap(mine[half:].astype(bf16), "y_hi").astype(f32)


def after(values, earlier):
    return lax.optimization_barrier((values, earlier))[0]


def normalize(values):
    centre = values - jnp.mean(values, axis=-1, keepdims=True)
    spread = lax.rsqrt(jnp.mean(centre * centre, axis=-1, keepdims=True) + norm_eps)
    return centre * spread, spread


def norm_back(grad_out, gain, normed, spread):
    grad_normed = grad_out * gain
    return spread * (
        grad_normed
        - jnp.mean(grad_normed, axis=-1, keepdims=True)
        - normed * jnp.mean(grad_normed * normed, axis=-1, keepdims=True)
    )


def rotate(values, cos_table, sin_table):
    half = KEY // 2
    first, second = values[:, :half], values[:, half:]
    return jnp.concatenate(
        [first * cos_table - second * sin_table, second * cos_table + first * sin_table], axis=1
    )


def pairs_apart(values):
    shape = values.shape
    return jnp.swapaxes(values.reshape(shape[:-1] + (KEY // 2, 2)), -1, -2).reshape(shape)


def pairs_together(values):
    shape = values.shape
    return jnp.swapaxes(values.reshape(shape[:-1] + (2, KEY // 2)), -1, -2).reshape(shape)


def sequence_labels(seq_length, seq_group, group, place):
    mine = seq_group == group
    lengths = jnp.where(mine, seq_length, 0)
    ends = jnp.cumsum(lengths, dtype=jnp.int32)
    starts = ends - lengths
    inside = mine[None, :] & (place[:, None] >= starts[None, :]) & (place[:, None] < ends[None, :])
    number = jnp.arange(1, seq_length.shape[0] + 1, dtype=jnp.int32)
    return jnp.sum(jnp.where(inside, number[None, :], 0), axis=1, dtype=jnp.int32)


TILE = 256
WIDTH = 1024


def iterate_kernel(
    chunk_ref, near_ref, far_ref, out_ref, whole, gram, high, low, shifted, rest, prod, prod_b, own, own_b
):
    tiles = WIDTH // TILE
    at = [pl.ds(TILE * i, TILE) for i in range(tiles)]
    eye = (
        lax.broadcasted_iota(jnp.int32, (TILE, TILE), 0)
        == lax.broadcasted_iota(jnp.int32, (TILE, TILE), 1)
    ).astype(f32)
    keep = lax.broadcasted_iota(jnp.int32, (WIDTH, 128), 1) < VAL - 384
    for p in range(4):
        source = near_ref if p < 2 else far_ref
        piece = source[:, p % 2].reshape(WIDTH, LANES)
        whole[p, :, 0:384] = piece[:, 0:384]
        whole[p, :, 384:512] = jnp.where(keep, piece[:, 384:512], jnp.zeros((), bf16))

    trace = jnp.float32(0.0)
    for i in range(tiles):
        for j in range(tiles):
            block = jnp.zeros((TILE, TILE), f32)
            for p in range(4):
                block += nt(whole[p, at[i], :], whole[p, at[j], :])
            gram[at[i], at[j]] = block
            if i == j:
                trace += jnp.sum(block * eye)
    inverse = 1.0 / (jnp.sqrt(trace) + 1e-07)
    for q in range(4):

        @pl.when(chunk_ref[0] == q)
        def _():
            own[...] = whole[0, :, 128 * q : 128 * (q + 1)].astype(f32) * inverse

    def store(i, j, block, mean):
        gram[at[i], at[j]] = block
        top = block.astype(bf16)
        high[at[i], at[j]] = top
        low[at[i], at[j]] = (block - top.astype(f32)).astype(bf16)
        if i == j:
            top = (block - mean * eye).astype(bf16)
        shifted[at[i], at[j]] = top

    mean = trace * inverse * inverse * (1.0 / WIDTH)
    for i in range(tiles):
        for j in range(tiles):
            store(i, j, gram[at[i], at[j]] * (inverse * inverse), mean)

    def advance(mean):
        level = ns_second * mean + ns_third * mean * mean
        alpha = ns_first + level
        for i in range(tiles):
            for j in range(tiles):
                block = (ns_second + 2.0 * ns_third * mean) * gram[at[i], at[j]] + ns_third * nn(
                    shifted[at[i], :], shifted[:, at[j]]
                )
                if i == j:
                    block -= (ns_third * mean * mean + level) * eye
                rest[at[i], at[j]] = block.astype(bf16)
        values = own[...]
        top = values.astype(bf16)
        own_b[:, 0:128] = top
        own_b[:, 128:256] = (values - top.astype(f32)).astype(bf16)
        for i in range(tiles):
            moved = nn(rest[at[i], :], own_b[...])
            own[at[i], :] = alpha * own[at[i], :] + (moved[:, 0:128] + moved[:, 128:256])
        return alpha

    def turn(_, mean):
        alpha = advance(mean)
        for i in range(tiles):
            for j in range(tiles):
                block = nn(high[at[i], :], rest[:, at[j]]) + nn(low[at[i], :], rest[:, at[j]])
                prod[at[i], at[j]] = block
                prod_b[at[i], at[j]] = block.astype(bf16)
        trace = jnp.float32(0.0)
        for i in range(tiles):
            for j in range(tiles):
                block = alpha * prod[at[i], at[j]] + 0.5 * nn(rest[at[i], :], prod_b[:, at[j]])
                prod[at[i], at[j]] = block
                if i == j:
                    trace += jnp.sum(block * eye)
        later = alpha * alpha * mean + trace * (2.0 / WIDTH)
        for i in range(tiles):
            for j in range(tiles):
                block = (alpha * alpha) * gram[at[i], at[j]] + (
                    prod[at[i], at[j]] + prod[at[j], at[i]].T
                )
                store(i, j, block, later)
        return later

    advance(lax.fori_loop(0, NS_ITERS - 1, turn, mean))
    out_ref[...] = own[...].astype(bf16)


def orthogonal(chunk, near, far):
    square = (WIDTH, WIDTH)
    return pl.pallas_call(
        iterate_kernel,
        out_shape=jax.ShapeDtypeStruct((WIDTH, 128), bf16),
        in_specs=[pl.BlockSpec(memory_space=pltpu.SMEM)]
        + [pl.BlockSpec(memory_space=pltpu.VMEM)] * 2,
        out_specs=pl.BlockSpec(memory_space=pltpu.VMEM),
        scratch_shapes=[
            pltpu.VMEM((4, WIDTH, LANES), bf16),
            pltpu.VMEM(square, f32),
            pltpu.VMEM(square, bf16),
            pltpu.VMEM(square, bf16),
            pltpu.VMEM(square, bf16),
            pltpu.VMEM(square, bf16),
            pltpu.VMEM(square, f32),
            pltpu.VMEM(square, bf16),
            pltpu.VMEM((WIDTH, 128), f32),
            pltpu.VMEM((WIDTH, 256), bf16),
        ],
        compiler_params=pltpu.CompilerParams(vmem_limit_bytes=48 * 2**20),
        cost_estimate=pl.CostEstimate(
            flops=42 * 10**9, bytes_accessed=5 * 2**20, transcendentals=0
        ),
        name="orthogonalize",
    )(chunk, near, far)


def shards(
    tokens,
    cotangent,
    qk_w,
    vg_w,
    mlp_w,
    out_w,
    qk_mom,
    vg_mom,
    mlp_mom,
    out_mom,
    norm_params,
    norm_moment,
    norm_second,
    decay_gap,
    seq_length,
    seq_group,
):
    rows, width = tokens.shape
    slots = 4 * rows
    groups = 32
    value_width = 4 * VAL
    key_scale = KEY ** (-0.5)
    dp_index = lax.axis_index(DP)
    tensor_index = lax.axis_index(TENSOR)
    chunk_index = lax.axis_index(("y_lo", "z_hi"))

    gain_one = norm_params[0:width]
    shift_one = norm_params[width : 2 * width]
    group_gain = jnp.pad(
        lax.dynamic_slice_in_dim(norm_params, 2 * width + tensor_index * VAL, VAL),
        (0, LANES - VAL),
    )
    gain_two = norm_params[2 * width + value_width : 3 * width + value_width]
    shift_two = norm_params[3 * width + value_width : 4 * width + value_width]

    out_rows = jnp.swapaxes(out_w, 1, 2)
    packed = jnp.concatenate(
        [
            pairs_apart(qk_w[0]),
            pairs_apart(qk_w[1]),
            widen(vg_w[0]),
            widen(vg_w[1]),
            widen(mlp_w[0]),
            widen(mlp_w[1]),
            widen(out_rows[0]),
            widen(out_rows[1]),
        ],
        axis=1,
    ).astype(bf16)
    packed_far = swap(packed, "y_lo")
    first_half = lax.axis_index("y_lo") == 0
    pair = jnp.stack(
        [jnp.where(first_half, packed, packed_far), jnp.where(first_half, packed_far, packed)]
    )
    gathered = lax.all_gather(pair, ("z_hi", "z_lo", "x"), axis=1, tiled=True).reshape(width, -1)
    w_q = gathered[:, 0:256]
    w_k = gathered[:, 256:512]
    w_v, w_g, w_1, w_2, w_o, w_3 = (
        gathered[:, LANES * i : LANES * (i + 1)] for i in range(1, 7)
    )

    whole_tokens = tensor_gather(tokens)
    whole_cot = tensor_gather(cotangent)
    order = jnp.stack([tensor_index, tensor_index ^ 2, tensor_index ^ 1, tensor_index ^ 3])
    place = (order[:, None] * rows + jnp.arange(rows, dtype=jnp.int32)[None, :]).reshape(slots)

    freqs = 1.0 / 10000.0 ** np.linspace(0.0, 1.0, KEY // 2)
    angles = np.arange(slots)[:, None] * freqs[None, :]
    tables = jnp.asarray(
        np.concatenate([np.cos(angles), np.sin(angles)], axis=1).astype(np.float32)
    ).reshape(4, rows, KEY)
    turned = tables[order].reshape(slots, KEY)
    cos_table, sin_table = turned[:, : KEY // 2], turned[:, KEY // 2 :]

    labels = sequence_labels(seq_length, seq_group, dp_index, place)
    linked = (
        (labels[:, None] == labels[None, :])
        & (labels[:, None] > 0)
        & (place[:, None] >= place[None, :])
    )
    log_decay = jnp.log1p(-decay_gap[0])
    away = (place - slots // 2).astype(f32) * log_decay
    decay_row = jnp.exp(away)[:, None]
    decay_column = jnp.exp(-away)[None, :]

    def masked(scores):
        return jnp.where(linked, scores * (decay_row * decay_column), 0.0)

    hat_one, inv_one = normalize(whole_tokens.astype(f32))
    whole_one = (hat_one * gain_one + shift_one).astype(bf16)
    query = nn(whole_one, w_q)
    keys = nn(whole_one, w_k) * key_scale
    values = nn(whole_one, w_v).astype(bf16)
    gate = nn(whole_one, w_g)
    query_rot = rotate(query, cos_table, sin_table).astype(bf16)
    key_rot = rotate(keys, cos_table, sin_table).astype(bf16)
    weights = masked(nt(query_rot, key_rot)).astype(bf16)
    retained = nn(weights, values)
    inv_group = lax.rsqrt(
        jnp.sum(retained * retained, axis=-1, keepdims=True) * (1.0 / VAL) + group_eps
    )
    hat_group = retained * inv_group
    grouped = hat_group * group_gain
    sig_gate = jax.nn.sigmoid(gate)
    swish = gate * sig_gate
    mixed = (grouped * swish).astype(bf16)
    half = slots // 2
    inputs = tokens.astype(f32)
    middle = inputs + tensor_sum(lambda part: nt(mixed[part * half : (part + 1) * half], w_o))
    hat_two, inv_two = normalize(middle)
    whole_two = tensor_gather((hat_two * gain_two + shift_two).astype(bf16))
    pre_gate = nn(whole_two, w_1)
    pre_up = nn(whole_two, w_2)
    cumulative = 0.5 * (1.0 + lax.erf(pre_gate * (1.0 / math.sqrt(2.0))))
    gelu_gate = pre_gate * cumulative
    hidden = (gelu_gate * pre_up).astype(bf16)
    grad_hidden = nn(whole_cot, w_3)
    density = jnp.exp(-0.5 * pre_gate * pre_gate) * (1.0 / math.sqrt(2.0 * math.pi))
    grad_gate = (grad_hidden * pre_up * (cumulative + pre_gate * density)).astype(bf16)
    grad_up = (grad_hidden * gelu_gate).astype(bf16)
    grad_normed_two = tensor_sum(
        lambda part: nt(grad_gate[part * half : (part + 1) * half], w_1)
        + nt(grad_up[part * half : (part + 1) * half], w_2)
    )
    early = jnp.concatenate(
        [
            tn(whole_two, grad_gate).astype(bf16),
            tn(whole_two, grad_up).astype(bf16),
            tn(whole_cot, hidden).astype(bf16),
        ],
        axis=1,
    )
    early_in = lax.all_to_all(
        early.reshape(groups, BLOCK, -1), DP, split_axis=0, concat_axis=0, tiled=True
    )
    early_sum = jnp.sum(early_in.astype(f32), axis=0)
    grad_normed_two = after(grad_normed_two, early)

    grad_middle = cotangent.astype(f32) + norm_back(grad_normed_two, gain_two, hat_two, inv_two)
    grad_one = tensor_gather(grad_middle.astype(bf16))
    gain_two_grad = jnp.sum(grad_normed_two * hat_two, axis=0)
    shift_two_grad = jnp.sum(grad_normed_two, axis=0)

    out_in = lax.all_to_all(
        tn(grad_one, mixed).astype(bf16).reshape(groups, BLOCK, LANES),
        DP,
        split_axis=0,
        concat_axis=0,
        tiled=True,
    )
    out_sum = jnp.sum(out_in.astype(f32), axis=0)

    later_hidden = after(hidden, grad_one)
    result = (
        middle + tensor_sum(lambda part: nt(later_hidden[part * half : (part + 1) * half], w_3))
    ).astype(bf16)

    grad_mixed = nn(grad_one, w_o)
    grad_grouped = grad_mixed * swish
    grad_gate_ret = (grad_mixed * grouped * (sig_gate + swish * (1.0 - sig_gate))).astype(bf16)
    group_gain_grad = jnp.sum(grad_grouped * hat_group, axis=0)
    grad_hat = grad_grouped * group_gain
    grad_retained = (
        inv_group
        * (
            grad_hat
            - hat_group * (jnp.sum(grad_hat * hat_group, axis=-1, keepdims=True) * (1.0 / VAL))
        )
    ).astype(bf16)
    grad_scores = masked(nt(grad_retained, values)).astype(bf16)
    grad_values = tn(weights, grad_retained).astype(bf16)
    grad_query = rotate(nn(grad_scores, key_rot), cos_table, -sin_table).astype(bf16)
    grad_key = rotate(tn(grad_scores, query_rot), cos_table, -sin_table).astype(bf16)
    grad_normed_one = tensor_sum(
        lambda part: nt(grad_query[part * half : (part + 1) * half], w_q)
        + nt(grad_key[part * half : (part + 1) * half], w_k) * key_scale
        + nt(grad_values[part * half : (part + 1) * half], w_v)
        + nt(grad_gate_ret[part * half : (part + 1) * half], w_g)
    )
    own_hat, own_inv = hat_one[:rows], inv_one[:rows]
    gain_one_grad = jnp.sum(grad_normed_one * own_hat, axis=0)
    shift_one_grad = jnp.sum(grad_normed_one, axis=0)
    input_grad = grad_middle + norm_back(grad_normed_one, gain_one, own_hat, own_inv)

    small = jnp.stack(
        [gain_two_grad, shift_two_grad, jnp.pad(group_gain_grad, (0, width - LANES))], axis=1
    )
    small_high, small_low = split(small)
    riders = jnp.pad(
        jnp.concatenate([small_high, small_low], axis=1), ((0, 0), (VAL, LANES - VAL - 6))
    )
    late = jnp.concatenate(
        [
            tn(whole_one, grad_query).astype(bf16),
            (tn(whole_one, grad_key) * key_scale).astype(bf16),
            tn(whole_one, grad_values).astype(bf16) + riders,
            tn(whole_one, grad_gate_ret).astype(bf16),
        ],
        axis=1,
    )
    late_in = lax.all_to_all(
        late.reshape(groups, BLOCK, -1), DP, split_axis=0, concat_axis=0, tiled=True
    )
    late_sum = jnp.sum(late_in.astype(f32), axis=0)
    small_sum = late_sum[:, LANES + VAL : LANES + VAL + 6]
    small_sum = small_sum[:, :3] + small_sum[:, 3:]

    grad_qk = pairs_together(jnp.stack([late_sum[:, 0:256], late_sum[:, 256:512]]))
    grad_vg = jnp.stack([late_sum[:, 512 : 512 + VAL], late_sum[:, 1024 : 1024 + VAL]])
    grad_mlp = jnp.stack([early_sum[:, 0:VAL], early_sum[:, 512 : 512 + VAL]])
    grad_out_t = jnp.stack([out_sum[:, :VAL], early_sum[:, 1024 : 1024 + VAL]])
    mom_qk = muon_beta * qk_mom + grad_qk
    mom_vg = muon_beta * vg_mom + grad_vg
    mom_mlp = muon_beta * mlp_mom + grad_mlp
    mom_out = muon_beta * out_mom + jnp.swapaxes(grad_out_t, 1, 2)

    piece_high, piece_low = split(small_sum)
    first_norm = jnp.concatenate([gain_one_grad, shift_one_grad]).astype(bf16)
    extra = jnp.pad(
        jnp.concatenate([piece_high, piece_low, first_norm.reshape(BLOCK, 64)], axis=1),
        ((0, 0), (VAL, LANES - VAL - 70)),
    )
    stacked = (
        jnp.concatenate(
            [widen(mom_qk), widen(mom_vg), widen(mom_mlp), widen(jnp.swapaxes(mom_out, 1, 2))],
            axis=0,
        ).astype(bf16)
        + extra[None]
    )
    both = jnp.stack([stacked, swap(stacked, "y_hi")], axis=1)
    spread = jnp.broadcast_to(both[None], (4,) + both.shape).reshape((groups,) + both.shape[1:])
    arrived = lax.all_to_all(spread, DP, split_axis=0, concat_axis=0, tiled=True)
    far = swap(arrived, "core")
    own = orthogonal(jnp.reshape(chunk_index, (1,)).astype(jnp.int32), arrived, far)
    returned = lax.all_to_all(
        own.reshape(groups, BLOCK, 128), DP, split_axis=0, concat_axis=0, tiled=True
    ).astype(f32)
    returned = jnp.concatenate([returned[8 * i : 8 * i + 8] for i in range(4)], axis=2)

    shrink = 1.0 - muon_rate * decay_rate
    square_scale = 0.2 * math.sqrt(width)
    wide_scale = 0.2 * math.sqrt(max(width, value_width))
    new_qk = qk_w * shrink - (muon_rate * square_scale) * returned[0:2, :, :KEY]
    new_vg = vg_w * shrink - (muon_rate * wide_scale) * returned[2:4, :, :VAL]
    new_mlp = mlp_w * shrink - (muon_rate * wide_scale) * returned[4:6, :, :VAL]
    new_out = out_w * shrink - (muon_rate * wide_scale) * jnp.swapaxes(returned[6:8, :, :VAL], 1, 2)

    rode = jnp.concatenate(
        [jnp.swapaxes(part[..., VAL : VAL + 70], 0, 1) for part in (arrived, far)], axis=0
    ).astype(f32)
    first_total = jnp.sum(rode[..., 6:], axis=(0, 1)).reshape(2 * width)
    rode = (rode[..., :3] + rode[..., 3:6]).reshape(4, width, 3)
    vectors = jnp.sum(rode[:, :, :2], axis=0)
    group_parts = rode[:, :VAL, 2]
    which = jnp.arange(4, dtype=jnp.int32)[:, None] == order[None, :]
    group_whole = jnp.sum(
        jnp.where(which[:, :, None], group_parts[None], 0.0), axis=1
    ).reshape(value_width)
    small_total = jnp.concatenate(
        [first_total, group_whole, vectors[:, 0], vectors[:, 1]]
    )
    moment_new = beta_first * norm_moment + (1.0 - beta_first) * small_total
    second_new = beta_second * norm_second + (1.0 - beta_second) * small_total * small_total
    params_new = norm_params - adam_rate * (moment_new / (1.0 - beta_first**OPT_STEP)) / (
        jnp.sqrt(second_new / (1.0 - beta_second**OPT_STEP)) + adam_eps
    )
    return (
        result,
        input_grad,
        mom_qk,
        mom_vg,
        mom_mlp,
        mom_out,
        new_qk,
        new_vg,
        new_mlp,
        new_out,
        moment_new,
        second_new,
        params_new,
    )


def solution(mesh):
    fine = Mesh(np.asarray(mesh.devices).reshape(SIZES), AXES)
    by_rows = P(DP + TENSOR, None)
    by_columns = P(None, DP, TENSOR)
    by_out = P(None, TENSOR, DP)
    return jax.shard_map(
        shards,
        mesh=fine,
        in_specs=(
            by_rows,
            by_rows,
            by_columns,
            by_columns,
            by_columns,
            by_out,
            by_columns,
            by_columns,
            by_columns,
            by_out,
            P(),
            P(),
            P(),
            P(TENSOR),
            P(),
            P(),
        ),
        out_specs=(
            by_rows,
            by_rows,
            by_columns,
            by_columns,
            by_columns,
            by_out,
            by_columns,
            by_columns,
            by_columns,
            by_out,
            P(),
            P(),
            P(),
        ),
        check_vma=False,
    )
```

```python
import math

import jax
import jax.numpy as jnp
import numpy as np
from jax import lax
from jax.experimental import pallas as pl
from jax.experimental.pallas import tpu as pltpu
from jax.sharding import Mesh
from jax.sharding import PartitionSpec as P

HEADS = 4
NS_ITERS = 5
OPT_STEP = 10
KEY = 256
VAL = 432
LANES = 512
BLOCK = 32

norm_eps = 1e-05
group_eps = 0.01
ns_first = 3.4445
ns_second = -4.775
ns_third = 2.0315
muon_rate = 0.15
muon_beta = 0.95
decay_rate = 0.01
adam_rate = 0.6
beta_first = 0.9
beta_second = 0.95
adam_eps = 1e-08

AXES = ("y_lo", "z_hi", "z_lo", "x", "y_hi", "core")
SIZES = (2, 2, 2, 4, 2, 2)
DP = ("y_lo", "z_hi", "z_lo", "x")
PLANE = ("z_hi", "z_lo", "x")
TENSOR = ("y_hi", "core")
bf16 = jnp.bfloat16
f32 = jnp.float32


def swap(values, axis):
    return lax.ppermute(values, axis, [(0, 1), (1, 0)])


def dot(left, right, dims):
    return lax.dot_general(left, right, (dims, ((), ())), preferred_element_type=f32)


def nn(left, right):
    return dot(left, right, ((1,), (0,)))


def nt(left, right):
    return dot(left, right, ((1,), (1,)))


def tn(left, right):
    return dot(left, right, ((0,), (0,)))


def split(values):
    high = lax.reduce_precision(values, 8, 7)
    return high.astype(bf16), (values - high).astype(bf16)


def widen(values):
    return jnp.pad(values, ((0, 0),) * (values.ndim - 1) + ((0, LANES - values.shape[-1]),))


def tensor_gather(own):
    far = swap(own, "y_hi")
    near = jnp.concatenate([own, far], axis=0)
    return jnp.concatenate([near, swap(near, "core")], axis=0)


def tensor_sum(make):
    other = swap(make(1).astype(bf16), "core")
    mine = make(0) + other.astype(f32)
    half = mine.shape[0] // 2
    return mine[:half] + swap(mine[half:].astype(bf16), "y_hi").astype(f32)


def after(values, earlier):
    return lax.optimization_barrier((values, earlier))[0]


def normalize(values):
    centre = values - jnp.mean(values, axis=-1, keepdims=True)
    spread = lax.rsqrt(jnp.mean(centre * centre, axis=-1, keepdims=True) + norm_eps)
    return centre * spread, spread


def norm_back(grad_out, gain, normed, spread):
    grad_normed = grad_out * gain
    return spread * (
        grad_normed
        - jnp.mean(grad_normed, axis=-1, keepdims=True)
        - normed * jnp.mean(grad_normed * normed, axis=-1, keepdims=True)
    )


def rotate(values, cos_table, sin_table):
    half = KEY // 2
    first, second = values[:, :half], values[:, half:]
    return jnp.concatenate(
        [first * cos_table - second * sin_table, second * cos_table + first * sin_table], axis=1
    )


def pairs_apart(values):
    shape = values.shape
    return jnp.swapaxes(values.reshape(shape[:-1] + (KEY // 2, 2)), -1, -2).reshape(shape)


def pairs_together(values):
    shape = values.shape
    return jnp.swapaxes(values.reshape(shape[:-1] + (2, KEY // 2)), -1, -2).reshape(shape)


def sequence_labels(seq_length, seq_group, group, place):
    mine = seq_group == group
    lengths = jnp.where(mine, seq_length, 0)
    ends = jnp.cumsum(lengths, dtype=jnp.int32)
    starts = ends - lengths
    inside = mine[None, :] & (place[:, None] >= starts[None, :]) & (place[:, None] < ends[None, :])
    number = jnp.arange(1, seq_length.shape[0] + 1, dtype=jnp.int32)
    return jnp.sum(jnp.where(inside, number[None, :], 0), axis=1, dtype=jnp.int32)


TILE = 256
WIDTH = 1024


def iterate_kernel(
    chunk_ref, near_ref, far_ref, out_ref, whole, gram, high, low, shifted, rest, prod, prod_b, own, own_b
):
    tiles = WIDTH // TILE
    at = [pl.ds(TILE * i, TILE) for i in range(tiles)]
    eye = (
        lax.broadcasted_iota(jnp.int32, (TILE, TILE), 0)
        == lax.broadcasted_iota(jnp.int32, (TILE, TILE), 1)
    ).astype(f32)
    keep = lax.broadcasted_iota(jnp.int32, (WIDTH, 128), 1) < VAL - 384
    for p in range(4):
        source = near_ref if p < 2 else far_ref
        piece = source[:, p % 2].reshape(WIDTH, LANES)
        whole[p, :, 0:384] = piece[:, 0:384]
        whole[p, :, 384:512] = jnp.where(keep, piece[:, 384:512], jnp.zeros((), bf16))

    trace = jnp.float32(0.0)
    for i in range(tiles):
        for j in range(tiles):
            block = jnp.zeros((TILE, TILE), f32)
            for p in range(4):
                block += nt(whole[p, at[i], :], whole[p, at[j], :])
            gram[at[i], at[j]] = block
            if i == j:
                trace += jnp.sum(block * eye)
    inverse = 1.0 / (jnp.sqrt(trace) + 1e-07)
    for q in range(4):

        @pl.when(chunk_ref[0] == q)
        def _():
            own[...] = whole[0, :, 128 * q : 128 * (q + 1)].astype(f32) * inverse

    def store(i, j, block, mean):
        gram[at[i], at[j]] = block
        top = block.astype(bf16)
        high[at[i], at[j]] = top
        low[at[i], at[j]] = (block - top.astype(f32)).astype(bf16)
        if i == j:
            top = (block - mean * eye).astype(bf16)
        shifted[at[i], at[j]] = top

    mean = trace * inverse * inverse * (1.0 / WIDTH)
    for i in range(tiles):
        for j in range(tiles):
            store(i, j, gram[at[i], at[j]] * (inverse * inverse), mean)

    def advance(mean):
        level = ns_second * mean + ns_third * mean * mean
        alpha = ns_first + level
        for i in range(tiles):
            for j in range(tiles):
                block = (ns_second + 2.0 * ns_third * mean) * gram[at[i], at[j]] + ns_third * nn(
                    shifted[at[i], :], shifted[:, at[j]]
                )
                if i == j:
                    block -= (ns_third * mean * mean + level) * eye
                rest[at[i], at[j]] = block.astype(bf16)
        values = own[...]
        top = values.astype(bf16)
        own_b[:, 0:128] = top
        own_b[:, 128:256] = (values - top.astype(f32)).astype(bf16)
        for i in range(tiles):
            moved = nn(rest[at[i], :], own_b[...])
            own[at[i], :] = alpha * own[at[i], :] + (moved[:, 0:128] + moved[:, 128:256])
        return alpha

    def turn(_, mean):
        alpha = advance(mean)
        for i in range(tiles):
            for j in range(tiles):
                block = nn(high[at[i], :], rest[:, at[j]]) + nn(low[at[i], :], rest[:, at[j]])
                prod[at[i], at[j]] = block
                prod_b[at[i], at[j]] = block.astype(bf16)
        trace = jnp.float32(0.0)
        for i in range(tiles):
            for j in range(tiles):
                block = alpha * prod[at[i], at[j]] + 0.5 * nn(rest[at[i], :], prod_b[:, at[j]])
                prod[at[i], at[j]] = block
                if i == j:
                    trace += jnp.sum(block * eye)
        later = alpha * alpha * mean + trace * (2.0 / WIDTH)
        for i in range(tiles):
            for j in range(tiles):
                block = (alpha * alpha) * gram[at[i], at[j]] + (
                    prod[at[i], at[j]] + prod[at[j], at[i]].T
                )
                store(i, j, block, later)
        return later

    advance(lax.fori_loop(0, NS_ITERS - 1, turn, mean))
    out_ref[...] = own[...].astype(bf16)


def orthogonal(chunk, near, far):
    square = (WIDTH, WIDTH)
    return pl.pallas_call(
        iterate_kernel,
        out_shape=jax.ShapeDtypeStruct((WIDTH, 128), bf16),
        in_specs=[pl.BlockSpec(memory_space=pltpu.SMEM)]
        + [pl.BlockSpec(memory_space=pltpu.VMEM)] * 2,
        out_specs=pl.BlockSpec(memory_space=pltpu.VMEM),
        scratch_shapes=[
            pltpu.VMEM((4, WIDTH, LANES), bf16),
            pltpu.VMEM(square, f32),
            pltpu.VMEM(square, bf16),
            pltpu.VMEM(square, bf16),
            pltpu.VMEM(square, bf16),
            pltpu.VMEM(square, bf16),
            pltpu.VMEM(square, f32),
            pltpu.VMEM(square, bf16),
            pltpu.VMEM((WIDTH, 128), f32),
            pltpu.VMEM((WIDTH, 256), bf16),
        ],
        compiler_params=pltpu.CompilerParams(vmem_limit_bytes=48 * 2**20),
        cost_estimate=pl.CostEstimate(
            flops=42 * 10**9, bytes_accessed=5 * 2**20, transcendentals=0
        ),
        name="orthogonalize",
    )(chunk, near, far)


def shards(
    tokens,
    cotangent,
    qk_w,
    vg_w,
    mlp_w,
    out_w,
    qk_mom,
    vg_mom,
    mlp_mom,
    out_mom,
    norm_params,
    norm_moment,
    norm_second,
    decay_gap,
    seq_length,
    seq_group,
):
    rows, width = tokens.shape
    slots = 4 * rows
    groups = 32
    value_width = 4 * VAL
    key_scale = KEY ** (-0.5)
    dp_index = lax.axis_index(DP)
    tensor_index = lax.axis_index(TENSOR)
    chunk_index = lax.axis_index(("y_lo", "z_hi"))

    gain_one = norm_params[0:width]
    shift_one = norm_params[width : 2 * width]
    group_gain = jnp.pad(
        lax.dynamic_slice_in_dim(norm_params, 2 * width + tensor_index * VAL, VAL),
        (0, LANES - VAL),
    )
    gain_two = norm_params[2 * width + value_width : 3 * width + value_width]
    shift_two = norm_params[3 * width + value_width : 4 * width + value_width]

    out_rows = jnp.swapaxes(out_w, 1, 2)
    first_half = lax.axis_index("y_lo") == 0

    def weight_rows(parts):
        packed = jnp.concatenate(parts, axis=1).astype(bf16)
        far = swap(packed, "y_lo")
        pair = jnp.stack([jnp.where(first_half, packed, far), jnp.where(first_half, far, packed)])
        return pair

    def weight_gather(pair):
        return lax.all_gather(pair, PLANE, axis=1, tiled=True).reshape(width, -1)

    pair_ret = weight_rows(
        [
            pairs_apart(qk_w[0]),
            pairs_apart(qk_w[1]),
            widen(vg_w[0]),
            widen(vg_w[1]),
            widen(out_rows[0]),
        ]
    )
    pair_ff = weight_rows([widen(mlp_w[0]), widen(mlp_w[1]), widen(out_rows[1])])
    gathered = weight_gather(pair_ret)
    w_q = gathered[:, 0:256]
    w_k = gathered[:, 256:512]
    w_v, w_g, w_o = (gathered[:, LANES * i : LANES * (i + 1)] for i in range(1, 4))
    gathered_ff = weight_gather(after(pair_ff, gathered))
    w_1, w_2, w_3 = (gathered_ff[:, LANES * i : LANES * (i + 1)] for i in range(3))

    whole_tokens = tensor_gather(tokens)
    whole_cot = tensor_gather(after(cotangent, whole_tokens))
    order = jnp.stack([tensor_index, tensor_index ^ 2, tensor_index ^ 1, tensor_index ^ 3])
    place = (order[:, None] * rows + jnp.arange(rows, dtype=jnp.int32)[None, :]).reshape(slots)

    freqs = 1.0 / 10000.0 ** np.linspace(0.0, 1.0, KEY // 2)
    angles = np.arange(slots)[:, None] * freqs[None, :]
    tables = jnp.asarray(
        np.concatenate([np.cos(angles), np.sin(angles)], axis=1).astype(np.float32)
    ).reshape(4, rows, KEY)
    turned = tables[order].reshape(slots, KEY)
    cos_table, sin_table = turned[:, : KEY // 2], turned[:, KEY // 2 :]

    labels = sequence_labels(seq_length, seq_group, dp_index, place)
    linked = (
        (labels[:, None] == labels[None, :])
        & (labels[:, None] > 0)
        & (place[:, None] >= place[None, :])
    )
    log_decay = jnp.log1p(-decay_gap[0])
    away = (place - slots // 2).astype(f32) * log_decay
    decay_row = jnp.exp(away)[:, None]
    decay_column = jnp.exp(-away)[None, :]

    def masked(scores):
        return jnp.where(linked, scores * (decay_row * decay_column), 0.0)

    hat_one, inv_one = normalize(whole_tokens.astype(f32))
    whole_one = after((hat_one * gain_one + shift_one).astype(bf16), whole_cot)
    query = nn(whole_one, w_q)
    keys = nn(whole_one, w_k) * key_scale
    values = nn(whole_one, w_v).astype(bf16)
    gate = nn(whole_one, w_g)
    query_rot = rotate(query, cos_table, sin_table).astype(bf16)
    key_rot = rotate(keys, cos_table, sin_table).astype(bf16)
    weights = masked(nt(query_rot, key_rot)).astype(bf16)
    retained = nn(weights, values)
    inv_group = lax.rsqrt(
        jnp.sum(retained * retained, axis=-1, keepdims=True) * (1.0 / VAL) + group_eps
    )
    hat_group = retained * inv_group
    grouped = hat_group * group_gain
    sig_gate = jax.nn.sigmoid(gate)
    swish = gate * sig_gate
    mixed = (grouped * swish).astype(bf16)
    half = slots // 2
    inputs = tokens.astype(f32)
    middle = inputs + tensor_sum(lambda part: nt(mixed[part * half : (part + 1) * half], w_o))
    hat_two, inv_two = normalize(middle)
    whole_two = tensor_gather((hat_two * gain_two + shift_two).astype(bf16))
    pre_gate = nn(whole_two, w_1)
    pre_up = nn(whole_two, w_2)
    cumulative = 0.5 * (1.0 + lax.erf(pre_gate * (1.0 / math.sqrt(2.0))))
    gelu_gate = pre_gate * cumulative
    hidden = (gelu_gate * pre_up).astype(bf16)
    grad_hidden = nn(whole_cot, w_3)
    density = jnp.exp(-0.5 * pre_gate * pre_gate) * (1.0 / math.sqrt(2.0 * math.pi))
    grad_gate = (grad_hidden * pre_up * (cumulative + pre_gate * density)).astype(bf16)
    grad_up = (grad_hidden * gelu_gate).astype(bf16)
    grad_normed_two = tensor_sum(
        lambda part: nt(grad_gate[part * half : (part + 1) * half], w_1)
        + nt(grad_up[part * half : (part + 1) * half], w_2)
    )
    early = jnp.concatenate(
        [
            tn(whole_two, grad_gate).astype(bf16),
            tn(whole_two, grad_up).astype(bf16),
            tn(whole_cot, hidden).astype(bf16),
        ],
        axis=1,
    )
    early_in = lax.all_to_all(
        early.reshape(2, groups // 2, BLOCK, -1), PLANE, split_axis=1, concat_axis=1, tiled=True
    )
    early_halves = jnp.sum(early_in.astype(f32), axis=1)
    early_far = swap(
        jnp.where(first_half, early_halves[1], early_halves[0]).astype(bf16), "y_lo"
    )
    early_sum = jnp.where(first_half, early_halves[0], early_halves[1]) + early_far.astype(f32)
    grad_normed_two = after(grad_normed_two, early)

    grad_middle = cotangent.astype(f32) + norm_back(grad_normed_two, gain_two, hat_two, inv_two)
    grad_one = tensor_gather(grad_middle.astype(bf16))
    gain_two_grad = jnp.sum(grad_normed_two * hat_two, axis=0)
    shift_two_grad = jnp.sum(grad_normed_two, axis=0)

    later_hidden = after(hidden, grad_one)
    result = (
        middle + tensor_sum(lambda part: nt(later_hidden[part * half : (part + 1) * half], w_3))
    ).astype(bf16)

    grad_mixed = nn(grad_one, w_o)
    grad_grouped = grad_mixed * swish
    grad_gate_ret = (grad_mixed * grouped * (sig_gate + swish * (1.0 - sig_gate))).astype(bf16)
    group_gain_grad = jnp.sum(grad_grouped * hat_group, axis=0)
    grad_hat = grad_grouped * group_gain
    grad_retained = (
        inv_group
        * (
            grad_hat
            - hat_group * (jnp.sum(grad_hat * hat_group, axis=-1, keepdims=True) * (1.0 / VAL))
        )
    ).astype(bf16)
    grad_scores = masked(nt(grad_retained, values)).astype(bf16)
    grad_values = tn(weights, grad_retained).astype(bf16)
    grad_query = rotate(nn(grad_scores, key_rot), cos_table, -sin_table).astype(bf16)
    grad_key = rotate(tn(grad_scores, query_rot), cos_table, -sin_table).astype(bf16)
    grad_normed_one = tensor_sum(
        lambda part: nt(grad_query[part * half : (part + 1) * half], w_q)
        + nt(grad_key[part * half : (part + 1) * half], w_k) * key_scale
        + nt(grad_values[part * half : (part + 1) * half], w_v)
        + nt(grad_gate_ret[part * half : (part + 1) * half], w_g)
    )
    own_hat, own_inv = hat_one[:rows], inv_one[:rows]
    gain_one_grad = jnp.sum(grad_normed_one * own_hat, axis=0)
    shift_one_grad = jnp.sum(grad_normed_one, axis=0)
    input_grad = grad_middle + norm_back(grad_normed_one, gain_one, own_hat, own_inv)

    small = jnp.stack(
        [gain_two_grad, shift_two_grad, jnp.pad(group_gain_grad, (0, width - LANES))], axis=1
    )
    small_high, small_low = split(small)
    riders = jnp.pad(
        jnp.concatenate([small_high, small_low], axis=1), ((0, 0), (VAL, LANES - VAL - 6))
    )
    late = jnp.concatenate(
        [
            tn(whole_one, grad_query).astype(bf16),
            (tn(whole_one, grad_key) * key_scale).astype(bf16),
            tn(whole_one, grad_values).astype(bf16) + riders,
            tn(whole_one, grad_gate_ret).astype(bf16),
            tn(grad_one, mixed).astype(bf16),
        ],
        axis=1,
    )
    late_in = lax.all_to_all(
        late.reshape(groups, BLOCK, -1), DP, split_axis=0, concat_axis=0, tiled=True
    )
    late_sum = jnp.sum(late_in.astype(f32), axis=0)
    small_sum = late_sum[:, LANES + VAL : LANES + VAL + 6]
    small_sum = small_sum[:, :3] + small_sum[:, 3:]

    grad_qk = pairs_together(jnp.stack([late_sum[:, 0:256], late_sum[:, 256:512]]))
    grad_vg = jnp.stack([late_sum[:, 512 : 512 + VAL], late_sum[:, 1024 : 1024 + VAL]])
    grad_mlp = jnp.stack([early_sum[:, 0:VAL], early_sum[:, 512 : 512 + VAL]])
    grad_out_t = jnp.stack([late_sum[:, 1536 : 1536 + VAL], early_sum[:, 1024 : 1024 + VAL]])
    mom_qk = muon_beta * qk_mom + grad_qk
    mom_vg = muon_beta * vg_mom + grad_vg
    mom_mlp = muon_beta * mlp_mom + grad_mlp
    mom_out = muon_beta * out_mom + jnp.swapaxes(grad_out_t, 1, 2)

    piece_high, piece_low = split(small_sum)
    first_norm = jnp.concatenate([gain_one_grad, shift_one_grad]).astype(bf16)
    extra = jnp.pad(
        jnp.concatenate([piece_high, piece_low, first_norm.reshape(BLOCK, 64)], axis=1),
        ((0, 0), (VAL, LANES - VAL - 70)),
    )
    stacked = (
        jnp.concatenate(
            [widen(mom_qk), widen(mom_vg), widen(mom_mlp), widen(jnp.swapaxes(mom_out, 1, 2))],
            axis=0,
        ).astype(bf16)
        + extra[None]
    )
    both = jnp.stack([stacked, swap(stacked, "y_hi")], axis=1)
    spread = jnp.broadcast_to(both[None], (4,) + both.shape).reshape((groups,) + both.shape[1:])
    arrived = lax.all_to_all(spread, DP, split_axis=0, concat_axis=0, tiled=True)
    far = swap(arrived, "core")
    own = orthogonal(jnp.reshape(chunk_index, (1,)).astype(jnp.int32), arrived, far)
    returned = lax.all_to_all(
        own.reshape(groups, BLOCK, 128), DP, split_axis=0, concat_axis=0, tiled=True
    ).astype(f32)
    returned = jnp.concatenate([returned[8 * i : 8 * i + 8] for i in range(4)], axis=2)

    shrink = 1.0 - muon_rate * decay_rate
    square_scale = 0.2 * math.sqrt(width)
    wide_scale = 0.2 * math.sqrt(max(width, value_width))
    new_qk = qk_w * shrink - (muon_rate * square_scale) * returned[0:2, :, :KEY]
    new_vg = vg_w * shrink - (muon_rate * wide_scale) * returned[2:4, :, :VAL]
    new_mlp = mlp_w * shrink - (muon_rate * wide_scale) * returned[4:6, :, :VAL]
    new_out = out_w * shrink - (muon_rate * wide_scale) * jnp.swapaxes(returned[6:8, :, :VAL], 1, 2)

    rode = jnp.concatenate(
        [jnp.swapaxes(part[..., VAL : VAL + 70], 0, 1) for part in after((arrived, far), own)], axis=0
    ).astype(f32)
    first_total = jnp.sum(rode[..., 6:], axis=(0, 1)).reshape(2 * width)
    rode = (rode[..., :3] + rode[..., 3:6]).reshape(4, width, 3)
    vectors = jnp.sum(rode[:, :, :2], axis=0)
    group_parts = rode[:, :VAL, 2]
    which = jnp.arange(4, dtype=jnp.int32)[:, None] == order[None, :]
    group_whole = jnp.sum(
        jnp.where(which[:, :, None], group_parts[None], 0.0), axis=1
    ).reshape(value_width)
    small_total = jnp.concatenate(
        [first_total, group_whole, vectors[:, 0], vectors[:, 1]]
    )
    moment_new = beta_first * norm_moment + (1.0 - beta_first) * small_total
    second_new = beta_second * norm_second + (1.0 - beta_second) * small_total * small_total
    params_new = norm_params - adam_rate * (moment_new / (1.0 - beta_first**OPT_STEP)) / (
        jnp.sqrt(second_new / (1.0 - beta_second**OPT_STEP)) + adam_eps
    )
    return (
        result,
        input_grad,
        mom_qk,
        mom_vg,
        mom_mlp,
        mom_out,
        new_qk,
        new_vg,
        new_mlp,
        new_out,
        moment_new,
        second_new,
        params_new,
    )


def solution(mesh):
    fine = Mesh(np.asarray(mesh.devices).reshape(SIZES), AXES)
    by_rows = P(DP + TENSOR, None)
    by_columns = P(None, DP, TENSOR)
    by_out = P(None, TENSOR, DP)
    return jax.shard_map(
        shards,
        mesh=fine,
        in_specs=(
            by_rows,
            by_rows,
            by_columns,
            by_columns,
            by_columns,
            by_out,
            by_columns,
            by_columns,
            by_columns,
            by_out,
            P(),
            P(),
            P(),
            P(TENSOR),
            P(),
            P(),
        ),
        out_specs=(
            by_rows,
            by_rows,
            by_columns,
            by_columns,
            by_columns,
            by_out,
            by_columns,
            by_columns,
            by_columns,
            by_out,
            P(),
            P(),
            P(),
        ),
        check_vma=False,
    )
```

```python
import math

import jax
import jax.numpy as jnp
import numpy as np
from jax import lax
from jax.experimental import pallas as pl
from jax.experimental.pallas import tpu as pltpu
from jax.sharding import Mesh
from jax.sharding import PartitionSpec as P

HEADS = 4
NS_ITERS = 5
OPT_STEP = 10
KEY = 256
VAL = 432
LANES = 512
BLOCK = 32

norm_eps = 1e-05
group_eps = 0.01
ns_first = 3.4445
ns_second = -4.775
ns_third = 2.0315
muon_rate = 0.15
muon_beta = 0.95
decay_rate = 0.01
adam_rate = 0.6
beta_first = 0.9
beta_second = 0.95
adam_eps = 1e-08

AXES = ("y_lo", "z_hi", "z_lo", "x", "y_hi", "core")
SIZES = (2, 2, 2, 4, 2, 2)
DP = ("y_lo", "z_hi", "z_lo", "x")
PLANE = ("z_hi", "z_lo", "x")
TENSOR = ("y_hi", "core")
bf16 = jnp.bfloat16
f32 = jnp.float32


def swap(values, axis):
    return lax.ppermute(values, axis, [(0, 1), (1, 0)])


def dot(left, right, dims):
    return lax.dot_general(left, right, (dims, ((), ())), preferred_element_type=f32)


def nn(left, right):
    return dot(left, right, ((1,), (0,)))


def nt(left, right):
    return dot(left, right, ((1,), (1,)))


def tn(left, right):
    return dot(left, right, ((0,), (0,)))


def split(values):
    high = lax.reduce_precision(values, 8, 7)
    return high.astype(bf16), (values - high).astype(bf16)


def widen(values):
    return jnp.pad(values, ((0, 0),) * (values.ndim - 1) + ((0, LANES - values.shape[-1]),))


def tensor_gather(own):
    far = swap(own, "y_hi")
    near = jnp.concatenate([own, far], axis=0)
    return jnp.concatenate([near, swap(near, "core")], axis=0)


def tensor_sum(own, other, earlier=None):
    mine = own + swap(other, "core").astype(f32)
    half = mine.shape[0] // 2
    far = swap(mine[half:].astype(bf16), "y_hi").astype(f32)
    if earlier is not None:
        far = after(far, earlier)
    return mine[:half] + far


def after(values, earlier):
    return values + (earlier[(-1,) * earlier.ndim] * 0).astype(values.dtype)


def normalize(values):
    centre = values - jnp.mean(values, axis=-1, keepdims=True)
    spread = lax.rsqrt(jnp.mean(centre * centre, axis=-1, keepdims=True) + norm_eps)
    return centre * spread, spread


def norm_back(grad_out, gain, normed, spread):
    grad_normed = grad_out * gain
    return spread * (
        grad_normed
        - jnp.mean(grad_normed, axis=-1, keepdims=True)
        - normed * jnp.mean(grad_normed * normed, axis=-1, keepdims=True)
    )


def pairs_apart(values):
    shape = values.shape
    return jnp.swapaxes(values.reshape(shape[:-1] + (KEY // 2, 2)), -1, -2).reshape(shape)


def pairs_together(values):
    shape = values.shape
    return jnp.swapaxes(values.reshape(shape[:-1] + (2, KEY // 2)), -1, -2).reshape(shape)


def sequence_labels(seq_length, seq_group, group, place):
    mine = seq_group == group
    lengths = jnp.where(mine, seq_length, 0)
    ends = jnp.cumsum(lengths, dtype=jnp.int32)
    starts = ends - lengths
    inside = mine[None, :] & (place[:, None] >= starts[None, :]) & (place[:, None] < ends[None, :])
    number = jnp.arange(1, seq_length.shape[0] + 1, dtype=jnp.int32)
    return jnp.sum(jnp.where(inside, number[None, :], 0), axis=1, dtype=jnp.int32)


WIDTH = 1024
TILE = WIDTH // 2
NS_TILE = 256


ROWS = [pl.ds(TILE * i, TILE) for i in range(WIDTH // TILE)]


def in_vmem(kernel, name, out_shape, scratch, *operands):
    n_in, n_out = len(operands), len(out_shape)

    def body(*refs):
        ins, outs = refs[:n_in], refs[n_in : n_in + n_out]
        refs = refs[n_in + n_out :]
        local_in, local_out = refs[:n_in], refs[n_in : n_in + n_out]
        sem_in, sem_out = refs[n_in + n_out : n_in + n_out + 2]
        loads = [
            pltpu.make_async_copy(ins[i], local_in[i], sem_in.at[i]) for i in range(n_in)
        ]
        stores = [
            pltpu.make_async_copy(local_out[i], outs[i], sem_out.at[i]) for i in range(n_out)
        ]
        for load in loads:
            load.start()
        pending = set(range(n_in))
        started = set()

        def ready(*which):
            for i in which:
                if i in pending:
                    pending.remove(i)
                    loads[i].wait()

        def done(*which):
            for i in which:
                started.add(i)
                stores[i].start()

        kernel(ready, done, *local_in, *local_out, *refs[n_in + n_out + 2 :])
        ready(*range(n_in))
        done(*(i for i in range(n_out) if i not in started))
        for store in stores:
            store.wait()

    held = sum(math.prod(a.shape) * a.dtype.itemsize for a in (*operands, *out_shape))
    return pl.pallas_call(
        body,
        out_shape=[pltpu.HBM(a.shape, a.dtype) for a in out_shape],
        in_specs=[pl.BlockSpec(memory_space=pltpu.HBM)] * n_in,
        out_specs=[pl.BlockSpec(memory_space=pltpu.HBM)] * n_out,
        scratch_shapes=[pltpu.VMEM(a.shape, a.dtype) for a in operands]
        + [pltpu.VMEM(a.shape, a.dtype) for a in out_shape]
        + [pltpu.SemaphoreType.DMA((n_in,)), pltpu.SemaphoreType.DMA((n_out,))]
        + scratch,
        compiler_params=pltpu.CompilerParams(vmem_limit_bytes=held + 12 * 2**20),
        cost_estimate=pl.CostEstimate(flops=1, bytes_accessed=1, transcendentals=0),
        name=name,
    )(*(pltpu.with_memory_space_constraint(a, pltpu.HBM) for a in operands))


def put_halves(i, part, own_ref, other_ref):
    if i == 0:
        own_ref[...] = part
    else:
        other_ref[...] = part.astype(bf16)


def turn(first, second, cos_table, sin_table):
    return first * cos_table - second * sin_table, second * cos_table + first * sin_table


def masked(scores, rows, cols_ref, line_ref):
    label, place = cols_ref[rows, 0:1], cols_ref[rows, 1:2]
    linked = (label == line_ref[0:1, :]) & (label > 0.0) & (place >= line_ref[1:2, :])
    return jnp.where(linked, scores * (cols_ref[rows, 2:3] * line_ref[2:3, :]), 0.0)


def retention_kernel(
    ready, done, h_ref, w_ref, turn_ref, cols_ref, line_ref, gain_ref,
    q_ref, k_ref, v_ref, p_ref, gate_ref, hat_ref, inv_ref, mixed_ref, own_ref, other_ref,
):
    ready(0, 1, 2)
    half = KEY // 2
    for rows in ROWS:
        h = h_ref[rows, :]
        cos_table, sin_table = turn_ref[rows, :half], turn_ref[rows, half:]
        query = nn(h, w_ref[:, 0:KEY])
        first, second = turn(query[:, :half], query[:, half:], cos_table, sin_table)
        q_ref[rows, 0:half] = first.astype(bf16)
        q_ref[rows, half:KEY] = second.astype(bf16)
        keys = nn(h, w_ref[:, KEY : 2 * KEY]) * KEY**-0.5
        first, second = turn(keys[:, :half], keys[:, half:], cos_table, sin_table)
        k_ref[rows, 0:half] = first.astype(bf16)
        k_ref[rows, half:KEY] = second.astype(bf16)
        v_ref[rows, :] = nn(h, w_ref[:, LANES : 2 * LANES]).astype(bf16)
        gate_ref[rows, :] = nn(h, w_ref[:, 2 * LANES : 3 * LANES])
    done(0, 1, 2, 4)
    ready(3, 4, 5)
    for i, rows in enumerate(ROWS):
        weights = masked(nt(q_ref[rows, :], k_ref[...]), rows, cols_ref, line_ref).astype(bf16)
        p_ref[rows, :] = weights
        retained = nn(weights, v_ref[...])
        inverse = lax.rsqrt(
            jnp.sum(retained * retained, axis=-1, keepdims=True) * (1.0 / VAL) + group_eps
        )
        inv_ref[rows, :] = jnp.broadcast_to(inverse, (TILE, 128))
        hat = retained * inverse
        hat_ref[rows, :] = hat
        gate = gate_ref[rows, :]
        swish = gate * (1.0 / (1.0 + jnp.exp(-gate)))
        mixed = (hat * gain_ref[...] * swish).astype(bf16)
        mixed_ref[rows, :] = mixed
        put_halves(i, nt(mixed, w_ref[:, 3 * LANES : 4 * LANES]), own_ref, other_ref)


def retention(*operands):
    shape = jax.ShapeDtypeStruct
    return in_vmem(
        retention_kernel,
        "retention",
        [
            shape((WIDTH, KEY), bf16),
            shape((WIDTH, KEY), bf16),
            shape((WIDTH, LANES), bf16),
            shape((WIDTH, WIDTH), bf16),
            shape((WIDTH, LANES), f32),
            shape((WIDTH, LANES), f32),
            shape((WIDTH, 128), f32),
            shape((WIDTH, LANES), bf16),
            shape((WIDTH // 2, WIDTH), f32),
            shape((WIDTH // 2, WIDTH), bf16),
        ],
        [],
        *operands,
    )


def feed_kernel(
    ready, done, h_ref, cot_ref, w_ref, hidden_ref, gate_ref, up_ref, own_ref, other_ref
):
    ready(0, 2, 1)
    for i, rows in reversed(list(enumerate(ROWS))):
        pre_gate = nn(h_ref[rows, :], w_ref[:, 0:LANES])
        pre_up = nn(h_ref[rows, :], w_ref[:, LANES : 2 * LANES])
        grad_hidden = nn(cot_ref[rows, :], w_ref[:, 2 * LANES : 3 * LANES])
        cumulative = 0.5 * (1.0 + lax.erf(pre_gate * (1.0 / math.sqrt(2.0))))
        density = jnp.exp(-0.5 * pre_gate * pre_gate) * (1.0 / math.sqrt(2.0 * math.pi))
        gelu_gate = pre_gate * cumulative
        hidden_ref[rows, :] = (gelu_gate * pre_up).astype(bf16)
        grad_gate = (grad_hidden * pre_up * (cumulative + pre_gate * density)).astype(bf16)
        grad_up = (grad_hidden * gelu_gate).astype(bf16)
        gate_ref[rows, :] = grad_gate
        up_ref[rows, :] = grad_up
        part = nt(grad_gate, w_ref[:, 0:LANES]) + nt(grad_up, w_ref[:, LANES : 2 * LANES])
        put_halves(i, part, own_ref, other_ref)


def feed(*operands):
    shape = jax.ShapeDtypeStruct
    return in_vmem(
        feed_kernel,
        "feed_forward",
        [shape((WIDTH, LANES), bf16)] * 3
        + [shape((WIDTH // 2, WIDTH), f32), shape((WIDTH // 2, WIDTH), bf16)],
        [],
        *operands,
    )


def early_kernel(
    ready, done, h_ref, cot_ref, gate_ref, up_ref, hidden_ref, out_ref):
    ready(0, 1, 2, 3, 4)
    for i, at in enumerate(ROWS):
        for j, (left, right) in enumerate(
            ((h_ref, gate_ref), (h_ref, up_ref), (cot_ref, hidden_ref))
        ):
            part = tn(left[:, at], right[...]).astype(bf16)
            out_ref[:, i, :, pl.ds(LANES * j, LANES)] = part.reshape(16, BLOCK, LANES)


def early_grads(*operands):
    return in_vmem(
        early_kernel,
        "feed_forward_grads",
        [jax.ShapeDtypeStruct((16, 2, BLOCK, 3 * LANES), bf16)],
        [],
        *operands,
    )[0]


def back_gate_kernel(
    ready, done, grad_ref, w_ref, gate_ref, hat_ref, inv_ref, gain_ref, gate_out, ret_out, gain_out
):
    ready(0, 1, 2, 3, 4, 5)
    total = jnp.zeros((1, LANES), f32)
    gain = gain_ref[...]
    for rows in ROWS:
        grad_mixed = nn(grad_ref[rows, :], w_ref[:, 3 * LANES : 4 * LANES])
        gate, hat, inverse = gate_ref[rows, :], hat_ref[rows, :], inv_ref[rows, 0:1]
        sig = 1.0 / (1.0 + jnp.exp(-gate))
        swish = gate * sig
        grad_grouped = grad_mixed * swish
        gate_out[rows, :] = (
            grad_mixed * (hat * gain) * (sig + swish * (1.0 - sig))
        ).astype(bf16)
        total += jnp.sum(grad_grouped * hat, axis=0, keepdims=True)
        grad_hat = grad_grouped * gain
        inner = jnp.sum(grad_hat * hat, axis=-1, keepdims=True) * (1.0 / VAL)
        ret_out[rows, :] = (inverse * (grad_hat - hat * inner)).astype(bf16)
    gain_out[...] = total


def back_gate(*operands):
    shape = jax.ShapeDtypeStruct
    return in_vmem(
        back_gate_kernel,
        "gate_backward",
        [shape((WIDTH, LANES), bf16)] * 2 + [shape((1, LANES), f32)],
        [],
        *operands,
    )


def back_scores_kernel(
    ready, done, ret_ref, q_ref, k_ref, v_ref, p_ref, turn_ref, cols_ref, line_ref, order_ref,
    q_out, k_out, v_out, scores,
):
    ready(0, 3, 6, 7, 2, 5)
    half = KEY // 2
    for rows in ROWS:
        part = masked(nt(ret_ref[rows, :], v_ref[...]), rows, cols_ref, line_ref).astype(bf16)
        scores[rows, :] = part
        turned = nn(part, k_ref[...])
        first, second = turn(
            turned[:, :half], turned[:, half:], turn_ref[rows, :half], -turn_ref[rows, half:]
        )
        q_out[rows, 0:half] = first.astype(bf16)
        q_out[rows, half:KEY] = second.astype(bf16)
    done(0)
    ready(4, 1)
    for rows in ROWS:
        v_out[rows, :] = tn(p_ref[:, rows], ret_ref[...]).astype(bf16)
        turned = tn(scores[:, rows], q_ref[...])
        first, second = turn(
            turned[:, :half], turned[:, half:], turn_ref[rows, :half], -turn_ref[rows, half:]
        )
        k_out[rows, 0:half] = first.astype(bf16)
        k_out[rows, half:KEY] = second.astype(bf16)


def back_scores(*operands):
    shape = jax.ShapeDtypeStruct
    return in_vmem(
        back_scores_kernel,
        "scores_backward",
        [shape((WIDTH, KEY), bf16)] * 2 + [shape((WIDTH, LANES), bf16)],
        [pltpu.VMEM((WIDTH, WIDTH), bf16)],
        *operands,
    )


def late_kernel(
    ready, done, h_ref, grad_ref, gate_ref, mixed_ref, q_ref, k_ref, v_ref, ride_ref, order_ref,
    out_ref,
):
    ready(*range(8))
    for rows in ROWS:
        left = h_ref[:, rows]
        out_ref[rows, 0:KEY] = tn(left, q_ref[...]).astype(bf16)
        out_ref[rows, KEY : 2 * KEY] = (tn(left, k_ref[...]) * KEY**-0.5).astype(bf16)
        part = tn(left, v_ref[...]).astype(bf16)
        out_ref[rows, LANES : LANES + 384] = part[:, 0:384]
        out_ref[rows, LANES + 384 : 2 * LANES] = part[:, 384:LANES] + ride_ref[rows, :]
        out_ref[rows, 2 * LANES : 3 * LANES] = tn(left, gate_ref[...]).astype(bf16)
        out_ref[rows, 3 * LANES : 4 * LANES] = tn(grad_ref[:, rows], mixed_ref[...]).astype(bf16)


def late_grads(*operands):
    return in_vmem(
        late_kernel,
        "retention_grads",
        [jax.ShapeDtypeStruct((WIDTH, 4 * LANES), bf16)],
        [],
        *operands,
    )[0]


def input_kernel(
    ready, done, q_ref, k_ref, v_ref, gate_ref, w_ref, order_ref, own_ref, other_ref
):
    ready(0, 1, 2, 3, 4)
    for i, rows in reversed(list(enumerate(ROWS))):
        part = nt(q_ref[rows, :], w_ref[:, 0:KEY])
        part += nt(k_ref[rows, :], w_ref[:, KEY : 2 * KEY]) * KEY**-0.5
        part += nt(v_ref[rows, :], w_ref[:, LANES : 2 * LANES])
        part += nt(gate_ref[rows, :], w_ref[:, 2 * LANES : 3 * LANES])
        put_halves(i, part, own_ref, other_ref)


def input_parts(*operands):
    shape = jax.ShapeDtypeStruct
    return in_vmem(
        input_kernel,
        "input_grad_parts",
        [shape((WIDTH // 2, WIDTH), f32), shape((WIDTH // 2, WIDTH), bf16)],
        [],
        *operands,
    )


def iterate_kernel(
    chunk_ref, near_ref, far_ref, out_ref, vector_ref, first_ref, whole, gram, high, low, shifted, rest, prod, prod_b, own, own_b
):
    tiles = WIDTH // NS_TILE
    at = [pl.ds(NS_TILE * i, NS_TILE) for i in range(tiles)]
    eye = (
        lax.broadcasted_iota(jnp.int32, (NS_TILE, NS_TILE), 0)
        == lax.broadcasted_iota(jnp.int32, (NS_TILE, NS_TILE), 1)
    ).astype(f32)
    keep = lax.broadcasted_iota(jnp.int32, (WIDTH, 128), 1) < VAL - 384
    riders = jnp.zeros((WIDTH, 128), f32)
    for p in range(4):
        source = near_ref if p < 2 else far_ref
        piece = source[:, p % 2].reshape(WIDTH, LANES)
        whole[p, :, 0:384] = piece[:, 0:384]
        whole[p, :, 384:512] = jnp.where(keep, piece[:, 384:512], jnp.zeros((), bf16))
        ride = piece[:, 384:512].astype(f32)
        riders += ride
        lines = ride.T
        vector_ref[2 + p : 3 + p, :] = lines[50:51, :] + lines[53:54, :]
    lines = riders.T
    vector_ref[0:2, :] = lines[48:50, :] + lines[51:53, :]
    vector_ref[6:8, :] = jnp.zeros((2, WIDTH), f32)
    first_ref[...] = jnp.sum(riders.reshape(WIDTH // BLOCK, BLOCK, 128), axis=0)

    trace = jnp.float32(0.0)
    for i in range(tiles):
        for j in range(tiles):
            block = jnp.zeros((NS_TILE, NS_TILE), f32)
            for p in range(4):
                block += nt(whole[p, at[i], :], whole[p, at[j], :])
            gram[at[i], at[j]] = block
            if i == j:
                trace += jnp.sum(block * eye)
    inverse = 1.0 / (jnp.sqrt(trace) + 1e-07)
    for q in range(4):

        @pl.when(chunk_ref[0] == q)
        def _():
            own[...] = whole[0, :, 128 * q : 128 * (q + 1)].astype(f32) * inverse

    def store(i, j, block, mean):
        gram[at[i], at[j]] = block
        top = block.astype(bf16)
        high[at[i], at[j]] = top
        low[at[i], at[j]] = (block - top.astype(f32)).astype(bf16)
        if i == j:
            top = (block - mean * eye).astype(bf16)
        shifted[at[i], at[j]] = top

    mean = trace * inverse * inverse * (1.0 / WIDTH)
    for i in range(tiles):
        for j in range(tiles):
            store(i, j, gram[at[i], at[j]] * (inverse * inverse), mean)

    def advance(mean):
        level = ns_second * mean + ns_third * mean * mean
        alpha = ns_first + level
        for i in range(tiles):
            for j in range(tiles):
                block = (ns_second + 2.0 * ns_third * mean) * gram[at[i], at[j]] + ns_third * nn(
                    shifted[at[i], :], shifted[:, at[j]]
                )
                if i == j:
                    block -= (ns_third * mean * mean + level) * eye
                rest[at[i], at[j]] = block.astype(bf16)
        values = own[...]
        top = values.astype(bf16)
        own_b[:, 0:128] = top
        own_b[:, 128:256] = (values - top.astype(f32)).astype(bf16)
        for i in range(tiles):
            moved = nn(rest[at[i], :], own_b[...])
            own[at[i], :] = alpha * own[at[i], :] + (moved[:, 0:128] + moved[:, 128:256])
        return alpha

    def turn(_, mean):
        alpha = advance(mean)
        for i in range(tiles):
            for j in range(tiles):
                block = nn(high[at[i], :], rest[:, at[j]]) + nn(low[at[i], :], rest[:, at[j]])
                prod[at[i], at[j]] = block
                prod_b[at[i], at[j]] = block.astype(bf16)
        trace = jnp.float32(0.0)
        for i in range(tiles):
            for j in range(tiles):
                block = alpha * prod[at[i], at[j]] + 0.5 * nn(rest[at[i], :], prod_b[:, at[j]])
                prod[at[i], at[j]] = block
                if i == j:
                    trace += jnp.sum(block * eye)
        later = alpha * alpha * mean + trace * (2.0 / WIDTH)
        for i in range(tiles):
            for j in range(tiles):
                block = (alpha * alpha) * gram[at[i], at[j]] + (
                    prod[at[i], at[j]] + prod[at[j], at[i]].T
                )
                store(i, j, block, later)
        return later

    advance(lax.fori_loop(0, NS_ITERS - 1, turn, mean))
    out_ref[...] = own[...].astype(bf16)


def orthogonal(chunk, near, far):
    square = (WIDTH, WIDTH)
    return pl.pallas_call(
        iterate_kernel,
        out_shape=[
            jax.ShapeDtypeStruct((WIDTH, 128), bf16),
            jax.ShapeDtypeStruct((8, WIDTH), f32),
            jax.ShapeDtypeStruct((BLOCK, 128), f32),
        ],
        in_specs=[pl.BlockSpec(memory_space=pltpu.SMEM)]
        + [pl.BlockSpec(memory_space=pltpu.VMEM)] * 2,
        out_specs=[pl.BlockSpec(memory_space=pltpu.VMEM)] * 3,
        scratch_shapes=[
            pltpu.VMEM((4, WIDTH, LANES), bf16),
            pltpu.VMEM(square, f32),
            pltpu.VMEM(square, bf16),
            pltpu.VMEM(square, bf16),
            pltpu.VMEM(square, bf16),
            pltpu.VMEM(square, bf16),
            pltpu.VMEM(square, f32),
            pltpu.VMEM(square, bf16),
            pltpu.VMEM((WIDTH, 128), f32),
            pltpu.VMEM((WIDTH, 256), bf16),
        ],
        compiler_params=pltpu.CompilerParams(vmem_limit_bytes=48 * 2**20),
        cost_estimate=pl.CostEstimate(
            flops=42 * 10**9, bytes_accessed=5 * 2**20, transcendentals=0
        ),
        name="orthogonalize",
    )(chunk, near, far)


def shards(
    tokens,
    cotangent,
    qk_w,
    vg_w,
    mlp_w,
    out_w,
    qk_mom,
    vg_mom,
    mlp_mom,
    out_mom,
    norm_params,
    norm_moment,
    norm_second,
    decay_gap,
    seq_length,
    seq_group,
):
    rows, width = tokens.shape
    slots = 4 * rows
    groups = 32
    value_width = 4 * VAL
    key_scale = KEY ** (-0.5)
    dp_index = lax.axis_index(DP)
    tensor_index = lax.axis_index(TENSOR)
    chunk_index = lax.axis_index(("y_lo", "z_hi"))

    gain_one = norm_params[0:width]
    shift_one = norm_params[width : 2 * width]
    group_gain = jnp.pad(
        lax.dynamic_slice_in_dim(norm_params, 2 * width + tensor_index * VAL, VAL),
        (0, LANES - VAL),
    )
    gain_two = norm_params[2 * width + value_width : 3 * width + value_width]
    shift_two = norm_params[3 * width + value_width : 4 * width + value_width]

    out_rows = jnp.swapaxes(out_w, 1, 2)
    first_half = lax.axis_index("y_lo") == 0

    def weight_rows(parts):
        packed = jnp.concatenate(parts, axis=1).astype(bf16)
        far = swap(packed, "y_lo")
        pair = jnp.stack([jnp.where(first_half, packed, far), jnp.where(first_half, far, packed)])
        return pair

    def weight_gather(pair):
        return lax.all_gather(pair, PLANE, axis=1, tiled=True).reshape(width, -1)

    pair_ret = weight_rows(
        [
            pairs_apart(qk_w[0]),
            pairs_apart(qk_w[1]),
            widen(vg_w[0]),
            widen(vg_w[1]),
            widen(out_rows[0]),
        ]
    )
    pair_ff = weight_rows([widen(mlp_w[0]), widen(mlp_w[1]), widen(out_rows[1])])
    gathered = weight_gather(pair_ret)
    gathered_ff = weight_gather(after(pair_ff, gathered))

    whole_tokens = tensor_gather(tokens)
    whole_cot = tensor_gather(after(cotangent, whole_tokens))
    order = jnp.stack([tensor_index, tensor_index ^ 2, tensor_index ^ 1, tensor_index ^ 3])
    place = (order[:, None] * rows + jnp.arange(rows, dtype=jnp.int32)[None, :]).reshape(slots)

    freqs = 1.0 / 10000.0 ** np.linspace(0.0, 1.0, KEY // 2)
    angles = np.arange(slots)[:, None] * freqs[None, :]
    tables = jnp.asarray(
        np.concatenate([np.cos(angles), np.sin(angles)], axis=1).astype(np.float32)
    ).reshape(4, rows, KEY)
    turned = tables[order].reshape(slots, KEY)

    labels = sequence_labels(seq_length, seq_group, dp_index, place)
    log_decay = jnp.log1p(-decay_gap[0])
    away = (place - slots // 2).astype(f32) * log_decay
    label_place = [labels.astype(f32), place.astype(f32)]
    columns = jnp.pad(jnp.stack(label_place + [jnp.exp(away)], axis=1), ((0, 0), (0, 125)))
    line = jnp.pad(jnp.stack(label_place + [jnp.exp(-away)], axis=0), ((0, 5), (0, 0)))
    gain_line = after(group_gain[None, :], whole_cot)

    hat_one, _ = normalize(whole_tokens.astype(f32))
    whole_one = (hat_one * gain_one + shift_one).astype(bf16)
    query, keys, values, weights, gate, hat_group, inv_group, mixed, own, other = retention(
        whole_one, gathered, turned, columns, line, gain_line
    )
    middle = tokens.astype(f32) + tensor_sum(own, other)
    hat_two, inv_two = normalize(middle)
    whole_two = tensor_gather((hat_two * gain_two + shift_two).astype(bf16))
    hidden, grad_gate, grad_up, own, other = feed(whole_two, whole_cot, gathered_ff)
    early = early_grads(whole_two, whole_cot, grad_gate, grad_up, hidden)
    grad_normed_two = tensor_sum(own, other, early)

    early_in = lax.all_to_all(early, PLANE, split_axis=0, concat_axis=0, tiled=True)
    early_halves = jnp.sum(early_in.astype(f32), axis=0)
    early_far = swap(
        jnp.where(first_half, early_halves[1], early_halves[0]).astype(bf16), "y_lo"
    )
    early_sum = jnp.where(first_half, early_halves[0], early_halves[1]) + early_far.astype(f32)

    grad_middle = cotangent.astype(f32) + norm_back(grad_normed_two, gain_two, hat_two, inv_two)
    grad_one = tensor_gather(grad_middle.astype(bf16))
    gain_two_grad = jnp.sum(grad_normed_two * hat_two, axis=0)
    shift_two_grad = jnp.sum(grad_normed_two, axis=0)

    grad_gate_ret, grad_retained, group_gain_grad = back_gate(
        grad_one, gathered, gate, hat_group, inv_group, gain_line
    )
    w_3 = gathered_ff[:, 2 * LANES : 3 * LANES]
    half = slots // 2
    later_hidden = after(hidden, grad_one)
    other = nt(later_hidden[half:], w_3).astype(bf16)
    near = nt(later_hidden[:half], w_3) + swap(other, "core").astype(f32)
    near_far = near[rows:].astype(bf16)
    result = (middle + near[:rows] + swap(near_far, "y_hi").astype(f32)).astype(bf16)
    grad_query, grad_key, grad_values = back_scores(
        grad_retained, query, keys, values, weights, turned, columns, line,
        near_far[:16, :128],
    )
    small = jnp.stack(
        [gain_two_grad, shift_two_grad, jnp.pad(group_gain_grad[0], (0, width - LANES))], axis=1
    )
    small_high, small_low = split(small)
    riders = jnp.pad(
        jnp.concatenate([small_high, small_low], axis=1), ((0, 0), (VAL - 384, LANES - VAL - 6))
    )
    late = late_grads(
        whole_one, grad_one, grad_gate_ret, mixed, grad_query, grad_key, grad_values, riders,
        result[:16, :128],
    )
    late_in = lax.all_to_all(
        late.reshape(groups, BLOCK, -1), DP, split_axis=0, concat_axis=0, tiled=True
    )
    own, other = input_parts(
        grad_query, grad_key, grad_values, grad_gate_ret, gathered, late[:16, :128]
    )
    grad_normed_one = tensor_sum(own, other)
    own_hat, own_inv = normalize(after(tokens, late).astype(f32))
    gain_one_grad = jnp.sum(grad_normed_one * own_hat, axis=0)
    shift_one_grad = jnp.sum(grad_normed_one, axis=0)
    input_grad = grad_middle + norm_back(grad_normed_one, gain_one, own_hat, own_inv)

    late_sum = jnp.sum(late_in.astype(f32), axis=0)
    small_sum = late_sum[:, LANES + VAL : LANES + VAL + 6]
    small_sum = small_sum[:, :3] + small_sum[:, 3:]

    grad_qk = pairs_together(jnp.stack([late_sum[:, 0:256], late_sum[:, 256:512]]))
    grad_vg = jnp.stack([late_sum[:, 512 : 512 + VAL], late_sum[:, 1024 : 1024 + VAL]])
    grad_mlp = jnp.stack([early_sum[:, 0:VAL], early_sum[:, 512 : 512 + VAL]])
    grad_out_t = jnp.stack([late_sum[:, 1536 : 1536 + VAL], early_sum[:, 1024 : 1024 + VAL]])
    mom_qk = muon_beta * qk_mom + grad_qk
    mom_vg = muon_beta * vg_mom + grad_vg
    mom_mlp = muon_beta * mlp_mom + grad_mlp
    mom_out = muon_beta * out_mom + jnp.swapaxes(grad_out_t, 1, 2)

    piece_high, piece_low = split(small_sum)
    first_norm = jnp.concatenate([gain_one_grad, shift_one_grad]).astype(bf16)
    extra = jnp.pad(
        jnp.concatenate([piece_high, piece_low, first_norm.reshape(BLOCK, 64)], axis=1),
        ((0, 0), (VAL, LANES - VAL - 70)),
    )
    stacked = (
        jnp.concatenate(
            [widen(mom_qk), widen(mom_vg), widen(mom_mlp), widen(jnp.swapaxes(mom_out, 1, 2))],
            axis=0,
        ).astype(bf16)
        + extra[None]
    )
    both = jnp.stack([stacked, swap(stacked, "y_hi")], axis=1)
    spread = jnp.broadcast_to(both[None], (4,) + both.shape).reshape((groups,) + both.shape[1:])
    arrived = lax.all_to_all(spread, DP, split_axis=0, concat_axis=0, tiled=True)
    far = swap(arrived, "core")
    own, vectors, first_total = orthogonal(
        jnp.reshape(chunk_index, (1,)).astype(jnp.int32), arrived, far
    )
    returned = lax.all_to_all(
        own.reshape(groups, BLOCK, 128), DP, split_axis=0, concat_axis=0, tiled=True
    ).astype(f32)
    returned = jnp.concatenate([returned[8 * i : 8 * i + 8] for i in range(4)], axis=2)

    shrink = 1.0 - muon_rate * decay_rate
    square_scale = 0.2 * math.sqrt(width)
    wide_scale = 0.2 * math.sqrt(max(width, value_width))
    new_qk = qk_w * shrink - (muon_rate * square_scale) * returned[0:2, :, :KEY]
    new_vg = vg_w * shrink - (muon_rate * wide_scale) * returned[2:4, :, :VAL]
    new_mlp = mlp_w * shrink - (muon_rate * wide_scale) * returned[4:6, :, :VAL]
    new_out = out_w * shrink - (muon_rate * wide_scale) * jnp.swapaxes(returned[6:8, :, :VAL], 1, 2)

    first_total = first_total[:, 54:118].reshape(2 * width)
    group_parts = vectors[2:6, :VAL]
    which = jnp.arange(4, dtype=jnp.int32)[:, None] == order[None, :]
    group_whole = jnp.sum(
        jnp.where(which[:, :, None], group_parts[None], 0.0), axis=1
    ).reshape(value_width)
    small_total = jnp.concatenate(
        [first_total, group_whole, vectors[0], vectors[1]]
    )
    moment_new = beta_first * norm_moment + (1.0 - beta_first) * small_total
    second_new = beta_second * norm_second + (1.0 - beta_second) * small_total * small_total
    params_new = norm_params - adam_rate * (moment_new / (1.0 - beta_first**OPT_STEP)) / (
        jnp.sqrt(second_new / (1.0 - beta_second**OPT_STEP)) + adam_eps
    )
    return (
        result,
        input_grad,
        mom_qk,
        mom_vg,
        mom_mlp,
        mom_out,
        new_qk,
        new_vg,
        new_mlp,
        new_out,
        moment_new,
        second_new,
        params_new,
    )


def solution(mesh):
    fine = Mesh(np.asarray(mesh.devices).reshape(SIZES), AXES)
    by_rows = P(DP + TENSOR, None)
    by_columns = P(None, DP, TENSOR)
    by_out = P(None, TENSOR, DP)
    return jax.shard_map(
        shards,
        mesh=fine,
        in_specs=(
            by_rows,
            by_rows,
            by_columns,
            by_columns,
            by_columns,
            by_out,
            by_columns,
            by_columns,
            by_columns,
            by_out,
            P(),
            P(),
            P(),
            P(TENSOR),
            P(),
            P(),
        ),
        out_specs=(
            by_rows,
            by_rows,
            by_columns,
            by_columns,
            by_columns,
            by_out,
            by_columns,
            by_columns,
            by_columns,
            by_out,
            P(),
            P(),
            P(),
        ),
        check_vma=False,
    )
```

```python
import math

import jax
import jax.numpy as jnp
import numpy as np
from jax import lax
from jax.experimental import pallas as pl
from jax.experimental.pallas import tpu as pltpu
from jax.sharding import Mesh
from jax.sharding import PartitionSpec as P

HEADS = 4
NS_ITERS = 5
OPT_STEP = 10
KEY = 256
VAL = 432
LANES = 512
BLOCK = 32

norm_eps = 1e-05
group_eps = 0.01
ns_first = 3.4445
ns_second = -4.775
ns_third = 2.0315
muon_rate = 0.15
muon_beta = 0.95
decay_rate = 0.01
adam_rate = 0.6
beta_first = 0.9
beta_second = 0.95
adam_eps = 1e-08

AXES = ("y_lo", "z_hi", "z_lo", "x", "y_hi", "core")
SIZES = (2, 2, 2, 4, 2, 2)
DP = ("y_lo", "z_hi", "z_lo", "x")
PLANE = ("z_hi", "z_lo", "x")
TENSOR = ("y_hi", "core")
bf16 = jnp.bfloat16
f32 = jnp.float32


def swap(values, axis):
    return lax.ppermute(values, axis, [(0, 1), (1, 0)])


def dot(left, right, dims):
    return lax.dot_general(left, right, (dims, ((), ())), preferred_element_type=f32)


def nn(left, right):
    return dot(left, right, ((1,), (0,)))


def nt(left, right):
    return dot(left, right, ((1,), (1,)))


def tn(left, right):
    return dot(left, right, ((0,), (0,)))


def split(values):
    high = lax.reduce_precision(values, 8, 7)
    return high.astype(bf16), (values - high).astype(bf16)


def widen(values):
    return jnp.pad(values, ((0, 0),) * (values.ndim - 1) + ((0, LANES - values.shape[-1]),))


def tensor_gather(own):
    far = swap(own, "y_hi")
    near = jnp.concatenate([own, far], axis=0)
    return jnp.concatenate([near, swap(near, "core")], axis=0)


def tensor_sum(own, other):
    mine = own + swap(other, "core").astype(f32)
    half = mine.shape[0] // 2
    return mine[:half], swap(mine[half:].astype(bf16), "y_hi")


def together(first, second):
    return lax.optimization_barrier((first, second))


def normalize(values):
    centre = values - jnp.mean(values, axis=-1, keepdims=True)
    spread = lax.rsqrt(jnp.mean(centre * centre, axis=-1, keepdims=True) + norm_eps)
    return centre * spread, spread


def norm_back(grad_out, gain, normed, spread):
    grad_normed = grad_out * gain
    return spread * (
        grad_normed
        - jnp.mean(grad_normed, axis=-1, keepdims=True)
        - normed * jnp.mean(grad_normed * normed, axis=-1, keepdims=True)
    )


def pairs_apart(values):
    shape = values.shape
    return jnp.swapaxes(values.reshape(shape[:-1] + (KEY // 2, 2)), -1, -2).reshape(shape)


def pairs_together(values):
    shape = values.shape
    return jnp.swapaxes(values.reshape(shape[:-1] + (2, KEY // 2)), -1, -2).reshape(shape)


def sequence_labels(seq_length, seq_group, group, place):
    mine = seq_group == group
    lengths = jnp.where(mine, seq_length, 0)
    ends = jnp.cumsum(lengths, dtype=jnp.int32)
    starts = ends - lengths
    inside = mine[None, :] & (place[:, None] >= starts[None, :]) & (place[:, None] < ends[None, :])
    number = jnp.arange(1, seq_length.shape[0] + 1, dtype=jnp.int32)
    return jnp.sum(jnp.where(inside, number[None, :], 0), axis=1, dtype=jnp.int32)


WIDTH = 1024
TILE = WIDTH // 2
NS_TILE = 256


ROWS = [pl.ds(TILE * i, TILE) for i in range(WIDTH // TILE)]


STORES = 12


def in_vmem(kernel, name, out_shape, scratch, *operands):
    operands = [a if isinstance(a, tuple) else (a, 0, a.shape[1]) for a in operands]
    n_in, n_out = len(operands), len(out_shape)

    def body(*refs):
        ins, outs = refs[:n_in], refs[n_in : n_in + n_out]
        refs = refs[n_in + n_out :]
        local_in, local_out = refs[:n_in], refs[n_in : n_in + n_out]
        sem_in, sem_out = refs[n_in + n_out : n_in + n_out + 2]
        loads = []
        for i, (array, first, columns) in enumerate(operands):
            source = ins[i] if columns == array.shape[1] else ins[i].at[:, pl.ds(first, columns)]
            loads.append(pltpu.make_async_copy(source, local_in[i], sem_in.at[i]))
            loads[i].start()
        pending = set(range(n_in))
        stores = []

        def ready(*which):
            for i in which:
                if i in pending:
                    pending.remove(i)
                    loads[i].wait()

        def done(i, *index):
            source, target = local_out[i], outs[i]
            if index:
                source, target = source.at[index], target.at[index]
            stores.append(pltpu.make_async_copy(source, target, sem_out.at[len(stores)]))
            stores[-1].start()

        kernel(ready, done, *local_in, *local_out, *refs[n_in + n_out + 2 :])
        ready(*range(n_in))
        for store in stores:
            store.wait()

    local = [pltpu.VMEM((a.shape[0], columns), a.dtype) for a, _, columns in operands]
    local += [pltpu.VMEM(a.shape, a.dtype) for a in out_shape]
    held = sum(math.prod(a.shape) * jnp.dtype(a.dtype).itemsize for a in local)
    return pl.pallas_call(
        body,
        out_shape=[pltpu.HBM(a.shape, a.dtype) for a in out_shape],
        in_specs=[pl.BlockSpec(memory_space=pltpu.HBM)] * n_in,
        out_specs=[pl.BlockSpec(memory_space=pltpu.HBM)] * n_out,
        scratch_shapes=local
        + [pltpu.SemaphoreType.DMA((n_in,)), pltpu.SemaphoreType.DMA((STORES,))]
        + scratch,
        compiler_params=pltpu.CompilerParams(vmem_limit_bytes=held + 14 * 2**20),
        cost_estimate=pl.CostEstimate(flops=1, bytes_accessed=1, transcendentals=0),
        name=name,
    )(*(pltpu.with_memory_space_constraint(a, pltpu.HBM) for a, _, _ in operands))


def put_halves(done, i, part, own_ref, other_ref, own, other):
    if i == 0:
        own_ref[...] = part
        done(own)
    else:
        other_ref[...] = part.astype(bf16)
        done(other)


def turn(first, second, cos_table, sin_table):
    return first * cos_table - second * sin_table, second * cos_table + first * sin_table


def masked(scores, rows, cols_ref, line_ref):
    label, place = cols_ref[rows, 0:1], cols_ref[rows, 1:2]
    linked = (label == line_ref[0:1, :]) & (label > 0.0) & (place >= line_ref[1:2, :])
    return jnp.where(linked, scores * (cols_ref[rows, 2:3] * line_ref[2:3, :]), 0.0)


def retention_kernel(
    ready, done, h_ref, wqk_ref, wv_ref, wg_ref, wo_ref, turn_ref, cols_ref, line_ref, gain_ref,
    q_ref, k_ref, v_ref, p_ref, gate_ref, hat_ref, inv_ref, mixed_ref, own_ref, other_ref,
):
    half = KEY // 2
    ready(0, 1, 5)
    for rows in ROWS:
        cos_table, sin_table = turn_ref[rows, :half], turn_ref[rows, half:]
        both = nn(h_ref[rows, :], wqk_ref[...])
        query, keys = both[:, :KEY], both[:, KEY:] * KEY**-0.5
        first, second = turn(query[:, :half], query[:, half:], cos_table, sin_table)
        q_ref[rows, 0:half] = first.astype(bf16)
        q_ref[rows, half:KEY] = second.astype(bf16)
        first, second = turn(keys[:, :half], keys[:, half:], cos_table, sin_table)
        k_ref[rows, 0:half] = first.astype(bf16)
        k_ref[rows, half:KEY] = second.astype(bf16)
    done(0)
    done(1)
    ready(2)
    for rows in ROWS:
        v_ref[rows, :] = nn(h_ref[rows, :], wv_ref[...]).astype(bf16)
    done(2)
    ready(3)
    for rows in ROWS:
        gate_ref[rows, :] = nn(h_ref[rows, :], wg_ref[...])
    done(4)
    ready(4, 6, 7, 8)
    for i, rows in reversed(list(enumerate(ROWS))):
        weights = masked(nt(q_ref[rows, :], k_ref[...]), rows, cols_ref, line_ref).astype(bf16)
        p_ref[rows, :] = weights
        done(3, rows)
        retained = nn(weights, v_ref[...])
        inverse = lax.rsqrt(
            jnp.sum(retained * retained, axis=-1, keepdims=True) * (1.0 / VAL) + group_eps
        )
        inv_ref[rows, :] = jnp.broadcast_to(inverse, (TILE, 128))
        hat = retained * inverse
        hat_ref[rows, :] = hat
        done(5, rows)
        gate = gate_ref[rows, :]
        swish = gate * (1.0 / (1.0 + jnp.exp(-gate)))
        mixed = (hat * gain_ref[...] * swish).astype(bf16)
        mixed_ref[rows, :] = mixed
        put_halves(done, i, nt(mixed, wo_ref[...]), own_ref, other_ref, 8, 9)
    done(6)
    done(7)


def retention(*operands):
    shape = jax.ShapeDtypeStruct
    return in_vmem(
        retention_kernel,
        "retention",
        [
            shape((WIDTH, KEY), bf16),
            shape((WIDTH, KEY), bf16),
            shape((WIDTH, LANES), bf16),
            shape((WIDTH, WIDTH), bf16),
            shape((WIDTH, LANES), f32),
            shape((WIDTH, LANES), f32),
            shape((WIDTH, 128), f32),
            shape((WIDTH, LANES), bf16),
            shape((WIDTH // 2, WIDTH), f32),
            shape((WIDTH // 2, WIDTH), bf16),
        ],
        [],
        *operands,
    )


def feed_kernel(
    ready, done, h_ref, w1_ref, w2_ref, cot_ref, w3_ref,
    hidden_ref, gate_ref, up_ref, own_ref, other_ref,
):
    for i, rows in reversed(list(enumerate(ROWS))):
        ready(0, 1)
        pre_gate = nn(h_ref[rows, :], w1_ref[...])
        ready(2)
        pre_up = nn(h_ref[rows, :], w2_ref[...])
        ready(3, 4)
        grad_hidden = nn(cot_ref[rows, :], w3_ref[...])
        cumulative = 0.5 * (1.0 + lax.erf(pre_gate * (1.0 / math.sqrt(2.0))))
        density = jnp.exp(-0.5 * pre_gate * pre_gate) * (1.0 / math.sqrt(2.0 * math.pi))
        gelu_gate = pre_gate * cumulative
        hidden_ref[rows, :] = (gelu_gate * pre_up).astype(bf16)
        grad_gate = (grad_hidden * pre_up * (cumulative + pre_gate * density)).astype(bf16)
        grad_up = (grad_hidden * gelu_gate).astype(bf16)
        gate_ref[rows, :] = grad_gate
        up_ref[rows, :] = grad_up
        for k in range(3):
            done(k, rows)
        part = nt(grad_gate, w1_ref[...]) + nt(grad_up, w2_ref[...])
        put_halves(done, i, part, own_ref, other_ref, 3, 4)


def feed(*operands):
    shape = jax.ShapeDtypeStruct
    return in_vmem(
        feed_kernel,
        "feed_forward",
        [shape((WIDTH, LANES), bf16)] * 3
        + [shape((WIDTH // 2, WIDTH), f32), shape((WIDTH // 2, WIDTH), bf16)],
        [],
        *operands,
    )


def early_kernel(
    ready, done, h_ref, gate_ref, up_ref, cot_ref, hidden_ref, w3_ref, out_ref, own_ref, other_ref
):
    for j, (left, right) in enumerate(
        ((h_ref, gate_ref), (h_ref, up_ref), (cot_ref, hidden_ref))
    ):
        ready(*((0, 1), (2,), (3, 4))[j])
        columns = pl.ds(LANES * j, LANES)
        for i, at in enumerate(ROWS):
            part = tn(left[:, at], right[...]).astype(bf16)
            out_ref[:, i, :, columns] = part.reshape(16, BLOCK, LANES)
        done(0, slice(None), slice(None), slice(None), columns)
    ready(5)
    for i, rows in reversed(list(enumerate(ROWS))):
        put_halves(done, i, nt(hidden_ref[rows, :], w3_ref[...]), own_ref, other_ref, 1, 2)


def early_grads(*operands):
    shape = jax.ShapeDtypeStruct
    return in_vmem(
        early_kernel,
        "feed_forward_grads",
        [
            shape((16, 2, BLOCK, 3 * LANES), bf16),
            shape((WIDTH // 2, WIDTH), f32),
            shape((WIDTH // 2, WIDTH), bf16),
        ],
        [],
        *operands,
    )


def back_gate_kernel(
    ready, done, grad_ref, w_ref, gate_ref, hat_ref, inv_ref, gain_ref, gate_out, ret_out, gain_out
):
    total = jnp.zeros((1, LANES), f32)
    for rows in ROWS:
        ready(0, 1)
        grad_mixed = nn(grad_ref[rows, :], w_ref[...])
        ready(2, 3, 4, 5)
        gain = gain_ref[...]
        gate, hat, inverse = gate_ref[rows, :], hat_ref[rows, :], inv_ref[rows, 0:1]
        sig = 1.0 / (1.0 + jnp.exp(-gate))
        swish = gate * sig
        grad_grouped = grad_mixed * swish
        gate_out[rows, :] = (
            grad_mixed * (hat * gain) * (sig + swish * (1.0 - sig))
        ).astype(bf16)
        done(0, rows)
        total += jnp.sum(grad_grouped * hat, axis=0, keepdims=True)
        grad_hat = grad_grouped * gain
        inner = jnp.sum(grad_hat * hat, axis=-1, keepdims=True) * (1.0 / VAL)
        ret_out[rows, :] = (inverse * (grad_hat - hat * inner)).astype(bf16)
        done(1, rows)
    gain_out[...] = total
    done(2)


def back_gate(*operands):
    shape = jax.ShapeDtypeStruct
    return in_vmem(
        back_gate_kernel,
        "gate_backward",
        [shape((WIDTH, LANES), bf16)] * 2 + [shape((1, LANES), f32)],
        [],
        *operands,
    )


def back_scores_kernel(
    ready, done, ret_ref, v_ref, cols_ref, line_ref, k_ref, turn_ref, p_ref, q_ref,
    q_out, k_out, v_out, scores,
):
    half = KEY // 2
    ready(0, 1, 2, 3)
    for rows in ROWS:
        part = masked(nt(ret_ref[rows, :], v_ref[...]), rows, cols_ref, line_ref).astype(bf16)
        scores[rows, :] = part
        ready(4, 5)
        turned = nn(part, k_ref[...])
        first, second = turn(
            turned[:, :half], turned[:, half:], turn_ref[rows, :half], -turn_ref[rows, half:]
        )
        q_out[rows, 0:half] = first.astype(bf16)
        q_out[rows, half:KEY] = second.astype(bf16)
    done(0)
    ready(6, 7)
    for rows in ROWS:
        v_out[rows, :] = tn(p_ref[:, rows], ret_ref[...]).astype(bf16)
        done(2, rows)
    for rows in ROWS:
        turned = tn(scores[:, rows], q_ref[...])
        first, second = turn(
            turned[:, :half], turned[:, half:], turn_ref[rows, :half], -turn_ref[rows, half:]
        )
        k_out[rows, 0:half] = first.astype(bf16)
        k_out[rows, half:KEY] = second.astype(bf16)
    done(1)


def back_scores(*operands):
    shape = jax.ShapeDtypeStruct
    return in_vmem(
        back_scores_kernel,
        "scores_backward",
        [shape((WIDTH, KEY), bf16)] * 2 + [shape((WIDTH, LANES), bf16)],
        [pltpu.VMEM((WIDTH, WIDTH), bf16)],
        *operands,
    )


def late_kernel(
    ready, done, grad_ref, mixed_ref, h_ref, gate_ref, v_ref, ride_ref, q_ref, k_ref, out_ref
):
    def columns(i):
        return slice(None), pl.ds(LANES * i, LANES)

    ready(0, 1)
    for rows in ROWS:
        out_ref[rows, 3 * LANES : 4 * LANES] = tn(grad_ref[:, rows], mixed_ref[...]).astype(bf16)
    done(0, *columns(3))
    ready(2, 3)
    for rows in ROWS:
        out_ref[rows, 2 * LANES : 3 * LANES] = tn(h_ref[:, rows], gate_ref[...]).astype(bf16)
    done(0, *columns(2))
    ready(4, 5)
    for rows in ROWS:
        part = tn(h_ref[:, rows], v_ref[...]).astype(bf16)
        out_ref[rows, LANES : LANES + 384] = part[:, 0:384]
        out_ref[rows, LANES + 384 : 2 * LANES] = part[:, 384:LANES] + ride_ref[rows, :]
    done(0, *columns(1))
    ready(6, 7)
    for rows in ROWS:
        left = h_ref[:, rows]
        out_ref[rows, 0:KEY] = tn(left, q_ref[...]).astype(bf16)
        out_ref[rows, KEY : 2 * KEY] = (tn(left, k_ref[...]) * KEY**-0.5).astype(bf16)
    done(0, *columns(0))


def late_grads(*operands):
    return in_vmem(
        late_kernel,
        "retention_grads",
        [jax.ShapeDtypeStruct((WIDTH, 4 * LANES), bf16)],
        [],
        *operands,
    )[0]


def input_kernel(
    ready, done, gate_ref, wg_ref, v_ref, wv_ref, q_ref, k_ref, wqk_ref, own_ref, other_ref
):
    for i, rows in reversed(list(enumerate(ROWS))):
        ready(0, 1)
        part = nt(gate_ref[rows, :], wg_ref[...])
        ready(2, 3)
        part += nt(v_ref[rows, :], wv_ref[...])
        ready(4, 5, 6)
        part += nt(q_ref[rows, :], wqk_ref[:, 0:KEY])
        part += nt(k_ref[rows, :], wqk_ref[:, KEY : 2 * KEY]) * KEY**-0.5
        put_halves(done, i, part, own_ref, other_ref, 0, 1)


def input_parts(*operands):
    shape = jax.ShapeDtypeStruct
    return in_vmem(
        input_kernel,
        "input_grad_parts",
        [shape((WIDTH // 2, WIDTH), f32), shape((WIDTH // 2, WIDTH), bf16)],
        [],
        *operands,
    )


def iterate_kernel(
    chunk_ref, near_ref, far_ref, out_ref, vector_ref, first_ref, whole, gram, high, low, shifted, rest, prod, prod_b, own, own_b
):
    tiles = WIDTH // NS_TILE
    at = [pl.ds(NS_TILE * i, NS_TILE) for i in range(tiles)]
    eye = (
        lax.broadcasted_iota(jnp.int32, (NS_TILE, NS_TILE), 0)
        == lax.broadcasted_iota(jnp.int32, (NS_TILE, NS_TILE), 1)
    ).astype(f32)
    keep = lax.broadcasted_iota(jnp.int32, (WIDTH, 128), 1) < VAL - 384
    riders = jnp.zeros((WIDTH, 128), f32)
    for p in range(4):
        source = near_ref if p < 2 else far_ref
        piece = source[:, p % 2].reshape(WIDTH, LANES)
        whole[p, :, 0:384] = piece[:, 0:384]
        whole[p, :, 384:512] = jnp.where(keep, piece[:, 384:512], jnp.zeros((), bf16))
        ride = piece[:, 384:512].astype(f32)
        riders += ride
        lines = ride.T
        vector_ref[2 + p : 3 + p, :] = lines[50:51, :] + lines[53:54, :]
    lines = riders.T
    vector_ref[0:2, :] = lines[48:50, :] + lines[51:53, :]
    vector_ref[6:8, :] = jnp.zeros((2, WIDTH), f32)
    first_ref[...] = jnp.sum(riders.reshape(WIDTH // BLOCK, BLOCK, 128), axis=0)

    trace = jnp.float32(0.0)
    for i in range(tiles):
        for j in range(tiles):
            block = jnp.zeros((NS_TILE, NS_TILE), f32)
            for p in range(4):
                block += nt(whole[p, at[i], :], whole[p, at[j], :])
            gram[at[i], at[j]] = block
            if i == j:
                trace += jnp.sum(block * eye)
    inverse = 1.0 / (jnp.sqrt(trace) + 1e-07)
    for q in range(4):

        @pl.when(chunk_ref[0] == q)
        def _():
            own[...] = whole[0, :, 128 * q : 128 * (q + 1)].astype(f32) * inverse

    def store(i, j, block, mean):
        gram[at[i], at[j]] = block
        top = block.astype(bf16)
        high[at[i], at[j]] = top
        low[at[i], at[j]] = (block - top.astype(f32)).astype(bf16)
        if i == j:
            top = (block - mean * eye).astype(bf16)
        shifted[at[i], at[j]] = top

    mean = trace * inverse * inverse * (1.0 / WIDTH)
    for i in range(tiles):
        for j in range(tiles):
            store(i, j, gram[at[i], at[j]] * (inverse * inverse), mean)

    def advance(mean):
        level = ns_second * mean + ns_third * mean * mean
        alpha = ns_first + level
        for i in range(tiles):
            for j in range(tiles):
                block = (ns_second + 2.0 * ns_third * mean) * gram[at[i], at[j]] + ns_third * nn(
                    shifted[at[i], :], shifted[:, at[j]]
                )
                if i == j:
                    block -= (ns_third * mean * mean + level) * eye
                rest[at[i], at[j]] = block.astype(bf16)
        values = own[...]
        top = values.astype(bf16)
        own_b[:, 0:128] = top
        own_b[:, 128:256] = (values - top.astype(f32)).astype(bf16)
        for i in range(tiles):
            moved = nn(rest[at[i], :], own_b[...])
            own[at[i], :] = alpha * own[at[i], :] + (moved[:, 0:128] + moved[:, 128:256])
        return alpha

    def turn(_, mean):
        alpha = advance(mean)
        for i in range(tiles):
            for j in range(tiles):
                block = nn(high[at[i], :], rest[:, at[j]]) + nn(low[at[i], :], rest[:, at[j]])
                prod[at[i], at[j]] = block
                prod_b[at[i], at[j]] = block.astype(bf16)
        trace = jnp.float32(0.0)
        for i in range(tiles):
            for j in range(tiles):
                block = alpha * prod[at[i], at[j]] + 0.5 * nn(rest[at[i], :], prod_b[:, at[j]])
                prod[at[i], at[j]] = block
                if i == j:
                    trace += jnp.sum(block * eye)
        later = alpha * alpha * mean + trace * (2.0 / WIDTH)
        for i in range(tiles):
            for j in range(tiles):
                block = (alpha * alpha) * gram[at[i], at[j]] + (
                    prod[at[i], at[j]] + prod[at[j], at[i]].T
                )
                store(i, j, block, later)
        return later

    advance(lax.fori_loop(0, NS_ITERS - 1, turn, mean))
    out_ref[...] = own[...].astype(bf16)


def orthogonal(chunk, near, far):
    square = (WIDTH, WIDTH)
    return pl.pallas_call(
        iterate_kernel,
        out_shape=[
            jax.ShapeDtypeStruct((WIDTH, 128), bf16),
            jax.ShapeDtypeStruct((8, WIDTH), f32),
            jax.ShapeDtypeStruct((BLOCK, 128), f32),
        ],
        in_specs=[pl.BlockSpec(memory_space=pltpu.SMEM)]
        + [pl.BlockSpec(memory_space=pltpu.VMEM)] * 2,
        out_specs=[pl.BlockSpec(memory_space=pltpu.VMEM)] * 3,
        scratch_shapes=[
            pltpu.VMEM((4, WIDTH, LANES), bf16),
            pltpu.VMEM(square, f32),
            pltpu.VMEM(square, bf16),
            pltpu.VMEM(square, bf16),
            pltpu.VMEM(square, bf16),
            pltpu.VMEM(square, bf16),
            pltpu.VMEM(square, f32),
            pltpu.VMEM(square, bf16),
            pltpu.VMEM((WIDTH, 128), f32),
            pltpu.VMEM((WIDTH, 256), bf16),
        ],
        compiler_params=pltpu.CompilerParams(vmem_limit_bytes=48 * 2**20),
        cost_estimate=pl.CostEstimate(
            flops=42 * 10**9, bytes_accessed=5 * 2**20, transcendentals=0
        ),
        name="orthogonalize",
    )(chunk, near, far)


def shards(
    tokens,
    cotangent,
    qk_w,
    vg_w,
    mlp_w,
    out_w,
    qk_mom,
    vg_mom,
    mlp_mom,
    out_mom,
    norm_params,
    norm_moment,
    norm_second,
    decay_gap,
    seq_length,
    seq_group,
):
    rows, width = tokens.shape
    slots = 4 * rows
    groups = 32
    value_width = 4 * VAL
    key_scale = KEY ** (-0.5)
    dp_index = lax.axis_index(DP)
    tensor_index = lax.axis_index(TENSOR)
    chunk_index = lax.axis_index(("y_lo", "z_hi"))

    gain_one = norm_params[0:width]
    shift_one = norm_params[width : 2 * width]
    group_gain = jnp.pad(
        lax.dynamic_slice_in_dim(norm_params, 2 * width + tensor_index * VAL, VAL),
        (0, LANES - VAL),
    )
    gain_two = norm_params[2 * width + value_width : 3 * width + value_width]
    shift_two = norm_params[3 * width + value_width : 4 * width + value_width]

    out_rows = jnp.swapaxes(out_w, 1, 2)
    first_half = lax.axis_index("y_lo") == 0

    def weight_rows(parts):
        packed = jnp.concatenate(parts, axis=1).astype(bf16)
        far = swap(packed, "y_lo")
        pair = jnp.stack([jnp.where(first_half, packed, far), jnp.where(first_half, far, packed)])
        return pair

    def weight_gather(pair):
        return lax.all_gather(pair, PLANE, axis=1, tiled=True).reshape(width, -1)

    pair_ret = weight_rows(
        [
            pairs_apart(qk_w[0]),
            pairs_apart(qk_w[1]),
            widen(vg_w[0]),
            widen(vg_w[1]),
            widen(out_rows[0]),
        ]
    )
    pair_ff = weight_rows([widen(mlp_w[0]), widen(mlp_w[1]), widen(out_rows[1])])
    gathered = weight_gather(pair_ret)
    pair_ff, gathered = together(pair_ff, gathered)
    gathered_ff = weight_gather(pair_ff)
    w_qk, w_v, w_g, w_o = ((gathered, LANES * i, LANES) for i in range(4))
    w_1, w_2, w_3 = ((gathered_ff, LANES * i, LANES) for i in range(3))

    whole_tokens = tensor_gather(tokens)
    order = jnp.stack([tensor_index, tensor_index ^ 2, tensor_index ^ 1, tensor_index ^ 3])
    place = (order[:, None] * rows + jnp.arange(rows, dtype=jnp.int32)[None, :]).reshape(slots)

    freqs = 1.0 / 10000.0 ** np.linspace(0.0, 1.0, KEY // 2)
    angles = np.arange(slots)[:, None] * freqs[None, :]
    tables = jnp.asarray(
        np.concatenate([np.cos(angles), np.sin(angles)], axis=1).astype(np.float32)
    ).reshape(4, rows, KEY)
    turned = tables[order].reshape(slots, KEY)

    labels = sequence_labels(seq_length, seq_group, dp_index, place)
    log_decay = jnp.log1p(-decay_gap[0])
    away = (place - slots // 2).astype(f32) * log_decay
    label_place = [labels.astype(f32), place.astype(f32)]
    columns = jnp.pad(jnp.stack(label_place + [jnp.exp(away)], axis=1), ((0, 0), (0, 125)))
    line = jnp.pad(jnp.stack(label_place + [jnp.exp(-away)], axis=0), ((0, 5), (0, 0)))
    gain_line = group_gain[None, :]

    hat_one, _ = normalize(whole_tokens.astype(f32))
    whole_one = (hat_one * gain_one + shift_one).astype(bf16)
    cot_first, whole_one = together(cotangent, whole_one)
    whole_cot = tensor_gather(cot_first)
    gain_line, whole_cot = together(gain_line, whole_cot)
    query, keys, values, weights, gate, hat_group, inv_group, mixed, own, other = retention(
        whole_one, w_qk, w_v, w_g, w_o, turned, columns, line, gain_line
    )
    near, far = tensor_sum(own, other)
    middle = tokens.astype(f32) + near + far.astype(f32)
    hat_two, inv_two = normalize(middle)
    whole_two = tensor_gather((hat_two * gain_two + shift_two).astype(bf16))
    hidden, grad_gate, grad_up, own, other = feed(whole_two, w_1, w_2, whole_cot, w_3)
    near, far = tensor_sum(own, other)
    early, out_own, out_other = early_grads(whole_two, grad_gate, grad_up, whole_cot, hidden, w_3)
    far, early = together(far, early)
    grad_normed_two = near + far.astype(f32)
    grad_middle = cotangent.astype(f32) + norm_back(grad_normed_two, gain_two, hat_two, inv_two)
    grad_first, early = together(grad_middle.astype(bf16), early)
    grad_one = tensor_gather(grad_first)

    early_in = lax.all_to_all(early, PLANE, split_axis=0, concat_axis=0, tiled=True)
    early_halves = jnp.sum(early_in.astype(f32), axis=0)
    early_far = swap(
        jnp.where(first_half, early_halves[1], early_halves[0]).astype(bf16), "y_lo"
    )
    early_sum = jnp.where(first_half, early_halves[0], early_halves[1]) + early_far.astype(f32)
    gain_two_grad = jnp.sum(grad_normed_two * hat_two, axis=0)
    shift_two_grad = jnp.sum(grad_normed_two, axis=0)

    out_other, grad_one = together(out_other, grad_one)
    out_near, out_far = tensor_sum(out_own, out_other)
    grad_gate_ret, grad_retained, group_gain_grad = back_gate(
        grad_one, w_o, gate, hat_group, inv_group, gain_line
    )
    grad_query, grad_key, grad_values = back_scores(
        grad_retained, values, columns, line, keys, turned, weights, query
    )
    result = (middle + out_near + out_far.astype(f32)).astype(bf16)
    result, grad_query = together(result, grad_query)
    small = jnp.stack(
        [gain_two_grad, shift_two_grad, jnp.pad(group_gain_grad[0], (0, width - LANES))], axis=1
    )
    small_high, small_low = split(small)
    riders = jnp.pad(
        jnp.concatenate([small_high, small_low], axis=1), ((0, 0), (VAL - 384, LANES - VAL - 6))
    )
    riders, early_sum = together(riders, early_sum)
    late = late_grads(
        grad_one, mixed, whole_one, grad_gate_ret, grad_values, riders, grad_query, grad_key
    )
    late, grad_gate_ret = together(late, grad_gate_ret)
    late_in = lax.all_to_all(
        late.reshape(groups, BLOCK, -1), DP, split_axis=0, concat_axis=0, tiled=True
    )
    own, other = input_parts(
        grad_gate_ret, w_g, grad_values, w_v, grad_query, grad_key, w_qk
    )
    near, far = tensor_sum(own, other)
    grad_normed_one = near + far.astype(f32)
    own_hat, own_inv = normalize(tokens.astype(f32))
    gain_one_grad = jnp.sum(grad_normed_one * own_hat, axis=0)
    shift_one_grad = jnp.sum(grad_normed_one, axis=0)
    input_grad = grad_middle + norm_back(grad_normed_one, gain_one, own_hat, own_inv)

    late_sum = jnp.sum(late_in.astype(f32), axis=0)
    small_sum = late_sum[:, LANES + VAL : LANES + VAL + 6]
    small_sum = small_sum[:, :3] + small_sum[:, 3:]

    grad_qk = pairs_together(jnp.stack([late_sum[:, 0:256], late_sum[:, 256:512]]))
    grad_vg = jnp.stack([late_sum[:, 512 : 512 + VAL], late_sum[:, 1024 : 1024 + VAL]])
    grad_mlp = jnp.stack([early_sum[:, 0:VAL], early_sum[:, 512 : 512 + VAL]])
    grad_out_t = jnp.stack([late_sum[:, 1536 : 1536 + VAL], early_sum[:, 1024 : 1024 + VAL]])
    mom_qk = muon_beta * qk_mom + grad_qk
    mom_vg = muon_beta * vg_mom + grad_vg
    mom_mlp = muon_beta * mlp_mom + grad_mlp
    mom_out = muon_beta * out_mom + jnp.swapaxes(grad_out_t, 1, 2)

    piece_high, piece_low = split(small_sum)
    first_norm = jnp.concatenate([gain_one_grad, shift_one_grad]).astype(bf16)
    extra = jnp.pad(
        jnp.concatenate([piece_high, piece_low, first_norm.reshape(BLOCK, 64)], axis=1),
        ((0, 0), (VAL, LANES - VAL - 70)),
    )
    stacked = (
        jnp.concatenate(
            [widen(mom_qk), widen(mom_vg), widen(mom_mlp), widen(jnp.swapaxes(mom_out, 1, 2))],
            axis=0,
        ).astype(bf16)
        + extra[None]
    )
    both = jnp.stack([stacked, swap(stacked, "y_hi")], axis=1)
    spread = jnp.broadcast_to(both[None], (4,) + both.shape).reshape((groups,) + both.shape[1:])
    arrived = lax.all_to_all(spread, DP, split_axis=0, concat_axis=0, tiled=True)
    far = swap(arrived, "core")
    own, vectors, first_total = orthogonal(
        jnp.reshape(chunk_index, (1,)).astype(jnp.int32), arrived, far
    )
    returned = lax.all_to_all(
        own.reshape(groups, BLOCK, 128), DP, split_axis=0, concat_axis=0, tiled=True
    ).astype(f32)
    returned = jnp.concatenate([returned[8 * i : 8 * i + 8] for i in range(4)], axis=2)

    shrink = 1.0 - muon_rate * decay_rate
    square_scale = 0.2 * math.sqrt(width)
    wide_scale = 0.2 * math.sqrt(max(width, value_width))
    new_qk = qk_w * shrink - (muon_rate * square_scale) * returned[0:2, :, :KEY]
    new_vg = vg_w * shrink - (muon_rate * wide_scale) * returned[2:4, :, :VAL]
    new_mlp = mlp_w * shrink - (muon_rate * wide_scale) * returned[4:6, :, :VAL]
    new_out = out_w * shrink - (muon_rate * wide_scale) * jnp.swapaxes(returned[6:8, :, :VAL], 1, 2)

    first_total = first_total[:, 54:118].reshape(2 * width)
    group_parts = vectors[2:6, :VAL]
    which = jnp.arange(4, dtype=jnp.int32)[:, None] == order[None, :]
    group_whole = jnp.sum(
        jnp.where(which[:, :, None], group_parts[None], 0.0), axis=1
    ).reshape(value_width)
    small_total = jnp.concatenate(
        [first_total, group_whole, vectors[0], vectors[1]]
    )
    moment_new = beta_first * norm_moment + (1.0 - beta_first) * small_total
    second_new = beta_second * norm_second + (1.0 - beta_second) * small_total * small_total
    params_new = norm_params - adam_rate * (moment_new / (1.0 - beta_first**OPT_STEP)) / (
        jnp.sqrt(second_new / (1.0 - beta_second**OPT_STEP)) + adam_eps
    )
    return (
        result,
        input_grad,
        mom_qk,
        mom_vg,
        mom_mlp,
        mom_out,
        new_qk,
        new_vg,
        new_mlp,
        new_out,
        moment_new,
        second_new,
        params_new,
    )


def solution(mesh):
    fine = Mesh(np.asarray(mesh.devices).reshape(SIZES), AXES)
    by_rows = P(DP + TENSOR, None)
    by_columns = P(None, DP, TENSOR)
    by_out = P(None, TENSOR, DP)
    return jax.shard_map(
        shards,
        mesh=fine,
        in_specs=(
            by_rows,
            by_rows,
            by_columns,
            by_columns,
            by_columns,
            by_out,
            by_columns,
            by_columns,
            by_columns,
            by_out,
            P(),
            P(),
            P(),
            P(TENSOR),
            P(),
            P(),
        ),
        out_specs=(
            by_rows,
            by_rows,
            by_columns,
            by_columns,
            by_columns,
            by_out,
            by_columns,
            by_columns,
            by_columns,
            by_out,
            P(),
            P(),
            P(),
        ),
        check_vma=False,
    )
```

```python
import math

import jax
import jax.numpy as jnp
import numpy as np
from jax import lax
from jax.experimental import pallas as pl
from jax.experimental.pallas import tpu as pltpu
from jax.sharding import Mesh
from jax.sharding import PartitionSpec as P

HEADS = 4
NS_ITERS = 5
OPT_STEP = 10
KEY = 256
VAL = 432
LANES = 512
BLOCK = 32

norm_eps = 1e-05
group_eps = 0.01
ns_first = 3.4445
ns_second = -4.775
ns_third = 2.0315
muon_rate = 0.15
muon_beta = 0.95
decay_rate = 0.01
adam_rate = 0.6
beta_first = 0.9
beta_second = 0.95
adam_eps = 1e-08

AXES = ("y_lo", "z_hi", "z_lo", "x", "y_hi", "core")
SIZES = (2, 2, 2, 4, 2, 2)
DP = ("y_lo", "z_hi", "z_lo", "x")
PLANE = ("z_hi", "z_lo", "x")
TENSOR = ("y_hi", "core")
bf16 = jnp.bfloat16
f32 = jnp.float32


def swap(values, axis):
    return lax.ppermute(values, axis, [(0, 1), (1, 0)])


def dot(left, right, dims):
    return lax.dot_general(left, right, (dims, ((), ())), preferred_element_type=f32)


def nn(left, right):
    return dot(left, right, ((1,), (0,)))


def nt(left, right):
    return dot(left, right, ((1,), (1,)))


def tn(left, right):
    return dot(left, right, ((0,), (0,)))


def split(values):
    high = lax.reduce_precision(values, 8, 7)
    return high.astype(bf16), (values - high).astype(bf16)


def widen(values):
    return jnp.pad(values, ((0, 0),) * (values.ndim - 1) + ((0, LANES - values.shape[-1]),))


def tensor_gather(own):
    far = swap(own, "y_hi")
    return [own, far, swap(own, "core"), swap(far, "core")]


def tensor_sum(own, other):
    half = own.shape[0] // 2
    arrived = swap(other, "core")
    far = (own[half:] + arrived[half:].astype(f32)).astype(bf16)
    return own[:half] + arrived[:half].astype(f32), swap(far, "y_hi")


def together(first, second):
    return lax.optimization_barrier((first, second))


def normalize(values):
    centre = values - jnp.mean(values, axis=-1, keepdims=True)
    spread = lax.rsqrt(jnp.mean(centre * centre, axis=-1, keepdims=True) + norm_eps)
    return centre * spread, spread


def norm_back(grad_out, gain, normed, spread):
    grad_normed = grad_out * gain
    return spread * (
        grad_normed
        - jnp.mean(grad_normed, axis=-1, keepdims=True)
        - normed * jnp.mean(grad_normed * normed, axis=-1, keepdims=True)
    )


def pairs_apart(values):
    shape = values.shape
    return jnp.swapaxes(values.reshape(shape[:-1] + (KEY // 2, 2)), -1, -2).reshape(shape)


def pairs_together(values):
    shape = values.shape
    return jnp.swapaxes(values.reshape(shape[:-1] + (2, KEY // 2)), -1, -2).reshape(shape)


def sequence_labels(seq_length, seq_group, group, place):
    mine = seq_group == group
    lengths = jnp.where(mine, seq_length, 0)
    ends = jnp.cumsum(lengths, dtype=jnp.int32)
    starts = ends - lengths
    inside = mine[None, :] & (place[:, None] >= starts[None, :]) & (place[:, None] < ends[None, :])
    number = jnp.arange(1, seq_length.shape[0] + 1, dtype=jnp.int32)
    return jnp.sum(jnp.where(inside, number[None, :], 0), axis=1, dtype=jnp.int32)


WIDTH = 1024
TILE = WIDTH // 2
NS_TILE = 256


ROWS = [pl.ds(TILE * i, TILE) for i in range(WIDTH // TILE)]


STORES = 12


def in_vmem(kernel, name, out_shape, scratch, *operands):
    arrays, pieces, local = [], [], []
    for a in operands:
        parts = a if isinstance(a, list) else [a]
        top, piece = 0, []
        for part in parts:
            array, first, columns = part if isinstance(part, tuple) else (part, 0, part.shape[1])
            whole = columns == array.shape[1]
            piece.append((len(arrays), None if whole else (first, columns), top, array.shape[0]))
            fixed = not isinstance(a, list)
            arrays.append(pltpu.with_memory_space_constraint(array, pltpu.HBM) if fixed else array)
            top += array.shape[0]
        pieces.append(piece)
        local.append(pltpu.VMEM((top, columns), array.dtype))
    n_in, n_out, n_local = len(arrays), len(out_shape), len(local)

    def body(*refs):
        ins, outs = refs[:n_in], refs[n_in : n_in + n_out]
        refs = refs[n_in + n_out :]
        local_in, local_out = refs[:n_local], refs[n_local : n_local + n_out]
        sem_in, sem_out = refs[n_local + n_out : n_local + n_out + 2]
        loads = []
        for i, piece in enumerate(pieces):
            loads.append([])
            for which, cut, top, rows in piece:
                source = ins[which] if cut is None else ins[which].at[:, pl.ds(*cut)]
                target = local_in[i] if len(piece) == 1 else local_in[i].at[pl.ds(top, rows), :]
                loads[i].append(pltpu.make_async_copy(source, target, sem_in.at[which]))
                loads[i][-1].start()
        pending = set(range(n_local))
        stores = []

        def ready(*which):
            for i in which:
                if i in pending:
                    pending.remove(i)
                    for load in loads[i]:
                        load.wait()

        def done(i, *index):
            source, target = local_out[i], outs[i]
            if index:
                source, target = source.at[index], target.at[index]
            stores.append(pltpu.make_async_copy(source, target, sem_out.at[len(stores)]))
            stores[-1].start()

        kernel(ready, done, *local_in, *local_out, *refs[n_local + n_out + 2 :])
        ready(*range(n_local))
        for store in stores:
            store.wait()

    local += [pltpu.VMEM(a.shape, a.dtype) for a in out_shape]
    held = sum(math.prod(a.shape) * jnp.dtype(a.dtype).itemsize for a in local)
    return pl.pallas_call(
        body,
        out_shape=[pltpu.HBM(a.shape, a.dtype) for a in out_shape],
        in_specs=[pl.BlockSpec(memory_space=pl.ANY)] * n_in,
        out_specs=[pl.BlockSpec(memory_space=pltpu.HBM)] * n_out,
        scratch_shapes=local
        + [pltpu.SemaphoreType.DMA((n_in,)), pltpu.SemaphoreType.DMA((STORES,))]
        + scratch,
        compiler_params=pltpu.CompilerParams(vmem_limit_bytes=held + 14 * 2**20),
        cost_estimate=pl.CostEstimate(flops=1, bytes_accessed=1, transcendentals=0),
        name=name,
    )(*arrays)


def put_halves(done, i, part, own_ref, other_ref, own, other):
    if i == 0:
        own_ref[...] = part
        done(own)
    else:
        other_ref[...] = part.astype(bf16)
        done(other)


def turn(first, second, cos_table, sin_table):
    return first * cos_table - second * sin_table, second * cos_table + first * sin_table


def masked(scores, rows, cols_ref, line_ref):
    label, place = cols_ref[rows, 0:1], cols_ref[rows, 1:2]
    linked = (label == line_ref[0:1, :]) & (label > 0.0) & (place >= line_ref[1:2, :])
    return jnp.where(linked, scores * (cols_ref[rows, 2:3] * line_ref[2:3, :]), 0.0)


def retention_kernel(
    ready, done, h_ref, wqk_ref, wv_ref, wg_ref, wo_ref, turn_ref, cols_ref, line_ref, gain_ref,
    q_ref, k_ref, v_ref, p_ref, gate_ref, hat_ref, inv_ref, mixed_ref, own_ref, other_ref,
):
    half = KEY // 2
    ready(0, 1, 5)
    for rows in ROWS:
        cos_table, sin_table = turn_ref[rows, :half], turn_ref[rows, half:]
        both = nn(h_ref[rows, :], wqk_ref[...])
        query, keys = both[:, :KEY], both[:, KEY:] * KEY**-0.5
        first, second = turn(query[:, :half], query[:, half:], cos_table, sin_table)
        q_ref[rows, 0:half] = first.astype(bf16)
        q_ref[rows, half:KEY] = second.astype(bf16)
        first, second = turn(keys[:, :half], keys[:, half:], cos_table, sin_table)
        k_ref[rows, 0:half] = first.astype(bf16)
        k_ref[rows, half:KEY] = second.astype(bf16)
    done(0)
    done(1)
    ready(2)
    for rows in ROWS:
        v_ref[rows, :] = nn(h_ref[rows, :], wv_ref[...]).astype(bf16)
    done(2)
    ready(3)
    for rows in ROWS:
        gate_ref[rows, :] = nn(h_ref[rows, :], wg_ref[...])
    done(4)
    ready(4, 6, 7, 8)
    for i, rows in reversed(list(enumerate(ROWS))):
        weights = masked(nt(q_ref[rows, :], k_ref[...]), rows, cols_ref, line_ref).astype(bf16)
        p_ref[rows, :] = weights
        done(3, rows)
        retained = nn(weights, v_ref[...])
        inverse = lax.rsqrt(
            jnp.sum(retained * retained, axis=-1, keepdims=True) * (1.0 / VAL) + group_eps
        )
        inv_ref[rows, :] = jnp.broadcast_to(inverse, (TILE, 128))
        hat = retained * inverse
        hat_ref[rows, :] = hat
        done(5, rows)
        gate = gate_ref[rows, :]
        swish = gate * (1.0 / (1.0 + jnp.exp(-gate)))
        mixed = (hat * gain_ref[...] * swish).astype(bf16)
        mixed_ref[rows, :] = mixed
        put_halves(done, i, nt(mixed, wo_ref[...]), own_ref, other_ref, 8, 9)
    done(6)
    done(7)


def retention(*operands):
    shape = jax.ShapeDtypeStruct
    return in_vmem(
        retention_kernel,
        "retention",
        [
            shape((WIDTH, KEY), bf16),
            shape((WIDTH, KEY), bf16),
            shape((WIDTH, LANES), bf16),
            shape((WIDTH, WIDTH), bf16),
            shape((WIDTH, LANES), f32),
            shape((WIDTH, LANES), f32),
            shape((WIDTH, 128), f32),
            shape((WIDTH, LANES), bf16),
            shape((WIDTH // 2, WIDTH), f32),
            shape((WIDTH // 2, WIDTH), bf16),
        ],
        [],
        *operands,
    )


def feed_kernel(
    ready, done, h_ref, w1_ref, w2_ref, cot_ref, w3_ref,
    hidden_ref, gate_ref, up_ref, own_ref, other_ref,
):
    for i, rows in reversed(list(enumerate(ROWS))):
        ready(0, 1)
        pre_gate = nn(h_ref[rows, :], w1_ref[...])
        ready(2)
        pre_up = nn(h_ref[rows, :], w2_ref[...])
        ready(3, 4)
        grad_hidden = nn(cot_ref[rows, :], w3_ref[...])
        cumulative = 0.5 * (1.0 + lax.erf(pre_gate * (1.0 / math.sqrt(2.0))))
        density = jnp.exp(-0.5 * pre_gate * pre_gate) * (1.0 / math.sqrt(2.0 * math.pi))
        gelu_gate = pre_gate * cumulative
        hidden_ref[rows, :] = (gelu_gate * pre_up).astype(bf16)
        grad_gate = (grad_hidden * pre_up * (cumulative + pre_gate * density)).astype(bf16)
        grad_up = (grad_hidden * gelu_gate).astype(bf16)
        gate_ref[rows, :] = grad_gate
        up_ref[rows, :] = grad_up
        for k in range(3):
            done(k, rows)
        part = nt(grad_gate, w1_ref[...]) + nt(grad_up, w2_ref[...])
        put_halves(done, i, part, own_ref, other_ref, 3, 4)


def feed(*operands):
    shape = jax.ShapeDtypeStruct
    return in_vmem(
        feed_kernel,
        "feed_forward",
        [shape((WIDTH, LANES), bf16)] * 3
        + [shape((WIDTH // 2, WIDTH), f32), shape((WIDTH // 2, WIDTH), bf16)],
        [],
        *operands,
    )


def early_kernel(
    ready, done, h_ref, gate_ref, up_ref, cot_ref, hidden_ref, w3_ref, out_ref, own_ref, other_ref
):
    for j, (left, right) in enumerate(
        ((h_ref, gate_ref), (h_ref, up_ref), (cot_ref, hidden_ref))
    ):
        ready(*((0, 1), (2,), (3, 4))[j])
        columns = pl.ds(LANES * j, LANES)
        for i, at in enumerate(ROWS):
            part = tn(left[:, at], right[...]).astype(bf16)
            out_ref[:, i, :, columns] = part.reshape(16, BLOCK, LANES)
        done(0, slice(None), slice(None), slice(None), columns)
    ready(5)
    for i, rows in reversed(list(enumerate(ROWS))):
        put_halves(done, i, nt(hidden_ref[rows, :], w3_ref[...]), own_ref, other_ref, 1, 2)


def early_grads(*operands):
    shape = jax.ShapeDtypeStruct
    return in_vmem(
        early_kernel,
        "feed_forward_grads",
        [
            shape((16, 2, BLOCK, 3 * LANES), bf16),
            shape((WIDTH // 2, WIDTH), f32),
            shape((WIDTH // 2, WIDTH), bf16),
        ],
        [],
        *operands,
    )


def back_gate_kernel(
    ready, done, grad_ref, w_ref, gate_ref, hat_ref, inv_ref, gain_ref, gate_out, ret_out, gain_out
):
    total = jnp.zeros((1, LANES), f32)
    for rows in ROWS:
        ready(0, 1)
        grad_mixed = nn(grad_ref[rows, :], w_ref[...])
        ready(2, 3, 4, 5)
        gain = gain_ref[...]
        gate, hat, inverse = gate_ref[rows, :], hat_ref[rows, :], inv_ref[rows, 0:1]
        sig = 1.0 / (1.0 + jnp.exp(-gate))
        swish = gate * sig
        grad_grouped = grad_mixed * swish
        gate_out[rows, :] = (
            grad_mixed * (hat * gain) * (sig + swish * (1.0 - sig))
        ).astype(bf16)
        done(0, rows)
        total += jnp.sum(grad_grouped * hat, axis=0, keepdims=True)
        grad_hat = grad_grouped * gain
        inner = jnp.sum(grad_hat * hat, axis=-1, keepdims=True) * (1.0 / VAL)
        ret_out[rows, :] = (inverse * (grad_hat - hat * inner)).astype(bf16)
        done(1, rows)
    gain_out[...] = total
    done(2)


def back_gate(*operands):
    shape = jax.ShapeDtypeStruct
    return in_vmem(
        back_gate_kernel,
        "gate_backward",
        [shape((WIDTH, LANES), bf16)] * 2 + [shape((1, LANES), f32)],
        [],
        *operands,
    )


def back_scores_kernel(
    ready, done, ret_ref, v_ref, cols_ref, line_ref, k_ref, turn_ref, p_ref, q_ref,
    q_out, k_out, v_out, scores,
):
    half = KEY // 2
    ready(0, 1, 2, 3)
    for rows in ROWS:
        part = masked(nt(ret_ref[rows, :], v_ref[...]), rows, cols_ref, line_ref).astype(bf16)
        scores[rows, :] = part
        ready(4, 5)
        turned = nn(part, k_ref[...])
        first, second = turn(
            turned[:, :half], turned[:, half:], turn_ref[rows, :half], -turn_ref[rows, half:]
        )
        q_out[rows, 0:half] = first.astype(bf16)
        q_out[rows, half:KEY] = second.astype(bf16)
    done(0)
    ready(6, 7)
    for rows in ROWS:
        v_out[rows, :] = tn(p_ref[:, rows], ret_ref[...]).astype(bf16)
        done(2, rows)
    for rows in ROWS:
        turned = tn(scores[:, rows], q_ref[...])
        first, second = turn(
            turned[:, :half], turned[:, half:], turn_ref[rows, :half], -turn_ref[rows, half:]
        )
        k_out[rows, 0:half] = first.astype(bf16)
        k_out[rows, half:KEY] = second.astype(bf16)
    done(1)


def back_scores(*operands):
    shape = jax.ShapeDtypeStruct
    return in_vmem(
        back_scores_kernel,
        "scores_backward",
        [shape((WIDTH, KEY), bf16)] * 2 + [shape((WIDTH, LANES), bf16)],
        [pltpu.VMEM((WIDTH, WIDTH), bf16)],
        *operands,
    )


def late_kernel(
    ready, done, grad_ref, mixed_ref, h_ref, gate_ref, v_ref, ride_ref, q_ref, k_ref, out_ref
):
    def columns(i):
        return slice(None), pl.ds(LANES * i, LANES)

    ready(0, 1)
    for rows in ROWS:
        out_ref[rows, 3 * LANES : 4 * LANES] = tn(grad_ref[:, rows], mixed_ref[...]).astype(bf16)
    done(0, *columns(3))
    ready(2, 3)
    for rows in ROWS:
        out_ref[rows, 2 * LANES : 3 * LANES] = tn(h_ref[:, rows], gate_ref[...]).astype(bf16)
    done(0, *columns(2))
    ready(4, 5)
    for rows in ROWS:
        part = tn(h_ref[:, rows], v_ref[...]).astype(bf16)
        out_ref[rows, LANES : LANES + 384] = part[:, 0:384]
        out_ref[rows, LANES + 384 : 2 * LANES] = part[:, 384:LANES] + ride_ref[rows, :]
    done(0, *columns(1))
    ready(6, 7)
    for rows in ROWS:
        left = h_ref[:, rows]
        out_ref[rows, 0:KEY] = tn(left, q_ref[...]).astype(bf16)
        out_ref[rows, KEY : 2 * KEY] = (tn(left, k_ref[...]) * KEY**-0.5).astype(bf16)
    done(0, *columns(0))


def late_grads(*operands):
    return in_vmem(
        late_kernel,
        "retention_grads",
        [jax.ShapeDtypeStruct((WIDTH, 4 * LANES), bf16)],
        [],
        *operands,
    )[0]


def input_kernel(
    ready, done, gate_ref, wg_ref, v_ref, wv_ref, q_ref, k_ref, wqk_ref, own_ref, other_ref
):
    for i, rows in reversed(list(enumerate(ROWS))):
        ready(0, 1)
        part = nt(gate_ref[rows, :], wg_ref[...])
        ready(2, 3)
        part += nt(v_ref[rows, :], wv_ref[...])
        ready(4, 5, 6)
        part += nt(q_ref[rows, :], wqk_ref[:, 0:KEY])
        part += nt(k_ref[rows, :], wqk_ref[:, KEY : 2 * KEY]) * KEY**-0.5
        put_halves(done, i, part, own_ref, other_ref, 0, 1)


def input_parts(*operands):
    shape = jax.ShapeDtypeStruct
    return in_vmem(
        input_kernel,
        "input_grad_parts",
        [shape((WIDTH // 2, WIDTH), f32), shape((WIDTH // 2, WIDTH), bf16)],
        [],
        *operands,
    )


def iterate_kernel(
    chunk_ref, near_ref, far_ref, out_ref, vector_ref, first_ref, whole, gram, high, low, shifted, rest, prod, prod_b, own, own_b
):
    tiles = WIDTH // NS_TILE
    at = [pl.ds(NS_TILE * i, NS_TILE) for i in range(tiles)]
    eye = (
        lax.broadcasted_iota(jnp.int32, (NS_TILE, NS_TILE), 0)
        == lax.broadcasted_iota(jnp.int32, (NS_TILE, NS_TILE), 1)
    ).astype(f32)
    keep = lax.broadcasted_iota(jnp.int32, (WIDTH, 128), 1) < VAL - 384
    riders = jnp.zeros((WIDTH, 128), f32)
    for p in range(4):
        source = near_ref if p < 2 else far_ref
        piece = source[:, p % 2].reshape(WIDTH, LANES)
        whole[p, :, 0:384] = piece[:, 0:384]
        whole[p, :, 384:512] = jnp.where(keep, piece[:, 384:512], jnp.zeros((), bf16))
        ride = piece[:, 384:512].astype(f32)
        riders += ride
        lines = ride.T
        vector_ref[2 + p : 3 + p, :] = lines[50:51, :] + lines[53:54, :]
    lines = riders.T
    vector_ref[0:2, :] = lines[48:50, :] + lines[51:53, :]
    vector_ref[6:8, :] = jnp.zeros((2, WIDTH), f32)
    first_ref[...] = jnp.sum(riders.reshape(WIDTH // BLOCK, BLOCK, 128), axis=0)

    trace = jnp.float32(0.0)
    for i in range(tiles):
        for j in range(i, tiles):
            block = jnp.zeros((NS_TILE, NS_TILE), f32)
            for p in range(4):
                block += nt(whole[p, at[i], :], whole[p, at[j], :])
            gram[at[i], at[j]] = block
            if i < j:
                gram[at[j], at[i]] = block.T
            if i == j:
                trace += jnp.sum(block * eye)
    inverse = 1.0 / (jnp.sqrt(trace) + 1e-07)
    for q in range(4):

        @pl.when(chunk_ref[0] == q)
        def _():
            own[...] = whole[0, :, 128 * q : 128 * (q + 1)].astype(f32) * inverse

    def store(i, j, block, mean):
        gram[at[i], at[j]] = block
        top = block.astype(bf16)
        high[at[i], at[j]] = top
        low[at[i], at[j]] = (block - top.astype(f32)).astype(bf16)
        if i == j:
            top = (block - mean * eye).astype(bf16)
        shifted[at[i], at[j]] = top

    mean = trace * inverse * inverse * (1.0 / WIDTH)
    for i in range(tiles):
        for j in range(tiles):
            store(i, j, gram[at[i], at[j]] * (inverse * inverse), mean)

    def advance(mean):
        level = ns_second * mean + ns_third * mean * mean
        alpha = ns_first + level
        for i in range(tiles):
            for j in range(i, tiles):
                block = (ns_second + 2.0 * ns_third * mean) * gram[at[i], at[j]] + ns_third * nn(
                    shifted[at[i], :], shifted[:, at[j]]
                )
                if i == j:
                    block -= (ns_third * mean * mean + level) * eye
                block = block.astype(bf16)
                rest[at[i], at[j]] = block
                if i < j:
                    rest[at[j], at[i]] = block.T
        values = own[...]
        top = values.astype(bf16)
        own_b[:, 0:128] = top
        own_b[:, 128:256] = (values - top.astype(f32)).astype(bf16)
        for i in range(tiles):
            moved = nn(rest[at[i], :], own_b[...])
            own[at[i], :] = alpha * own[at[i], :] + (moved[:, 0:128] + moved[:, 128:256])
        return alpha

    def turn(_, mean):
        alpha = advance(mean)
        for i in range(tiles):
            for j in range(tiles):
                block = nn(high[at[i], :], rest[:, at[j]]) + nn(low[at[i], :], rest[:, at[j]])
                prod[at[i], at[j]] = block
                prod_b[at[i], at[j]] = block.astype(bf16)
        trace = jnp.float32(0.0)
        for i in range(tiles):
            for j in range(tiles):
                block = alpha * prod[at[i], at[j]] + 0.5 * nn(rest[at[i], :], prod_b[:, at[j]])
                prod[at[i], at[j]] = block
                if i == j:
                    trace += jnp.sum(block * eye)
        later = alpha * alpha * mean + trace * (2.0 / WIDTH)
        for i in range(tiles):
            for j in range(tiles):
                block = (alpha * alpha) * gram[at[i], at[j]] + (
                    prod[at[i], at[j]] + prod[at[j], at[i]].T
                )
                store(i, j, block, later)
        return later

    advance(lax.fori_loop(0, NS_ITERS - 1, turn, mean))
    out_ref[...] = own[...].astype(bf16)


def orthogonal(chunk, near, far):
    square = (WIDTH, WIDTH)
    return pl.pallas_call(
        iterate_kernel,
        out_shape=[
            jax.ShapeDtypeStruct((WIDTH, 128), bf16),
            jax.ShapeDtypeStruct((8, WIDTH), f32),
            jax.ShapeDtypeStruct((BLOCK, 128), f32),
        ],
        in_specs=[pl.BlockSpec(memory_space=pltpu.SMEM)]
        + [pl.BlockSpec(memory_space=pltpu.VMEM)] * 2,
        out_specs=[pl.BlockSpec(memory_space=pltpu.VMEM)] * 3,
        scratch_shapes=[
            pltpu.VMEM((4, WIDTH, LANES), bf16),
            pltpu.VMEM(square, f32),
            pltpu.VMEM(square, bf16),
            pltpu.VMEM(square, bf16),
            pltpu.VMEM(square, bf16),
            pltpu.VMEM(square, bf16),
            pltpu.VMEM(square, f32),
            pltpu.VMEM(square, bf16),
            pltpu.VMEM((WIDTH, 128), f32),
            pltpu.VMEM((WIDTH, 256), bf16),
        ],
        compiler_params=pltpu.CompilerParams(vmem_limit_bytes=48 * 2**20),
        cost_estimate=pl.CostEstimate(
            flops=42 * 10**9, bytes_accessed=5 * 2**20, transcendentals=0
        ),
        name="orthogonalize",
    )(chunk, near, far)


def shards(
    tokens,
    cotangent,
    qk_w,
    vg_w,
    mlp_w,
    out_w,
    qk_mom,
    vg_mom,
    mlp_mom,
    out_mom,
    norm_params,
    norm_moment,
    norm_second,
    decay_gap,
    seq_length,
    seq_group,
):
    rows, width = tokens.shape
    slots = 4 * rows
    groups = 32
    value_width = 4 * VAL
    key_scale = KEY ** (-0.5)
    dp_index = lax.axis_index(DP)
    tensor_index = lax.axis_index(TENSOR)
    chunk_index = lax.axis_index(("y_lo", "z_hi"))

    gain_one = norm_params[0:width]
    shift_one = norm_params[width : 2 * width]
    group_gain = jnp.pad(
        lax.dynamic_slice_in_dim(norm_params, 2 * width + tensor_index * VAL, VAL),
        (0, LANES - VAL),
    )
    gain_two = norm_params[2 * width + value_width : 3 * width + value_width]
    shift_two = norm_params[3 * width + value_width : 4 * width + value_width]

    out_rows = jnp.swapaxes(out_w, 1, 2)
    first_half = lax.axis_index("y_lo") == 0

    def weight_rows(parts):
        packed = jnp.concatenate(parts, axis=1).astype(bf16)
        far = swap(packed, "y_lo")
        pair = jnp.stack([jnp.where(first_half, packed, far), jnp.where(first_half, far, packed)])
        return pair

    def weight_gather(pair):
        return lax.all_gather(pair, PLANE, axis=1, tiled=True).reshape(width, -1)

    direct = jnp.concatenate(
        [pairs_apart(qk_w[0]), pairs_apart(qk_w[1]), widen(vg_w[0])], axis=1
    ).astype(bf16)
    gathered_qkv = lax.all_to_all(
        jnp.broadcast_to(direct[None], (groups,) + direct.shape),
        DP,
        split_axis=0,
        concat_axis=0,
        tiled=True,
    ).reshape(width, -1)
    pair_ret = weight_rows([widen(vg_w[1]), widen(out_rows[0])])
    pair_ff = weight_rows([widen(mlp_w[0]), widen(mlp_w[1]), widen(out_rows[1])])
    gathered_go = weight_gather(pair_ret)
    w_g, w_o = (gathered_go, 0, LANES), (gathered_go, LANES, LANES)

    whole_tokens = jnp.concatenate(tensor_gather(tokens), axis=0)
    order = jnp.stack([tensor_index, tensor_index ^ 2, tensor_index ^ 1, tensor_index ^ 3])
    place = (order[:, None] * rows + jnp.arange(rows, dtype=jnp.int32)[None, :]).reshape(slots)

    freqs = 1.0 / 10000.0 ** np.linspace(0.0, 1.0, KEY // 2)
    angles = np.arange(slots)[:, None] * freqs[None, :]
    tables = jnp.asarray(
        np.concatenate([np.cos(angles), np.sin(angles)], axis=1).astype(np.float32)
    ).reshape(4, rows, KEY)
    turned = tables[order].reshape(slots, KEY)

    labels = sequence_labels(seq_length, seq_group, dp_index, place)
    log_decay = jnp.log1p(-decay_gap[0])
    away = (place - slots // 2).astype(f32) * log_decay
    label_place = [labels.astype(f32), place.astype(f32)]
    columns = jnp.pad(jnp.stack(label_place + [jnp.exp(away)], axis=1), ((0, 0), (0, 125)))
    line = jnp.pad(jnp.stack(label_place + [jnp.exp(-away)], axis=0), ((0, 5), (0, 0)))
    gain_line = group_gain[None, :]

    hat_one, _ = normalize(whole_tokens.astype(f32))
    whole_one = (hat_one * gain_one + shift_one).astype(bf16)
    prepared = (whole_one, turned, columns, line)
    gathered_qkv, (whole_one, turned, columns, line) = together(gathered_qkv, prepared)
    cot_first, gathered_qkv = together(cotangent, gathered_qkv)
    w_qk, w_v = (gathered_qkv, 0, LANES), (gathered_qkv, LANES, LANES)
    whole_cot = tensor_gather(cot_first)
    (gain_line, pair_ff), whole_cot[1] = together((gain_line, pair_ff), whole_cot[1])
    gathered_ff = weight_gather(pair_ff)
    w_1, w_2, w_3 = ((gathered_ff, LANES * i, LANES) for i in range(3))
    query, keys, values, weights, gate, hat_group, inv_group, mixed, own, other = retention(
        whole_one, w_qk, w_v, w_g, w_o, turned, columns, line, gain_line
    )
    near, far = tensor_sum(own, other)
    middle = tokens.astype(f32) + near + far.astype(f32)
    hat_two, inv_two = normalize(middle)
    whole_two = tensor_gather((hat_two * gain_two + shift_two).astype(bf16))
    hidden, grad_gate, grad_up, own, other = feed(whole_two, w_1, w_2, whole_cot, w_3)
    near, far = tensor_sum(own, other)
    early, out_own, out_other = early_grads(whole_two, grad_gate, grad_up, whole_cot, hidden, w_3)
    far, early = together(far, early)
    grad_normed_two = near + far.astype(f32)
    grad_middle = cotangent.astype(f32) + norm_back(grad_normed_two, gain_two, hat_two, inv_two)
    grad_first, early = together(grad_middle.astype(bf16), early)
    grad_one = tensor_gather(grad_first)

    early_in = lax.all_to_all(early, PLANE, split_axis=0, concat_axis=0, tiled=True)
    early_halves = jnp.sum(early_in.astype(f32), axis=0)
    early_far = swap(
        jnp.where(first_half, early_halves[1], early_halves[0]).astype(bf16), "y_lo"
    )
    gain_two_grad = jnp.sum(grad_normed_two * hat_two, axis=0)
    shift_two_grad = jnp.sum(grad_normed_two, axis=0)

    grad_gate_ret, grad_retained, group_gain_grad = back_gate(
        grad_one, w_o, gate, hat_group, inv_group, gain_line
    )
    grad_query, grad_key, grad_values = back_scores(
        grad_retained, values, columns, line, keys, turned, weights, query
    )
    out_other, grad_query = together(out_other, grad_query)
    out_near, out_far = tensor_sum(out_own, out_other)
    result = (middle + out_near + out_far.astype(f32)).astype(bf16)
    small = jnp.stack(
        [gain_two_grad, shift_two_grad, jnp.pad(group_gain_grad[0], (0, width - LANES))], axis=1
    )
    small_high, small_low = split(small)
    riders = jnp.pad(
        jnp.concatenate([small_high, small_low], axis=1), ((0, 0), (VAL - 384, LANES - VAL - 6))
    )
    late = late_grads(
        grad_one, mixed, whole_one, grad_gate_ret, grad_values, riders, grad_query, grad_key
    )
    late, (grad_gate_ret, result) = together(late, (grad_gate_ret, result))
    late_in = lax.all_to_all(
        late.reshape(groups, BLOCK, -1), DP, split_axis=0, concat_axis=0, tiled=True
    )
    own, other = input_parts(
        grad_gate_ret, w_g, grad_values, w_v, grad_query, grad_key, w_qk
    )
    near, far = tensor_sum(own, other)
    far, early_far = together(far, early_far)
    early_sum = jnp.where(first_half, early_halves[0], early_halves[1]) + early_far.astype(f32)
    grad_normed_one = near + far.astype(f32)
    own_hat, own_inv = normalize(tokens.astype(f32))
    gain_one_grad = jnp.sum(grad_normed_one * own_hat, axis=0)
    shift_one_grad = jnp.sum(grad_normed_one, axis=0)
    input_grad = grad_middle + norm_back(grad_normed_one, gain_one, own_hat, own_inv)

    late_sum = jnp.sum(late_in.astype(f32), axis=0)
    small_sum = late_sum[:, LANES + VAL : LANES + VAL + 6]
    small_sum = small_sum[:, :3] + small_sum[:, 3:]

    grad_qk = pairs_together(jnp.stack([late_sum[:, 0:256], late_sum[:, 256:512]]))
    grad_vg = jnp.stack([late_sum[:, 512 : 512 + VAL], late_sum[:, 1024 : 1024 + VAL]])
    grad_mlp = jnp.stack([early_sum[:, 0:VAL], early_sum[:, 512 : 512 + VAL]])
    grad_out_t = jnp.stack([late_sum[:, 1536 : 1536 + VAL], early_sum[:, 1024 : 1024 + VAL]])
    mom_qk = muon_beta * qk_mom + grad_qk
    mom_vg = muon_beta * vg_mom + grad_vg
    mom_mlp = muon_beta * mlp_mom + grad_mlp
    mom_out = muon_beta * out_mom + jnp.swapaxes(grad_out_t, 1, 2)

    piece_high, piece_low = split(small_sum)
    first_norm = jnp.concatenate([gain_one_grad, shift_one_grad]).astype(bf16)
    extra = jnp.pad(
        jnp.concatenate([piece_high, piece_low, first_norm.reshape(BLOCK, 64)], axis=1),
        ((0, 0), (VAL, LANES - VAL - 70)),
    )
    stacked = (
        jnp.concatenate(
            [widen(mom_qk), widen(mom_vg), widen(mom_mlp), widen(jnp.swapaxes(mom_out, 1, 2))],
            axis=0,
        ).astype(bf16)
        + extra[None]
    )
    both = jnp.stack([stacked, swap(stacked, "y_hi")], axis=1)
    spread = jnp.broadcast_to(both[None], (4,) + both.shape).reshape((groups,) + both.shape[1:])
    arrived = lax.all_to_all(spread, DP, split_axis=0, concat_axis=0, tiled=True)
    far = swap(arrived, "core")
    own, vectors, first_total = orthogonal(
        jnp.reshape(chunk_index, (1,)).astype(jnp.int32), arrived, far
    )
    returned = lax.all_to_all(
        own.reshape(groups, BLOCK, 128), DP, split_axis=0, concat_axis=0, tiled=True
    ).astype(f32)
    returned = jnp.concatenate([returned[8 * i : 8 * i + 8] for i in range(4)], axis=2)

    shrink = 1.0 - muon_rate * decay_rate
    square_scale = 0.2 * math.sqrt(width)
    wide_scale = 0.2 * math.sqrt(max(width, value_width))
    new_qk = qk_w * shrink - (muon_rate * square_scale) * returned[0:2, :, :KEY]
    new_vg = vg_w * shrink - (muon_rate * wide_scale) * returned[2:4, :, :VAL]
    new_mlp = mlp_w * shrink - (muon_rate * wide_scale) * returned[4:6, :, :VAL]
    new_out = out_w * shrink - (muon_rate * wide_scale) * jnp.swapaxes(returned[6:8, :, :VAL], 1, 2)

    first_total = first_total[:, 54:118].reshape(2 * width)
    group_parts = vectors[2:6, :VAL]
    which = jnp.arange(4, dtype=jnp.int32)[:, None] == order[None, :]
    group_whole = jnp.sum(
        jnp.where(which[:, :, None], group_parts[None], 0.0), axis=1
    ).reshape(value_width)
    small_total = jnp.concatenate(
        [first_total, group_whole, vectors[0], vectors[1]]
    )
    moment_new = beta_first * norm_moment + (1.0 - beta_first) * small_total
    second_new = beta_second * norm_second + (1.0 - beta_second) * small_total * small_total
    params_new = norm_params - adam_rate * (moment_new / (1.0 - beta_first**OPT_STEP)) / (
        jnp.sqrt(second_new / (1.0 - beta_second**OPT_STEP)) + adam_eps
    )
    return (
        result,
        input_grad,
        mom_qk,
        mom_vg,
        mom_mlp,
        mom_out,
        new_qk,
        new_vg,
        new_mlp,
        new_out,
        moment_new,
        second_new,
        params_new,
    )


def solution(mesh):
    fine = Mesh(np.asarray(mesh.devices).reshape(SIZES), AXES)
    by_rows = P(DP + TENSOR, None)
    by_columns = P(None, DP, TENSOR)
    by_out = P(None, TENSOR, DP)
    return jax.shard_map(
        shards,
        mesh=fine,
        in_specs=(
            by_rows,
            by_rows,
            by_columns,
            by_columns,
            by_columns,
            by_out,
            by_columns,
            by_columns,
            by_columns,
            by_out,
            P(),
            P(),
            P(),
            P(TENSOR),
            P(),
            P(),
        ),
        out_specs=(
            by_rows,
            by_rows,
            by_columns,
            by_columns,
            by_columns,
            by_out,
            by_columns,
            by_columns,
            by_columns,
            by_out,
            P(),
            P(),
            P(),
        ),
        check_vma=False,
    )
```

```python
import math

import jax
import jax.numpy as jnp
import numpy as np
from jax import lax
from jax.experimental import pallas as pl
from jax.experimental.pallas import tpu as pltpu
from jax.sharding import Mesh
from jax.sharding import PartitionSpec as P

HEADS = 4
NS_ITERS = 5
OPT_STEP = 10
KEY = 256
VAL = 432
LANES = 512
BLOCK = 32

norm_eps = 1e-05
group_eps = 0.01
ns_first = 3.4445
ns_second = -4.775
ns_third = 2.0315
muon_rate = 0.15
muon_beta = 0.95
decay_rate = 0.01
adam_rate = 0.6
beta_first = 0.9
beta_second = 0.95
adam_eps = 1e-08

AXES = ("y_lo", "z_hi", "z_lo", "x", "y_hi", "core")
SIZES = (2, 2, 2, 4, 2, 2)
DP = ("y_lo", "z_hi", "z_lo", "x")
PLANE = ("z_hi", "z_lo", "x")
TENSOR = ("y_hi", "core")
bf16 = jnp.bfloat16
f32 = jnp.float32


def swap(values, axis):
    return lax.ppermute(values, axis, [(0, 1), (1, 0)])


def dot(left, right, dims):
    return lax.dot_general(left, right, (dims, ((), ())), preferred_element_type=f32)


def nn(left, right):
    return dot(left, right, ((1,), (0,)))


def nt(left, right):
    return dot(left, right, ((1,), (1,)))


def tn(left, right):
    return dot(left, right, ((0,), (0,)))


def split(values):
    high = lax.reduce_precision(values, 8, 7)
    return high.astype(bf16), (values - high).astype(bf16)


def widen(values):
    return jnp.pad(values, ((0, 0),) * (values.ndim - 1) + ((0, LANES - values.shape[-1]),))


def tensor_gather(own):
    far = swap(own, "y_hi")
    return [own, far, swap(own, "core"), swap(far, "core")]


def tensor_sum(own, other):
    half = own.shape[0] // 2
    arrived = swap(other, "core")
    far = (own[half:] + arrived[half:].astype(f32)).astype(bf16)
    return own[:half] + arrived[:half].astype(f32), swap(far, "y_hi")


def together(first, second):
    return lax.optimization_barrier((first, second))


def normalize(values):
    centre = values - jnp.mean(values, axis=-1, keepdims=True)
    spread = lax.rsqrt(jnp.mean(centre * centre, axis=-1, keepdims=True) + norm_eps)
    return centre * spread, spread


def norm_back(grad_out, gain, normed, spread):
    grad_normed = grad_out * gain
    return spread * (
        grad_normed
        - jnp.mean(grad_normed, axis=-1, keepdims=True)
        - normed * jnp.mean(grad_normed * normed, axis=-1, keepdims=True)
    )


def pairs_apart(values):
    shape = values.shape
    return jnp.swapaxes(values.reshape(shape[:-1] + (KEY // 2, 2)), -1, -2).reshape(shape)


def pairs_together(values):
    shape = values.shape
    return jnp.swapaxes(values.reshape(shape[:-1] + (2, KEY // 2)), -1, -2).reshape(shape)


def sequence_labels(seq_length, seq_group, group, place):
    mine = seq_group == group
    lengths = jnp.where(mine, seq_length, 0)
    ends = jnp.cumsum(lengths, dtype=jnp.int32)
    starts = ends - lengths
    inside = mine[None, :] & (place[:, None] >= starts[None, :]) & (place[:, None] < ends[None, :])
    number = jnp.arange(1, seq_length.shape[0] + 1, dtype=jnp.int32)
    return jnp.sum(jnp.where(inside, number[None, :], 0), axis=1, dtype=jnp.int32)


WIDTH = 1024
TILE = WIDTH // 2
EARLY = 1408
LATE = 1920
NS_TILE = 256


ROWS = [pl.ds(TILE * i, TILE) for i in range(WIDTH // TILE)]


STORES = 12


def in_vmem(kernel, name, out_shape, scratch, *operands):
    arrays, pieces, local = [], [], []
    for a in operands:
        parts = a if isinstance(a, list) else [a]
        top, piece = 0, []
        for part in parts:
            array, first, columns, *free = (
                part if isinstance(part, tuple) else (part, 0, part.shape[1])
            )
            whole = columns == array.shape[1]
            piece.append((len(arrays), None if whole else (first, columns), top, array.shape[0]))
            fixed = not free and (not isinstance(a, list) or isinstance(part, tuple))
            arrays.append(pltpu.with_memory_space_constraint(array, pltpu.HBM) if fixed else array)
            top += array.shape[0]
        pieces.append(piece)
        local.append(pltpu.VMEM((top, columns), array.dtype))
    n_in, n_out, n_local = len(arrays), len(out_shape), len(local)

    def body(*refs):
        ins, outs = refs[:n_in], refs[n_in : n_in + n_out]
        refs = refs[n_in + n_out :]
        local_in, local_out = refs[:n_local], refs[n_local : n_local + n_out]
        sem_in, sem_out = refs[n_local + n_out : n_local + n_out + 2]
        loads = []
        for i, piece in enumerate(pieces):
            loads.append([])
            for which, cut, top, rows in piece:
                source = ins[which] if cut is None else ins[which].at[:, pl.ds(*cut)]
                target = local_in[i] if len(piece) == 1 else local_in[i].at[pl.ds(top, rows), :]
                loads[i].append(pltpu.make_async_copy(source, target, sem_in.at[which]))
                loads[i][-1].start()
        pending = set(range(n_local))
        stores = []

        def ready(*which):
            for i in which:
                if i in pending:
                    pending.remove(i)
                    for load in loads[i]:
                        load.wait()

        def done(i, *index):
            source, target = local_out[i], outs[i]
            if index:
                source, target = source.at[index], target.at[index]
            stores.append(pltpu.make_async_copy(source, target, sem_out.at[len(stores)]))
            stores[-1].start()

        kernel(ready, done, *local_in, *local_out, *refs[n_local + n_out + 2 :])
        ready(*range(n_local))
        for store in stores:
            store.wait()

    local += [pltpu.VMEM(a.shape, a.dtype) for a in out_shape]
    held = sum(math.prod(a.shape) * jnp.dtype(a.dtype).itemsize for a in local)
    return pl.pallas_call(
        body,
        out_shape=[pltpu.HBM(a.shape, a.dtype) for a in out_shape],
        in_specs=[pl.BlockSpec(memory_space=pl.ANY)] * n_in,
        out_specs=[pl.BlockSpec(memory_space=pltpu.HBM)] * n_out,
        scratch_shapes=local
        + [pltpu.SemaphoreType.DMA((n_in,)), pltpu.SemaphoreType.DMA((STORES,))]
        + scratch,
        compiler_params=pltpu.CompilerParams(vmem_limit_bytes=held + 14 * 2**20),
        cost_estimate=pl.CostEstimate(flops=1, bytes_accessed=1, transcendentals=0),
        name=name,
    )(*arrays)


def put_halves(done, i, part, own_ref, other_ref, own, other):
    if i == 0:
        own_ref[...] = part
        done(own)
    else:
        other_ref[...] = part.astype(bf16)
        done(other)


def turn(first, second, cos_table, sin_table):
    return first * cos_table - second * sin_table, second * cos_table + first * sin_table


def masked(scores, rows, cols_ref, line_ref):
    label, place = cols_ref[rows, 0:1], cols_ref[rows, 1:2]
    linked = (label == line_ref[0:1, :]) & (label > 0.0) & (place >= line_ref[1:2, :])
    return jnp.where(linked, scores * (cols_ref[rows, 2:3] * line_ref[2:3, :]), 0.0)


def scores_kernel(
    ready, done, h_ref, wqk_ref, turn_ref, wv_ref, cols_ref, line_ref,
    q_ref, k_ref, v_ref, p_ref, hat_ref, inv_ref,
):
    half = KEY // 2
    ready(0, 1, 2)
    for rows in ROWS:
        cos_table, sin_table = turn_ref[rows, :half], turn_ref[rows, half:]
        both = nn(h_ref[rows, :], wqk_ref[...])
        query, keys = both[:, :KEY], both[:, KEY:] * KEY**-0.5
        first, second = turn(query[:, :half], query[:, half:], cos_table, sin_table)
        q_ref[rows, 0:half] = first.astype(bf16)
        q_ref[rows, half:KEY] = second.astype(bf16)
        first, second = turn(keys[:, :half], keys[:, half:], cos_table, sin_table)
        k_ref[rows, 0:half] = first.astype(bf16)
        k_ref[rows, half:KEY] = second.astype(bf16)
    done(0)
    done(1)
    ready(3)
    for rows in ROWS:
        v_ref[rows, :] = nn(h_ref[rows, :], wv_ref[...]).astype(bf16)
    done(2)
    ready(4, 5)
    for rows in ROWS:
        weights = masked(nt(q_ref[rows, :], k_ref[...]), rows, cols_ref, line_ref).astype(bf16)
        p_ref[rows, :] = weights
        done(3, rows)
        retained = nn(weights, v_ref[...])
        inverse = lax.rsqrt(
            jnp.sum(retained * retained, axis=-1, keepdims=True) * (1.0 / VAL) + group_eps
        )
        inv_ref[rows, :] = jnp.broadcast_to(inverse, (TILE, 128))
        hat_ref[rows, :] = retained * inverse
        done(4, rows)
    done(5)


def scores(*operands):
    shape = jax.ShapeDtypeStruct
    return in_vmem(
        scores_kernel,
        "retention",
        [
            shape((WIDTH, KEY), bf16),
            shape((WIDTH, KEY), bf16),
            shape((WIDTH, LANES), bf16),
            shape((WIDTH, WIDTH), bf16),
            shape((WIDTH, LANES), f32),
            shape((WIDTH, 128), f32),
        ],
        [],
        *operands,
    )


def gating_kernel(
    ready, done, h_ref, wg_ref, hat_ref, gain_ref, wo_ref, gate_ref, mixed_ref, own_ref, other_ref
):
    ready(0, 1)
    for i, rows in reversed(list(enumerate(ROWS))):
        gate = nn(h_ref[rows, :], wg_ref[...])
        gate_ref[rows, :] = gate
        done(0, rows)
        swish = gate * (1.0 / (1.0 + jnp.exp(-gate)))
        ready(2, 3)
        mixed = (hat_ref[rows, :] * gain_ref[...] * swish).astype(bf16)
        mixed_ref[rows, :] = mixed
        done(1, rows)
        ready(4)
        put_halves(done, i, nt(mixed, wo_ref[...]), own_ref, other_ref, 2, 3)


def gating(*operands):
    shape = jax.ShapeDtypeStruct
    return in_vmem(
        gating_kernel,
        "gate",
        [
            shape((WIDTH, LANES), f32),
            shape((WIDTH, LANES), bf16),
            shape((WIDTH // 2, WIDTH), f32),
            shape((WIDTH // 2, WIDTH), bf16),
        ],
        [],
        *operands,
    )


def feed_kernel(
    ready, done, h_ref, w1_ref, w2_ref, cot_ref, w3_ref,
    hidden_ref, gate_ref, up_ref, own_ref, other_ref,
):
    for i, rows in reversed(list(enumerate(ROWS))):
        ready(0, 1)
        pre_gate = nn(h_ref[rows, :], w1_ref[...])
        ready(2)
        pre_up = nn(h_ref[rows, :], w2_ref[...])
        ready(3, 4)
        grad_hidden = nn(cot_ref[rows, :], w3_ref[...])
        cumulative = 0.5 * (1.0 + lax.erf(pre_gate * (1.0 / math.sqrt(2.0))))
        density = jnp.exp(-0.5 * pre_gate * pre_gate) * (1.0 / math.sqrt(2.0 * math.pi))
        gelu_gate = pre_gate * cumulative
        hidden_ref[rows, :] = (gelu_gate * pre_up).astype(bf16)
        grad_gate = (grad_hidden * pre_up * (cumulative + pre_gate * density)).astype(bf16)
        grad_up = (grad_hidden * gelu_gate).astype(bf16)
        gate_ref[rows, :] = grad_gate
        up_ref[rows, :] = grad_up
        for k in range(3):
            done(k, rows)
        part = nt(grad_gate, w1_ref[...]) + nt(grad_up, w2_ref[...])
        put_halves(done, i, part, own_ref, other_ref, 3, 4)


def feed(*operands):
    shape = jax.ShapeDtypeStruct
    return in_vmem(
        feed_kernel,
        "feed_forward",
        [shape((WIDTH, LANES), bf16)] * 3
        + [shape((WIDTH // 2, WIDTH), f32), shape((WIDTH // 2, WIDTH), bf16)],
        [],
        *operands,
    )


def early_kernel(
    ready, done, h_ref, gate_ref, up_ref, cot_ref, hidden_ref, w3_ref, out_ref, own_ref, other_ref
):
    for j, (left, right) in enumerate(
        ((h_ref, gate_ref), (h_ref, up_ref), (cot_ref, hidden_ref))
    ):
        ready(*((0, 1), (2,), (3, 4))[j])
        columns = pl.ds(VAL * j, VAL)
        for i, at in enumerate(ROWS):
            part = tn(left[:, at], right[...]).astype(bf16)[:, :VAL]
            out_ref[:, i, :, columns] = part.reshape(16, BLOCK, VAL)
    out_ref[:, :, :, 3 * VAL : EARLY] = jnp.zeros((16, 2, BLOCK, EARLY - 3 * VAL), bf16)
    done(0)
    ready(5)
    for i, rows in reversed(list(enumerate(ROWS))):
        put_halves(done, i, nt(hidden_ref[rows, :], w3_ref[...]), own_ref, other_ref, 1, 2)


def early_grads(*operands):
    shape = jax.ShapeDtypeStruct
    return in_vmem(
        early_kernel,
        "feed_forward_grads",
        [
            shape((16, 2, BLOCK, EARLY), bf16),
            shape((WIDTH // 2, WIDTH), f32),
            shape((WIDTH // 2, WIDTH), bf16),
        ],
        [],
        *operands,
    )


def back_gate_kernel(
    ready, done, grad_ref, w_ref, gate_ref, hat_ref, inv_ref, gain_ref, gate_out, ret_out, gain_out
):
    total = jnp.zeros((1, LANES), f32)
    for rows in ROWS:
        ready(0, 1)
        grad_mixed = nn(grad_ref[rows, :], w_ref[...])
        ready(2, 3, 4, 5)
        gain = gain_ref[...]
        gate, hat, inverse = gate_ref[rows, :], hat_ref[rows, :], inv_ref[rows, 0:1]
        sig = 1.0 / (1.0 + jnp.exp(-gate))
        swish = gate * sig
        grad_grouped = grad_mixed * swish
        gate_out[rows, :] = (
            grad_mixed * (hat * gain) * (sig + swish * (1.0 - sig))
        ).astype(bf16)
        done(0, rows)
        total += jnp.sum(grad_grouped * hat, axis=0, keepdims=True)
        grad_hat = grad_grouped * gain
        inner = jnp.sum(grad_hat * hat, axis=-1, keepdims=True) * (1.0 / VAL)
        ret_out[rows, :] = (inverse * (grad_hat - hat * inner)).astype(bf16)
        done(1, rows)
    gain_out[...] = total
    done(2)


def back_gate(*operands):
    shape = jax.ShapeDtypeStruct
    return in_vmem(
        back_gate_kernel,
        "gate_backward",
        [shape((WIDTH, LANES), bf16)] * 2 + [shape((1, LANES), f32)],
        [],
        *operands,
    )


def back_scores_kernel(
    ready, done, ret_ref, v_ref, cols_ref, line_ref, k_ref, turn_ref, p_ref, q_ref,
    q_out, k_out, v_out, scores,
):
    half = KEY // 2
    ready(0, 1, 2, 3)
    for rows in ROWS:
        part = masked(nt(ret_ref[rows, :], v_ref[...]), rows, cols_ref, line_ref).astype(bf16)
        scores[rows, :] = part
        ready(4, 5)
        turned = nn(part, k_ref[...])
        first, second = turn(
            turned[:, :half], turned[:, half:], turn_ref[rows, :half], -turn_ref[rows, half:]
        )
        q_out[rows, 0:half] = first.astype(bf16)
        q_out[rows, half:KEY] = second.astype(bf16)
    done(0)
    ready(6, 7)
    for rows in ROWS:
        v_out[rows, :] = tn(p_ref[:, rows], ret_ref[...]).astype(bf16)
        done(2, rows)
    for rows in ROWS:
        turned = tn(scores[:, rows], q_ref[...])
        first, second = turn(
            turned[:, :half], turned[:, half:], turn_ref[rows, :half], -turn_ref[rows, half:]
        )
        k_out[rows, 0:half] = first.astype(bf16)
        k_out[rows, half:KEY] = second.astype(bf16)
    done(1)


def back_scores(*operands):
    shape = jax.ShapeDtypeStruct
    return in_vmem(
        back_scores_kernel,
        "scores_backward",
        [shape((WIDTH, KEY), bf16)] * 2 + [shape((WIDTH, LANES), bf16)],
        [pltpu.VMEM((WIDTH, WIDTH), bf16)],
        *operands,
    )


def late_kernel(
    ready, done, grad_ref, mixed_ref, h_ref, gate_ref, v_ref, ride_ref, q_ref, k_ref, out_ref
):
    ready(0, 1)
    for rows in ROWS:
        part = tn(grad_ref[:, rows], mixed_ref[...]).astype(bf16)
        out_ref[rows, 2 * KEY + 2 * VAL : 2 * KEY + 3 * VAL] = part[:, :VAL]
    ready(2, 3)
    for rows in ROWS:
        part = tn(h_ref[:, rows], gate_ref[...]).astype(bf16)
        out_ref[rows, 2 * KEY + VAL : 2 * KEY + 2 * VAL] = part[:, :VAL]
    ready(4, 5)
    for rows in ROWS:
        part = tn(h_ref[:, rows], v_ref[...]).astype(bf16)
        out_ref[rows, 2 * KEY : 2 * KEY + VAL] = part[:, :VAL]
        out_ref[rows, 2 * KEY + 3 * VAL : LATE] = ride_ref[rows, : LATE - 2 * KEY - 3 * VAL]
    ready(6, 7)
    for rows in ROWS:
        left = h_ref[:, rows]
        out_ref[rows, 0:KEY] = tn(left, q_ref[...]).astype(bf16)
        out_ref[rows, KEY : 2 * KEY] = (tn(left, k_ref[...]) * KEY**-0.5).astype(bf16)
    done(0)


def late_grads(*operands):
    return in_vmem(
        late_kernel,
        "retention_grads",
        [jax.ShapeDtypeStruct((WIDTH, LATE), bf16)],
        [],
        *operands,
    )[0]


def input_kernel(
    ready, done, gate_ref, wg_ref, v_ref, wv_ref, q_ref, k_ref, wqk_ref, own_ref, other_ref
):
    for i, rows in reversed(list(enumerate(ROWS))):
        ready(0, 1)
        part = nt(gate_ref[rows, :], wg_ref[...])
        ready(2, 3)
        part += nt(v_ref[rows, :], wv_ref[...])
        ready(4, 5, 6)
        part += nt(q_ref[rows, :], wqk_ref[:, 0:KEY])
        part += nt(k_ref[rows, :], wqk_ref[:, KEY : 2 * KEY]) * KEY**-0.5
        put_halves(done, i, part, own_ref, other_ref, 0, 1)


def input_parts(*operands):
    shape = jax.ShapeDtypeStruct
    return in_vmem(
        input_kernel,
        "input_grad_parts",
        [shape((WIDTH // 2, WIDTH), f32), shape((WIDTH // 2, WIDTH), bf16)],
        [],
        *operands,
    )


def iterate_kernel(
    chunk_ref, near_ref, far_ref, out_ref, vector_ref, first_ref, whole, gram, high, low, shifted, rest, prod, prod_b, own, own_b
):
    tiles = WIDTH // NS_TILE
    at = [pl.ds(NS_TILE * i, NS_TILE) for i in range(tiles)]
    eye = (
        lax.broadcasted_iota(jnp.int32, (NS_TILE, NS_TILE), 0)
        == lax.broadcasted_iota(jnp.int32, (NS_TILE, NS_TILE), 1)
    ).astype(f32)
    keep = lax.broadcasted_iota(jnp.int32, (WIDTH, 128), 1) < VAL - 384
    riders = jnp.zeros((WIDTH, 128), f32)
    for p in range(4):
        source = near_ref if p < 2 else far_ref
        piece = source[:, p % 2].reshape(WIDTH, LANES)
        whole[p, :, 0:384] = piece[:, 0:384]
        whole[p, :, 384:512] = jnp.where(keep, piece[:, 384:512], jnp.zeros((), bf16))
        ride = piece[:, 384:512].astype(f32)
        riders += ride
        lines = ride.T
        vector_ref[2 + p : 3 + p, :] = lines[50:51, :] + lines[53:54, :]
    lines = riders.T
    vector_ref[0:2, :] = lines[48:50, :] + lines[51:53, :]
    vector_ref[6:8, :] = jnp.zeros((2, WIDTH), f32)
    first_ref[...] = jnp.sum(riders.reshape(WIDTH // BLOCK, BLOCK, 128), axis=0)

    trace = jnp.float32(0.0)
    for i in range(tiles):
        for j in range(i, tiles):
            block = jnp.zeros((NS_TILE, NS_TILE), f32)
            for p in range(4):
                block += nt(whole[p, at[i], :], whole[p, at[j], :])
            gram[at[i], at[j]] = block
            if i < j:
                gram[at[j], at[i]] = block.T
            if i == j:
                trace += jnp.sum(block * eye)
    inverse = 1.0 / (jnp.sqrt(trace) + 1e-07)
    for q in range(4):

        @pl.when(chunk_ref[0] == q)
        def _():
            own[...] = whole[0, :, 128 * q : 128 * (q + 1)].astype(f32) * inverse

    def store(i, j, block, mean):
        gram[at[i], at[j]] = block
        top = block.astype(bf16)
        high[at[i], at[j]] = top
        low[at[i], at[j]] = (block - top.astype(f32)).astype(bf16)
        if i == j:
            top = (block - mean * eye).astype(bf16)
        shifted[at[i], at[j]] = top

    mean = trace * inverse * inverse * (1.0 / WIDTH)
    for i in range(tiles):
        for j in range(tiles):
            store(i, j, gram[at[i], at[j]] * (inverse * inverse), mean)

    def advance(mean):
        level = ns_second * mean + ns_third * mean * mean
        alpha = ns_first + level
        for i in range(tiles):
            for j in range(i, tiles):
                block = (ns_second + 2.0 * ns_third * mean) * gram[at[i], at[j]] + ns_third * nn(
                    shifted[at[i], :], shifted[:, at[j]]
                )
                if i == j:
                    block -= (ns_third * mean * mean + level) * eye
                block = block.astype(bf16)
                rest[at[i], at[j]] = block
                if i < j:
                    rest[at[j], at[i]] = block.T
        values = own[...]
        top = values.astype(bf16)
        own_b[:, 0:128] = top
        own_b[:, 128:256] = (values - top.astype(f32)).astype(bf16)
        for i in range(tiles):
            moved = nn(rest[at[i], :], own_b[...])
            own[at[i], :] = alpha * own[at[i], :] + (moved[:, 0:128] + moved[:, 128:256])
        return alpha

    def turn(_, mean):
        alpha = advance(mean)
        for i in range(tiles):
            for j in range(tiles):
                block = nn(high[at[i], :], rest[:, at[j]]) + nn(low[at[i], :], rest[:, at[j]])
                prod[at[i], at[j]] = block
                prod_b[at[i], at[j]] = block.astype(bf16)
        trace = jnp.float32(0.0)
        for i in range(tiles):
            for j in range(tiles):
                block = alpha * prod[at[i], at[j]] + 0.5 * nn(rest[at[i], :], prod_b[:, at[j]])
                prod[at[i], at[j]] = block
                if i == j:
                    trace += jnp.sum(block * eye)
        later = alpha * alpha * mean + trace * (2.0 / WIDTH)
        for i in range(tiles):
            for j in range(tiles):
                block = (alpha * alpha) * gram[at[i], at[j]] + (
                    prod[at[i], at[j]] + prod[at[j], at[i]].T
                )
                store(i, j, block, later)
        return later

    advance(lax.fori_loop(0, NS_ITERS - 1, turn, mean))
    out_ref[...] = own[...].astype(bf16)


def orthogonal(chunk, near, far):
    square = (WIDTH, WIDTH)
    return pl.pallas_call(
        iterate_kernel,
        out_shape=[
            jax.ShapeDtypeStruct((WIDTH, 128), bf16),
            jax.ShapeDtypeStruct((8, WIDTH), f32),
            jax.ShapeDtypeStruct((BLOCK, 128), f32),
        ],
        in_specs=[pl.BlockSpec(memory_space=pltpu.SMEM)]
        + [pl.BlockSpec(memory_space=pltpu.VMEM)] * 2,
        out_specs=[pl.BlockSpec(memory_space=pltpu.VMEM)] * 3,
        scratch_shapes=[
            pltpu.VMEM((4, WIDTH, LANES), bf16),
            pltpu.VMEM(square, f32),
            pltpu.VMEM(square, bf16),
            pltpu.VMEM(square, bf16),
            pltpu.VMEM(square, bf16),
            pltpu.VMEM(square, bf16),
            pltpu.VMEM(square, f32),
            pltpu.VMEM(square, bf16),
            pltpu.VMEM((WIDTH, 128), f32),
            pltpu.VMEM((WIDTH, 256), bf16),
        ],
        compiler_params=pltpu.CompilerParams(vmem_limit_bytes=48 * 2**20),
        cost_estimate=pl.CostEstimate(
            flops=42 * 10**9, bytes_accessed=5 * 2**20, transcendentals=0
        ),
        name="orthogonalize",
    )(chunk, near, far)


def shards(
    tokens,
    cotangent,
    qk_w,
    vg_w,
    mlp_w,
    out_w,
    qk_mom,
    vg_mom,
    mlp_mom,
    out_mom,
    norm_params,
    norm_moment,
    norm_second,
    decay_gap,
    seq_length,
    seq_group,
):
    rows, width = tokens.shape
    slots = 4 * rows
    groups = 32
    value_width = 4 * VAL
    key_scale = KEY ** (-0.5)
    dp_index = lax.axis_index(DP)
    tensor_index = lax.axis_index(TENSOR)
    chunk_index = lax.axis_index(("y_lo", "z_hi"))

    gain_one = norm_params[0:width]
    shift_one = norm_params[width : 2 * width]
    group_gain = jnp.pad(
        lax.dynamic_slice_in_dim(norm_params, 2 * width + tensor_index * VAL, VAL),
        (0, LANES - VAL),
    )
    gain_two = norm_params[2 * width + value_width : 3 * width + value_width]
    shift_two = norm_params[3 * width + value_width : 4 * width + value_width]

    out_rows = jnp.swapaxes(out_w, 1, 2)
    first_half = lax.axis_index("y_lo") == 0

    def weight_rows(parts):
        packed = jnp.concatenate(parts, axis=1).astype(bf16)
        far = swap(packed, "y_lo")
        pair = jnp.stack([jnp.where(first_half, packed, far), jnp.where(first_half, far, packed)])
        return pair

    def weight_gather(pair):
        return lax.all_gather(pair, PLANE, axis=1, tiled=True).reshape(width, -1)

    direct = jnp.concatenate(
        [pairs_apart(qk_w[0]), pairs_apart(qk_w[1]), widen(vg_w[0])], axis=1
    ).astype(bf16)
    pair_ret = weight_rows([widen(vg_w[1]), widen(out_rows[0])])
    (direct, tokens_first), pair_ret = together((direct, tokens), pair_ret)
    gathered_qkv = lax.all_to_all(
        jnp.broadcast_to(direct[None], (groups,) + direct.shape),
        DP,
        split_axis=0,
        concat_axis=0,
        tiled=True,
    ).reshape(width, -1)
    pair_ff = weight_rows([widen(mlp_w[0]), widen(mlp_w[1]), widen(out_rows[1])])
    gathered_go = weight_gather(pair_ret)
    w_g, w_o = (gathered_go, 0, LANES), (gathered_go, LANES, LANES)

    whole_tokens = jnp.concatenate(tensor_gather(tokens_first), axis=0)
    order = jnp.stack([tensor_index, tensor_index ^ 2, tensor_index ^ 1, tensor_index ^ 3])
    place = (order[:, None] * rows + jnp.arange(rows, dtype=jnp.int32)[None, :]).reshape(slots)

    freqs = 1.0 / 10000.0 ** np.linspace(0.0, 1.0, KEY // 2)
    angles = np.arange(slots)[:, None] * freqs[None, :]
    tables = jnp.asarray(
        np.concatenate([np.cos(angles), np.sin(angles)], axis=1).astype(np.float32)
    ).reshape(4, rows, KEY)
    turned = tables[order].reshape(slots, KEY)

    labels = sequence_labels(seq_length, seq_group, dp_index, place)
    log_decay = jnp.log1p(-decay_gap[0])
    away = (place - slots // 2).astype(f32) * log_decay
    label_place = [labels.astype(f32), place.astype(f32)]
    columns = jnp.pad(jnp.stack(label_place + [jnp.exp(away)], axis=1), ((0, 0), (0, 125)))
    line = jnp.pad(jnp.stack(label_place + [jnp.exp(-away)], axis=0), ((0, 5), (0, 0)))
    gain_line = group_gain[None, :]

    hat_one, _ = normalize(whole_tokens.astype(f32))
    whole_one = (hat_one * gain_one + shift_one).astype(bf16)
    prepared = (whole_one, turned, columns, line)
    gathered_qkv, (whole_one, turned, columns, line) = together(gathered_qkv, prepared)
    cot_first, gathered_qkv = together(cotangent, gathered_qkv)
    w_qk, w_v = (gathered_qkv, 0, LANES, True), (gathered_qkv, LANES, LANES, True)
    cot_far, cot_core = swap(cot_first, "y_hi"), swap(cot_first, "core")
    query, keys, values, weights, hat_group, inv_group = scores(
        whole_one, w_qk, turned, w_v, columns, line
    )
    cot_far, hat_group = together(cot_far, hat_group)
    cot_last = swap(cot_far, "core")
    (gain_line, pair_ff), cot_last = together((gain_line, pair_ff), cot_last)
    whole_cot = [(part, 0, width) for part in (cotangent, cot_far, cot_core, cot_last)]
    gathered_ff = weight_gather(pair_ff)
    w_1, w_2, w_3 = ((gathered_ff, LANES * i, LANES) for i in range(3))
    gate, mixed, own, other = gating(whole_one, w_g, hat_group, gain_line, w_o)
    near, far = tensor_sum(own, other)
    middle = tokens.astype(f32) + near + far.astype(f32)
    hat_two, inv_two = normalize(middle)
    whole_two = tensor_gather((hat_two * gain_two + shift_two).astype(bf16))
    hidden, grad_gate, grad_up, own, other = feed(whole_two, w_1, w_2, whole_cot, w_3)
    near, far = tensor_sum(own, other)
    early, out_own, out_other = early_grads(whole_two, grad_gate, grad_up, whole_cot, hidden, w_3)
    far, early = together(far, early)
    grad_normed_two = near + far.astype(f32)
    grad_middle = cotangent.astype(f32) + norm_back(grad_normed_two, gain_two, hat_two, inv_two)
    grad_first, early = together(grad_middle.astype(bf16), early)
    grad_one = tensor_gather(grad_first)

    early_in = lax.all_to_all(early, PLANE, split_axis=0, concat_axis=0, tiled=True)
    early_halves = jnp.sum(early_in.astype(f32), axis=0)
    early_far = swap(
        jnp.where(first_half, early_halves[1], early_halves[0]).astype(bf16), "y_lo"
    )
    gain_two_grad = jnp.sum(grad_normed_two * hat_two, axis=0)
    shift_two_grad = jnp.sum(grad_normed_two, axis=0)

    grad_gate_ret, grad_retained, group_gain_grad = back_gate(
        grad_one, w_o, gate, hat_group, inv_group, gain_line
    )
    grad_query, grad_key, grad_values = back_scores(
        grad_retained, values, columns, line, keys, turned, weights, query
    )
    out_other, grad_query = together(out_other, grad_query)
    out_near, out_far = tensor_sum(out_own, out_other)
    result = (middle + out_near + out_far.astype(f32)).astype(bf16)
    small = jnp.stack(
        [gain_two_grad, shift_two_grad, jnp.pad(group_gain_grad[0], (0, width - LANES))], axis=1
    )
    small_high, small_low = split(small)
    riders = jnp.pad(
        jnp.concatenate([small_high, small_low], axis=1), ((0, 0), (0, 128 - 6))
    )
    late = late_grads(
        grad_one, mixed, whole_one, grad_gate_ret, grad_values, riders, grad_query, grad_key
    )
    late, (grad_gate_ret, result) = together(late, (grad_gate_ret, result))
    late_in = lax.all_to_all(
        late.reshape(groups, BLOCK, -1), DP, split_axis=0, concat_axis=0, tiled=True
    )
    own, other = input_parts(
        grad_gate_ret, w_g, grad_values, w_v, grad_query, grad_key, w_qk
    )
    near, far = tensor_sum(own, other)
    grad_normed_one = near + far.astype(f32)
    own_hat, own_inv = normalize(tokens.astype(f32))
    gain_one_grad = jnp.sum(grad_normed_one * own_hat, axis=0)
    shift_one_grad = jnp.sum(grad_normed_one, axis=0)
    input_grad = grad_middle + norm_back(grad_normed_one, gain_one, own_hat, own_inv)
    gain_one_grad, early_far = together(gain_one_grad, early_far)
    early_sum = jnp.where(first_half, early_halves[0], early_halves[1]) + early_far.astype(f32)

    late_sum = jnp.sum(late_in.astype(f32), axis=0)
    first_value = 2 * KEY
    at = [first_value + VAL * i for i in range(4)]
    small_sum = late_sum[:, at[3] : at[3] + 6]
    small_sum = small_sum[:, :3] + small_sum[:, 3:]

    grad_qk = pairs_together(jnp.stack([late_sum[:, 0:256], late_sum[:, 256:512]]))
    grad_vg = jnp.stack([late_sum[:, at[0] : at[1]], late_sum[:, at[1] : at[2]]])
    grad_mlp = jnp.stack([early_sum[:, 0:VAL], early_sum[:, VAL : 2 * VAL]])
    grad_out_t = jnp.stack([late_sum[:, at[2] : at[3]], early_sum[:, 2 * VAL : 3 * VAL]])
    mom_qk = muon_beta * qk_mom + grad_qk
    mom_vg = muon_beta * vg_mom + grad_vg
    mom_mlp = muon_beta * mlp_mom + grad_mlp
    mom_out = muon_beta * out_mom + jnp.swapaxes(grad_out_t, 1, 2)

    piece_high, piece_low = split(small_sum)
    first_norm = jnp.concatenate([gain_one_grad, shift_one_grad]).astype(bf16)
    extra = jnp.pad(
        jnp.concatenate([piece_high, piece_low, first_norm.reshape(BLOCK, 64)], axis=1),
        ((0, 0), (VAL, LANES - VAL - 70)),
    )
    stacked = (
        jnp.concatenate(
            [widen(mom_qk), widen(mom_vg), widen(mom_mlp), widen(jnp.swapaxes(mom_out, 1, 2))],
            axis=0,
        ).astype(bf16)
        + extra[None]
    )
    both = jnp.stack([stacked, swap(stacked, "y_hi")], axis=1)
    spread = jnp.broadcast_to(both[None], (4,) + both.shape).reshape((groups,) + both.shape[1:])
    arrived = lax.all_to_all(spread, DP, split_axis=0, concat_axis=0, tiled=True)
    far = swap(arrived, "core")
    own, vectors, first_total = orthogonal(
        jnp.reshape(chunk_index, (1,)).astype(jnp.int32), arrived, far
    )
    returned = lax.all_to_all(
        own.reshape(groups, BLOCK, 128), DP, split_axis=0, concat_axis=0, tiled=True
    ).astype(f32)
    returned = jnp.concatenate([returned[8 * i : 8 * i + 8] for i in range(4)], axis=2)

    shrink = 1.0 - muon_rate * decay_rate
    square_scale = 0.2 * math.sqrt(width)
    wide_scale = 0.2 * math.sqrt(max(width, value_width))
    new_qk = qk_w * shrink - (muon_rate * square_scale) * returned[0:2, :, :KEY]
    new_vg = vg_w * shrink - (muon_rate * wide_scale) * returned[2:4, :, :VAL]
    new_mlp = mlp_w * shrink - (muon_rate * wide_scale) * returned[4:6, :, :VAL]
    new_out = out_w * shrink - (muon_rate * wide_scale) * jnp.swapaxes(returned[6:8, :, :VAL], 1, 2)

    first_total = first_total[:, 54:118].reshape(2 * width)
    group_parts = vectors[2:6, :VAL]
    which = jnp.arange(4, dtype=jnp.int32)[:, None] == order[None, :]
    group_whole = jnp.sum(
        jnp.where(which[:, :, None], group_parts[None], 0.0), axis=1
    ).reshape(value_width)
    small_total = jnp.concatenate(
        [first_total, group_whole, vectors[0], vectors[1]]
    )
    moment_new = beta_first * norm_moment + (1.0 - beta_first) * small_total
    second_new = beta_second * norm_second + (1.0 - beta_second) * small_total * small_total
    params_new = norm_params - adam_rate * (moment_new / (1.0 - beta_first**OPT_STEP)) / (
        jnp.sqrt(second_new / (1.0 - beta_second**OPT_STEP)) + adam_eps
    )
    return (
        result,
        input_grad,
        mom_qk,
        mom_vg,
        mom_mlp,
        mom_out,
        new_qk,
        new_vg,
        new_mlp,
        new_out,
        moment_new,
        second_new,
        params_new,
    )


def solution(mesh):
    fine = Mesh(np.asarray(mesh.devices).reshape(SIZES), AXES)
    by_rows = P(DP + TENSOR, None)
    by_columns = P(None, DP, TENSOR)
    by_out = P(None, TENSOR, DP)
    return jax.shard_map(
        shards,
        mesh=fine,
        in_specs=(
            by_rows,
            by_rows,
            by_columns,
            by_columns,
            by_columns,
            by_out,
            by_columns,
            by_columns,
            by_columns,
            by_out,
            P(),
            P(),
            P(),
            P(TENSOR),
            P(),
            P(),
        ),
        out_specs=(
            by_rows,
            by_rows,
            by_columns,
            by_columns,
            by_columns,
            by_out,
            by_columns,
            by_columns,
            by_columns,
            by_out,
            P(),
            P(),
            P(),
        ),
        check_vma=False,
    )
```

```python
import math

import jax
import jax.numpy as jnp
import numpy as np
from jax import lax
from jax.experimental import pallas as pl
from jax.experimental.pallas import tpu as pltpu
from jax.sharding import Mesh
from jax.sharding import PartitionSpec as P

HEADS = 4
NS_ITERS = 5
OPT_STEP = 10
KEY = 256
VAL = 432
LANES = 512
BLOCK = 32

norm_eps = 1e-05
group_eps = 0.01
ns_first = 3.4445
ns_second = -4.775
ns_third = 2.0315
muon_rate = 0.15
muon_beta = 0.95
decay_rate = 0.01
adam_rate = 0.6
beta_first = 0.9
beta_second = 0.95
adam_eps = 1e-08

AXES = ("y_lo", "z_hi", "z_lo", "x", "y_hi", "core")
SIZES = (2, 2, 2, 4, 2, 2)
DP = ("y_lo", "z_hi", "z_lo", "x")
PLANE = ("z_hi", "z_lo", "x")
TENSOR = ("y_hi", "core")
bf16 = jnp.bfloat16
f32 = jnp.float32


def swap(values, axis):
    return lax.ppermute(values, axis, [(0, 1), (1, 0)])


def dot(left, right, dims):
    return lax.dot_general(left, right, (dims, ((), ())), preferred_element_type=f32)


def nn(left, right):
    return dot(left, right, ((1,), (0,)))


def nt(left, right):
    return dot(left, right, ((1,), (1,)))


def tn(left, right):
    return dot(left, right, ((0,), (0,)))


def split(values):
    high = lax.reduce_precision(values, 8, 7)
    return high.astype(bf16), (values - high).astype(bf16)


def widen(values):
    return jnp.pad(values, ((0, 0),) * (values.ndim - 1) + ((0, LANES - values.shape[-1]),))


def tensor_gather(own):
    far = swap(own, "y_hi")
    return [own, far, swap(own, "core"), swap(far, "core")]


def half_sum(own, other):
    half = own.shape[0] // 2
    arrived = swap(other, "core")
    far = (own[half:] + arrived[half:].astype(f32)).astype(bf16)
    return own[:half] + arrived[:half].astype(f32), far


def tensor_sum(own, other):
    near, far = half_sum(own, other)
    return near, swap(far, "y_hi")


def together(first, second):
    return lax.optimization_barrier((first, second))


def normalize(values):
    centre = values - jnp.mean(values, axis=-1, keepdims=True)
    spread = lax.rsqrt(jnp.mean(centre * centre, axis=-1, keepdims=True) + norm_eps)
    return centre * spread, spread


def norm_back(grad_out, gain, normed, spread):
    grad_normed = grad_out * gain
    return spread * (
        grad_normed
        - jnp.mean(grad_normed, axis=-1, keepdims=True)
        - normed * jnp.mean(grad_normed * normed, axis=-1, keepdims=True)
    )


def pairs_apart(values):
    shape = values.shape
    return jnp.swapaxes(values.reshape(shape[:-1] + (KEY // 2, 2)), -1, -2).reshape(shape)


def pairs_together(values):
    shape = values.shape
    return jnp.swapaxes(values.reshape(shape[:-1] + (2, KEY // 2)), -1, -2).reshape(shape)


def sequence_labels(seq_length, seq_group, group, place):
    mine = seq_group == group
    lengths = jnp.where(mine, seq_length, 0)
    ends = jnp.cumsum(lengths, dtype=jnp.int32)
    starts = ends - lengths
    inside = mine[None, :] & (place[:, None] >= starts[None, :]) & (place[:, None] < ends[None, :])
    number = jnp.arange(1, seq_length.shape[0] + 1, dtype=jnp.int32)
    return jnp.sum(jnp.where(inside, number[None, :], 0), axis=1, dtype=jnp.int32)


WIDTH = 1024
TILE = WIDTH // 2
EARLY = 1408
LATE = 1920
NS_TILE = 256


ROWS = [pl.ds(TILE * i, TILE) for i in range(WIDTH // TILE)]


STORES = 12


def in_vmem(kernel, name, out_shape, scratch, *operands):
    arrays, pieces, local = [], [], []
    for a in operands:
        parts = a if isinstance(a, list) else [a]
        top, piece = 0, []
        for part in parts:
            array, first, columns, *free = (
                part if isinstance(part, tuple) else (part, 0, part.shape[1])
            )
            whole = columns == array.shape[1]
            piece.append((len(arrays), None if whole else (first, columns), top, array.shape[0]))
            fixed = not free and (not isinstance(a, list) or isinstance(part, tuple))
            arrays.append(pltpu.with_memory_space_constraint(array, pltpu.HBM) if fixed else array)
            top += array.shape[0]
        pieces.append(piece)
        local.append(pltpu.VMEM((top, columns), array.dtype))
    n_in, n_out, n_local = len(arrays), len(out_shape), len(local)

    def body(*refs):
        ins, outs = refs[:n_in], refs[n_in : n_in + n_out]
        refs = refs[n_in + n_out :]
        local_in, local_out = refs[:n_local], refs[n_local : n_local + n_out]
        sem_in, sem_out = refs[n_local + n_out : n_local + n_out + 2]
        loads = []
        for i, piece in enumerate(pieces):
            loads.append([])
            for which, cut, top, rows in piece:
                source = ins[which] if cut is None else ins[which].at[:, pl.ds(*cut)]
                target = local_in[i] if len(piece) == 1 else local_in[i].at[pl.ds(top, rows), :]
                loads[i].append(pltpu.make_async_copy(source, target, sem_in.at[which]))
                loads[i][-1].start()
        pending = set(range(n_local))
        stores = []

        def ready(*which):
            for i in which:
                if i in pending:
                    pending.remove(i)
                    for load in loads[i]:
                        load.wait()

        def done(i, *index):
            source, target = local_out[i], outs[i]
            if index:
                source, target = source.at[index], target.at[index]
            stores.append(pltpu.make_async_copy(source, target, sem_out.at[len(stores)]))
            stores[-1].start()

        kernel(ready, done, *local_in, *local_out, *refs[n_local + n_out + 2 :])
        ready(*range(n_local))
        for store in stores:
            store.wait()

    local += [pltpu.VMEM(a.shape, a.dtype) for a in out_shape]
    held = sum(math.prod(a.shape) * jnp.dtype(a.dtype).itemsize for a in local)
    return pl.pallas_call(
        body,
        out_shape=[pltpu.HBM(a.shape, a.dtype) for a in out_shape],
        in_specs=[pl.BlockSpec(memory_space=pl.ANY)] * n_in,
        out_specs=[pl.BlockSpec(memory_space=pltpu.HBM)] * n_out,
        scratch_shapes=local
        + [pltpu.SemaphoreType.DMA((n_in,)), pltpu.SemaphoreType.DMA((STORES,))]
        + scratch,
        compiler_params=pltpu.CompilerParams(vmem_limit_bytes=held + 14 * 2**20),
        cost_estimate=pl.CostEstimate(flops=1, bytes_accessed=1, transcendentals=0),
        name=name,
    )(*arrays)


def put_halves(done, i, part, own_ref, other_ref, own, other):
    if i == 0:
        own_ref[...] = part
        done(own)
    else:
        other_ref[...] = part.astype(bf16)
        done(other)


def turn(first, second, cos_table, sin_table):
    return first * cos_table - second * sin_table, second * cos_table + first * sin_table


def masked(scores, rows, cols_ref, line_ref):
    label, place = cols_ref[rows, 0:1], cols_ref[rows, 1:2]
    linked = (label == line_ref[0:1, :]) & (label > 0.0) & (place >= line_ref[1:2, :])
    return jnp.where(linked, scores * (cols_ref[rows, 2:3] * line_ref[2:3, :]), 0.0)


def retention_kernel(
    ready, done, h_ref, wqk_ref, wv_ref, wg_ref, wo_ref, turn_ref, cols_ref, line_ref, gain_ref,
    q_ref, k_ref, v_ref, p_ref, gate_ref, hat_ref, inv_ref, mixed_ref, own_ref, other_ref,
):
    half = KEY // 2
    ready(0, 1, 5)
    for rows in ROWS:
        cos_table, sin_table = turn_ref[rows, :half], turn_ref[rows, half:]
        both = nn(h_ref[rows, :], wqk_ref[...])
        query, keys = both[:, :KEY], both[:, KEY:] * KEY**-0.5
        first, second = turn(query[:, :half], query[:, half:], cos_table, sin_table)
        q_ref[rows, 0:half] = first.astype(bf16)
        q_ref[rows, half:KEY] = second.astype(bf16)
        first, second = turn(keys[:, :half], keys[:, half:], cos_table, sin_table)
        k_ref[rows, 0:half] = first.astype(bf16)
        k_ref[rows, half:KEY] = second.astype(bf16)
    done(0)
    done(1)
    ready(2)
    for rows in ROWS:
        v_ref[rows, :] = nn(h_ref[rows, :], wv_ref[...]).astype(bf16)
    done(2)
    ready(3)
    for rows in ROWS:
        gate_ref[rows, :] = nn(h_ref[rows, :], wg_ref[...])
    done(4)
    ready(4, 6, 7, 8)
    for i, rows in reversed(list(enumerate(ROWS))):
        weights = masked(nt(q_ref[rows, :], k_ref[...]), rows, cols_ref, line_ref).astype(bf16)
        p_ref[rows, :] = weights
        done(3, rows)
        retained = nn(weights, v_ref[...])
        inverse = lax.rsqrt(
            jnp.sum(retained * retained, axis=-1, keepdims=True) * (1.0 / VAL) + group_eps
        )
        inv_ref[rows, :] = jnp.broadcast_to(inverse, (TILE, 128))
        hat = retained * inverse
        hat_ref[rows, :] = hat
        done(5, rows)
        gate = gate_ref[rows, :]
        swish = gate * (1.0 / (1.0 + jnp.exp(-gate)))
        mixed = (hat * gain_ref[...] * swish).astype(bf16)
        mixed_ref[rows, :] = mixed
        put_halves(done, i, nt(mixed, wo_ref[...]), own_ref, other_ref, 8, 9)
    done(6)
    done(7)


def retention(*operands):
    shape = jax.ShapeDtypeStruct
    return in_vmem(
        retention_kernel,
        "retention",
        [
            shape((WIDTH, KEY), bf16),
            shape((WIDTH, KEY), bf16),
            shape((WIDTH, LANES), bf16),
            shape((WIDTH, WIDTH), bf16),
            shape((WIDTH, LANES), f32),
            shape((WIDTH, LANES), f32),
            shape((WIDTH, 128), f32),
            shape((WIDTH, LANES), bf16),
            shape((WIDTH // 2, WIDTH), f32),
            shape((WIDTH // 2, WIDTH), bf16),
        ],
        [],
        *operands,
    )


def feed_kernel(
    ready, done, h_ref, w1_ref, w2_ref, cot_ref, w3_ref,
    hidden_ref, gate_ref, up_ref, own_ref, other_ref,
):
    for i, rows in reversed(list(enumerate(ROWS))):
        ready(0, 1)
        pre_gate = nn(h_ref[rows, :], w1_ref[...])
        ready(2)
        pre_up = nn(h_ref[rows, :], w2_ref[...])
        ready(3, 4)
        grad_hidden = nn(cot_ref[rows, :], w3_ref[...])
        cumulative = 0.5 * (1.0 + lax.erf(pre_gate * (1.0 / math.sqrt(2.0))))
        density = jnp.exp(-0.5 * pre_gate * pre_gate) * (1.0 / math.sqrt(2.0 * math.pi))
        gelu_gate = pre_gate * cumulative
        hidden_ref[rows, :] = (gelu_gate * pre_up).astype(bf16)
        grad_gate = (grad_hidden * pre_up * (cumulative + pre_gate * density)).astype(bf16)
        grad_up = (grad_hidden * gelu_gate).astype(bf16)
        gate_ref[rows, :] = grad_gate
        up_ref[rows, :] = grad_up
        for k in range(3):
            done(k, rows)
        part = nt(grad_gate, w1_ref[...]) + nt(grad_up, w2_ref[...])
        put_halves(done, i, part, own_ref, other_ref, 3, 4)


def feed(*operands):
    shape = jax.ShapeDtypeStruct
    return in_vmem(
        feed_kernel,
        "feed_forward",
        [shape((WIDTH, LANES), bf16)] * 3
        + [shape((WIDTH // 2, WIDTH), f32), shape((WIDTH // 2, WIDTH), bf16)],
        [],
        *operands,
    )


def early_kernel(
    ready, done, h_ref, gate_ref, up_ref, cot_ref, hidden_ref, w3_ref, out_ref, own_ref, other_ref
):
    for j, (left, right) in enumerate(
        ((h_ref, gate_ref), (h_ref, up_ref), (cot_ref, hidden_ref))
    ):
        ready(*((0, 1), (2,), (3, 4))[j])
        columns = pl.ds(VAL * j, VAL)
        for i, at in enumerate(ROWS):
            part = tn(left[:, at], right[...]).astype(bf16)[:, :VAL]
            out_ref[:, i, :, columns] = part.reshape(16, BLOCK, VAL)
    out_ref[:, :, :, 3 * VAL : EARLY] = jnp.zeros((16, 2, BLOCK, EARLY - 3 * VAL), bf16)
    done(0)
    ready(5)
    for i, rows in reversed(list(enumerate(ROWS))):
        put_halves(done, i, nt(hidden_ref[rows, :], w3_ref[...]), own_ref, other_ref, 1, 2)


def early_grads(*operands):
    shape = jax.ShapeDtypeStruct
    return in_vmem(
        early_kernel,
        "feed_forward_grads",
        [
            shape((16, 2, BLOCK, EARLY), bf16),
            shape((WIDTH // 2, WIDTH), f32),
            shape((WIDTH // 2, WIDTH), bf16),
        ],
        [],
        *operands,
    )


def back_gate_kernel(
    ready, done, grad_ref, w_ref, gate_ref, hat_ref, inv_ref, gain_ref, gate_out, ret_out, gain_out
):
    total = jnp.zeros((1, LANES), f32)
    for rows in ROWS:
        ready(0, 1)
        grad_mixed = nn(grad_ref[rows, :], w_ref[...])
        ready(2, 3, 4, 5)
        gain = gain_ref[...]
        gate, hat, inverse = gate_ref[rows, :], hat_ref[rows, :], inv_ref[rows, 0:1]
        sig = 1.0 / (1.0 + jnp.exp(-gate))
        swish = gate * sig
        grad_grouped = grad_mixed * swish
        gate_out[rows, :] = (
            grad_mixed * (hat * gain) * (sig + swish * (1.0 - sig))
        ).astype(bf16)
        done(0, rows)
        total += jnp.sum(grad_grouped * hat, axis=0, keepdims=True)
        grad_hat = grad_grouped * gain
        inner = jnp.sum(grad_hat * hat, axis=-1, keepdims=True) * (1.0 / VAL)
        ret_out[rows, :] = (inverse * (grad_hat - hat * inner)).astype(bf16)
        done(1, rows)
    gain_out[...] = total
    done(2)


def back_gate(*operands):
    shape = jax.ShapeDtypeStruct
    return in_vmem(
        back_gate_kernel,
        "gate_backward",
        [shape((WIDTH, LANES), bf16)] * 2 + [shape((1, LANES), f32)],
        [],
        *operands,
    )


def back_scores_kernel(
    ready, done, ret_ref, v_ref, cols_ref, line_ref, k_ref, turn_ref, p_ref, q_ref,
    q_out, k_out, v_out, scores,
):
    half = KEY // 2
    ready(0, 1, 2, 3)
    for rows in ROWS:
        part = masked(nt(ret_ref[rows, :], v_ref[...]), rows, cols_ref, line_ref).astype(bf16)
        scores[rows, :] = part
        ready(4, 5)
        turned = nn(part, k_ref[...])
        first, second = turn(
            turned[:, :half], turned[:, half:], turn_ref[rows, :half], -turn_ref[rows, half:]
        )
        q_out[rows, 0:half] = first.astype(bf16)
        q_out[rows, half:KEY] = second.astype(bf16)
    done(0)
    ready(6, 7)
    for rows in ROWS:
        v_out[rows, :] = tn(p_ref[:, rows], ret_ref[...]).astype(bf16)
        done(2, rows)
    for rows in ROWS:
        turned = tn(scores[:, rows], q_ref[...])
        first, second = turn(
            turned[:, :half], turned[:, half:], turn_ref[rows, :half], -turn_ref[rows, half:]
        )
        k_out[rows, 0:half] = first.astype(bf16)
        k_out[rows, half:KEY] = second.astype(bf16)
    done(1)


def back_scores(*operands):
    shape = jax.ShapeDtypeStruct
    return in_vmem(
        back_scores_kernel,
        "scores_backward",
        [shape((WIDTH, KEY), bf16)] * 2 + [shape((WIDTH, LANES), bf16)],
        [pltpu.VMEM((WIDTH, WIDTH), bf16)],
        *operands,
    )


def late_kernel(
    ready, done, grad_ref, mixed_ref, h_ref, gate_ref, v_ref, ride_ref, q_ref, k_ref, out_ref
):
    ready(0, 1)
    for rows in ROWS:
        part = tn(grad_ref[:, rows], mixed_ref[...]).astype(bf16)
        out_ref[rows, 2 * KEY + 2 * VAL : 2 * KEY + 3 * VAL] = part[:, :VAL]
    ready(2, 3)
    for rows in ROWS:
        part = tn(h_ref[:, rows], gate_ref[...]).astype(bf16)
        out_ref[rows, 2 * KEY + VAL : 2 * KEY + 2 * VAL] = part[:, :VAL]
    ready(4, 5)
    for rows in ROWS:
        part = tn(h_ref[:, rows], v_ref[...]).astype(bf16)
        out_ref[rows, 2 * KEY : 2 * KEY + VAL] = part[:, :VAL]
        out_ref[rows, 2 * KEY + 3 * VAL : LATE] = ride_ref[rows, : LATE - 2 * KEY - 3 * VAL]
    ready(6, 7)
    for rows in ROWS:
        left = h_ref[:, rows]
        out_ref[rows, 0:KEY] = tn(left, q_ref[...]).astype(bf16)
        out_ref[rows, KEY : 2 * KEY] = (tn(left, k_ref[...]) * KEY**-0.5).astype(bf16)
    done(0)


def late_grads(*operands):
    return in_vmem(
        late_kernel,
        "retention_grads",
        [jax.ShapeDtypeStruct((WIDTH, LATE), bf16)],
        [],
        *operands,
    )[0]


def input_kernel(
    ready, done, gate_ref, wg_ref, v_ref, wv_ref, q_ref, k_ref, wqk_ref, own_ref, other_ref
):
    for i, rows in reversed(list(enumerate(ROWS))):
        ready(0, 1)
        part = nt(gate_ref[rows, :], wg_ref[...])
        ready(2, 3)
        part += nt(v_ref[rows, :], wv_ref[...])
        ready(4, 5, 6)
        part += nt(q_ref[rows, :], wqk_ref[:, 0:KEY])
        part += nt(k_ref[rows, :], wqk_ref[:, KEY : 2 * KEY]) * KEY**-0.5
        put_halves(done, i, part, own_ref, other_ref, 0, 1)


def input_parts(*operands):
    shape = jax.ShapeDtypeStruct
    return in_vmem(
        input_kernel,
        "input_grad_parts",
        [shape((WIDTH // 2, WIDTH), f32), shape((WIDTH // 2, WIDTH), bf16)],
        [],
        *operands,
    )


def iterate_kernel(
    chunk_ref, near_ref, far_ref, out_ref, vector_ref, first_ref, whole, gram, high, low, shifted, rest, prod, prod_b, own, own_b
):
    tiles = WIDTH // NS_TILE
    at = [pl.ds(NS_TILE * i, NS_TILE) for i in range(tiles)]
    eye = (
        lax.broadcasted_iota(jnp.int32, (NS_TILE, NS_TILE), 0)
        == lax.broadcasted_iota(jnp.int32, (NS_TILE, NS_TILE), 1)
    ).astype(f32)
    keep = lax.broadcasted_iota(jnp.int32, (WIDTH, 128), 1) < VAL - 384
    riders = jnp.zeros((WIDTH, 128), f32)
    for p in range(4):
        source = near_ref if p < 2 else far_ref
        piece = source[:, p % 2].reshape(WIDTH, LANES)
        whole[p, :, 0:384] = piece[:, 0:384]
        whole[p, :, 384:512] = jnp.where(keep, piece[:, 384:512], jnp.zeros((), bf16))
        ride = piece[:, 384:512].astype(f32)
        riders += ride
        lines = ride.T
        vector_ref[2 + p : 3 + p, :] = lines[50:51, :] + lines[53:54, :]
    lines = riders.T
    vector_ref[0:2, :] = lines[48:50, :] + lines[51:53, :]
    vector_ref[6:8, :] = jnp.zeros((2, WIDTH), f32)
    first_ref[...] = jnp.sum(riders.reshape(WIDTH // BLOCK, BLOCK, 128), axis=0)

    trace = jnp.float32(0.0)
    for i in range(tiles):
        for j in range(i, tiles):
            block = jnp.zeros((NS_TILE, NS_TILE), f32)
            for p in range(4):
                block += nt(whole[p, at[i], :], whole[p, at[j], :])
            gram[at[i], at[j]] = block
            if i < j:
                gram[at[j], at[i]] = block.T
            if i == j:
                trace += jnp.sum(block * eye)
    inverse = 1.0 / (jnp.sqrt(trace) + 1e-07)
    for q in range(4):

        @pl.when(chunk_ref[0] == q)
        def _():
            own[...] = whole[0, :, 128 * q : 128 * (q + 1)].astype(f32) * inverse

    def store(i, j, block, mean):
        gram[at[i], at[j]] = block
        top = block.astype(bf16)
        high[at[i], at[j]] = top
        low[at[i], at[j]] = (block - top.astype(f32)).astype(bf16)
        if i == j:
            top = (block - mean * eye).astype(bf16)
        shifted[at[i], at[j]] = top

    mean = trace * inverse * inverse * (1.0 / WIDTH)
    for i in range(tiles):
        for j in range(tiles):
            store(i, j, gram[at[i], at[j]] * (inverse * inverse), mean)

    def advance(mean):
        level = ns_second * mean + ns_third * mean * mean
        alpha = ns_first + level
        for i in range(tiles):
            for j in range(i, tiles):
                block = (ns_second + 2.0 * ns_third * mean) * gram[at[i], at[j]] + ns_third * nn(
                    shifted[at[i], :], shifted[:, at[j]]
                )
                if i == j:
                    block -= (ns_third * mean * mean + level) * eye
                block = block.astype(bf16)
                rest[at[i], at[j]] = block
                if i < j:
                    rest[at[j], at[i]] = block.T
        values = own[...]
        top = values.astype(bf16)
        own_b[:, 0:128] = top
        own_b[:, 128:256] = (values - top.astype(f32)).astype(bf16)
        for i in range(tiles):
            moved = nn(rest[at[i], :], own_b[...])
            own[at[i], :] = alpha * own[at[i], :] + (moved[:, 0:128] + moved[:, 128:256])
        return alpha

    def turn(_, mean):
        alpha = advance(mean)
        for i in range(tiles):
            for j in range(tiles):
                block = nn(high[at[i], :], rest[:, at[j]]) + nn(low[at[i], :], rest[:, at[j]])
                prod[at[i], at[j]] = block
                prod_b[at[i], at[j]] = block.astype(bf16)
        trace = jnp.float32(0.0)
        for i in range(tiles):
            for j in range(tiles):
                block = alpha * prod[at[i], at[j]] + 0.5 * nn(rest[at[i], :], prod_b[:, at[j]])
                prod[at[i], at[j]] = block
                if i == j:
                    trace += jnp.sum(block * eye)
        later = alpha * alpha * mean + trace * (2.0 / WIDTH)
        for i in range(tiles):
            for j in range(tiles):
                block = (alpha * alpha) * gram[at[i], at[j]] + (
                    prod[at[i], at[j]] + prod[at[j], at[i]].T
                )
                store(i, j, block, later)
        return later

    advance(lax.fori_loop(0, NS_ITERS - 1, turn, mean))
    out_ref[...] = own[...].astype(bf16)


def orthogonal(chunk, near, far):
    square = (WIDTH, WIDTH)
    return pl.pallas_call(
        iterate_kernel,
        out_shape=[
            jax.ShapeDtypeStruct((WIDTH, 128), bf16),
            jax.ShapeDtypeStruct((8, WIDTH), f32),
            jax.ShapeDtypeStruct((BLOCK, 128), f32),
        ],
        in_specs=[pl.BlockSpec(memory_space=pltpu.SMEM)]
        + [pl.BlockSpec(memory_space=pltpu.VMEM)] * 2,
        out_specs=[pl.BlockSpec(memory_space=pltpu.VMEM)] * 3,
        scratch_shapes=[
            pltpu.VMEM((4, WIDTH, LANES), bf16),
            pltpu.VMEM(square, f32),
            pltpu.VMEM(square, bf16),
            pltpu.VMEM(square, bf16),
            pltpu.VMEM(square, bf16),
            pltpu.VMEM(square, bf16),
            pltpu.VMEM(square, f32),
            pltpu.VMEM(square, bf16),
            pltpu.VMEM((WIDTH, 128), f32),
            pltpu.VMEM((WIDTH, 256), bf16),
        ],
        compiler_params=pltpu.CompilerParams(vmem_limit_bytes=48 * 2**20),
        cost_estimate=pl.CostEstimate(
            flops=42 * 10**9, bytes_accessed=5 * 2**20, transcendentals=0
        ),
        name="orthogonalize",
    )(chunk, near, far)


def shards(
    tokens,
    cotangent,
    qk_w,
    vg_w,
    mlp_w,
    out_w,
    qk_mom,
    vg_mom,
    mlp_mom,
    out_mom,
    norm_params,
    norm_moment,
    norm_second,
    decay_gap,
    seq_length,
    seq_group,
):
    rows, width = tokens.shape
    slots = 4 * rows
    groups = 32
    value_width = 4 * VAL
    key_scale = KEY ** (-0.5)
    dp_index = lax.axis_index(DP)
    tensor_index = lax.axis_index(TENSOR)
    chunk_index = lax.axis_index(("y_lo", "z_hi"))

    gain_one = norm_params[0:width]
    shift_one = norm_params[width : 2 * width]
    group_gain = jnp.pad(
        lax.dynamic_slice_in_dim(norm_params, 2 * width + tensor_index * VAL, VAL),
        (0, LANES - VAL),
    )
    gain_two = norm_params[2 * width + value_width : 3 * width + value_width]
    shift_two = norm_params[3 * width + value_width : 4 * width + value_width]

    out_rows = jnp.swapaxes(out_w, 1, 2)
    first_half = lax.axis_index("y_lo") == 0

    def weight_rows(parts):
        packed = jnp.concatenate(parts, axis=1).astype(bf16)
        far = swap(packed, "y_lo")
        pair = jnp.stack([jnp.where(first_half, packed, far), jnp.where(first_half, far, packed)])
        return pair

    def weight_gather(pair):
        return lax.all_gather(pair, PLANE, axis=1, tiled=True).reshape(width, -1)

    pair_ret = weight_rows(
        [
            pairs_apart(qk_w[0]),
            pairs_apart(qk_w[1]),
            widen(vg_w[0]),
            widen(vg_w[1]),
            widen(out_rows[0]),
        ]
    )
    tokens_first, pair_ret = together(tokens, pair_ret)
    gathered = weight_gather(pair_ret)
    w_qk, w_v, w_g, w_o = ((gathered, LANES * i, LANES) for i in range(4))
    pair_ff = weight_rows([widen(mlp_w[0]), widen(mlp_w[1]), widen(out_rows[1])])

    whole_tokens = jnp.concatenate(tensor_gather(tokens_first), axis=0)
    order = jnp.stack([tensor_index, tensor_index ^ 2, tensor_index ^ 1, tensor_index ^ 3])
    place = (order[:, None] * rows + jnp.arange(rows, dtype=jnp.int32)[None, :]).reshape(slots)

    freqs = 1.0 / 10000.0 ** np.linspace(0.0, 1.0, KEY // 2)
    angles = np.arange(slots)[:, None] * freqs[None, :]
    tables = jnp.asarray(
        np.concatenate([np.cos(angles), np.sin(angles)], axis=1).astype(np.float32)
    ).reshape(4, rows, KEY)
    turned = tables[order].reshape(slots, KEY)

    labels = sequence_labels(seq_length, seq_group, dp_index, place)
    log_decay = jnp.log1p(-decay_gap[0])
    away = (place - slots // 2).astype(f32) * log_decay
    label_place = [labels.astype(f32), place.astype(f32)]
    columns = jnp.pad(jnp.stack(label_place + [jnp.exp(away)], axis=1), ((0, 0), (0, 125)))
    line = jnp.pad(jnp.stack(label_place + [jnp.exp(-away)], axis=0), ((0, 5), (0, 0)))
    gain_line = group_gain[None, :]

    hat_one, _ = normalize(whole_tokens.astype(f32))
    whole_one = (hat_one * gain_one + shift_one).astype(bf16)
    prepared = (whole_one, turned, columns, line)
    cot_first, (whole_one, turned, columns, line) = together(cotangent, prepared)
    whole_cot = tensor_gather(cot_first)
    (gain_line, pair_ff), whole_cot = together((gain_line, pair_ff), whole_cot)
    whole_cot = [(part, 0, width) for part in whole_cot]
    gathered_ff = weight_gather(pair_ff)
    w_1, w_2, w_3 = ((gathered_ff, LANES * i, LANES) for i in range(3))
    query, keys, values, weights, gate, hat_group, inv_group, mixed, own, other = retention(
        whole_one, w_qk, w_v, w_g, w_o, turned, columns, line, gain_line
    )
    near, far = tensor_sum(own, other)
    middle = tokens.astype(f32) + near + far.astype(f32)
    hat_two, inv_two = normalize(middle)
    whole_two = tensor_gather((hat_two * gain_two + shift_two).astype(bf16))
    hidden, grad_gate, grad_up, own, other = feed(whole_two, w_1, w_2, whole_cot, w_3)
    near, far = tensor_sum(own, other)
    early, out_own, out_other = early_grads(whole_two, grad_gate, grad_up, whole_cot, hidden, w_3)
    far, out_other = together(far, out_other)
    grad_normed_two = near + far.astype(f32)
    grad_middle = cotangent.astype(f32) + norm_back(grad_normed_two, gain_two, hat_two, inv_two)
    grad_first = grad_middle.astype(bf16)
    grad_far, grad_core = swap(grad_first, "y_hi"), swap(grad_first, "core")
    out_near, out_far = half_sum(out_own, out_other)
    grad_far, out_far = together(grad_far, out_far)
    grad_one = [grad_first, grad_far, grad_core, swap(grad_far, "core")]
    result = (middle + out_near + swap(out_far, "y_hi").astype(f32)).astype(bf16)

    early_in = lax.all_to_all(early, PLANE, split_axis=0, concat_axis=0, tiled=True)
    early_halves = jnp.sum(early_in.astype(f32), axis=0)
    early_far = swap(
        jnp.where(first_half, early_halves[1], early_halves[0]).astype(bf16), "y_lo"
    )
    gain_two_grad = jnp.sum(grad_normed_two * hat_two, axis=0)
    shift_two_grad = jnp.sum(grad_normed_two, axis=0)

    grad_gate_ret, grad_retained, group_gain_grad = back_gate(
        grad_one, w_o, gate, hat_group, inv_group, gain_line
    )
    grad_query, grad_key, grad_values = back_scores(
        grad_retained, values, columns, line, keys, turned, weights, query
    )
    own, other = input_parts(
        grad_gate_ret, w_g, grad_values, w_v, grad_query, grad_key, w_qk
    )
    other, grad_values = together(other, grad_values)
    near, far = half_sum(own, other)
    small = jnp.stack(
        [gain_two_grad, shift_two_grad, jnp.pad(group_gain_grad[0], (0, width - LANES))], axis=1
    )
    small_high, small_low = split(small)
    riders = jnp.pad(
        jnp.concatenate([small_high, small_low], axis=1), ((0, 0), (0, 128 - 6))
    )
    late = late_grads(
        grad_one, mixed, whole_one, grad_gate_ret, grad_values, riders, grad_query, grad_key
    )
    (result, far), late = together((result, far), late)
    grad_normed_one = near + swap(far, "y_hi").astype(f32)
    late_in = lax.all_to_all(
        late.reshape(groups, BLOCK, -1), DP, split_axis=0, concat_axis=0, tiled=True
    )
    own_hat, own_inv = normalize(tokens.astype(f32))
    gain_one_grad = jnp.sum(grad_normed_one * own_hat, axis=0)
    shift_one_grad = jnp.sum(grad_normed_one, axis=0)
    input_grad = grad_middle + norm_back(grad_normed_one, gain_one, own_hat, own_inv)
    gain_one_grad, early_far = together(gain_one_grad, early_far)
    early_sum = jnp.where(first_half, early_halves[0], early_halves[1]) + early_far.astype(f32)

    late_sum = jnp.sum(late_in.astype(f32), axis=0)
    first_value = 2 * KEY
    at = [first_value + VAL * i for i in range(4)]
    small_sum = late_sum[:, at[3] : at[3] + 6]
    small_sum = small_sum[:, :3] + small_sum[:, 3:]

    grad_qk = pairs_together(jnp.stack([late_sum[:, 0:256], late_sum[:, 256:512]]))
    grad_vg = jnp.stack([late_sum[:, at[0] : at[1]], late_sum[:, at[1] : at[2]]])
    grad_mlp = jnp.stack([early_sum[:, 0:VAL], early_sum[:, VAL : 2 * VAL]])
    grad_out_t = jnp.stack([late_sum[:, at[2] : at[3]], early_sum[:, 2 * VAL : 3 * VAL]])
    mom_qk = muon_beta * qk_mom + grad_qk
    mom_vg = muon_beta * vg_mom + grad_vg
    mom_mlp = muon_beta * mlp_mom + grad_mlp
    mom_out = muon_beta * out_mom + jnp.swapaxes(grad_out_t, 1, 2)

    piece_high, piece_low = split(small_sum)
    first_norm = jnp.concatenate([gain_one_grad, shift_one_grad]).astype(bf16)
    extra = jnp.pad(
        jnp.concatenate([piece_high, piece_low, first_norm.reshape(BLOCK, 64)], axis=1),
        ((0, 0), (VAL, LANES - VAL - 70)),
    )
    stacked = (
        jnp.concatenate(
            [widen(mom_qk), widen(mom_vg), widen(mom_mlp), widen(jnp.swapaxes(mom_out, 1, 2))],
            axis=0,
        ).astype(bf16)
        + extra[None]
    )
    both = jnp.stack([stacked, swap(stacked, "y_hi")], axis=1)
    spread = jnp.broadcast_to(both[None], (4,) + both.shape).reshape((groups,) + both.shape[1:])
    arrived = lax.all_to_all(spread, DP, split_axis=0, concat_axis=0, tiled=True)
    far = swap(arrived, "core")
    own, vectors, first_total = orthogonal(
        jnp.reshape(chunk_index, (1,)).astype(jnp.int32), arrived, far
    )
    returned = lax.all_to_all(
        own.reshape(groups, BLOCK, 128), DP, split_axis=0, concat_axis=0, tiled=True
    ).astype(f32)
    returned = jnp.concatenate([returned[8 * i : 8 * i + 8] for i in range(4)], axis=2)

    shrink = 1.0 - muon_rate * decay_rate
    square_scale = 0.2 * math.sqrt(width)
    wide_scale = 0.2 * math.sqrt(max(width, value_width))
    new_qk = qk_w * shrink - (muon_rate * square_scale) * returned[0:2, :, :KEY]
    new_vg = vg_w * shrink - (muon_rate * wide_scale) * returned[2:4, :, :VAL]
    new_mlp = mlp_w * shrink - (muon_rate * wide_scale) * returned[4:6, :, :VAL]
    new_out = out_w * shrink - (muon_rate * wide_scale) * jnp.swapaxes(returned[6:8, :, :VAL], 1, 2)

    first_total = first_total[:, 54:118].reshape(2 * width)
    group_parts = vectors[2:6, :VAL]
    which = jnp.arange(4, dtype=jnp.int32)[:, None] == order[None, :]
    group_whole = jnp.sum(
        jnp.where(which[:, :, None], group_parts[None], 0.0), axis=1
    ).reshape(value_width)
    small_total = jnp.concatenate(
        [first_total, group_whole, vectors[0], vectors[1]]
    )
    moment_new = beta_first * norm_moment + (1.0 - beta_first) * small_total
    second_new = beta_second * norm_second + (1.0 - beta_second) * small_total * small_total
    params_new = norm_params - adam_rate * (moment_new / (1.0 - beta_first**OPT_STEP)) / (
        jnp.sqrt(second_new / (1.0 - beta_second**OPT_STEP)) + adam_eps
    )
    return (
        result,
        input_grad,
        mom_qk,
        mom_vg,
        mom_mlp,
        mom_out,
        new_qk,
        new_vg,
        new_mlp,
        new_out,
        moment_new,
        second_new,
        params_new,
    )


def solution(mesh):
    fine = Mesh(np.asarray(mesh.devices).reshape(SIZES), AXES)
    by_rows = P(DP + TENSOR, None)
    by_columns = P(None, DP, TENSOR)
    by_out = P(None, TENSOR, DP)
    return jax.shard_map(
        shards,
        mesh=fine,
        in_specs=(
            by_rows,
            by_rows,
            by_columns,
            by_columns,
            by_columns,
            by_out,
            by_columns,
            by_columns,
            by_columns,
            by_out,
            P(),
            P(),
            P(),
            P(TENSOR),
            P(),
            P(),
        ),
        out_specs=(
            by_rows,
            by_rows,
            by_columns,
            by_columns,
            by_columns,
            by_out,
            by_columns,
            by_columns,
            by_columns,
            by_out,
            P(),
            P(),
            P(),
        ),
        check_vma=False,
    )
```

```python
import math

import jax
import jax.numpy as jnp
import numpy as np
from jax import lax
from jax.experimental import pallas as pl
from jax.experimental.pallas import tpu as pltpu
from jax.sharding import Mesh
from jax.sharding import PartitionSpec as P

HEADS = 4
NS_ITERS = 5
OPT_STEP = 10
KEY = 256
VAL = 432
LANES = 512
BLOCK = 32

norm_eps = 1e-05
group_eps = 0.01
ns_first = 3.4445
ns_second = -4.775
ns_third = 2.0315
muon_rate = 0.15
muon_beta = 0.95
decay_rate = 0.01
adam_rate = 0.6
beta_first = 0.9
beta_second = 0.95
adam_eps = 1e-08

AXES = ("y_lo", "z_hi", "z_lo", "x", "y_hi", "core")
SIZES = (2, 2, 2, 4, 2, 2)
DP = ("y_lo", "z_hi", "z_lo", "x")
PLANE = ("z_hi", "z_lo", "x")
TENSOR = ("y_hi", "core")
bf16 = jnp.bfloat16
f32 = jnp.float32


def swap(values, axis):
    return lax.ppermute(values, axis, [(0, 1), (1, 0)])


def dot(left, right, dims):
    return lax.dot_general(left, right, (dims, ((), ())), preferred_element_type=f32)


def nn(left, right):
    return dot(left, right, ((1,), (0,)))


def nt(left, right):
    return dot(left, right, ((1,), (1,)))


def tn(left, right):
    return dot(left, right, ((0,), (0,)))


def split(values):
    high = lax.reduce_precision(values, 8, 7)
    return high.astype(bf16), (values - high).astype(bf16)


def widen(values):
    return jnp.pad(values, ((0, 0),) * (values.ndim - 1) + ((0, LANES - values.shape[-1]),))


def tensor_gather(own):
    far = swap(own, "y_hi")
    return [own, far, swap(own, "core"), swap(far, "core")]


def half_sum(own, other):
    half = own.shape[0] // 2
    arrived = swap(other, "core")
    far = (own[half:] + arrived[half:].astype(f32)).astype(bf16)
    return own[:half] + arrived[:half].astype(f32), far


def tensor_sum(own, other):
    near, far = half_sum(own, other)
    return near, swap(far, "y_hi")


def together(first, second):
    return lax.optimization_barrier((first, second))


def normalize(values):
    centre = values - jnp.mean(values, axis=-1, keepdims=True)
    spread = lax.rsqrt(jnp.mean(centre * centre, axis=-1, keepdims=True) + norm_eps)
    return centre * spread, spread


def norm_back(grad_out, gain, normed, spread):
    grad_normed = grad_out * gain
    return spread * (
        grad_normed
        - jnp.mean(grad_normed, axis=-1, keepdims=True)
        - normed * jnp.mean(grad_normed * normed, axis=-1, keepdims=True)
    )


def pairs_apart(values):
    shape = values.shape
    return jnp.swapaxes(values.reshape(shape[:-1] + (KEY // 2, 2)), -1, -2).reshape(shape)


def pairs_together(values):
    shape = values.shape
    return jnp.swapaxes(values.reshape(shape[:-1] + (2, KEY // 2)), -1, -2).reshape(shape)


def sequence_labels(seq_length, seq_group, group, place):
    mine = seq_group == group
    lengths = jnp.where(mine, seq_length, 0)
    ends = jnp.cumsum(lengths, dtype=jnp.int32)
    starts = ends - lengths
    inside = mine[None, :] & (place[:, None] >= starts[None, :]) & (place[:, None] < ends[None, :])
    number = jnp.arange(1, seq_length.shape[0] + 1, dtype=jnp.int32)
    return jnp.sum(jnp.where(inside, number[None, :], 0), axis=1, dtype=jnp.int32)


WIDTH = 1024
TILE = WIDTH // 2
EARLY = 1408
LATE = 1920
NS_TILE = 256


ROWS = [pl.ds(TILE * i, TILE) for i in range(WIDTH // TILE)]


STORES = 12


def in_vmem(kernel, name, out_shape, scratch, *operands):
    arrays, pieces, local = [], [], []
    for a in operands:
        parts = a if isinstance(a, list) else [a]
        top, piece = 0, []
        for part in parts:
            array, first, columns, *free = (
                part if isinstance(part, tuple) else (part, 0, part.shape[1])
            )
            whole = columns == array.shape[1]
            piece.append((len(arrays), None if whole else (first, columns), top, array.shape[0]))
            fixed = not free and (not isinstance(a, list) or isinstance(part, tuple))
            arrays.append(pltpu.with_memory_space_constraint(array, pltpu.HBM) if fixed else array)
            top += array.shape[0]
        pieces.append(piece)
        local.append(pltpu.VMEM((top, columns), array.dtype))
    n_in, n_out, n_local = len(arrays), len(out_shape), len(local)

    def body(*refs):
        ins, outs = refs[:n_in], refs[n_in : n_in + n_out]
        refs = refs[n_in + n_out :]
        local_in, local_out = refs[:n_local], refs[n_local : n_local + n_out]
        sem_in, sem_out = refs[n_local + n_out : n_local + n_out + 2]
        loads = []
        for i, piece in enumerate(pieces):
            loads.append([])
            for which, cut, top, rows in piece:
                source = ins[which] if cut is None else ins[which].at[:, pl.ds(*cut)]
                target = local_in[i] if len(piece) == 1 else local_in[i].at[pl.ds(top, rows), :]
                loads[i].append(pltpu.make_async_copy(source, target, sem_in.at[which]))
                loads[i][-1].start()
        pending = set(range(n_local))
        stores = []

        def ready(*which):
            for i in which:
                if i in pending:
                    pending.remove(i)
                    for load in loads[i]:
                        load.wait()

        def done(i, *index):
            source, target = local_out[i], outs[i]
            if index:
                source, target = source.at[index], target.at[index]
            stores.append(pltpu.make_async_copy(source, target, sem_out.at[len(stores)]))
            stores[-1].start()

        kernel(ready, done, *local_in, *local_out, *refs[n_local + n_out + 2 :])
        ready(*range(n_local))
        for store in stores:
            store.wait()

    local += [pltpu.VMEM(a.shape, a.dtype) for a in out_shape]
    held = sum(math.prod(a.shape) * jnp.dtype(a.dtype).itemsize for a in local)
    return pl.pallas_call(
        body,
        out_shape=[pltpu.HBM(a.shape, a.dtype) for a in out_shape],
        in_specs=[pl.BlockSpec(memory_space=pl.ANY)] * n_in,
        out_specs=[pl.BlockSpec(memory_space=pltpu.HBM)] * n_out,
        scratch_shapes=local
        + [pltpu.SemaphoreType.DMA((n_in,)), pltpu.SemaphoreType.DMA((STORES,))]
        + scratch,
        compiler_params=pltpu.CompilerParams(vmem_limit_bytes=held + 14 * 2**20),
        cost_estimate=pl.CostEstimate(flops=1, bytes_accessed=1, transcendentals=0),
        name=name,
    )(*arrays)


def put_halves(done, i, part, own_ref, other_ref, own, other):
    if i == 0:
        own_ref[...] = part
        done(own)
    else:
        other_ref[...] = part.astype(bf16)
        done(other)


def turn(first, second, cos_table, sin_table):
    return first * cos_table - second * sin_table, second * cos_table + first * sin_table


def masked(scores, rows, cols_ref, line_ref):
    label, place = cols_ref[rows, 0:1], cols_ref[rows, 1:2]
    linked = (label == line_ref[0:1, :]) & (label > 0.0) & (place >= line_ref[1:2, :])
    return jnp.where(linked, scores * (cols_ref[rows, 2:3] * line_ref[2:3, :]), 0.0)


def retention_kernel(
    ready, done, h_ref, wqk_ref, wv_ref, wg_ref, wo_ref, turn_ref, cols_ref, line_ref, gain_ref,
    q_ref, k_ref, v_ref, p_ref, gate_ref, hat_ref, inv_ref, mixed_ref, own_ref, other_ref,
):
    half = KEY // 2
    ready(0, 1, 5)
    for rows in ROWS:
        cos_table, sin_table = turn_ref[rows, :half], turn_ref[rows, half:]
        both = nn(h_ref[rows, :], wqk_ref[...])
        query, keys = both[:, :KEY], both[:, KEY:] * KEY**-0.5
        first, second = turn(query[:, :half], query[:, half:], cos_table, sin_table)
        q_ref[rows, 0:half] = first.astype(bf16)
        q_ref[rows, half:KEY] = second.astype(bf16)
        first, second = turn(keys[:, :half], keys[:, half:], cos_table, sin_table)
        k_ref[rows, 0:half] = first.astype(bf16)
        k_ref[rows, half:KEY] = second.astype(bf16)
    done(0)
    done(1)
    ready(2)
    for rows in ROWS:
        v_ref[rows, :] = nn(h_ref[rows, :], wv_ref[...]).astype(bf16)
    done(2)
    ready(3)
    for rows in ROWS:
        gate_ref[rows, :] = nn(h_ref[rows, :], wg_ref[...])
    done(4)
    ready(4, 6, 7, 8)
    for i, rows in reversed(list(enumerate(ROWS))):
        weights = masked(nt(q_ref[rows, :], k_ref[...]), rows, cols_ref, line_ref).astype(bf16)
        p_ref[rows, :] = weights
        done(3, rows)
        retained = nn(weights, v_ref[...])
        inverse = lax.rsqrt(
            jnp.sum(retained * retained, axis=-1, keepdims=True) * (1.0 / VAL) + group_eps
        )
        inv_ref[rows, :] = jnp.broadcast_to(inverse, (TILE, 128))
        hat = retained * inverse
        hat_ref[rows, :] = hat
        done(5, rows)
        gate = gate_ref[rows, :]
        swish = gate * (1.0 / (1.0 + jnp.exp(-gate)))
        mixed = (hat * gain_ref[...] * swish).astype(bf16)
        mixed_ref[rows, :] = mixed
        put_halves(done, i, nt(mixed, wo_ref[...]), own_ref, other_ref, 8, 9)
    done(6)
    done(7)


def retention(*operands):
    shape = jax.ShapeDtypeStruct
    return in_vmem(
        retention_kernel,
        "retention",
        [
            shape((WIDTH, KEY), bf16),
            shape((WIDTH, KEY), bf16),
            shape((WIDTH, LANES), bf16),
            shape((WIDTH, WIDTH), bf16),
            shape((WIDTH, LANES), f32),
            shape((WIDTH, LANES), f32),
            shape((WIDTH, 128), f32),
            shape((WIDTH, LANES), bf16),
            shape((WIDTH // 2, WIDTH), f32),
            shape((WIDTH // 2, WIDTH), bf16),
        ],
        [],
        *operands,
    )


def feed_kernel(
    ready, done, h_ref, w1_ref, w2_ref, cot_ref, w3_ref,
    hidden_ref, gate_ref, up_ref, own_ref, other_ref,
):
    for i, rows in reversed(list(enumerate(ROWS))):
        ready(0, 1)
        pre_gate = nn(h_ref[rows, :], w1_ref[...])
        ready(2)
        pre_up = nn(h_ref[rows, :], w2_ref[...])
        ready(3, 4)
        grad_hidden = nn(cot_ref[rows, :], w3_ref[...])
        cumulative = 0.5 * (1.0 + lax.erf(pre_gate * (1.0 / math.sqrt(2.0))))
        density = jnp.exp(-0.5 * pre_gate * pre_gate) * (1.0 / math.sqrt(2.0 * math.pi))
        gelu_gate = pre_gate * cumulative
        hidden_ref[rows, :] = (gelu_gate * pre_up).astype(bf16)
        grad_gate = (grad_hidden * pre_up * (cumulative + pre_gate * density)).astype(bf16)
        grad_up = (grad_hidden * gelu_gate).astype(bf16)
        gate_ref[rows, :] = grad_gate
        up_ref[rows, :] = grad_up
        for k in range(3):
            done(k, rows)
        part = nt(grad_gate, w1_ref[...]) + nt(grad_up, w2_ref[...])
        put_halves(done, i, part, own_ref, other_ref, 3, 4)


def feed(*operands):
    shape = jax.ShapeDtypeStruct
    return in_vmem(
        feed_kernel,
        "feed_forward",
        [shape((WIDTH, LANES), bf16)] * 3
        + [shape((WIDTH // 2, WIDTH), f32), shape((WIDTH // 2, WIDTH), bf16)],
        [],
        *operands,
    )


def early_kernel(
    ready, done, h_ref, gate_ref, up_ref, cot_ref, hidden_ref, w3_ref, out_ref, own_ref, other_ref
):
    for j, (left, right) in enumerate(
        ((h_ref, gate_ref), (h_ref, up_ref), (cot_ref, hidden_ref))
    ):
        ready(*((0, 1), (2,), (3, 4))[j])
        columns = pl.ds(VAL * j, VAL)
        for i, at in enumerate(ROWS):
            part = tn(left[:, at], right[...]).astype(bf16)[:, :VAL]
            out_ref[:, i, :, columns] = part.reshape(16, BLOCK, VAL)
    out_ref[:, :, :, 3 * VAL : EARLY] = jnp.zeros((16, 2, BLOCK, EARLY - 3 * VAL), bf16)
    done(0)
    ready(5)
    for i, rows in reversed(list(enumerate(ROWS))):
        put_halves(done, i, nt(hidden_ref[rows, :], w3_ref[...]), own_ref, other_ref, 1, 2)


def early_grads(*operands):
    shape = jax.ShapeDtypeStruct
    return in_vmem(
        early_kernel,
        "feed_forward_grads",
        [
            shape((16, 2, BLOCK, EARLY), bf16),
            shape((WIDTH // 2, WIDTH), f32),
            shape((WIDTH // 2, WIDTH), bf16),
        ],
        [],
        *operands,
    )


def back_gate_kernel(
    ready, done, grad_ref, w_ref, gate_ref, hat_ref, inv_ref, gain_ref, gate_out, ret_out, gain_out
):
    total = jnp.zeros((1, LANES), f32)
    for rows in ROWS:
        ready(0, 1)
        grad_mixed = nn(grad_ref[rows, :], w_ref[...])
        ready(2, 3, 4, 5)
        gain = gain_ref[...]
        gate, hat, inverse = gate_ref[rows, :], hat_ref[rows, :], inv_ref[rows, 0:1]
        sig = 1.0 / (1.0 + jnp.exp(-gate))
        swish = gate * sig
        grad_grouped = grad_mixed * swish
        gate_out[rows, :] = (
            grad_mixed * (hat * gain) * (sig + swish * (1.0 - sig))
        ).astype(bf16)
        done(0, rows)
        total += jnp.sum(grad_grouped * hat, axis=0, keepdims=True)
        grad_hat = grad_grouped * gain
        inner = jnp.sum(grad_hat * hat, axis=-1, keepdims=True) * (1.0 / VAL)
        ret_out[rows, :] = (inverse * (grad_hat - hat * inner)).astype(bf16)
        done(1, rows)
    gain_out[...] = total
    done(2)


def back_gate(*operands):
    shape = jax.ShapeDtypeStruct
    return in_vmem(
        back_gate_kernel,
        "gate_backward",
        [shape((WIDTH, LANES), bf16)] * 2 + [shape((1, LANES), f32)],
        [],
        *operands,
    )


def back_scores_kernel(
    ready, done, ret_ref, v_ref, cols_ref, line_ref, k_ref, turn_ref, p_ref, q_ref,
    q_out, k_out, v_out, scores,
):
    half = KEY // 2
    ready(0, 1, 2, 3)
    for rows in ROWS:
        part = masked(nt(ret_ref[rows, :], v_ref[...]), rows, cols_ref, line_ref).astype(bf16)
        scores[rows, :] = part
        ready(4, 5)
        turned = nn(part, k_ref[...])
        first, second = turn(
            turned[:, :half], turned[:, half:], turn_ref[rows, :half], -turn_ref[rows, half:]
        )
        q_out[rows, 0:half] = first.astype(bf16)
        q_out[rows, half:KEY] = second.astype(bf16)
    done(0)
    ready(6, 7)
    for rows in ROWS:
        v_out[rows, :] = tn(p_ref[:, rows], ret_ref[...]).astype(bf16)
        done(2, rows)
    for rows in ROWS:
        turned = tn(scores[:, rows], q_ref[...])
        first, second = turn(
            turned[:, :half], turned[:, half:], turn_ref[rows, :half], -turn_ref[rows, half:]
        )
        k_out[rows, 0:half] = first.astype(bf16)
        k_out[rows, half:KEY] = second.astype(bf16)
    done(1)


def back_scores(*operands):
    shape = jax.ShapeDtypeStruct
    return in_vmem(
        back_scores_kernel,
        "scores_backward",
        [shape((WIDTH, KEY), bf16)] * 2 + [shape((WIDTH, LANES), bf16)],
        [pltpu.VMEM((WIDTH, WIDTH), bf16)],
        *operands,
    )


def late_kernel(
    ready, done, grad_ref, mixed_ref, h_ref, gate_ref, v_ref, ride_ref, q_ref, k_ref, out_ref
):
    ready(0, 1)
    for rows in ROWS:
        part = tn(grad_ref[:, rows], mixed_ref[...]).astype(bf16)
        out_ref[rows, 2 * KEY + 2 * VAL : 2 * KEY + 3 * VAL] = part[:, :VAL]
    ready(2, 3)
    for rows in ROWS:
        part = tn(h_ref[:, rows], gate_ref[...]).astype(bf16)
        out_ref[rows, 2 * KEY + VAL : 2 * KEY + 2 * VAL] = part[:, :VAL]
    ready(4, 5)
    for rows in ROWS:
        part = tn(h_ref[:, rows], v_ref[...]).astype(bf16)
        out_ref[rows, 2 * KEY : 2 * KEY + VAL] = part[:, :VAL]
        out_ref[rows, 2 * KEY + 3 * VAL : LATE] = ride_ref[rows, : LATE - 2 * KEY - 3 * VAL]
    ready(6, 7)
    for rows in ROWS:
        left = h_ref[:, rows]
        out_ref[rows, 0:KEY] = tn(left, q_ref[...]).astype(bf16)
        out_ref[rows, KEY : 2 * KEY] = (tn(left, k_ref[...]) * KEY**-0.5).astype(bf16)
    done(0)


def late_grads(*operands):
    return in_vmem(
        late_kernel,
        "retention_grads",
        [jax.ShapeDtypeStruct((WIDTH, LATE), bf16)],
        [],
        *operands,
    )[0]


def input_kernel(
    ready, done, gate_ref, wg_ref, v_ref, wv_ref, q_ref, k_ref, wqk_ref, own_ref, other_ref
):
    for i, rows in reversed(list(enumerate(ROWS))):
        ready(0, 1)
        part = nt(gate_ref[rows, :], wg_ref[...])
        ready(2, 3)
        part += nt(v_ref[rows, :], wv_ref[...])
        ready(4, 5, 6)
        part += nt(q_ref[rows, :], wqk_ref[:, 0:KEY])
        part += nt(k_ref[rows, :], wqk_ref[:, KEY : 2 * KEY]) * KEY**-0.5
        put_halves(done, i, part, own_ref, other_ref, 0, 1)


def input_parts(*operands):
    shape = jax.ShapeDtypeStruct
    return in_vmem(
        input_kernel,
        "input_grad_parts",
        [shape((WIDTH // 2, WIDTH), f32), shape((WIDTH // 2, WIDTH), bf16)],
        [],
        *operands,
    )


def iterate_kernel(
    chunk_ref, near_ref, far_ref, out_ref, vector_ref, first_ref, whole, gram, high, low, shifted, rest, prod, prod_b, own, own_b
):
    tiles = WIDTH // NS_TILE
    at = [pl.ds(NS_TILE * i, NS_TILE) for i in range(tiles)]
    eye = (
        lax.broadcasted_iota(jnp.int32, (NS_TILE, NS_TILE), 0)
        == lax.broadcasted_iota(jnp.int32, (NS_TILE, NS_TILE), 1)
    ).astype(f32)
    keep = lax.broadcasted_iota(jnp.int32, (WIDTH, 128), 1) < VAL - 384
    riders = jnp.zeros((WIDTH, 128), f32)
    for p in range(4):
        source = near_ref if p < 2 else far_ref
        piece = source[:, p % 2].reshape(WIDTH, LANES)
        whole[p, :, 0:384] = piece[:, 0:384]
        whole[p, :, 384:512] = jnp.where(keep, piece[:, 384:512], jnp.zeros((), bf16))
        ride = piece[:, 384:512].astype(f32)
        riders += ride
        lines = ride.T
        vector_ref[2 + p : 3 + p, :] = lines[50:51, :] + lines[53:54, :]
    lines = riders.T
    vector_ref[0:2, :] = lines[48:50, :] + lines[51:53, :]
    vector_ref[6:8, :] = jnp.zeros((2, WIDTH), f32)
    first_ref[...] = jnp.sum(riders.reshape(WIDTH // BLOCK, BLOCK, 128), axis=0)

    trace = jnp.float32(0.0)
    for i in range(tiles):
        for j in range(i, tiles):
            block = jnp.zeros((NS_TILE, NS_TILE), f32)
            for p in range(4):
                block += nt(whole[p, at[i], :], whole[p, at[j], :])
            gram[at[i], at[j]] = block
            if i < j:
                gram[at[j], at[i]] = block.T
            if i == j:
                trace += jnp.sum(block * eye)
    inverse = 1.0 / (jnp.sqrt(trace) + 1e-07)
    for q in range(4):

        @pl.when(chunk_ref[0] == q)
        def _():
            own[...] = whole[0, :, 128 * q : 128 * (q + 1)].astype(f32) * inverse

    def store(i, j, block, mean):
        gram[at[i], at[j]] = block
        top = block.astype(bf16)
        high[at[i], at[j]] = top
        low[at[i], at[j]] = (block - top.astype(f32)).astype(bf16)
        if i == j:
            top = (block - mean * eye).astype(bf16)
        shifted[at[i], at[j]] = top

    mean = trace * inverse * inverse * (1.0 / WIDTH)
    for i in range(tiles):
        for j in range(tiles):
            store(i, j, gram[at[i], at[j]] * (inverse * inverse), mean)

    def advance(mean):
        level = ns_second * mean + ns_third * mean * mean
        alpha = ns_first + level
        for i in range(tiles):
            for j in range(i, tiles):
                block = (ns_second + 2.0 * ns_third * mean) * gram[at[i], at[j]] + ns_third * nn(
                    shifted[at[i], :], shifted[:, at[j]]
                )
                if i == j:
                    block -= (ns_third * mean * mean + level) * eye
                block = block.astype(bf16)
                rest[at[i], at[j]] = block
                if i < j:
                    rest[at[j], at[i]] = block.T
        values = own[...]
        top = values.astype(bf16)
        own_b[:, 0:128] = top
        own_b[:, 128:256] = (values - top.astype(f32)).astype(bf16)
        for i in range(tiles):
            moved = nn(rest[at[i], :], own_b[...])
            own[at[i], :] = alpha * own[at[i], :] + (moved[:, 0:128] + moved[:, 128:256])
        return alpha

    def turn(_, mean):
        alpha = advance(mean)
        for i in range(tiles):
            for j in range(tiles):
                block = nn(high[at[i], :], rest[:, at[j]]) + nn(low[at[i], :], rest[:, at[j]])
                prod[at[i], at[j]] = block
                prod_b[at[i], at[j]] = block.astype(bf16)
        trace = jnp.float32(0.0)
        for i in range(tiles):
            for j in range(tiles):
                block = alpha * prod[at[i], at[j]] + 0.5 * nn(rest[at[i], :], prod_b[:, at[j]])
                prod[at[i], at[j]] = block
                if i == j:
                    trace += jnp.sum(block * eye)
        later = alpha * alpha * mean + trace * (2.0 / WIDTH)
        for i in range(tiles):
            for j in range(tiles):
                block = (alpha * alpha) * gram[at[i], at[j]] + (
                    prod[at[i], at[j]] + prod[at[j], at[i]].T
                )
                store(i, j, block, later)
        return later

    advance(lax.fori_loop(0, NS_ITERS - 1, turn, mean))
    out_ref[...] = own[...].astype(bf16)


def orthogonal(chunk, near, far):
    square = (WIDTH, WIDTH)
    return pl.pallas_call(
        iterate_kernel,
        out_shape=[
            jax.ShapeDtypeStruct((WIDTH, 128), bf16),
            jax.ShapeDtypeStruct((8, WIDTH), f32),
            jax.ShapeDtypeStruct((BLOCK, 128), f32),
        ],
        in_specs=[pl.BlockSpec(memory_space=pltpu.SMEM)]
        + [pl.BlockSpec(memory_space=pltpu.VMEM)] * 2,
        out_specs=[pl.BlockSpec(memory_space=pltpu.VMEM)] * 3,
        scratch_shapes=[
            pltpu.VMEM((4, WIDTH, LANES), bf16),
            pltpu.VMEM(square, f32),
            pltpu.VMEM(square, bf16),
            pltpu.VMEM(square, bf16),
            pltpu.VMEM(square, bf16),
            pltpu.VMEM(square, bf16),
            pltpu.VMEM(square, f32),
            pltpu.VMEM(square, bf16),
            pltpu.VMEM((WIDTH, 128), f32),
            pltpu.VMEM((WIDTH, 256), bf16),
        ],
        compiler_params=pltpu.CompilerParams(vmem_limit_bytes=48 * 2**20),
        cost_estimate=pl.CostEstimate(
            flops=42 * 10**9, bytes_accessed=5 * 2**20, transcendentals=0
        ),
        name="orthogonalize",
    )(chunk, near, far)


def shards(
    tokens,
    cotangent,
    qk_w,
    vg_w,
    mlp_w,
    out_w,
    qk_mom,
    vg_mom,
    mlp_mom,
    out_mom,
    norm_params,
    norm_moment,
    norm_second,
    decay_gap,
    seq_length,
    seq_group,
):
    rows, width = tokens.shape
    slots = 4 * rows
    groups = 32
    value_width = 4 * VAL
    key_scale = KEY ** (-0.5)
    dp_index = lax.axis_index(DP)
    tensor_index = lax.axis_index(TENSOR)
    chunk_index = lax.axis_index(("y_lo", "z_hi"))

    gain_one = norm_params[0:width]
    shift_one = norm_params[width : 2 * width]
    group_gain = jnp.pad(
        lax.dynamic_slice_in_dim(norm_params, 2 * width + tensor_index * VAL, VAL),
        (0, LANES - VAL),
    )
    gain_two = norm_params[2 * width + value_width : 3 * width + value_width]
    shift_two = norm_params[3 * width + value_width : 4 * width + value_width]

    out_rows = jnp.swapaxes(out_w, 1, 2)
    first_half = lax.axis_index("y_lo") == 0

    def weight_rows(parts):
        packed = jnp.concatenate(parts, axis=1).astype(bf16)
        far = swap(packed, "y_lo")
        pair = jnp.stack([jnp.where(first_half, packed, far), jnp.where(first_half, far, packed)])
        return pair

    def weight_gather(pair):
        return lax.all_gather(pair, PLANE, axis=1, tiled=True).reshape(width, -1)

    pair_ret = weight_rows(
        [
            pairs_apart(qk_w[0]),
            pairs_apart(qk_w[1]),
            widen(vg_w[0]),
            widen(vg_w[1]),
            widen(out_rows[0]),
        ]
    )
    tokens_first, pair_ret = together(tokens, pair_ret)
    gathered = weight_gather(pair_ret)
    w_qk, w_v, w_g, w_o = ((gathered, LANES * i, LANES) for i in range(4))
    pair_ff = weight_rows([widen(mlp_w[0]), widen(mlp_w[1]), widen(out_rows[1])])

    whole_tokens = jnp.concatenate(tensor_gather(tokens_first), axis=0)
    order = jnp.stack([tensor_index, tensor_index ^ 2, tensor_index ^ 1, tensor_index ^ 3])
    place = (order[:, None] * rows + jnp.arange(rows, dtype=jnp.int32)[None, :]).reshape(slots)

    freqs = 1.0 / 10000.0 ** np.linspace(0.0, 1.0, KEY // 2)
    angles = np.arange(slots)[:, None] * freqs[None, :]
    tables = jnp.asarray(
        np.concatenate([np.cos(angles), np.sin(angles)], axis=1).astype(np.float32)
    ).reshape(4, rows, KEY)
    turned = tables[order].reshape(slots, KEY)

    labels = sequence_labels(seq_length, seq_group, dp_index, place)
    log_decay = jnp.log1p(-decay_gap[0])
    away = (place - slots // 2).astype(f32) * log_decay
    label_place = [labels.astype(f32), place.astype(f32)]
    columns = jnp.pad(jnp.stack(label_place + [jnp.exp(away)], axis=1), ((0, 0), (0, 125)))
    line = jnp.pad(jnp.stack(label_place + [jnp.exp(-away)], axis=0), ((0, 5), (0, 0)))
    gain_line = group_gain[None, :]

    hat_one, _ = normalize(whole_tokens.astype(f32))
    whole_one = (hat_one * gain_one + shift_one).astype(bf16)
    prepared = (whole_one, turned, columns, line)
    cot_first, (whole_one, turned, columns, line) = together(cotangent, prepared)
    whole_cot = tensor_gather(cot_first)
    (gain_line, pair_ff), whole_cot = together((gain_line, pair_ff), whole_cot)
    whole_cot = [(part, 0, width) for part in whole_cot]
    gathered_ff = weight_gather(pair_ff)
    w_1, w_2, w_3 = ((gathered_ff, LANES * i, LANES) for i in range(3))
    query, keys, values, weights, gate, hat_group, inv_group, mixed, own, other = retention(
        whole_one, w_qk, w_v, w_g, w_o, turned, columns, line, gain_line
    )
    near, far = tensor_sum(own, other)
    middle = tokens.astype(f32) + near + far.astype(f32)
    hat_two, inv_two = normalize(middle)
    whole_two = tensor_gather((hat_two * gain_two + shift_two).astype(bf16))
    hidden, grad_gate, grad_up, own, other = feed(whole_two, w_1, w_2, whole_cot, w_3)
    near, far = tensor_sum(own, other)
    early, out_own, out_other = early_grads(whole_two, grad_gate, grad_up, whole_cot, hidden, w_3)
    far, out_other = together(far, out_other)
    grad_normed_two = near + far.astype(f32)
    grad_middle = cotangent.astype(f32) + norm_back(grad_normed_two, gain_two, hat_two, inv_two)
    grad_first = grad_middle.astype(bf16)
    grad_far, grad_core = swap(grad_first, "y_hi"), swap(grad_first, "core")
    out_near, out_far = half_sum(out_own, out_other)
    grad_far, out_far = together(grad_far, out_far)
    grad_one = [grad_first, grad_far, grad_core, swap(grad_far, "core")]

    early_in = lax.all_to_all(early, PLANE, split_axis=0, concat_axis=0, tiled=True)
    early_halves = jnp.sum(early_in.astype(f32), axis=0)
    early_far = swap(
        jnp.where(first_half, early_halves[1], early_halves[0]).astype(bf16), "y_lo"
    )
    gain_two_grad = jnp.sum(grad_normed_two * hat_two, axis=0)
    shift_two_grad = jnp.sum(grad_normed_two, axis=0)

    grad_gate_ret, grad_retained, group_gain_grad = back_gate(
        grad_one, w_o, gate, hat_group, inv_group, gain_line
    )
    grad_query, grad_key, grad_values = back_scores(
        grad_retained, values, columns, line, keys, turned, weights, query
    )
    own, other = input_parts(
        grad_gate_ret, w_g, grad_values, w_v, grad_query, grad_key, w_qk
    )
    other, grad_values = together(other, grad_values)
    near, far = half_sum(own, other)
    small = jnp.stack(
        [gain_two_grad, shift_two_grad, jnp.pad(group_gain_grad[0], (0, width - LANES))], axis=1
    )
    small_high, small_low = split(small)
    riders = jnp.pad(
        jnp.concatenate([small_high, small_low], axis=1), ((0, 0), (0, 128 - 6))
    )
    late = late_grads(
        grad_one, mixed, whole_one, grad_gate_ret, grad_values, riders, grad_query, grad_key
    )
    far = swap(far, "y_hi")
    far, late = together(far, late)
    grad_normed_one = near + far.astype(f32)
    late_in = lax.all_to_all(
        late.reshape(groups, BLOCK, -1), DP, split_axis=0, concat_axis=0, tiled=True
    )
    own_hat, own_inv = normalize(tokens.astype(f32))
    gain_one_grad = jnp.sum(grad_normed_one * own_hat, axis=0)
    shift_one_grad = jnp.sum(grad_normed_one, axis=0)
    gain_one_grad, early_far = together(gain_one_grad, early_far)
    early_sum = jnp.where(first_half, early_halves[0], early_halves[1]) + early_far.astype(f32)

    late_sum = jnp.sum(late_in.astype(f32), axis=0)
    first_value = 2 * KEY
    at = [first_value + VAL * i for i in range(4)]
    small_sum = late_sum[:, at[3] : at[3] + 6]
    small_sum = small_sum[:, :3] + small_sum[:, 3:]

    grad_qk = pairs_together(jnp.stack([late_sum[:, 0:256], late_sum[:, 256:512]]))
    grad_vg = jnp.stack([late_sum[:, at[0] : at[1]], late_sum[:, at[1] : at[2]]])
    grad_mlp = jnp.stack([early_sum[:, 0:VAL], early_sum[:, VAL : 2 * VAL]])
    grad_out_t = jnp.stack([late_sum[:, at[2] : at[3]], early_sum[:, 2 * VAL : 3 * VAL]])
    mom_qk = muon_beta * qk_mom + grad_qk
    mom_vg = muon_beta * vg_mom + grad_vg
    mom_mlp = muon_beta * mlp_mom + grad_mlp
    mom_out = muon_beta * out_mom + jnp.swapaxes(grad_out_t, 1, 2)

    piece_high, piece_low = split(small_sum)
    first_norm = jnp.concatenate([gain_one_grad, shift_one_grad]).astype(bf16)
    extra = jnp.pad(
        jnp.concatenate([piece_high, piece_low, first_norm.reshape(BLOCK, 64)], axis=1),
        ((0, 0), (VAL, LANES - VAL - 70)),
    )
    stacked = (
        jnp.concatenate(
            [widen(mom_qk), widen(mom_vg), widen(mom_mlp), widen(jnp.swapaxes(mom_out, 1, 2))],
            axis=0,
        ).astype(bf16)
        + extra[None]
    )
    both = jnp.stack([stacked, swap(stacked, "y_hi")], axis=1)
    spread = jnp.broadcast_to(both[None], (4,) + both.shape).reshape((groups,) + both.shape[1:])
    arrived = lax.all_to_all(spread, DP, split_axis=0, concat_axis=0, tiled=True)
    far = swap(arrived, "core")
    own, vectors, first_total = orthogonal(
        jnp.reshape(chunk_index, (1,)).astype(jnp.int32), arrived, far
    )
    out_far = swap(out_far, "y_hi")
    (out_far, grad_normed_one), own = together((out_far, grad_normed_one), own)
    result = (middle + out_near + out_far.astype(f32)).astype(bf16)
    input_grad = grad_middle + norm_back(grad_normed_one, gain_one, own_hat, own_inv)
    returned = lax.all_to_all(
        own.reshape(groups, BLOCK, 128), DP, split_axis=0, concat_axis=0, tiled=True
    ).astype(f32)
    returned = jnp.concatenate([returned[8 * i : 8 * i + 8] for i in range(4)], axis=2)

    shrink = 1.0 - muon_rate * decay_rate
    square_scale = 0.2 * math.sqrt(width)
    wide_scale = 0.2 * math.sqrt(max(width, value_width))
    new_qk = qk_w * shrink - (muon_rate * square_scale) * returned[0:2, :, :KEY]
    new_vg = vg_w * shrink - (muon_rate * wide_scale) * returned[2:4, :, :VAL]
    new_mlp = mlp_w * shrink - (muon_rate * wide_scale) * returned[4:6, :, :VAL]
    new_out = out_w * shrink - (muon_rate * wide_scale) * jnp.swapaxes(returned[6:8, :, :VAL], 1, 2)

    first_total = first_total[:, 54:118].reshape(2 * width)
    group_parts = vectors[2:6, :VAL]
    which = jnp.arange(4, dtype=jnp.int32)[:, None] == order[None, :]
    group_whole = jnp.sum(
        jnp.where(which[:, :, None], group_parts[None], 0.0), axis=1
    ).reshape(value_width)
    small_total = jnp.concatenate(
        [first_total, group_whole, vectors[0], vectors[1]]
    )
    moment_new = beta_first * norm_moment + (1.0 - beta_first) * small_total
    second_new = beta_second * norm_second + (1.0 - beta_second) * small_total * small_total
    params_new = norm_params - adam_rate * (moment_new / (1.0 - beta_first**OPT_STEP)) / (
        jnp.sqrt(second_new / (1.0 - beta_second**OPT_STEP)) + adam_eps
    )
    return (
        result,
        input_grad,
        mom_qk,
        mom_vg,
        mom_mlp,
        mom_out,
        new_qk,
        new_vg,
        new_mlp,
        new_out,
        moment_new,
        second_new,
        params_new,
    )


def solution(mesh):
    fine = Mesh(np.asarray(mesh.devices).reshape(SIZES), AXES)
    by_rows = P(DP + TENSOR, None)
    by_columns = P(None, DP, TENSOR)
    by_out = P(None, TENSOR, DP)
    return jax.shard_map(
        shards,
        mesh=fine,
        in_specs=(
            by_rows,
            by_rows,
            by_columns,
            by_columns,
            by_columns,
            by_out,
            by_columns,
            by_columns,
            by_columns,
            by_out,
            P(),
            P(),
            P(),
            P(TENSOR),
            P(),
            P(),
        ),
        out_specs=(
            by_rows,
            by_rows,
            by_columns,
            by_columns,
            by_columns,
            by_out,
            by_columns,
            by_columns,
            by_columns,
            by_out,
            P(),
            P(),
            P(),
        ),
        check_vma=False,
    )
```

```python
import math

import jax
import jax.numpy as jnp
import numpy as np
from jax import lax
from jax.experimental import pallas as pl
from jax.experimental.pallas import tpu as pltpu
from jax.sharding import Mesh
from jax.sharding import PartitionSpec as P

HEADS = 4
NS_ITERS = 5
OPT_STEP = 10
KEY = 256
VAL = 432
LANES = 512
BLOCK = 32

norm_eps = 1e-05
group_eps = 0.01
ns_first = 3.4445
ns_second = -4.775
ns_third = 2.0315
muon_rate = 0.15
muon_beta = 0.95
decay_rate = 0.01
adam_rate = 0.6
beta_first = 0.9
beta_second = 0.95
adam_eps = 1e-08

AXES = ("y_lo", "z_hi", "z_lo", "x", "y_hi", "core")
SIZES = (2, 2, 2, 4, 2, 2)
DP = ("y_lo", "z_hi", "z_lo", "x")
PLANE = ("z_hi", "z_lo", "x")
TENSOR = ("y_hi", "core")
bf16 = jnp.bfloat16
f32 = jnp.float32


def swap(values, axis):
    return lax.ppermute(values, axis, [(0, 1), (1, 0)])


def dot(left, right, dims):
    return lax.dot_general(left, right, (dims, ((), ())), preferred_element_type=f32)


def nn(left, right):
    return dot(left, right, ((1,), (0,)))


def nt(left, right):
    return dot(left, right, ((1,), (1,)))


def tn(left, right):
    return dot(left, right, ((0,), (0,)))


def split(values):
    high = lax.reduce_precision(values, 8, 7)
    return high.astype(bf16), (values - high).astype(bf16)


def widen(values):
    return jnp.pad(values, ((0, 0),) * (values.ndim - 1) + ((0, LANES - values.shape[-1]),))


def tensor_gather(own):
    far = swap(own, "y_hi")
    return [own, far, swap(own, "core"), swap(far, "core")]


def half_sum(own, other):
    half = own.shape[0] // 2
    arrived = swap(other, "core")
    far = (own[half:] + arrived[half:].astype(f32)).astype(bf16)
    return own[:half] + arrived[:half].astype(f32), far


def tensor_sum(own, other):
    near, far = half_sum(own, other)
    return near, swap(far, "y_hi")


def together(first, second):
    return lax.optimization_barrier((first, second))


def normalize(values):
    centre = values - jnp.mean(values, axis=-1, keepdims=True)
    spread = lax.rsqrt(jnp.mean(centre * centre, axis=-1, keepdims=True) + norm_eps)
    return centre * spread, spread


def norm_back(grad_out, gain, normed, spread):
    grad_normed = grad_out * gain
    return spread * (
        grad_normed
        - jnp.mean(grad_normed, axis=-1, keepdims=True)
        - normed * jnp.mean(grad_normed * normed, axis=-1, keepdims=True)
    )


def pairs_apart(values):
    shape = values.shape
    return jnp.swapaxes(values.reshape(shape[:-1] + (KEY // 2, 2)), -1, -2).reshape(shape)


def pairs_together(values):
    shape = values.shape
    return jnp.swapaxes(values.reshape(shape[:-1] + (2, KEY // 2)), -1, -2).reshape(shape)


def sequence_labels(seq_length, seq_group, group, place):
    mine = seq_group == group
    lengths = jnp.where(mine, seq_length, 0)
    ends = jnp.cumsum(lengths, dtype=jnp.int32)
    starts = ends - lengths
    inside = mine[None, :] & (place[:, None] >= starts[None, :]) & (place[:, None] < ends[None, :])
    number = jnp.arange(1, seq_length.shape[0] + 1, dtype=jnp.int32)
    return jnp.sum(jnp.where(inside, number[None, :], 0), axis=1, dtype=jnp.int32)


WIDTH = 1024
TILE = WIDTH // 2
EARLY = 1408
LATE = 1920
NS_TILE = 256


ROWS = [pl.ds(TILE * i, TILE) for i in range(WIDTH // TILE)]


STORES = 12


def in_vmem(kernel, name, out_shape, scratch, *operands):
    arrays, pieces, local = [], [], []
    for a in operands:
        parts = a if isinstance(a, list) else [a]
        top, piece = 0, []
        for part in parts:
            array, first, columns, *free = (
                part if isinstance(part, tuple) else (part, 0, part.shape[1])
            )
            whole = columns == array.shape[1]
            piece.append((len(arrays), None if whole else (first, columns), top, array.shape[0]))
            fixed = not free and (not isinstance(a, list) or isinstance(part, tuple))
            arrays.append(pltpu.with_memory_space_constraint(array, pltpu.HBM) if fixed else array)
            top += array.shape[0]
        pieces.append(piece)
        local.append(pltpu.VMEM((top, columns), array.dtype))
    n_in, n_out, n_local = len(arrays), len(out_shape), len(local)

    def body(*refs):
        ins, outs = refs[:n_in], refs[n_in : n_in + n_out]
        refs = refs[n_in + n_out :]
        local_in, local_out = refs[:n_local], refs[n_local : n_local + n_out]
        sem_in, sem_out = refs[n_local + n_out : n_local + n_out + 2]
        loads = []
        for i, piece in enumerate(pieces):
            loads.append([])
            for which, cut, top, rows in piece:
                source = ins[which] if cut is None else ins[which].at[:, pl.ds(*cut)]
                target = local_in[i] if len(piece) == 1 else local_in[i].at[pl.ds(top, rows), :]
                loads[i].append(pltpu.make_async_copy(source, target, sem_in.at[which]))
                loads[i][-1].start()
        pending = set(range(n_local))
        stores = []

        def ready(*which):
            for i in which:
                if i in pending:
                    pending.remove(i)
                    for load in loads[i]:
                        load.wait()

        def done(i, *index):
            source, target = local_out[i], outs[i]
            if index:
                source, target = source.at[index], target.at[index]
            stores.append(pltpu.make_async_copy(source, target, sem_out.at[len(stores)]))
            stores[-1].start()

        kernel(ready, done, *local_in, *local_out, *refs[n_local + n_out + 2 :])
        ready(*range(n_local))
        for store in stores:
            store.wait()

    local += [pltpu.VMEM(a.shape, a.dtype) for a in out_shape]
    held = sum(math.prod(a.shape) * jnp.dtype(a.dtype).itemsize for a in local)
    return pl.pallas_call(
        body,
        out_shape=[pltpu.HBM(a.shape, a.dtype) for a in out_shape],
        in_specs=[pl.BlockSpec(memory_space=pl.ANY)] * n_in,
        out_specs=[pl.BlockSpec(memory_space=pltpu.HBM)] * n_out,
        scratch_shapes=local
        + [pltpu.SemaphoreType.DMA((n_in,)), pltpu.SemaphoreType.DMA((STORES,))]
        + scratch,
        compiler_params=pltpu.CompilerParams(vmem_limit_bytes=held + 14 * 2**20),
        cost_estimate=pl.CostEstimate(flops=1, bytes_accessed=1, transcendentals=0),
        name=name,
    )(*arrays)


def put_halves(done, i, part, own_ref, other_ref, own, other):
    if i == 0:
        own_ref[...] = part
        done(own)
    else:
        other_ref[...] = part.astype(bf16)
        done(other)


def turn(first, second, cos_table, sin_table):
    return first * cos_table - second * sin_table, second * cos_table + first * sin_table


def masked(scores, rows, cols_ref, line_ref):
    label, place = cols_ref[rows, 0:1], cols_ref[rows, 1:2]
    linked = (label == line_ref[0:1, :]) & (label > 0.0) & (place >= line_ref[1:2, :])
    return jnp.where(linked, scores * (cols_ref[rows, 2:3] * line_ref[2:3, :]), 0.0)


def retention_kernel(
    ready, done, h_ref, wqk_ref, wv_ref, wg_ref, wo_ref, turn_ref, cols_ref, line_ref, gain_ref,
    q_ref, k_ref, v_ref, p_ref, gate_ref, hat_ref, inv_ref, mixed_ref, own_ref, other_ref,
):
    half = KEY // 2
    ready(0, 1, 5)
    for rows in ROWS:
        cos_table, sin_table = turn_ref[rows, :half], turn_ref[rows, half:]
        both = nn(h_ref[rows, :], wqk_ref[...])
        query, keys = both[:, :KEY], both[:, KEY:] * KEY**-0.5
        first, second = turn(query[:, :half], query[:, half:], cos_table, sin_table)
        q_ref[rows, 0:half] = first.astype(bf16)
        q_ref[rows, half:KEY] = second.astype(bf16)
        first, second = turn(keys[:, :half], keys[:, half:], cos_table, sin_table)
        k_ref[rows, 0:half] = first.astype(bf16)
        k_ref[rows, half:KEY] = second.astype(bf16)
    done(0)
    done(1)
    ready(2)
    for rows in ROWS:
        v_ref[rows, :] = nn(h_ref[rows, :], wv_ref[...]).astype(bf16)
    done(2)
    ready(3)
    for rows in ROWS:
        gate_ref[rows, :] = nn(h_ref[rows, :], wg_ref[...])
    done(4)
    ready(4, 6, 7, 8)
    for i, rows in reversed(list(enumerate(ROWS))):
        weights = masked(nt(q_ref[rows, :], k_ref[...]), rows, cols_ref, line_ref).astype(bf16)
        p_ref[rows, :] = weights
        done(3, rows)
        retained = nn(weights, v_ref[...])
        inverse = lax.rsqrt(
            jnp.sum(retained * retained, axis=-1, keepdims=True) * (1.0 / VAL) + group_eps
        )
        inv_ref[rows, :] = jnp.broadcast_to(inverse, (TILE, 128))
        hat = retained * inverse
        hat_ref[rows, :] = hat
        done(5, rows)
        gate = gate_ref[rows, :]
        swish = gate * (1.0 / (1.0 + jnp.exp(-gate)))
        mixed = (hat * gain_ref[...] * swish).astype(bf16)
        mixed_ref[rows, :] = mixed
        put_halves(done, i, nt(mixed, wo_ref[...]), own_ref, other_ref, 8, 9)
    done(6)
    done(7)


def retention(*operands):
    shape = jax.ShapeDtypeStruct
    return in_vmem(
        retention_kernel,
        "retention",
        [
            shape((WIDTH, KEY), bf16),
            shape((WIDTH, KEY), bf16),
            shape((WIDTH, LANES), bf16),
            shape((WIDTH, WIDTH), bf16),
            shape((WIDTH, LANES), f32),
            shape((WIDTH, LANES), f32),
            shape((WIDTH, 128), f32),
            shape((WIDTH, LANES), bf16),
            shape((WIDTH // 2, WIDTH), f32),
            shape((WIDTH // 2, WIDTH), bf16),
        ],
        [],
        *operands,
    )


def feed_kernel(
    ready, done, h_ref, w1_ref, w2_ref, cot_ref, w3_ref,
    hidden_ref, gate_ref, up_ref, own_ref, other_ref,
):
    for i, rows in reversed(list(enumerate(ROWS))):
        ready(0, 1)
        pre_gate = nn(h_ref[rows, :], w1_ref[...])
        ready(2)
        pre_up = nn(h_ref[rows, :], w2_ref[...])
        ready(3, 4)
        grad_hidden = nn(cot_ref[rows, :], w3_ref[...])
        cumulative = 0.5 * (1.0 + lax.erf(pre_gate * (1.0 / math.sqrt(2.0))))
        density = jnp.exp(-0.5 * pre_gate * pre_gate) * (1.0 / math.sqrt(2.0 * math.pi))
        gelu_gate = pre_gate * cumulative
        hidden_ref[rows, :] = (gelu_gate * pre_up).astype(bf16)
        grad_gate = (grad_hidden * pre_up * (cumulative + pre_gate * density)).astype(bf16)
        grad_up = (grad_hidden * gelu_gate).astype(bf16)
        gate_ref[rows, :] = grad_gate
        up_ref[rows, :] = grad_up
        for k in range(3):
            done(k, rows)
        part = nt(grad_gate, w1_ref[...]) + nt(grad_up, w2_ref[...])
        put_halves(done, i, part, own_ref, other_ref, 3, 4)


def feed(*operands):
    shape = jax.ShapeDtypeStruct
    return in_vmem(
        feed_kernel,
        "feed_forward",
        [shape((WIDTH, LANES), bf16)] * 3
        + [shape((WIDTH // 2, WIDTH), f32), shape((WIDTH // 2, WIDTH), bf16)],
        [],
        *operands,
    )


def early_kernel(
    ready, done, h_ref, gate_ref, up_ref, cot_ref, hidden_ref, w3_ref, out_ref, own_ref, other_ref
):
    for j, (left, right) in enumerate(
        ((h_ref, gate_ref), (h_ref, up_ref), (cot_ref, hidden_ref))
    ):
        ready(*((0, 1), (2,), (3, 4))[j])
        columns = pl.ds(VAL * j, VAL)
        for i, at in enumerate(ROWS):
            part = tn(left[:, at], right[...]).astype(bf16)[:, :VAL]
            out_ref[:, i, :, columns] = part.reshape(16, BLOCK, VAL)
    out_ref[:, :, :, 3 * VAL : EARLY] = jnp.zeros((16, 2, BLOCK, EARLY - 3 * VAL), bf16)
    done(0)
    ready(5)
    for i, rows in reversed(list(enumerate(ROWS))):
        put_halves(done, i, nt(hidden_ref[rows, :], w3_ref[...]), own_ref, other_ref, 1, 2)


def early_grads(*operands):
    shape = jax.ShapeDtypeStruct
    return in_vmem(
        early_kernel,
        "feed_forward_grads",
        [
            shape((16, 2, BLOCK, EARLY), bf16),
            shape((WIDTH // 2, WIDTH), f32),
            shape((WIDTH // 2, WIDTH), bf16),
        ],
        [],
        *operands,
    )


def back_gate_kernel(
    ready, done, grad_ref, w_ref, gate_ref, hat_ref, inv_ref, gain_ref, gate_out, ret_out, gain_out
):
    total = jnp.zeros((1, LANES), f32)
    for rows in ROWS:
        ready(0, 1)
        grad_mixed = nn(grad_ref[rows, :], w_ref[...])
        ready(2, 3, 4, 5)
        gain = gain_ref[...]
        gate, hat, inverse = gate_ref[rows, :], hat_ref[rows, :], inv_ref[rows, 0:1]
        sig = 1.0 / (1.0 + jnp.exp(-gate))
        swish = gate * sig
        grad_grouped = grad_mixed * swish
        gate_out[rows, :] = (
            grad_mixed * (hat * gain) * (sig + swish * (1.0 - sig))
        ).astype(bf16)
        done(0, rows)
        total += jnp.sum(grad_grouped * hat, axis=0, keepdims=True)
        grad_hat = grad_grouped * gain
        inner = jnp.sum(grad_hat * hat, axis=-1, keepdims=True) * (1.0 / VAL)
        ret_out[rows, :] = (inverse * (grad_hat - hat * inner)).astype(bf16)
        done(1, rows)
    gain_out[...] = total
    done(2)


def back_gate(*operands):
    shape = jax.ShapeDtypeStruct
    return in_vmem(
        back_gate_kernel,
        "gate_backward",
        [shape((WIDTH, LANES), bf16)] * 2 + [shape((1, LANES), f32)],
        [],
        *operands,
    )


def back_scores_kernel(
    ready, done, ret_ref, v_ref, cols_ref, line_ref, k_ref, turn_ref, p_ref, q_ref,
    q_out, k_out, v_out, scores,
):
    half = KEY // 2
    ready(0, 1, 2, 3)
    for rows in ROWS:
        part = masked(nt(ret_ref[rows, :], v_ref[...]), rows, cols_ref, line_ref).astype(bf16)
        scores[rows, :] = part
        ready(4, 5)
        turned = nn(part, k_ref[...])
        first, second = turn(
            turned[:, :half], turned[:, half:], turn_ref[rows, :half], -turn_ref[rows, half:]
        )
        q_out[rows, 0:half] = first.astype(bf16)
        q_out[rows, half:KEY] = second.astype(bf16)
    done(0)
    ready(6, 7)
    for rows in ROWS:
        v_out[rows, :] = tn(p_ref[:, rows], ret_ref[...]).astype(bf16)
        done(2, rows)
    for rows in ROWS:
        turned = tn(scores[:, rows], q_ref[...])
        first, second = turn(
            turned[:, :half], turned[:, half:], turn_ref[rows, :half], -turn_ref[rows, half:]
        )
        k_out[rows, 0:half] = first.astype(bf16)
        k_out[rows, half:KEY] = second.astype(bf16)
    done(1)


def back_scores(*operands):
    shape = jax.ShapeDtypeStruct
    return in_vmem(
        back_scores_kernel,
        "scores_backward",
        [shape((WIDTH, KEY), bf16)] * 2 + [shape((WIDTH, LANES), bf16)],
        [pltpu.VMEM((WIDTH, WIDTH), bf16)],
        *operands,
    )


def late_kernel(
    ready, done, grad_ref, mixed_ref, h_ref, gate_ref, v_ref, ride_ref, q_ref, k_ref, out_ref
):
    ready(0, 1)
    for rows in ROWS:
        part = tn(grad_ref[:, rows], mixed_ref[...]).astype(bf16)
        out_ref[rows, 2 * KEY + 2 * VAL : 2 * KEY + 3 * VAL] = part[:, :VAL]
    ready(2, 3)
    for rows in ROWS:
        part = tn(h_ref[:, rows], gate_ref[...]).astype(bf16)
        out_ref[rows, 2 * KEY + VAL : 2 * KEY + 2 * VAL] = part[:, :VAL]
    ready(4, 5)
    for rows in ROWS:
        part = tn(h_ref[:, rows], v_ref[...]).astype(bf16)
        out_ref[rows, 2 * KEY : 2 * KEY + VAL] = part[:, :VAL]
        out_ref[rows, 2 * KEY + 3 * VAL : LATE] = ride_ref[rows, : LATE - 2 * KEY - 3 * VAL]
    ready(6, 7)
    for rows in ROWS:
        left = h_ref[:, rows]
        out_ref[rows, 0:KEY] = tn(left, q_ref[...]).astype(bf16)
        out_ref[rows, KEY : 2 * KEY] = (tn(left, k_ref[...]) * KEY**-0.5).astype(bf16)
    done(0)


def late_grads(*operands):
    return in_vmem(
        late_kernel,
        "retention_grads",
        [jax.ShapeDtypeStruct((WIDTH, LATE), bf16)],
        [],
        *operands,
    )[0]


def input_kernel(
    ready, done, gate_ref, wg_ref, v_ref, wv_ref, q_ref, k_ref, wqk_ref, own_ref, other_ref
):
    for i, rows in reversed(list(enumerate(ROWS))):
        ready(0, 1)
        part = nt(gate_ref[rows, :], wg_ref[...])
        ready(2, 3)
        part += nt(v_ref[rows, :], wv_ref[...])
        ready(4, 5, 6)
        part += nt(q_ref[rows, :], wqk_ref[:, 0:KEY])
        part += nt(k_ref[rows, :], wqk_ref[:, KEY : 2 * KEY]) * KEY**-0.5
        put_halves(done, i, part, own_ref, other_ref, 0, 1)


def input_parts(*operands):
    shape = jax.ShapeDtypeStruct
    return in_vmem(
        input_kernel,
        "input_grad_parts",
        [shape((WIDTH // 2, WIDTH), f32), shape((WIDTH // 2, WIDTH), bf16)],
        [],
        *operands,
    )


def iterate_kernel(
    chunk_ref, near_ref, far_ref, out_ref, vector_ref, first_ref, whole, gram, high, low, shifted, rest, prod, prod_b, own, own_b
):
    tiles = WIDTH // NS_TILE
    at = [pl.ds(NS_TILE * i, NS_TILE) for i in range(tiles)]
    eye = (
        lax.broadcasted_iota(jnp.int32, (NS_TILE, NS_TILE), 0)
        == lax.broadcasted_iota(jnp.int32, (NS_TILE, NS_TILE), 1)
    ).astype(f32)
    keep = lax.broadcasted_iota(jnp.int32, (WIDTH, 128), 1) < VAL - 384
    riders = jnp.zeros((WIDTH, 128), f32)
    for p in range(4):
        source = near_ref if p < 2 else far_ref
        piece = source[:, p % 2].reshape(WIDTH, LANES)
        whole[p, :, 0:384] = piece[:, 0:384]
        whole[p, :, 384:512] = jnp.where(keep, piece[:, 384:512], jnp.zeros((), bf16))
        ride = piece[:, 384:512].astype(f32)
        riders += ride
        lines = ride.T
        vector_ref[2 + p : 3 + p, :] = lines[50:51, :] + lines[53:54, :]
    lines = riders.T
    vector_ref[0:2, :] = lines[48:50, :] + lines[51:53, :]
    vector_ref[6:8, :] = jnp.zeros((2, WIDTH), f32)
    first_ref[...] = jnp.sum(riders.reshape(WIDTH // BLOCK, BLOCK, 128), axis=0)

    trace = jnp.float32(0.0)
    for i in range(tiles):
        for j in range(i, tiles):
            block = jnp.zeros((NS_TILE, NS_TILE), f32)
            for p in range(4):
                block += nt(whole[p, at[i], :], whole[p, at[j], :])
            gram[at[i], at[j]] = block
            if i == j:
                trace += jnp.sum(block * eye)
    inverse = 1.0 / (jnp.sqrt(trace) + 1e-07)
    for q in range(4):

        @pl.when(chunk_ref[0] == q)
        def _():
            own[...] = whole[0, :, 128 * q : 128 * (q + 1)].astype(f32) * inverse

    def store(i, j, block, mean):
        gram[at[i], at[j]] = block
        top = block.astype(bf16)
        bottom = (block - top.astype(f32)).astype(bf16)
        high[at[i], at[j]] = top
        low[at[i], at[j]] = bottom
        if i == j:
            shifted[at[i], at[j]] = (block - mean * eye).astype(bf16)
        else:
            shifted[at[i], at[j]] = top
            top = top.T
            high[at[j], at[i]] = top
            low[at[j], at[i]] = bottom.T
            shifted[at[j], at[i]] = top

    mean = trace * inverse * inverse * (1.0 / WIDTH)
    for i in range(tiles):
        for j in range(i, tiles):
            store(i, j, gram[at[i], at[j]] * (inverse * inverse), mean)

    def advance(mean):
        level = ns_second * mean + ns_third * mean * mean
        alpha = ns_first + level
        for i in range(tiles):
            for j in range(i, tiles):
                block = (ns_second + 2.0 * ns_third * mean) * gram[at[i], at[j]] + ns_third * nn(
                    shifted[at[i], :], shifted[:, at[j]]
                )
                if i == j:
                    block -= (ns_third * mean * mean + level) * eye
                block = block.astype(bf16)
                rest[at[i], at[j]] = block
                if i < j:
                    rest[at[j], at[i]] = block.T
        values = own[...]
        top = values.astype(bf16)
        own_b[:, 0:128] = top
        own_b[:, 128:256] = (values - top.astype(f32)).astype(bf16)
        for i in range(tiles):
            moved = nn(rest[at[i], :], own_b[...])
            own[at[i], :] = alpha * own[at[i], :] + (moved[:, 0:128] + moved[:, 128:256])
        return alpha

    def turn(_, mean):
        alpha = advance(mean)
        for i in range(tiles):
            for j in range(tiles):
                block = nn(high[at[i], :], rest[:, at[j]]) + nn(low[at[i], :], rest[:, at[j]])
                prod[at[i], at[j]] = block
                prod_b[at[i], at[j]] = block.astype(bf16)
        def moved(i, j):
            return (
                (alpha * alpha) * gram[at[i], at[j]]
                + alpha * (prod[at[i], at[j]] + prod[at[j], at[i]].T)
                + nn(rest[at[i], :], prod_b[:, at[j]])
            )

        trace = jnp.float32(0.0)
        for i in range(tiles):
            block = moved(i, i)
            block = 0.5 * (block + block.T)
            gram[at[i], at[i]] = block
            trace += jnp.sum(block * eye)
        later = trace * (1.0 / WIDTH)
        for i in range(tiles):
            store(i, i, gram[at[i], at[i]], later)
            for j in range(i + 1, tiles):
                store(i, j, moved(i, j), later)
        return later

    advance(lax.fori_loop(0, NS_ITERS - 1, turn, mean))
    out_ref[...] = own[...].astype(bf16)


def orthogonal(chunk, near, far):
    square = (WIDTH, WIDTH)
    return pl.pallas_call(
        iterate_kernel,
        out_shape=[
            jax.ShapeDtypeStruct((WIDTH, 128), bf16),
            jax.ShapeDtypeStruct((8, WIDTH), f32),
            jax.ShapeDtypeStruct((BLOCK, 128), f32),
        ],
        in_specs=[pl.BlockSpec(memory_space=pltpu.SMEM)]
        + [pl.BlockSpec(memory_space=pltpu.VMEM)] * 2,
        out_specs=[pl.BlockSpec(memory_space=pltpu.VMEM)] * 3,
        scratch_shapes=[
            pltpu.VMEM((4, WIDTH, LANES), bf16),
            pltpu.VMEM(square, f32),
            pltpu.VMEM(square, bf16),
            pltpu.VMEM(square, bf16),
            pltpu.VMEM(square, bf16),
            pltpu.VMEM(square, bf16),
            pltpu.VMEM(square, f32),
            pltpu.VMEM(square, bf16),
            pltpu.VMEM((WIDTH, 128), f32),
            pltpu.VMEM((WIDTH, 256), bf16),
        ],
        compiler_params=pltpu.CompilerParams(vmem_limit_bytes=48 * 2**20),
        cost_estimate=pl.CostEstimate(
            flops=42 * 10**9, bytes_accessed=5 * 2**20, transcendentals=0
        ),
        name="orthogonalize",
    )(chunk, near, far)


def shards(
    tokens,
    cotangent,
    qk_w,
    vg_w,
    mlp_w,
    out_w,
    qk_mom,
    vg_mom,
    mlp_mom,
    out_mom,
    norm_params,
    norm_moment,
    norm_second,
    decay_gap,
    seq_length,
    seq_group,
):
    rows, width = tokens.shape
    slots = 4 * rows
    groups = 32
    value_width = 4 * VAL
    key_scale = KEY ** (-0.5)
    dp_index = lax.axis_index(DP)
    tensor_index = lax.axis_index(TENSOR)
    chunk_index = lax.axis_index(("y_lo", "z_hi"))

    gain_one = norm_params[0:width]
    shift_one = norm_params[width : 2 * width]
    group_gain = jnp.pad(
        lax.dynamic_slice_in_dim(norm_params, 2 * width + tensor_index * VAL, VAL),
        (0, LANES - VAL),
    )
    gain_two = norm_params[2 * width + value_width : 3 * width + value_width]
    shift_two = norm_params[3 * width + value_width : 4 * width + value_width]

    out_rows = jnp.swapaxes(out_w, 1, 2)
    first_half = lax.axis_index("y_lo") == 0

    def weight_rows(parts):
        packed = jnp.concatenate(parts, axis=1).astype(bf16)
        far = swap(packed, "y_lo")
        pair = jnp.stack([jnp.where(first_half, packed, far), jnp.where(first_half, far, packed)])
        return pair

    def weight_gather(pair):
        return lax.all_gather(pair, PLANE, axis=1, tiled=True).reshape(width, -1)

    pair_ret = weight_rows(
        [
            pairs_apart(qk_w[0]),
            pairs_apart(qk_w[1]),
            widen(vg_w[0]),
            widen(vg_w[1]),
            widen(out_rows[0]),
        ]
    )
    (tokens_first, mlp_later), pair_ret = together((tokens, mlp_w), pair_ret)
    gathered = weight_gather(pair_ret)
    w_qk, w_v, w_g, w_o = ((gathered, LANES * i, LANES) for i in range(4))
    pair_ff = weight_rows([widen(mlp_later[0]), widen(mlp_later[1]), widen(out_rows[1])])

    whole_tokens = jnp.concatenate(tensor_gather(tokens_first), axis=0)
    order = jnp.stack([tensor_index, tensor_index ^ 2, tensor_index ^ 1, tensor_index ^ 3])
    place = (order[:, None] * rows + jnp.arange(rows, dtype=jnp.int32)[None, :]).reshape(slots)

    freqs = 1.0 / 10000.0 ** np.linspace(0.0, 1.0, KEY // 2)
    angles = np.arange(slots)[:, None] * freqs[None, :]
    tables = jnp.asarray(
        np.concatenate([np.cos(angles), np.sin(angles)], axis=1).astype(np.float32)
    ).reshape(4, rows, KEY)
    turned = tables[order].reshape(slots, KEY)

    labels = sequence_labels(seq_length, seq_group, dp_index, place)
    log_decay = jnp.log1p(-decay_gap[0])
    away = (place - slots // 2).astype(f32) * log_decay
    label_place = [labels.astype(f32), place.astype(f32)]
    columns = jnp.pad(jnp.stack(label_place + [jnp.exp(away)], axis=1), ((0, 0), (0, 125)))
    line = jnp.pad(jnp.stack(label_place + [jnp.exp(-away)], axis=0), ((0, 5), (0, 0)))
    gain_line = group_gain[None, :]

    hat_one, _ = normalize(whole_tokens.astype(f32))
    whole_one = (hat_one * gain_one + shift_one).astype(bf16)
    prepared = (whole_one, turned, columns, line)
    cot_first, (whole_one, turned, columns, line) = together(cotangent, prepared)
    whole_cot = tensor_gather(cot_first)
    (gain_line, pair_ff), whole_cot = together((gain_line, pair_ff), whole_cot)
    whole_cot = [(part, 0, width) for part in whole_cot]
    gathered_ff = weight_gather(pair_ff)
    w_1, w_2, w_3 = ((gathered_ff, LANES * i, LANES) for i in range(3))
    query, keys, values, weights, gate, hat_group, inv_group, mixed, own, other = retention(
        whole_one, w_qk, w_v, w_g, w_o, turned, columns, line, gain_line
    )
    near, far = tensor_sum(own, other)
    middle = tokens.astype(f32) + near + far.astype(f32)
    hat_two, inv_two = normalize(middle)
    whole_two = tensor_gather((hat_two * gain_two + shift_two).astype(bf16))
    hidden, grad_gate, grad_up, own, other = feed(whole_two, w_1, w_2, whole_cot, w_3)
    near, far = tensor_sum(own, other)
    early, out_own, out_other = early_grads(whole_two, grad_gate, grad_up, whole_cot, hidden, w_3)
    far, out_other = together(far, out_other)
    grad_normed_two = near + far.astype(f32)
    grad_middle = cotangent.astype(f32) + norm_back(grad_normed_two, gain_two, hat_two, inv_two)
    grad_first = grad_middle.astype(bf16)
    grad_far, grad_core = swap(grad_first, "y_hi"), swap(grad_first, "core")
    out_near, out_far = half_sum(out_own, out_other)
    grad_far, out_far = together(grad_far, out_far)
    grad_one = [grad_first, grad_far, grad_core, swap(grad_far, "core")]

    early_in = lax.all_to_all(early, PLANE, split_axis=0, concat_axis=0, tiled=True)
    early_halves = jnp.sum(early_in.astype(f32), axis=0)
    early_far = swap(
        jnp.where(first_half, early_halves[1], early_halves[0]).astype(bf16), "y_lo"
    )
    gain_two_grad = jnp.sum(grad_normed_two * hat_two, axis=0)
    shift_two_grad = jnp.sum(grad_normed_two, axis=0)

    grad_gate_ret, grad_retained, group_gain_grad = back_gate(
        grad_one, w_o, gate, hat_group, inv_group, gain_line
    )
    grad_query, grad_key, grad_values = back_scores(
        grad_retained, values, columns, line, keys, turned, weights, query
    )
    own, other = input_parts(
        grad_gate_ret, w_g, grad_values, w_v, grad_query, grad_key, w_qk
    )
    other, grad_values = together(other, grad_values)
    near, far = half_sum(own, other)
    small = jnp.stack(
        [gain_two_grad, shift_two_grad, jnp.pad(group_gain_grad[0], (0, width - LANES))], axis=1
    )
    small_high, small_low = split(small)
    riders = jnp.pad(
        jnp.concatenate([small_high, small_low], axis=1), ((0, 0), (0, 128 - 6))
    )
    late = late_grads(
        grad_one, mixed, whole_one, grad_gate_ret, grad_values, riders, grad_query, grad_key
    )
    far = swap(far, "y_hi")
    far, late = together(far, late)
    grad_normed_one = near + far.astype(f32)
    late_in = lax.all_to_all(
        late.reshape(groups, BLOCK, -1), DP, split_axis=0, concat_axis=0, tiled=True
    )
    own_hat, own_inv = normalize(tokens.astype(f32))
    gain_one_grad = jnp.sum(grad_normed_one * own_hat, axis=0)
    shift_one_grad = jnp.sum(grad_normed_one, axis=0)
    input_grad = grad_middle + norm_back(grad_normed_one, gain_one, own_hat, own_inv)
    (gain_one_grad, input_grad), early_far = together((gain_one_grad, input_grad), early_far)
    early_sum = jnp.where(first_half, early_halves[0], early_halves[1]) + early_far.astype(f32)

    late_sum = jnp.sum(late_in.astype(f32), axis=0)
    first_value = 2 * KEY
    at = [first_value + VAL * i for i in range(4)]
    small_sum = late_sum[:, at[3] : at[3] + 6]
    small_sum = small_sum[:, :3] + small_sum[:, 3:]

    grad_qk = pairs_together(jnp.stack([late_sum[:, 0:256], late_sum[:, 256:512]]))
    grad_vg = jnp.stack([late_sum[:, at[0] : at[1]], late_sum[:, at[1] : at[2]]])
    grad_mlp = jnp.stack([early_sum[:, 0:VAL], early_sum[:, VAL : 2 * VAL]])
    grad_out_t = jnp.stack([late_sum[:, at[2] : at[3]], early_sum[:, 2 * VAL : 3 * VAL]])
    mom_qk = muon_beta * qk_mom + grad_qk
    mom_vg = muon_beta * vg_mom + grad_vg
    mom_mlp = muon_beta * mlp_mom + grad_mlp
    mom_out = muon_beta * out_mom + jnp.swapaxes(grad_out_t, 1, 2)

    piece_high, piece_low = split(small_sum)
    first_norm = jnp.concatenate([gain_one_grad, shift_one_grad]).astype(bf16)
    extra = jnp.pad(
        jnp.concatenate([piece_high, piece_low, first_norm.reshape(BLOCK, 64)], axis=1),
        ((0, 0), (VAL, LANES - VAL - 70)),
    )
    stacked = (
        jnp.concatenate(
            [widen(mom_qk), widen(mom_vg), widen(mom_mlp), widen(jnp.swapaxes(mom_out, 1, 2))],
            axis=0,
        ).astype(bf16)
        + extra[None]
    )
    both = jnp.stack([stacked, swap(stacked, "y_hi")], axis=1)
    spread = jnp.broadcast_to(both[None], (4,) + both.shape).reshape((groups,) + both.shape[1:])
    arrived = lax.all_to_all(spread, DP, split_axis=0, concat_axis=0, tiled=True)
    far = swap(arrived, "core")
    own, vectors, first_total = orthogonal(
        jnp.reshape(chunk_index, (1,)).astype(jnp.int32), arrived, far
    )
    out_far = swap(out_far, "y_hi")
    out_far, own = together(out_far, own)
    result = (middle + out_near + out_far.astype(f32)).astype(bf16)
    returned = lax.all_to_all(
        own.reshape(groups, BLOCK, 128), DP, split_axis=0, concat_axis=0, tiled=True
    ).astype(f32)
    returned = jnp.concatenate([returned[8 * i : 8 * i + 8] for i in range(4)], axis=2)

    shrink = 1.0 - muon_rate * decay_rate
    square_scale = 0.2 * math.sqrt(width)
    wide_scale = 0.2 * math.sqrt(max(width, value_width))
    new_qk = qk_w * shrink - (muon_rate * square_scale) * returned[0:2, :, :KEY]
    new_vg = vg_w * shrink - (muon_rate * wide_scale) * returned[2:4, :, :VAL]
    new_mlp = mlp_w * shrink - (muon_rate * wide_scale) * returned[4:6, :, :VAL]
    new_out = out_w * shrink - (muon_rate * wide_scale) * jnp.swapaxes(returned[6:8, :, :VAL], 1, 2)

    first_total = first_total[:, 54:118].reshape(2 * width)
    group_parts = vectors[2:6, :VAL]
    which = jnp.arange(4, dtype=jnp.int32)[:, None] == order[None, :]
    group_whole = jnp.sum(
        jnp.where(which[:, :, None], group_parts[None], 0.0), axis=1
    ).reshape(value_width)
    small_total = jnp.concatenate(
        [first_total, group_whole, vectors[0], vectors[1]]
    )
    moment_new = beta_first * norm_moment + (1.0 - beta_first) * small_total
    second_new = beta_second * norm_second + (1.0 - beta_second) * small_total * small_total
    params_new = norm_params - adam_rate * (moment_new / (1.0 - beta_first**OPT_STEP)) / (
        jnp.sqrt(second_new / (1.0 - beta_second**OPT_STEP)) + adam_eps
    )
    return (
        result,
        input_grad,
        mom_qk,
        mom_vg,
        mom_mlp,
        mom_out,
        new_qk,
        new_vg,
        new_mlp,
        new_out,
        moment_new,
        second_new,
        params_new,
    )


def solution(mesh):
    fine = Mesh(np.asarray(mesh.devices).reshape(SIZES), AXES)
    by_rows = P(DP + TENSOR, None)
    by_columns = P(None, DP, TENSOR)
    by_out = P(None, TENSOR, DP)
    return jax.shard_map(
        shards,
        mesh=fine,
        in_specs=(
            by_rows,
            by_rows,
            by_columns,
            by_columns,
            by_columns,
            by_out,
            by_columns,
            by_columns,
            by_columns,
            by_out,
            P(),
            P(),
            P(),
            P(TENSOR),
            P(),
            P(),
        ),
        out_specs=(
            by_rows,
            by_rows,
            by_columns,
            by_columns,
            by_columns,
            by_out,
            by_columns,
            by_columns,
            by_columns,
            by_out,
            P(),
            P(),
            P(),
        ),
        check_vma=False,
    )
```

```python
import math

import jax
import jax.numpy as jnp
import numpy as np
from jax import lax
from jax.experimental import pallas as pl
from jax.experimental.pallas import tpu as pltpu
from jax.sharding import Mesh
from jax.sharding import PartitionSpec as P

HEADS = 4
NS_ITERS = 5
OPT_STEP = 10
KEY = 256
VAL = 432
LANES = 512
BLOCK = 32

norm_eps = 1e-05
group_eps = 0.01
ns_first = 3.4445
ns_second = -4.775
ns_third = 2.0315
muon_rate = 0.15
muon_beta = 0.95
decay_rate = 0.01
adam_rate = 0.6
beta_first = 0.9
beta_second = 0.95
adam_eps = 1e-08

AXES = ("y_lo", "z_hi", "z_lo", "x", "y_hi", "core")
SIZES = (2, 2, 2, 4, 2, 2)
DP = ("y_lo", "z_hi", "z_lo", "x")
PLANE = ("z_hi", "z_lo", "x")
TENSOR = ("y_hi", "core")
bf16 = jnp.bfloat16
f32 = jnp.float32


def swap(values, axis):
    return lax.ppermute(values, axis, [(0, 1), (1, 0)])


def dot(left, right, dims):
    return lax.dot_general(left, right, (dims, ((), ())), preferred_element_type=f32)


def nn(left, right):
    return dot(left, right, ((1,), (0,)))


def nt(left, right):
    return dot(left, right, ((1,), (1,)))


def tn(left, right):
    return dot(left, right, ((0,), (0,)))


def split(values):
    high = lax.reduce_precision(values, 8, 7)
    return high.astype(bf16), (values - high).astype(bf16)


def widen(values):
    return jnp.pad(values, ((0, 0),) * (values.ndim - 1) + ((0, LANES - values.shape[-1]),))


def tensor_gather(own):
    far = swap(own, "y_hi")
    return [own, far, swap(own, "core"), swap(far, "core")]


def half_sum(own, other):
    half = own.shape[0] // 2
    arrived = swap(other, "core")
    far = (own[half:] + arrived[half:].astype(f32)).astype(bf16)
    return own[:half] + arrived[:half].astype(f32), far


def tensor_sum(own, other):
    near, far = half_sum(own, other)
    return near, swap(far, "y_hi")


def together(first, second):
    return lax.optimization_barrier((first, second))


def normalize(values):
    centre = values - jnp.mean(values, axis=-1, keepdims=True)
    spread = lax.rsqrt(jnp.mean(centre * centre, axis=-1, keepdims=True) + norm_eps)
    return centre * spread, spread


def norm_back(grad_out, gain, normed, spread):
    grad_normed = grad_out * gain
    return spread * (
        grad_normed
        - jnp.mean(grad_normed, axis=-1, keepdims=True)
        - normed * jnp.mean(grad_normed * normed, axis=-1, keepdims=True)
    )


def pairs_apart(values):
    shape = values.shape
    return jnp.swapaxes(values.reshape(shape[:-1] + (KEY // 2, 2)), -1, -2).reshape(shape)


def pairs_together(values):
    shape = values.shape
    return jnp.swapaxes(values.reshape(shape[:-1] + (2, KEY // 2)), -1, -2).reshape(shape)


def sequence_labels(seq_length, seq_group, group, place):
    mine = seq_group == group
    lengths = jnp.where(mine, seq_length, 0)
    ends = jnp.cumsum(lengths, dtype=jnp.int32)
    starts = ends - lengths
    inside = mine[None, :] & (place[:, None] >= starts[None, :]) & (place[:, None] < ends[None, :])
    number = jnp.arange(1, seq_length.shape[0] + 1, dtype=jnp.int32)
    return jnp.sum(jnp.where(inside, number[None, :], 0), axis=1, dtype=jnp.int32)


WIDTH = 1024
TILE = WIDTH // 2
EARLY = 1408
LATE = 1920
NS_TILE = 256


ROWS = [pl.ds(TILE * i, TILE) for i in range(WIDTH // TILE)]


STORES = 12


def in_vmem(kernel, name, out_shape, scratch, *operands):
    arrays, pieces, local = [], [], []
    for a in operands:
        parts = a if isinstance(a, list) else [a]
        top, piece = 0, []
        for part in parts:
            array, first, columns, *free = (
                part if isinstance(part, tuple) else (part, 0, part.shape[1])
            )
            whole = columns == array.shape[1]
            piece.append((len(arrays), None if whole else (first, columns), top, array.shape[0]))
            fixed = not free and (not isinstance(a, list) or isinstance(part, tuple))
            arrays.append(pltpu.with_memory_space_constraint(array, pltpu.HBM) if fixed else array)
            top += array.shape[0]
        pieces.append(piece)
        local.append(pltpu.VMEM((top, columns), array.dtype))
    n_in, n_out, n_local = len(arrays), len(out_shape), len(local)

    def body(*refs):
        ins, outs = refs[:n_in], refs[n_in : n_in + n_out]
        refs = refs[n_in + n_out :]
        local_in, local_out = refs[:n_local], refs[n_local : n_local + n_out]
        sem_in, sem_out = refs[n_local + n_out : n_local + n_out + 2]
        loads = []
        for i, piece in enumerate(pieces):
            loads.append([])
            for which, cut, top, rows in piece:
                source = ins[which] if cut is None else ins[which].at[:, pl.ds(*cut)]
                target = local_in[i] if len(piece) == 1 else local_in[i].at[pl.ds(top, rows), :]
                loads[i].append(pltpu.make_async_copy(source, target, sem_in.at[which]))
                loads[i][-1].start()
        pending = set(range(n_local))
        stores = []

        def ready(*which):
            for i in which:
                if i in pending:
                    pending.remove(i)
                    for load in loads[i]:
                        load.wait()

        def done(i, *index):
            source, target = local_out[i], outs[i]
            if index:
                source, target = source.at[index], target.at[index]
            stores.append(pltpu.make_async_copy(source, target, sem_out.at[len(stores)]))
            stores[-1].start()

        kernel(ready, done, *local_in, *local_out, *refs[n_local + n_out + 2 :])
        ready(*range(n_local))
        for store in stores:
            store.wait()

    local += [pltpu.VMEM(a.shape, a.dtype) for a in out_shape]
    held = sum(math.prod(a.shape) * jnp.dtype(a.dtype).itemsize for a in local)
    return pl.pallas_call(
        body,
        out_shape=[pltpu.HBM(a.shape, a.dtype) for a in out_shape],
        in_specs=[pl.BlockSpec(memory_space=pl.ANY)] * n_in,
        out_specs=[pl.BlockSpec(memory_space=pltpu.HBM)] * n_out,
        scratch_shapes=local
        + [pltpu.SemaphoreType.DMA((n_in,)), pltpu.SemaphoreType.DMA((STORES,))]
        + scratch,
        compiler_params=pltpu.CompilerParams(vmem_limit_bytes=held + 14 * 2**20),
        cost_estimate=pl.CostEstimate(flops=1, bytes_accessed=1, transcendentals=0),
        name=name,
    )(*arrays)


def put_halves(done, i, part, own_ref, other_ref, own, other):
    if i == 0:
        own_ref[...] = part
        done(own)
    else:
        other_ref[...] = part.astype(bf16)
        done(other)


def turn(first, second, cos_table, sin_table):
    return first * cos_table - second * sin_table, second * cos_table + first * sin_table


def masked(scores, rows, cols_ref, line_ref):
    label, place = cols_ref[rows, 0:1], cols_ref[rows, 1:2]
    linked = (label == line_ref[0:1, :]) & (label > 0.0) & (place >= line_ref[1:2, :])
    return jnp.where(linked, scores * (cols_ref[rows, 2:3] * line_ref[2:3, :]), 0.0)


def retention_kernel(
    ready, done, h_ref, wqk_ref, wv_ref, wg_ref, wo_ref, turn_ref, cols_ref, line_ref, gain_ref,
    q_ref, k_ref, v_ref, p_ref, gate_ref, hat_ref, inv_ref, mixed_ref, own_ref, other_ref,
):
    half = KEY // 2
    ready(0, 1, 5)
    for rows in ROWS:
        cos_table, sin_table = turn_ref[rows, :half], turn_ref[rows, half:]
        both = nn(h_ref[rows, :], wqk_ref[...])
        query, keys = both[:, :KEY], both[:, KEY:] * KEY**-0.5
        first, second = turn(query[:, :half], query[:, half:], cos_table, sin_table)
        q_ref[rows, 0:half] = first.astype(bf16)
        q_ref[rows, half:KEY] = second.astype(bf16)
        first, second = turn(keys[:, :half], keys[:, half:], cos_table, sin_table)
        k_ref[rows, 0:half] = first.astype(bf16)
        k_ref[rows, half:KEY] = second.astype(bf16)
    done(0)
    done(1)
    ready(2)
    for rows in ROWS:
        v_ref[rows, :] = nn(h_ref[rows, :], wv_ref[...]).astype(bf16)
    done(2)
    ready(3)
    for rows in ROWS:
        gate_ref[rows, :] = nn(h_ref[rows, :], wg_ref[...])
    done(4)
    ready(4, 6, 7, 8)
    for i, rows in reversed(list(enumerate(ROWS))):
        weights = masked(nt(q_ref[rows, :], k_ref[...]), rows, cols_ref, line_ref).astype(bf16)
        p_ref[rows, :] = weights
        done(3, rows)
        retained = nn(weights, v_ref[...])
        inverse = lax.rsqrt(
            jnp.sum(retained * retained, axis=-1, keepdims=True) * (1.0 / VAL) + group_eps
        )
        inv_ref[rows, :] = jnp.broadcast_to(inverse, (TILE, 128))
        hat = retained * inverse
        hat_ref[rows, :] = hat
        done(5, rows)
        gate = gate_ref[rows, :]
        swish = gate * (1.0 / (1.0 + jnp.exp(-gate)))
        mixed = (hat * gain_ref[...] * swish).astype(bf16)
        mixed_ref[rows, :] = mixed
        put_halves(done, i, nt(mixed, wo_ref[...]), own_ref, other_ref, 8, 9)
    done(6)
    done(7)


def retention(*operands):
    shape = jax.ShapeDtypeStruct
    return in_vmem(
        retention_kernel,
        "retention",
        [
            shape((WIDTH, KEY), bf16),
            shape((WIDTH, KEY), bf16),
            shape((WIDTH, LANES), bf16),
            shape((WIDTH, WIDTH), bf16),
            shape((WIDTH, LANES), f32),
            shape((WIDTH, LANES), f32),
            shape((WIDTH, 128), f32),
            shape((WIDTH, LANES), bf16),
            shape((WIDTH // 2, WIDTH), f32),
            shape((WIDTH // 2, WIDTH), bf16),
        ],
        [],
        *operands,
    )


def feed_kernel(
    ready, done, h_ref, w1_ref, w2_ref, cot_ref, w3_ref,
    hidden_ref, gate_ref, up_ref, own_ref, other_ref,
):
    for i, rows in reversed(list(enumerate(ROWS))):
        ready(0, 1)
        pre_gate = nn(h_ref[rows, :], w1_ref[...])
        ready(2)
        pre_up = nn(h_ref[rows, :], w2_ref[...])
        ready(3, 4)
        grad_hidden = nn(cot_ref[rows, :], w3_ref[...])
        cumulative = 0.5 * (1.0 + lax.erf(pre_gate * (1.0 / math.sqrt(2.0))))
        density = jnp.exp(-0.5 * pre_gate * pre_gate) * (1.0 / math.sqrt(2.0 * math.pi))
        gelu_gate = pre_gate * cumulative
        hidden_ref[rows, :] = (gelu_gate * pre_up).astype(bf16)
        grad_gate = (grad_hidden * pre_up * (cumulative + pre_gate * density)).astype(bf16)
        grad_up = (grad_hidden * gelu_gate).astype(bf16)
        gate_ref[rows, :] = grad_gate
        up_ref[rows, :] = grad_up
        for k in range(3):
            done(k, rows)
        part = nt(grad_gate, w1_ref[...]) + nt(grad_up, w2_ref[...])
        put_halves(done, i, part, own_ref, other_ref, 3, 4)


def feed(*operands):
    shape = jax.ShapeDtypeStruct
    return in_vmem(
        feed_kernel,
        "feed_forward",
        [shape((WIDTH, LANES), bf16)] * 3
        + [shape((WIDTH // 2, WIDTH), f32), shape((WIDTH // 2, WIDTH), bf16)],
        [],
        *operands,
    )


def early_kernel(
    ready, done, h_ref, gate_ref, up_ref, cot_ref, hidden_ref, w3_ref, out_ref, own_ref, other_ref
):
    for j, (left, right) in enumerate(
        ((h_ref, gate_ref), (h_ref, up_ref), (cot_ref, hidden_ref))
    ):
        ready(*((0, 1), (2,), (3, 4))[j])
        columns = pl.ds(VAL * j, VAL)
        for i, at in enumerate(ROWS):
            part = tn(left[:, at], right[...]).astype(bf16)[:, :VAL]
            out_ref[:, i, :, columns] = part.reshape(16, BLOCK, VAL)
    out_ref[:, :, :, 3 * VAL : EARLY] = jnp.zeros((16, 2, BLOCK, EARLY - 3 * VAL), bf16)
    done(0)
    ready(5)
    for i, rows in reversed(list(enumerate(ROWS))):
        put_halves(done, i, nt(hidden_ref[rows, :], w3_ref[...]), own_ref, other_ref, 1, 2)


def early_grads(*operands):
    shape = jax.ShapeDtypeStruct
    return in_vmem(
        early_kernel,
        "feed_forward_grads",
        [
            shape((16, 2, BLOCK, EARLY), bf16),
            shape((WIDTH // 2, WIDTH), f32),
            shape((WIDTH // 2, WIDTH), bf16),
        ],
        [],
        *operands,
    )


def back_gate_kernel(
    ready, done, grad_ref, w_ref, gate_ref, hat_ref, inv_ref, gain_ref, gate_out, ret_out, gain_out
):
    total = jnp.zeros((1, LANES), f32)
    for rows in ROWS:
        ready(0, 1)
        grad_mixed = nn(grad_ref[rows, :], w_ref[...])
        ready(2, 3, 4, 5)
        gain = gain_ref[...]
        gate, hat, inverse = gate_ref[rows, :], hat_ref[rows, :], inv_ref[rows, 0:1]
        sig = 1.0 / (1.0 + jnp.exp(-gate))
        swish = gate * sig
        grad_grouped = grad_mixed * swish
        gate_out[rows, :] = (
            grad_mixed * (hat * gain) * (sig + swish * (1.0 - sig))
        ).astype(bf16)
        done(0, rows)
        total += jnp.sum(grad_grouped * hat, axis=0, keepdims=True)
        grad_hat = grad_grouped * gain
        inner = jnp.sum(grad_hat * hat, axis=-1, keepdims=True) * (1.0 / VAL)
        ret_out[rows, :] = (inverse * (grad_hat - hat * inner)).astype(bf16)
        done(1, rows)
    gain_out[...] = total
    done(2)


def back_scores_kernel(
    ready, done, ret_ref, v_ref, cols_ref, line_ref, k_ref, turn_ref, p_ref, q_ref,
    q_out, k_out, v_out, scores,
):
    half = KEY // 2
    ready(0, 1, 2, 3)
    for rows in ROWS:
        part = masked(nt(ret_ref[rows, :], v_ref[...]), rows, cols_ref, line_ref).astype(bf16)
        scores[rows, :] = part
        ready(4, 5)
        turned = nn(part, k_ref[...])
        first, second = turn(
            turned[:, :half], turned[:, half:], turn_ref[rows, :half], -turn_ref[rows, half:]
        )
        q_out[rows, 0:half] = first.astype(bf16)
        q_out[rows, half:KEY] = second.astype(bf16)
    done(0)
    ready(6, 7)
    for rows in ROWS:
        v_out[rows, :] = tn(p_ref[:, rows], ret_ref[...]).astype(bf16)
        done(2, rows)
    for rows in ROWS:
        turned = tn(scores[:, rows], q_ref[...])
        first, second = turn(
            turned[:, :half], turned[:, half:], turn_ref[rows, :half], -turn_ref[rows, half:]
        )
        k_out[rows, 0:half] = first.astype(bf16)
        k_out[rows, half:KEY] = second.astype(bf16)
    done(1)


def late_kernel(
    ready, done, grad_ref, mixed_ref, h_ref, gate_ref, v_ref, ride_ref, q_ref, k_ref, out_ref
):
    ready(0, 1)
    for rows in ROWS:
        part = tn(grad_ref[:, rows], mixed_ref[...]).astype(bf16)
        out_ref[rows, 2 * KEY + 2 * VAL : 2 * KEY + 3 * VAL] = part[:, :VAL]
    ready(2, 3)
    for rows in ROWS:
        part = tn(h_ref[:, rows], gate_ref[...]).astype(bf16)
        out_ref[rows, 2 * KEY + VAL : 2 * KEY + 2 * VAL] = part[:, :VAL]
    ready(4, 5)
    for rows in ROWS:
        part = tn(h_ref[:, rows], v_ref[...]).astype(bf16)
        out_ref[rows, 2 * KEY : 2 * KEY + VAL] = part[:, :VAL]
        out_ref[rows, 2 * KEY + 3 * VAL : LATE] = ride_ref[rows, : LATE - 2 * KEY - 3 * VAL]
    ready(6, 7)
    for rows in ROWS:
        left = h_ref[:, rows]
        out_ref[rows, 0:KEY] = tn(left, q_ref[...]).astype(bf16)
        out_ref[rows, KEY : 2 * KEY] = (tn(left, k_ref[...]) * KEY**-0.5).astype(bf16)
    done(0)


def late_grads(*operands):
    return in_vmem(
        late_kernel,
        "retention_grads",
        [jax.ShapeDtypeStruct((WIDTH, LATE), bf16)],
        [],
        *operands,
    )[0]


def input_kernel(
    ready, done, gate_ref, wg_ref, v_ref, wv_ref, q_ref, k_ref, wqk_ref, own_ref, other_ref
):
    for i, rows in reversed(list(enumerate(ROWS))):
        ready(0, 1)
        part = nt(gate_ref[rows, :], wg_ref[...])
        ready(2, 3)
        part += nt(v_ref[rows, :], wv_ref[...])
        ready(4, 5, 6)
        part += nt(q_ref[rows, :], wqk_ref[:, 0:KEY])
        part += nt(k_ref[rows, :], wqk_ref[:, KEY : 2 * KEY]) * KEY**-0.5
        put_halves(done, i, part, own_ref, other_ref, 0, 1)


def back_kernel(
    ready, done, grad_ref, wo_ref, gate_ref, hat_ref, inv_ref, gain_ref, v_ref, cols_ref, line_ref,
    k_ref, turn_ref, p_ref, q_ref, wg_ref, wv_ref, wqk_ref,
    gate_out, gain_out, q_out, k_out, v_out, own_ref, other_ref, ret, scores,
):
    def numbered(call, table):
        def mapped(i, *index):
            if table[i] is not None:
                call(table[i], *index)

        return mapped

    def waits(table):
        mapped = numbered(ready, table)
        return lambda *which: [mapped(i) for i in which]

    back_gate_kernel(
        ready, numbered(done, (0, None, 1)),
        grad_ref, wo_ref, gate_ref, hat_ref, inv_ref, gain_ref, gate_out, ret, gain_out,
    )
    back_scores_kernel(
        waits((None, 6, 7, 8, 9, 10, 11, 12)), numbered(done, (2, 3, 4)),
        ret, v_ref, cols_ref, line_ref, k_ref, turn_ref, p_ref, q_ref, q_out, k_out, v_out, scores,
    )
    input_kernel(
        waits((None, 13, None, 14, None, None, 15)), numbered(done, (5, 6)),
        gate_out, wg_ref, v_out, wv_ref, q_out, k_out, wqk_ref, own_ref, other_ref,
    )


def retention_back(*operands):
    shape = jax.ShapeDtypeStruct
    return in_vmem(
        back_kernel,
        "retention_backward",
        [
            shape((WIDTH, LANES), bf16),
            shape((1, LANES), f32),
            shape((WIDTH, KEY), bf16),
            shape((WIDTH, KEY), bf16),
            shape((WIDTH, LANES), bf16),
            shape((WIDTH // 2, WIDTH), f32),
            shape((WIDTH // 2, WIDTH), bf16),
        ],
        [pltpu.VMEM((WIDTH, LANES), bf16), pltpu.VMEM((WIDTH, WIDTH), bf16)],
        *operands,
    )


def iterate_kernel(
    chunk_ref, near_ref, far_ref, out_ref, vector_ref, first_ref, whole, gram, high, low, shifted, rest, prod, prod_b, own, own_b
):
    tiles = WIDTH // NS_TILE
    at = [pl.ds(NS_TILE * i, NS_TILE) for i in range(tiles)]
    eye = (
        lax.broadcasted_iota(jnp.int32, (NS_TILE, NS_TILE), 0)
        == lax.broadcasted_iota(jnp.int32, (NS_TILE, NS_TILE), 1)
    ).astype(f32)
    keep = lax.broadcasted_iota(jnp.int32, (WIDTH, 128), 1) < VAL - 384
    riders = jnp.zeros((WIDTH, 128), f32)
    for p in range(4):
        source = near_ref if p < 2 else far_ref
        piece = source[:, p % 2].reshape(WIDTH, LANES)
        whole[p, :, 0:384] = piece[:, 0:384]
        whole[p, :, 384:512] = jnp.where(keep, piece[:, 384:512], jnp.zeros((), bf16))
        ride = piece[:, 384:512].astype(f32)
        riders += ride
        lines = ride.T
        vector_ref[2 + p : 3 + p, :] = lines[50:51, :] + lines[53:54, :]
    lines = riders.T
    vector_ref[0:2, :] = lines[48:50, :] + lines[51:53, :]
    vector_ref[6:8, :] = jnp.zeros((2, WIDTH), f32)
    first_ref[...] = jnp.sum(riders.reshape(WIDTH // BLOCK, BLOCK, 128), axis=0)

    trace = jnp.float32(0.0)
    for i in range(tiles):
        for j in range(i, tiles):
            block = jnp.zeros((NS_TILE, NS_TILE), f32)
            for p in range(4):
                block += nt(whole[p, at[i], :], whole[p, at[j], :])
            gram[at[i], at[j]] = block
            if i == j:
                trace += jnp.sum(block * eye)
    inverse = 1.0 / (jnp.sqrt(trace) + 1e-07)
    for q in range(4):

        @pl.when(chunk_ref[0] == q)
        def _():
            own[...] = whole[0, :, 128 * q : 128 * (q + 1)].astype(f32) * inverse

    def store(i, j, block, mean):
        gram[at[i], at[j]] = block
        top = block.astype(bf16)
        bottom = (block - top.astype(f32)).astype(bf16)
        high[at[i], at[j]] = top
        low[at[i], at[j]] = bottom
        if i == j:
            shifted[at[i], at[j]] = (block - mean * eye).astype(bf16)
        else:
            shifted[at[i], at[j]] = top
            top = top.T
            high[at[j], at[i]] = top
            low[at[j], at[i]] = bottom.T
            shifted[at[j], at[i]] = top

    mean = trace * inverse * inverse * (1.0 / WIDTH)
    for i in range(tiles):
        for j in range(i, tiles):
            store(i, j, gram[at[i], at[j]] * (inverse * inverse), mean)

    def advance(mean):
        level = ns_second * mean + ns_third * mean * mean
        alpha = ns_first + level
        for i in range(tiles):
            for j in range(i, tiles):
                block = (ns_second + 2.0 * ns_third * mean) * gram[at[i], at[j]] + ns_third * nn(
                    shifted[at[i], :], shifted[:, at[j]]
                )
                if i == j:
                    block -= (ns_third * mean * mean + level) * eye
                block = block.astype(bf16)
                rest[at[i], at[j]] = block
                if i < j:
                    rest[at[j], at[i]] = block.T
        values = own[...]
        top = values.astype(bf16)
        own_b[:, 0:128] = top
        own_b[:, 128:256] = (values - top.astype(f32)).astype(bf16)
        for i in range(tiles):
            moved = nn(rest[at[i], :], own_b[...])
            own[at[i], :] = alpha * own[at[i], :] + (moved[:, 0:128] + moved[:, 128:256])
        return alpha

    def turn(_, mean):
        alpha = advance(mean)
        for i in range(tiles):
            for j in range(tiles):
                block = nn(high[at[i], :], rest[:, at[j]]) + nn(low[at[i], :], rest[:, at[j]])
                prod[at[i], at[j]] = block
                prod_b[at[i], at[j]] = block.astype(bf16)
        def moved(i, j):
            return (
                (alpha * alpha) * gram[at[i], at[j]]
                + alpha * (prod[at[i], at[j]] + prod[at[j], at[i]].T)
                + nn(rest[at[i], :], prod_b[:, at[j]])
            )

        trace = jnp.float32(0.0)
        for i in range(tiles):
            block = moved(i, i)
            block = 0.5 * (block + block.T)
            gram[at[i], at[i]] = block
            trace += jnp.sum(block * eye)
        later = trace * (1.0 / WIDTH)
        for i in range(tiles):
            store(i, i, gram[at[i], at[i]], later)
            for j in range(i + 1, tiles):
                store(i, j, moved(i, j), later)
        return later

    for step in range(NS_ITERS - 1):
        mean = turn(step, mean)
    advance(mean)
    out_ref[...] = own[...].astype(bf16)


def orthogonal(chunk, near, far):
    square = (WIDTH, WIDTH)
    return pl.pallas_call(
        iterate_kernel,
        out_shape=[
            jax.ShapeDtypeStruct((WIDTH, 128), bf16),
            jax.ShapeDtypeStruct((8, WIDTH), f32),
            jax.ShapeDtypeStruct((BLOCK, 128), f32),
        ],
        in_specs=[pl.BlockSpec(memory_space=pltpu.SMEM)]
        + [pl.BlockSpec(memory_space=pltpu.VMEM)] * 2,
        out_specs=[pl.BlockSpec(memory_space=pltpu.VMEM)] * 3,
        scratch_shapes=[
            pltpu.VMEM((4, WIDTH, LANES), bf16),
            pltpu.VMEM(square, f32),
            pltpu.VMEM(square, bf16),
            pltpu.VMEM(square, bf16),
            pltpu.VMEM(square, bf16),
            pltpu.VMEM(square, bf16),
            pltpu.VMEM(square, f32),
            pltpu.VMEM(square, bf16),
            pltpu.VMEM((WIDTH, 128), f32),
            pltpu.VMEM((WIDTH, 256), bf16),
        ],
        compiler_params=pltpu.CompilerParams(vmem_limit_bytes=48 * 2**20),
        cost_estimate=pl.CostEstimate(
            flops=42 * 10**9, bytes_accessed=5 * 2**20, transcendentals=0
        ),
        name="orthogonalize",
    )(chunk, near, far)


def shards(
    tokens,
    cotangent,
    qk_w,
    vg_w,
    mlp_w,
    out_w,
    qk_mom,
    vg_mom,
    mlp_mom,
    out_mom,
    norm_params,
    norm_moment,
    norm_second,
    decay_gap,
    seq_length,
    seq_group,
):
    rows, width = tokens.shape
    slots = 4 * rows
    groups = 32
    value_width = 4 * VAL
    key_scale = KEY ** (-0.5)
    dp_index = lax.axis_index(DP)
    tensor_index = lax.axis_index(TENSOR)
    chunk_index = lax.axis_index(("y_lo", "z_hi"))

    gain_one = norm_params[0:width]
    shift_one = norm_params[width : 2 * width]
    group_gain = jnp.pad(
        lax.dynamic_slice_in_dim(norm_params, 2 * width + tensor_index * VAL, VAL),
        (0, LANES - VAL),
    )
    gain_two = norm_params[2 * width + value_width : 3 * width + value_width]
    shift_two = norm_params[3 * width + value_width : 4 * width + value_width]

    out_rows = jnp.swapaxes(out_w, 1, 2)
    first_half = lax.axis_index("y_lo") == 0

    def weight_rows(parts):
        packed = jnp.concatenate(parts, axis=1).astype(bf16)
        far = swap(packed, "y_lo")
        pair = jnp.stack([jnp.where(first_half, packed, far), jnp.where(first_half, far, packed)])
        return pair

    def weight_gather(pair):
        return lax.all_gather(pair, PLANE, axis=1, tiled=True).reshape(width, -1)

    pair_ret = weight_rows(
        [
            pairs_apart(qk_w[0]),
            pairs_apart(qk_w[1]),
            widen(vg_w[0]),
            widen(vg_w[1]),
            widen(out_rows[0]),
        ]
    )
    (tokens_first, mlp_later), pair_ret = together((tokens, mlp_w), pair_ret)
    gathered = weight_gather(pair_ret)
    w_qk, w_v, w_g, w_o = ((gathered, LANES * i, LANES) for i in range(4))
    pair_ff = weight_rows([widen(mlp_later[0]), widen(mlp_later[1]), widen(out_rows[1])])

    whole_tokens = jnp.concatenate(tensor_gather(tokens_first), axis=0)
    order = jnp.stack([tensor_index, tensor_index ^ 2, tensor_index ^ 1, tensor_index ^ 3])
    place = (order[:, None] * rows + jnp.arange(rows, dtype=jnp.int32)[None, :]).reshape(slots)

    freqs = 1.0 / 10000.0 ** np.linspace(0.0, 1.0, KEY // 2)
    angles = np.arange(slots)[:, None] * freqs[None, :]
    tables = jnp.asarray(
        np.concatenate([np.cos(angles), np.sin(angles)], axis=1).astype(np.float32)
    ).reshape(4, rows, KEY)
    turned = tables[order].reshape(slots, KEY)

    labels = sequence_labels(seq_length, seq_group, dp_index, place)
    log_decay = jnp.log1p(-decay_gap[0])
    away = (place - slots // 2).astype(f32) * log_decay
    label_place = [labels.astype(f32), place.astype(f32)]
    columns = jnp.pad(jnp.stack(label_place + [jnp.exp(away)], axis=1), ((0, 0), (0, 125)))
    line = jnp.pad(jnp.stack(label_place + [jnp.exp(-away)], axis=0), ((0, 5), (0, 0)))
    gain_line = group_gain[None, :]

    hat_one, _ = normalize(whole_tokens.astype(f32))
    whole_one = (hat_one * gain_one + shift_one).astype(bf16)
    prepared = (whole_one, turned, columns, line)
    cot_first, (whole_one, turned, columns, line) = together(cotangent, prepared)
    whole_cot = tensor_gather(cot_first)
    (gain_line, pair_ff), whole_cot = together((gain_line, pair_ff), whole_cot)
    whole_cot = [(part, 0, width) for part in whole_cot]
    gathered_ff = weight_gather(pair_ff)
    w_1, w_2, w_3 = ((gathered_ff, LANES * i, LANES) for i in range(3))
    query, keys, values, weights, gate, hat_group, inv_group, mixed, own, other = retention(
        whole_one, w_qk, w_v, w_g, w_o, turned, columns, line, gain_line
    )
    near, far = tensor_sum(own, other)
    middle = tokens.astype(f32) + near + far.astype(f32)
    hat_two, inv_two = normalize(middle)
    whole_two = tensor_gather((hat_two * gain_two + shift_two).astype(bf16))
    hidden, grad_gate, grad_up, own, other = feed(whole_two, w_1, w_2, whole_cot, w_3)
    near, far = tensor_sum(own, other)
    early, out_own, out_other = early_grads(whole_two, grad_gate, grad_up, whole_cot, hidden, w_3)
    far, out_other = together(far, out_other)
    grad_normed_two = near + far.astype(f32)
    grad_middle = cotangent.astype(f32) + norm_back(grad_normed_two, gain_two, hat_two, inv_two)
    grad_first = grad_middle.astype(bf16)
    grad_far, grad_core = swap(grad_first, "y_hi"), swap(grad_first, "core")
    out_near, out_far = half_sum(out_own, out_other)
    grad_far, out_far = together(grad_far, out_far)
    grad_one = [grad_first, grad_far, grad_core, swap(grad_far, "core")]

    early_in = lax.all_to_all(early, PLANE, split_axis=0, concat_axis=0, tiled=True)
    early_halves = jnp.sum(early_in.astype(f32), axis=0)
    early_far = swap(
        jnp.where(first_half, early_halves[1], early_halves[0]).astype(bf16), "y_lo"
    )
    gain_two_grad = jnp.sum(grad_normed_two * hat_two, axis=0)
    shift_two_grad = jnp.sum(grad_normed_two, axis=0)

    grad_gate_ret, group_gain_grad, grad_query, grad_key, grad_values, own, other = retention_back(
        grad_one, w_o, gate, hat_group, inv_group, gain_line, values, columns, line, keys, turned,
        weights, query, w_g, w_v, w_qk,
    )
    other, grad_values = together(other, grad_values)
    near, far = half_sum(own, other)
    small = jnp.stack(
        [gain_two_grad, shift_two_grad, jnp.pad(group_gain_grad[0], (0, width - LANES))], axis=1
    )
    small_high, small_low = split(small)
    riders = jnp.pad(
        jnp.concatenate([small_high, small_low], axis=1), ((0, 0), (0, 128 - 6))
    )
    late = late_grads(
        grad_one, mixed, whole_one, grad_gate_ret, grad_values, riders, grad_query, grad_key
    )
    far = swap(far, "y_hi")
    far, late = together(far, late)
    grad_normed_one = near + far.astype(f32)
    late_in = lax.all_to_all(
        late.reshape(groups, BLOCK, -1), DP, split_axis=0, concat_axis=0, tiled=True
    )
    own_hat, own_inv = normalize(tokens.astype(f32))
    gain_one_grad = jnp.sum(grad_normed_one * own_hat, axis=0)
    shift_one_grad = jnp.sum(grad_normed_one, axis=0)
    input_grad = grad_middle + norm_back(grad_normed_one, gain_one, own_hat, own_inv)
    (gain_one_grad, input_grad), early_far = together((gain_one_grad, input_grad), early_far)
    early_sum = jnp.where(first_half, early_halves[0], early_halves[1]) + early_far.astype(f32)

    late_sum = jnp.sum(late_in.astype(f32), axis=0)
    first_value = 2 * KEY
    at = [first_value + VAL * i for i in range(4)]
    small_sum = late_sum[:, at[3] : at[3] + 6]
    small_sum = small_sum[:, :3] + small_sum[:, 3:]

    grad_qk = pairs_together(jnp.stack([late_sum[:, 0:256], late_sum[:, 256:512]]))
    grad_vg = jnp.stack([late_sum[:, at[0] : at[1]], late_sum[:, at[1] : at[2]]])
    grad_mlp = jnp.stack([early_sum[:, 0:VAL], early_sum[:, VAL : 2 * VAL]])
    grad_out_t = jnp.stack([late_sum[:, at[2] : at[3]], early_sum[:, 2 * VAL : 3 * VAL]])
    mom_qk = muon_beta * qk_mom + grad_qk
    mom_vg = muon_beta * vg_mom + grad_vg
    mom_mlp = muon_beta * mlp_mom + grad_mlp
    mom_out = muon_beta * out_mom + jnp.swapaxes(grad_out_t, 1, 2)

    piece_high, piece_low = split(small_sum)
    first_norm = jnp.concatenate([gain_one_grad, shift_one_grad]).astype(bf16)
    extra = jnp.pad(
        jnp.concatenate([piece_high, piece_low, first_norm.reshape(BLOCK, 64)], axis=1),
        ((0, 0), (VAL, LANES - VAL - 70)),
    )
    stacked = (
        jnp.concatenate(
            [widen(mom_qk), widen(mom_vg), widen(mom_mlp), widen(jnp.swapaxes(mom_out, 1, 2))],
            axis=0,
        ).astype(bf16)
        + extra[None]
    )
    both = jnp.stack([stacked, swap(stacked, "y_hi")], axis=1)
    spread = jnp.broadcast_to(both[None], (4,) + both.shape).reshape((groups,) + both.shape[1:])
    arrived = lax.all_to_all(spread, DP, split_axis=0, concat_axis=0, tiled=True)
    far = swap(arrived, "core")
    own, vectors, first_total = orthogonal(
        jnp.reshape(chunk_index, (1,)).astype(jnp.int32), arrived, far
    )
    out_far = swap(out_far, "y_hi")
    out_far, own = together(out_far, own)
    result = (middle + out_near + out_far.astype(f32)).astype(bf16)
    returned = lax.all_to_all(
        own.reshape(groups, BLOCK, 128), DP, split_axis=0, concat_axis=0, tiled=True
    ).astype(f32)
    returned = jnp.concatenate([returned[8 * i : 8 * i + 8] for i in range(4)], axis=2)

    shrink = 1.0 - muon_rate * decay_rate
    square_scale = 0.2 * math.sqrt(width)
    wide_scale = 0.2 * math.sqrt(max(width, value_width))
    new_qk = qk_w * shrink - (muon_rate * square_scale) * returned[0:2, :, :KEY]
    new_vg = vg_w * shrink - (muon_rate * wide_scale) * returned[2:4, :, :VAL]
    new_mlp = mlp_w * shrink - (muon_rate * wide_scale) * returned[4:6, :, :VAL]
    new_out = out_w * shrink - (muon_rate * wide_scale) * jnp.swapaxes(returned[6:8, :, :VAL], 1, 2)

    first_total = first_total[:, 54:118].reshape(2 * width)
    group_parts = vectors[2:6, :VAL]
    which = jnp.arange(4, dtype=jnp.int32)[:, None] == order[None, :]
    group_whole = jnp.sum(
        jnp.where(which[:, :, None], group_parts[None], 0.0), axis=1
    ).reshape(value_width)
    small_total = jnp.concatenate(
        [first_total, group_whole, vectors[0], vectors[1]]
    )
    moment_new = beta_first * norm_moment + (1.0 - beta_first) * small_total
    second_new = beta_second * norm_second + (1.0 - beta_second) * small_total * small_total
    params_new = norm_params - adam_rate * (moment_new / (1.0 - beta_first**OPT_STEP)) / (
        jnp.sqrt(second_new / (1.0 - beta_second**OPT_STEP)) + adam_eps
    )
    return (
        result,
        input_grad,
        mom_qk,
        mom_vg,
        mom_mlp,
        mom_out,
        new_qk,
        new_vg,
        new_mlp,
        new_out,
        moment_new,
        second_new,
        params_new,
    )


def solution(mesh):
    fine = Mesh(np.asarray(mesh.devices).reshape(SIZES), AXES)
    by_rows = P(DP + TENSOR, None)
    by_columns = P(None, DP, TENSOR)
    by_out = P(None, TENSOR, DP)
    return jax.shard_map(
        shards,
        mesh=fine,
        in_specs=(
            by_rows,
            by_rows,
            by_columns,
            by_columns,
            by_columns,
            by_out,
            by_columns,
            by_columns,
            by_columns,
            by_out,
            P(),
            P(),
            P(),
            P(TENSOR),
            P(),
            P(),
        ),
        out_specs=(
            by_rows,
            by_rows,
            by_columns,
            by_columns,
            by_columns,
            by_out,
            by_columns,
            by_columns,
            by_columns,
            by_out,
            P(),
            P(),
            P(),
        ),
        check_vma=False,
    )
```

```python
import math

import jax
import jax.numpy as jnp
import numpy as np
from jax import lax
from jax.experimental import pallas as pl
from jax.experimental.pallas import tpu as pltpu
from jax.sharding import Mesh
from jax.sharding import PartitionSpec as P

HEADS = 4
NS_ITERS = 5
OPT_STEP = 10
KEY = 256
VAL = 432
LANES = 512
BLOCK = 32

norm_eps = 1e-05
group_eps = 0.01
ns_first = 3.4445
ns_second = -4.775
ns_third = 2.0315
muon_rate = 0.15
muon_beta = 0.95
decay_rate = 0.01
adam_rate = 0.6
beta_first = 0.9
beta_second = 0.95
adam_eps = 1e-08

AXES = ("y_lo", "z_hi", "z_lo", "x", "y_hi", "core")
SIZES = (2, 2, 2, 4, 2, 2)
DP = ("y_lo", "z_hi", "z_lo", "x")
PLANE = ("z_hi", "z_lo", "x")
TENSOR = ("y_hi", "core")
bf16 = jnp.bfloat16
f32 = jnp.float32


def swap(values, axis):
    return lax.ppermute(values, axis, [(0, 1), (1, 0)])


def dot(left, right, dims):
    return lax.dot_general(left, right, (dims, ((), ())), preferred_element_type=f32)


def nn(left, right):
    return dot(left, right, ((1,), (0,)))


def nt(left, right):
    return dot(left, right, ((1,), (1,)))


def tn(left, right):
    return dot(left, right, ((0,), (0,)))


def split(values):
    high = lax.reduce_precision(values, 8, 7)
    return high.astype(bf16), (values - high).astype(bf16)


def widen(values):
    return jnp.pad(values, ((0, 0),) * (values.ndim - 1) + ((0, LANES - values.shape[-1]),))


def tensor_gather(own):
    far = swap(own, "y_hi")
    return [own, far, swap(own, "core"), swap(far, "core")]


def half_sum(own, other):
    half = own.shape[0] // 2
    arrived = swap(other, "core")
    far = (own[half:] + arrived[half:].astype(f32)).astype(bf16)
    return own[:half] + arrived[:half].astype(f32), far


def tensor_sum(own, other):
    near, far = half_sum(own, other)
    return near, swap(far, "y_hi")


def together(first, second):
    return lax.optimization_barrier((first, second))


def normalize(values):
    centre = values - jnp.mean(values, axis=-1, keepdims=True)
    spread = lax.rsqrt(jnp.mean(centre * centre, axis=-1, keepdims=True) + norm_eps)
    return centre * spread, spread


def norm_back(grad_out, gain, normed, spread):
    grad_normed = grad_out * gain
    return spread * (
        grad_normed
        - jnp.mean(grad_normed, axis=-1, keepdims=True)
        - normed * jnp.mean(grad_normed * normed, axis=-1, keepdims=True)
    )


def pairs_apart(values):
    shape = values.shape
    return jnp.swapaxes(values.reshape(shape[:-1] + (KEY // 2, 2)), -1, -2).reshape(shape)


def pairs_together(values):
    shape = values.shape
    return jnp.swapaxes(values.reshape(shape[:-1] + (2, KEY // 2)), -1, -2).reshape(shape)


def sequence_labels(seq_length, seq_group, group, place):
    mine = seq_group == group
    lengths = jnp.where(mine, seq_length, 0)
    ends = jnp.cumsum(lengths, dtype=jnp.int32)
    starts = ends - lengths
    inside = mine[None, :] & (place[:, None] >= starts[None, :]) & (place[:, None] < ends[None, :])
    number = jnp.arange(1, seq_length.shape[0] + 1, dtype=jnp.int32)
    return jnp.sum(jnp.where(inside, number[None, :], 0), axis=1, dtype=jnp.int32)


WIDTH = 1024
TILE = WIDTH // 2
EARLY = 1408
LATE = 1920
NS_TILE = 256


ROWS = [pl.ds(TILE * i, TILE) for i in range(WIDTH // TILE)]


STORES = 12


def in_vmem(kernel, name, out_shape, scratch, *operands):
    arrays, pieces, local = [], [], []
    for a in operands:
        parts = a if isinstance(a, list) else [a]
        top, piece = 0, []
        for part in parts:
            array, first, columns, *free = (
                part if isinstance(part, tuple) else (part, 0, part.shape[1])
            )
            whole = columns == array.shape[1]
            piece.append((len(arrays), None if whole else (first, columns), top, array.shape[0]))
            fixed = not free and (not isinstance(a, list) or isinstance(part, tuple))
            arrays.append(pltpu.with_memory_space_constraint(array, pltpu.HBM) if fixed else array)
            top += array.shape[0]
        pieces.append(piece)
        local.append(pltpu.VMEM((top, columns), array.dtype))
    n_in, n_out, n_local = len(arrays), len(out_shape), len(local)

    def body(*refs):
        ins, outs = refs[:n_in], refs[n_in : n_in + n_out]
        refs = refs[n_in + n_out :]
        local_in, local_out = refs[:n_local], refs[n_local : n_local + n_out]
        sem_in, sem_out = refs[n_local + n_out : n_local + n_out + 2]
        loads = []
        for i, piece in enumerate(pieces):
            loads.append([])
            for which, cut, top, rows in piece:
                source = ins[which] if cut is None else ins[which].at[:, pl.ds(*cut)]
                target = local_in[i] if len(piece) == 1 else local_in[i].at[pl.ds(top, rows), :]
                loads[i].append(pltpu.make_async_copy(source, target, sem_in.at[which]))
                loads[i][-1].start()
        pending = set(range(n_local))
        stores = []

        def ready(*which):
            for i in which:
                if i in pending:
                    pending.remove(i)
                    for load in loads[i]:
                        load.wait()

        def done(i, *index):
            source, target = local_out[i], outs[i]
            if index:
                source, target = source.at[index], target.at[index]
            stores.append(pltpu.make_async_copy(source, target, sem_out.at[len(stores)]))
            stores[-1].start()

        kernel(ready, done, *local_in, *local_out, *refs[n_local + n_out + 2 :])
        ready(*range(n_local))
        for store in stores:
            store.wait()

    local += [pltpu.VMEM(a.shape, a.dtype) for a in out_shape]
    held = sum(math.prod(a.shape) * jnp.dtype(a.dtype).itemsize for a in local)
    return pl.pallas_call(
        body,
        out_shape=[pltpu.HBM(a.shape, a.dtype) for a in out_shape],
        in_specs=[pl.BlockSpec(memory_space=pl.ANY)] * n_in,
        out_specs=[pl.BlockSpec(memory_space=pltpu.HBM)] * n_out,
        scratch_shapes=local
        + [pltpu.SemaphoreType.DMA((n_in,)), pltpu.SemaphoreType.DMA((STORES,))]
        + scratch,
        compiler_params=pltpu.CompilerParams(vmem_limit_bytes=held + 14 * 2**20),
        cost_estimate=pl.CostEstimate(flops=1, bytes_accessed=1, transcendentals=0),
        name=name,
    )(*arrays)


def put_halves(done, i, part, own_ref, other_ref, own, other):
    if i == 0:
        own_ref[...] = part
        done(own)
    else:
        other_ref[...] = part.astype(bf16)
        done(other)


def turn(first, second, cos_table, sin_table):
    return first * cos_table - second * sin_table, second * cos_table + first * sin_table


def masked(scores, rows, cols_ref, line_ref):
    label, place = cols_ref[rows, 0:1], cols_ref[rows, 1:2]
    linked = (label == line_ref[0:1, :]) & (label > 0.0) & (place >= line_ref[1:2, :])
    return jnp.where(linked, scores * (cols_ref[rows, 2:3] * line_ref[2:3, :]), 0.0)


def retention_kernel(
    ready, done, h_ref, wqk_ref, wv_ref, wg_ref, wo_ref, turn_ref, cols_ref, line_ref, gain_ref,
    q_ref, k_ref, v_ref, p_ref, gate_ref, hat_ref, inv_ref, mixed_ref, own_ref, other_ref,
):
    half = KEY // 2
    ready(0, 1, 5)
    for rows in ROWS:
        cos_table, sin_table = turn_ref[rows, :half], turn_ref[rows, half:]
        both = nn(h_ref[rows, :], wqk_ref[...])
        query, keys = both[:, :KEY], both[:, KEY:] * KEY**-0.5
        first, second = turn(query[:, :half], query[:, half:], cos_table, sin_table)
        q_ref[rows, 0:half] = first.astype(bf16)
        q_ref[rows, half:KEY] = second.astype(bf16)
        first, second = turn(keys[:, :half], keys[:, half:], cos_table, sin_table)
        k_ref[rows, 0:half] = first.astype(bf16)
        k_ref[rows, half:KEY] = second.astype(bf16)
    done(0)
    done(1)
    ready(2)
    for rows in ROWS:
        v_ref[rows, :] = nn(h_ref[rows, :], wv_ref[...]).astype(bf16)
    done(2)
    ready(3)
    for rows in ROWS:
        gate_ref[rows, :] = nn(h_ref[rows, :], wg_ref[...])
    done(4)
    ready(4, 6, 7, 8)
    for i, rows in reversed(list(enumerate(ROWS))):
        weights = masked(nt(q_ref[rows, :], k_ref[...]), rows, cols_ref, line_ref).astype(bf16)
        p_ref[rows, :] = weights
        done(3, rows)
        retained = nn(weights, v_ref[...])
        inverse = lax.rsqrt(
            jnp.sum(retained * retained, axis=-1, keepdims=True) * (1.0 / VAL) + group_eps
        )
        inv_ref[rows, :] = jnp.broadcast_to(inverse, (TILE, 128))
        hat = retained * inverse
        hat_ref[rows, :] = hat
        done(5, rows)
        gate = gate_ref[rows, :]
        swish = gate * (1.0 / (1.0 + jnp.exp(-gate)))
        mixed = (hat * gain_ref[...] * swish).astype(bf16)
        mixed_ref[rows, :] = mixed
        put_halves(done, i, nt(mixed, wo_ref[...]), own_ref, other_ref, 8, 9)
    done(6)
    done(7)


def retention(*operands):
    shape = jax.ShapeDtypeStruct
    return in_vmem(
        retention_kernel,
        "retention",
        [
            shape((WIDTH, KEY), bf16),
            shape((WIDTH, KEY), bf16),
            shape((WIDTH, LANES), bf16),
            shape((WIDTH, WIDTH), bf16),
            shape((WIDTH, LANES), f32),
            shape((WIDTH, LANES), f32),
            shape((WIDTH, 128), f32),
            shape((WIDTH, LANES), bf16),
            shape((WIDTH // 2, WIDTH), f32),
            shape((WIDTH // 2, WIDTH), bf16),
        ],
        [],
        *operands,
    )


def feed_kernel(
    ready, done, h_ref, w1_ref, w2_ref, cot_ref, w3_ref,
    hidden_ref, gate_ref, up_ref, own_ref, other_ref,
):
    for i, rows in reversed(list(enumerate(ROWS))):
        ready(0, 1)
        pre_gate = nn(h_ref[rows, :], w1_ref[...])
        ready(2)
        pre_up = nn(h_ref[rows, :], w2_ref[...])
        ready(3, 4)
        grad_hidden = nn(cot_ref[rows, :], w3_ref[...])
        cumulative = 0.5 * (1.0 + lax.erf(pre_gate * (1.0 / math.sqrt(2.0))))
        density = jnp.exp(-0.5 * pre_gate * pre_gate) * (1.0 / math.sqrt(2.0 * math.pi))
        gelu_gate = pre_gate * cumulative
        hidden_ref[rows, :] = (gelu_gate * pre_up).astype(bf16)
        grad_gate = (grad_hidden * pre_up * (cumulative + pre_gate * density)).astype(bf16)
        grad_up = (grad_hidden * gelu_gate).astype(bf16)
        gate_ref[rows, :] = grad_gate
        up_ref[rows, :] = grad_up
        for k in range(3):
            done(k, rows)
        part = nt(grad_gate, w1_ref[...]) + nt(grad_up, w2_ref[...])
        put_halves(done, i, part, own_ref, other_ref, 3, 4)


def feed(*operands):
    shape = jax.ShapeDtypeStruct
    return in_vmem(
        feed_kernel,
        "feed_forward",
        [shape((WIDTH, LANES), bf16)] * 3
        + [shape((WIDTH // 2, WIDTH), f32), shape((WIDTH // 2, WIDTH), bf16)],
        [],
        *operands,
    )


def early_kernel(
    ready, done, h_ref, gate_ref, up_ref, cot_ref, hidden_ref, w3_ref, out_ref, own_ref, other_ref
):
    for j, (left, right) in enumerate(
        ((h_ref, gate_ref), (h_ref, up_ref), (cot_ref, hidden_ref))
    ):
        ready(*((0, 1), (2,), (3, 4))[j])
        columns = pl.ds(VAL * j, VAL)
        for i, at in enumerate(ROWS):
            part = tn(left[:, at], right[...]).astype(bf16)[:, :VAL]
            out_ref[:, i, :, columns] = part.reshape(16, BLOCK, VAL)
    out_ref[:, :, :, 3 * VAL : EARLY] = jnp.zeros((16, 2, BLOCK, EARLY - 3 * VAL), bf16)
    done(0)
    ready(5)
    for i, rows in reversed(list(enumerate(ROWS))):
        put_halves(done, i, nt(hidden_ref[rows, :], w3_ref[...]), own_ref, other_ref, 1, 2)


def early_grads(*operands):
    shape = jax.ShapeDtypeStruct
    return in_vmem(
        early_kernel,
        "feed_forward_grads",
        [
            shape((16, 2, BLOCK, EARLY), bf16),
            shape((WIDTH // 2, WIDTH), f32),
            shape((WIDTH // 2, WIDTH), bf16),
        ],
        [],
        *operands,
    )


def back_gate_kernel(
    ready, done, grad_ref, w_ref, gate_ref, hat_ref, inv_ref, gain_ref, gate_out, ret_out, gain_out
):
    total = jnp.zeros((1, LANES), f32)
    for rows in ROWS:
        ready(0, 1)
        grad_mixed = nn(grad_ref[rows, :], w_ref[...])
        ready(2, 3, 4, 5)
        gain = gain_ref[...]
        gate, hat, inverse = gate_ref[rows, :], hat_ref[rows, :], inv_ref[rows, 0:1]
        sig = 1.0 / (1.0 + jnp.exp(-gate))
        swish = gate * sig
        grad_grouped = grad_mixed * swish
        gate_out[rows, :] = (
            grad_mixed * (hat * gain) * (sig + swish * (1.0 - sig))
        ).astype(bf16)
        done(0, rows)
        total += jnp.sum(grad_grouped * hat, axis=0, keepdims=True)
        grad_hat = grad_grouped * gain
        inner = jnp.sum(grad_hat * hat, axis=-1, keepdims=True) * (1.0 / VAL)
        ret_out[rows, :] = (inverse * (grad_hat - hat * inner)).astype(bf16)
        done(1, rows)
    gain_out[...] = total
    done(2)


def back_scores_kernel(
    ready, done, ret_ref, v_ref, cols_ref, line_ref, k_ref, turn_ref, p_ref, q_ref,
    q_out, k_out, v_out, scores,
):
    half = KEY // 2
    ready(0, 1, 2, 3)
    for rows in ROWS:
        part = masked(nt(ret_ref[rows, :], v_ref[...]), rows, cols_ref, line_ref).astype(bf16)
        scores[rows, :] = part
        ready(4, 5)
        turned = nn(part, k_ref[...])
        first, second = turn(
            turned[:, :half], turned[:, half:], turn_ref[rows, :half], -turn_ref[rows, half:]
        )
        q_out[rows, 0:half] = first.astype(bf16)
        q_out[rows, half:KEY] = second.astype(bf16)
    done(0)
    ready(6, 7)
    for rows in ROWS:
        v_out[rows, :] = tn(p_ref[:, rows], ret_ref[...]).astype(bf16)
        done(2, rows)
    for rows in ROWS:
        turned = tn(scores[:, rows], q_ref[...])
        first, second = turn(
            turned[:, :half], turned[:, half:], turn_ref[rows, :half], -turn_ref[rows, half:]
        )
        k_out[rows, 0:half] = first.astype(bf16)
        k_out[rows, half:KEY] = second.astype(bf16)
    done(1)


def late_kernel(
    ready, done, grad_ref, mixed_ref, h_ref, gate_ref, v_ref, ride_ref, q_ref, k_ref, out_ref
):
    ready(0, 1)
    for rows in ROWS:
        part = tn(grad_ref[:, rows], mixed_ref[...]).astype(bf16)
        out_ref[rows, 2 * KEY + 2 * VAL : 2 * KEY + 3 * VAL] = part[:, :VAL]
    ready(2, 3)
    for rows in ROWS:
        part = tn(h_ref[:, rows], gate_ref[...]).astype(bf16)
        out_ref[rows, 2 * KEY + VAL : 2 * KEY + 2 * VAL] = part[:, :VAL]
    ready(4, 5)
    for rows in ROWS:
        part = tn(h_ref[:, rows], v_ref[...]).astype(bf16)
        out_ref[rows, 2 * KEY : 2 * KEY + VAL] = part[:, :VAL]
        out_ref[rows, 2 * KEY + 3 * VAL : LATE] = ride_ref[rows, : LATE - 2 * KEY - 3 * VAL]
    ready(6, 7)
    for rows in ROWS:
        left = h_ref[:, rows]
        out_ref[rows, 0:KEY] = tn(left, q_ref[...]).astype(bf16)
        out_ref[rows, KEY : 2 * KEY] = (tn(left, k_ref[...]) * KEY**-0.5).astype(bf16)
    done(0)


def late_grads(*operands):
    return in_vmem(
        late_kernel,
        "retention_grads",
        [jax.ShapeDtypeStruct((WIDTH, LATE), bf16)],
        [],
        *operands,
    )[0]


def input_kernel(
    ready, done, gate_ref, wg_ref, v_ref, wv_ref, q_ref, k_ref, wqk_ref, own_ref, other_ref
):
    for i, rows in reversed(list(enumerate(ROWS))):
        ready(0, 1)
        part = nt(gate_ref[rows, :], wg_ref[...])
        ready(2, 3)
        part += nt(v_ref[rows, :], wv_ref[...])
        ready(4, 5, 6)
        part += nt(q_ref[rows, :], wqk_ref[:, 0:KEY])
        part += nt(k_ref[rows, :], wqk_ref[:, KEY : 2 * KEY]) * KEY**-0.5
        put_halves(done, i, part, own_ref, other_ref, 0, 1)


def back_kernel(
    ready, done, grad_ref, wo_ref, gate_ref, hat_ref, inv_ref, gain_ref, v_ref, cols_ref, line_ref,
    k_ref, turn_ref, p_ref, q_ref, wg_ref, wv_ref, wqk_ref,
    gate_out, gain_out, q_out, k_out, v_out, own_ref, other_ref, ret, scores,
):
    def numbered(call, table):
        def mapped(i, *index):
            if table[i] is not None:
                call(table[i], *index)

        return mapped

    def waits(table):
        mapped = numbered(ready, table)
        return lambda *which: [mapped(i) for i in which]

    back_gate_kernel(
        ready, numbered(done, (0, None, 1)),
        grad_ref, wo_ref, gate_ref, hat_ref, inv_ref, gain_ref, gate_out, ret, gain_out,
    )
    back_scores_kernel(
        waits((None, 6, 7, 8, 9, 10, 11, 12)), numbered(done, (2, 3, 4)),
        ret, v_ref, cols_ref, line_ref, k_ref, turn_ref, p_ref, q_ref, q_out, k_out, v_out, scores,
    )
    input_kernel(
        waits((None, 13, None, 14, None, None, 15)), numbered(done, (5, 6)),
        gate_out, wg_ref, v_out, wv_ref, q_out, k_out, wqk_ref, own_ref, other_ref,
    )


def retention_back(*operands):
    shape = jax.ShapeDtypeStruct
    return in_vmem(
        back_kernel,
        "retention_backward",
        [
            shape((WIDTH, LANES), bf16),
            shape((1, LANES), f32),
            shape((WIDTH, KEY), bf16),
            shape((WIDTH, KEY), bf16),
            shape((WIDTH, LANES), bf16),
            shape((WIDTH // 2, WIDTH), f32),
            shape((WIDTH // 2, WIDTH), bf16),
        ],
        [pltpu.VMEM((WIDTH, LANES), bf16), pltpu.VMEM((WIDTH, WIDTH), bf16)],
        *operands,
    )


def iterate_kernel(
    chunk_ref, near_ref, far_ref, out_ref, vector_ref, first_ref, whole, gram, high, low, shifted, rest, prod, prod_b, own, own_b
):
    tiles = WIDTH // NS_TILE
    at = [pl.ds(NS_TILE * i, NS_TILE) for i in range(tiles)]
    eye = (
        lax.broadcasted_iota(jnp.int32, (NS_TILE, NS_TILE), 0)
        == lax.broadcasted_iota(jnp.int32, (NS_TILE, NS_TILE), 1)
    ).astype(f32)
    keep = lax.broadcasted_iota(jnp.int32, (WIDTH, 128), 1) < VAL - 384
    riders = jnp.zeros((WIDTH, 128), f32)
    for p in range(4):
        source = near_ref if p < 2 else far_ref
        piece = source[:, p % 2].reshape(WIDTH, LANES)
        whole[p, :, 0:384] = piece[:, 0:384]
        whole[p, :, 384:512] = jnp.where(keep, piece[:, 384:512], jnp.zeros((), bf16))
        ride = piece[:, 384:512].astype(f32)
        riders += ride
        lines = ride.T
        vector_ref[2 + p : 3 + p, :] = lines[50:51, :] + lines[53:54, :]
    lines = riders.T
    vector_ref[0:2, :] = lines[48:50, :] + lines[51:53, :]
    vector_ref[6:8, :] = jnp.zeros((2, WIDTH), f32)
    first_ref[...] = jnp.sum(riders.reshape(WIDTH // BLOCK, BLOCK, 128), axis=0)

    trace = jnp.float32(0.0)
    for i in range(tiles):
        for j in range(i, tiles):
            block = jnp.zeros((NS_TILE, NS_TILE), f32)
            for p in range(4):
                block += nt(whole[p, at[i], :], whole[p, at[j], :])
            gram[at[i], at[j]] = block
            if i == j:
                trace += jnp.sum(block * eye)
    inverse = 1.0 / (jnp.sqrt(trace) + 1e-07)
    for q in range(4):

        @pl.when(chunk_ref[0] == q)
        def _():
            own[...] = whole[0, :, 128 * q : 128 * (q + 1)].astype(f32) * inverse

    def store(i, j, block, mean):
        gram[at[i], at[j]] = block
        top = block.astype(bf16)
        bottom = (block - top.astype(f32)).astype(bf16)
        high[at[i], at[j]] = top
        low[at[i], at[j]] = bottom
        if i == j:
            shifted[at[i], at[j]] = (block - mean * eye).astype(bf16)
        else:
            shifted[at[i], at[j]] = top
            top = top.T
            high[at[j], at[i]] = top
            low[at[j], at[i]] = bottom.T
            shifted[at[j], at[i]] = top

    mean = trace * inverse * inverse * (1.0 / WIDTH)
    for i in range(tiles):
        for j in range(i, tiles):
            store(i, j, gram[at[i], at[j]] * (inverse * inverse), mean)

    def advance(mean):
        level = ns_second * mean + ns_third * mean * mean
        alpha = ns_first + level
        for i in range(tiles):
            for j in range(i, tiles):
                block = (ns_second + 2.0 * ns_third * mean) * gram[at[i], at[j]] + ns_third * nn(
                    shifted[at[i], :], shifted[:, at[j]]
                )
                if i == j:
                    block -= (ns_third * mean * mean + level) * eye
                block = block.astype(bf16)
                rest[at[i], at[j]] = block
                if i < j:
                    rest[at[j], at[i]] = block.T
        values = own[...]
        top = values.astype(bf16)
        own_b[:, 0:128] = top
        own_b[:, 128:256] = (values - top.astype(f32)).astype(bf16)
        for i in range(tiles):
            moved = nn(rest[at[i], :], own_b[...])
            own[at[i], :] = alpha * own[at[i], :] + (moved[:, 0:128] + moved[:, 128:256])
        return alpha

    def turn(_, mean):
        alpha = advance(mean)
        for i in range(tiles):
            for j in range(tiles):
                block = nn(high[at[i], :], rest[:, at[j]]) + nn(low[at[i], :], rest[:, at[j]])
                prod[at[i], at[j]] = block
                prod_b[at[i], at[j]] = block.astype(bf16)
        def moved(i, j):
            return (
                (alpha * alpha) * gram[at[i], at[j]]
                + alpha * (prod[at[i], at[j]] + prod[at[j], at[i]].T)
                + nn(rest[at[i], :], prod_b[:, at[j]])
            )

        trace = jnp.float32(0.0)
        for i in range(tiles):
            block = moved(i, i)
            block = 0.5 * (block + block.T)
            gram[at[i], at[i]] = block
            trace += jnp.sum(block * eye)
        later = trace * (1.0 / WIDTH)
        for i in range(tiles):
            store(i, i, gram[at[i], at[i]], later)
            for j in range(i + 1, tiles):
                store(i, j, moved(i, j), later)
        return later

    for step in range(NS_ITERS - 1):
        mean = turn(step, mean)
    advance(mean)
    out_ref[...] = own[...].astype(bf16)


def orthogonal(chunk, near, far):
    square = (WIDTH, WIDTH)
    return pl.pallas_call(
        iterate_kernel,
        out_shape=[
            jax.ShapeDtypeStruct((WIDTH, 128), bf16),
            jax.ShapeDtypeStruct((8, WIDTH), f32),
            jax.ShapeDtypeStruct((BLOCK, 128), f32),
        ],
        in_specs=[pl.BlockSpec(memory_space=pltpu.SMEM)]
        + [pl.BlockSpec(memory_space=pltpu.VMEM)] * 2,
        out_specs=[pl.BlockSpec(memory_space=pltpu.VMEM)] * 3,
        scratch_shapes=[
            pltpu.VMEM((4, WIDTH, LANES), bf16),
            pltpu.VMEM(square, f32),
            pltpu.VMEM(square, bf16),
            pltpu.VMEM(square, bf16),
            pltpu.VMEM(square, bf16),
            pltpu.VMEM(square, bf16),
            pltpu.VMEM(square, f32),
            pltpu.VMEM(square, bf16),
            pltpu.VMEM((WIDTH, 128), f32),
            pltpu.VMEM((WIDTH, 256), bf16),
        ],
        compiler_params=pltpu.CompilerParams(vmem_limit_bytes=48 * 2**20),
        cost_estimate=pl.CostEstimate(
            flops=42 * 10**9, bytes_accessed=5 * 2**20, transcendentals=0
        ),
        name="orthogonalize",
    )(chunk, near, far)


def shards(
    tokens,
    cotangent,
    qk_w,
    vg_w,
    mlp_w,
    out_w,
    qk_mom,
    vg_mom,
    mlp_mom,
    out_mom,
    norm_params,
    norm_moment,
    norm_second,
    decay_gap,
    seq_length,
    seq_group,
):
    rows, width = tokens.shape
    slots = 4 * rows
    groups = 32
    value_width = 4 * VAL
    key_scale = KEY ** (-0.5)
    dp_index = lax.axis_index(DP)
    tensor_index = lax.axis_index(TENSOR)
    chunk_index = lax.axis_index(("y_lo", "z_hi"))

    gain_one = norm_params[0:width]
    shift_one = norm_params[width : 2 * width]
    group_gain = jnp.pad(
        lax.dynamic_slice_in_dim(norm_params, 2 * width + tensor_index * VAL, VAL),
        (0, LANES - VAL),
    )
    gain_two = norm_params[2 * width + value_width : 3 * width + value_width]
    shift_two = norm_params[3 * width + value_width : 4 * width + value_width]

    out_rows = jnp.swapaxes(out_w, 1, 2)
    first_half = lax.axis_index("y_lo") == 0

    def weight_rows(parts):
        packed = jnp.concatenate(parts, axis=1).astype(bf16)
        far = swap(packed, "y_lo")
        pair = jnp.stack([jnp.where(first_half, packed, far), jnp.where(first_half, far, packed)])
        return pair

    def weight_gather(pair):
        return lax.all_gather(pair, PLANE, axis=1, tiled=True).reshape(width, -1)

    pair_ret = weight_rows(
        [
            pairs_apart(qk_w[0]),
            pairs_apart(qk_w[1]),
            widen(vg_w[0]),
            widen(vg_w[1]),
            widen(out_rows[0]),
        ]
    )
    (tokens_first, mlp_later), pair_ret = together((tokens, mlp_w), pair_ret)
    gathered = weight_gather(pair_ret)
    w_qk, w_v, w_g, w_o = ((gathered, LANES * i, LANES) for i in range(4))
    pair_ff = weight_rows([widen(mlp_later[0]), widen(mlp_later[1]), widen(out_rows[1])])

    whole_tokens = jnp.concatenate(tensor_gather(tokens_first), axis=0)
    order = jnp.stack([tensor_index, tensor_index ^ 2, tensor_index ^ 1, tensor_index ^ 3])
    place = (order[:, None] * rows + jnp.arange(rows, dtype=jnp.int32)[None, :]).reshape(slots)

    freqs = 1.0 / 10000.0 ** np.linspace(0.0, 1.0, KEY // 2)
    angles = np.arange(slots)[:, None] * freqs[None, :]
    tables = jnp.asarray(
        np.concatenate([np.cos(angles), np.sin(angles)], axis=1).astype(np.float32)
    ).reshape(4, rows, KEY)
    turned = tables[order].reshape(slots, KEY)

    labels = sequence_labels(seq_length, seq_group, dp_index, place)
    log_decay = jnp.log1p(-decay_gap[0])
    away = (place - slots // 2).astype(f32) * log_decay
    label_place = [labels.astype(f32), place.astype(f32)]
    columns = jnp.pad(jnp.stack(label_place + [jnp.exp(away)], axis=1), ((0, 0), (0, 125)))
    line = jnp.pad(jnp.stack(label_place + [jnp.exp(-away)], axis=0), ((0, 5), (0, 0)))
    gain_line = group_gain[None, :]

    hat_one, _ = normalize(whole_tokens.astype(f32))
    whole_one = (hat_one * gain_one + shift_one).astype(bf16)
    prepared = (whole_one, turned, columns, line)
    cot_first, (whole_one, turned, columns, line) = together(cotangent, prepared)
    whole_cot = tensor_gather(cot_first)
    (gain_line, pair_ff), whole_cot = together((gain_line, pair_ff), whole_cot)
    whole_cot = [(part, 0, width) for part in whole_cot]
    gathered_ff = weight_gather(pair_ff)
    w_1, w_2, w_3 = ((gathered_ff, LANES * i, LANES) for i in range(3))
    query, keys, values, weights, gate, hat_group, inv_group, mixed, own, other = retention(
        whole_one, w_qk, w_v, w_g, w_o, turned, columns, line, gain_line
    )
    near, far = tensor_sum(own, other)
    middle = tokens.astype(f32) + near + far.astype(f32)
    hat_two, inv_two = normalize(middle)
    whole_two = tensor_gather((hat_two * gain_two + shift_two).astype(bf16))
    hidden, grad_gate, grad_up, own, other = feed(whole_two, w_1, w_2, whole_cot, w_3)
    near, far = tensor_sum(own, other)
    early, out_own, out_other = early_grads(whole_two, grad_gate, grad_up, whole_cot, hidden, w_3)
    far, out_other = together(far, out_other)
    grad_normed_two = near + far.astype(f32)
    grad_middle = cotangent.astype(f32) + norm_back(grad_normed_two, gain_two, hat_two, inv_two)
    grad_first = grad_middle.astype(bf16)
    grad_far, grad_core = swap(grad_first, "y_hi"), swap(grad_first, "core")
    out_near, out_far = half_sum(out_own, out_other)
    grad_far, out_far = together(grad_far, out_far)
    grad_one = [grad_first, grad_far, grad_core, swap(grad_far, "core")]

    early_in = lax.all_to_all(early, PLANE, split_axis=0, concat_axis=0, tiled=True)
    early_halves = jnp.sum(early_in.astype(f32), axis=0)
    early_far = swap(
        jnp.where(first_half, early_halves[1], early_halves[0]).astype(bf16), "y_lo"
    )
    gain_two_grad = jnp.sum(grad_normed_two * hat_two, axis=0)
    shift_two_grad = jnp.sum(grad_normed_two, axis=0)

    grad_gate_ret, group_gain_grad, grad_query, grad_key, grad_values, own, other = retention_back(
        grad_one, w_o, gate, hat_group, inv_group, gain_line, values, columns, line, keys, turned,
        weights, query, w_g, w_v, w_qk,
    )
    other, grad_values = together(other, grad_values)
    small = jnp.stack(
        [gain_two_grad, shift_two_grad, jnp.pad(group_gain_grad[0], (0, width - LANES))], axis=1
    )
    small_high, small_low = split(small)
    riders = jnp.pad(
        jnp.concatenate([small_high, small_low], axis=1), ((0, 0), (0, 128 - 6))
    )
    arrived, riders = together(swap(other, "core"), riders)
    half = slots // 2 // 2
    near = own[:half] + arrived[:half].astype(f32)
    far = (own[half:] + arrived[half:].astype(f32)).astype(bf16)
    late = late_grads(
        grad_one, mixed, whole_one, grad_gate_ret, grad_values, riders, grad_query, grad_key
    )
    far = swap(far, "y_hi")
    far, late = together(far, late)
    grad_normed_one = near + far.astype(f32)
    late_in = lax.all_to_all(
        late.reshape(groups, BLOCK, -1), DP, split_axis=0, concat_axis=0, tiled=True
    )
    own_hat, own_inv = normalize(tokens.astype(f32))
    gain_one_grad = jnp.sum(grad_normed_one * own_hat, axis=0)
    shift_one_grad = jnp.sum(grad_normed_one, axis=0)
    input_grad = grad_middle + norm_back(grad_normed_one, gain_one, own_hat, own_inv)
    (gain_one_grad, input_grad), early_far = together((gain_one_grad, input_grad), early_far)
    early_sum = jnp.where(first_half, early_halves[0], early_halves[1]) + early_far.astype(f32)

    late_sum = jnp.sum(late_in.astype(f32), axis=0)
    first_value = 2 * KEY
    at = [first_value + VAL * i for i in range(4)]
    small_sum = late_sum[:, at[3] : at[3] + 6]
    small_sum = small_sum[:, :3] + small_sum[:, 3:]

    grad_qk = pairs_together(jnp.stack([late_sum[:, 0:256], late_sum[:, 256:512]]))
    grad_vg = jnp.stack([late_sum[:, at[0] : at[1]], late_sum[:, at[1] : at[2]]])
    grad_mlp = jnp.stack([early_sum[:, 0:VAL], early_sum[:, VAL : 2 * VAL]])
    grad_out_t = jnp.stack([late_sum[:, at[2] : at[3]], early_sum[:, 2 * VAL : 3 * VAL]])
    mom_qk = muon_beta * qk_mom + grad_qk
    mom_vg = muon_beta * vg_mom + grad_vg
    mom_mlp = muon_beta * mlp_mom + grad_mlp
    mom_out = muon_beta * out_mom + jnp.swapaxes(grad_out_t, 1, 2)

    piece_high, piece_low = split(small_sum)
    first_norm = jnp.concatenate([gain_one_grad, shift_one_grad]).astype(bf16)
    extra = jnp.pad(
        jnp.concatenate([piece_high, piece_low, first_norm.reshape(BLOCK, 64)], axis=1),
        ((0, 0), (VAL, LANES - VAL - 70)),
    )
    stacked = (
        jnp.concatenate(
            [widen(mom_qk), widen(mom_vg), widen(mom_mlp), widen(jnp.swapaxes(mom_out, 1, 2))],
            axis=0,
        ).astype(bf16)
        + extra[None]
    )
    both = jnp.stack([stacked, swap(stacked, "y_hi")], axis=1)
    spread = jnp.broadcast_to(both[None], (4,) + both.shape).reshape((groups,) + both.shape[1:])
    arrived = lax.all_to_all(spread, DP, split_axis=0, concat_axis=0, tiled=True)
    far = swap(arrived, "core")
    own, vectors, first_total = orthogonal(
        jnp.reshape(chunk_index, (1,)).astype(jnp.int32), arrived, far
    )
    out_far = swap(out_far, "y_hi")
    out_far, own = together(out_far, own)
    result = (middle + out_near + out_far.astype(f32)).astype(bf16)
    returned = lax.all_to_all(
        own.reshape(groups, BLOCK, 128), DP, split_axis=0, concat_axis=0, tiled=True
    ).astype(f32)
    returned = jnp.concatenate([returned[8 * i : 8 * i + 8] for i in range(4)], axis=2)

    shrink = 1.0 - muon_rate * decay_rate
    square_scale = 0.2 * math.sqrt(width)
    wide_scale = 0.2 * math.sqrt(max(width, value_width))
    new_qk = qk_w * shrink - (muon_rate * square_scale) * returned[0:2, :, :KEY]
    new_vg = vg_w * shrink - (muon_rate * wide_scale) * returned[2:4, :, :VAL]
    new_mlp = mlp_w * shrink - (muon_rate * wide_scale) * returned[4:6, :, :VAL]
    new_out = out_w * shrink - (muon_rate * wide_scale) * jnp.swapaxes(returned[6:8, :, :VAL], 1, 2)

    first_total = first_total[:, 54:118].reshape(2 * width)
    group_parts = vectors[2:6, :VAL]
    which = jnp.arange(4, dtype=jnp.int32)[:, None] == order[None, :]
    group_whole = jnp.sum(
        jnp.where(which[:, :, None], group_parts[None], 0.0), axis=1
    ).reshape(value_width)
    small_total = jnp.concatenate(
        [first_total, group_whole, vectors[0], vectors[1]]
    )
    moment_new = beta_first * norm_moment + (1.0 - beta_first) * small_total
    second_new = beta_second * norm_second + (1.0 - beta_second) * small_total * small_total
    params_new = norm_params - adam_rate * (moment_new / (1.0 - beta_first**OPT_STEP)) / (
        jnp.sqrt(second_new / (1.0 - beta_second**OPT_STEP)) + adam_eps
    )
    return (
        result,
        input_grad,
        mom_qk,
        mom_vg,
        mom_mlp,
        mom_out,
        new_qk,
        new_vg,
        new_mlp,
        new_out,
        moment_new,
        second_new,
        params_new,
    )


def solution(mesh):
    fine = Mesh(np.asarray(mesh.devices).reshape(SIZES), AXES)
    by_rows = P(DP + TENSOR, None)
    by_columns = P(None, DP, TENSOR)
    by_out = P(None, TENSOR, DP)
    return jax.shard_map(
        shards,
        mesh=fine,
        in_specs=(
            by_rows,
            by_rows,
            by_columns,
            by_columns,
            by_columns,
            by_out,
            by_columns,
            by_columns,
            by_columns,
            by_out,
            P(),
            P(),
            P(),
            P(TENSOR),
            P(),
            P(),
        ),
        out_specs=(
            by_rows,
            by_rows,
            by_columns,
            by_columns,
            by_columns,
            by_out,
            by_columns,
            by_columns,
            by_columns,
            by_out,
            P(),
            P(),
            P(),
        ),
        check_vma=False,
    )
```
